32 devices in a mesh: band: 4 (over z), row: 2 (over x), col: 4 (over y, core).
Axes of the slice: x: 2, y: 2, z: 4, core: 2. Of those that a mesh axis runs over, the one named last changes fastest.
Arguments:
- spectral_cube: bfloat16 [88, 8, 4096], P('band', ('row', 'col')), may hold values from -6 to 6
- aperture: int32 [8, 4096], P(('row', 'col')), may hold values 0 or 1
- measurement: float32 [8, 4444], P(('row', 'col')), may hold values from -48 to 48
- shears: int32 [88], P('band'), may hold values from 0 to 348, as said below
- step_sizes: float32 [88], P('band'), may hold values from 0.5 to 2
- spatial_weight: bfloat16 [16, 9], replicated, may hold values from -2 to 2
- spatial_bias: float32 [16], replicated, may hold values from -3 to 3
- spectral_weight: bfloat16 [7, 16, 16], replicated, may hold values from -0.5 to 0.5
- spectral_bias: float32 [16], replicated, may hold values from -3 to 3
- out_weight: float32 [16], replicated, may hold values from -1.5 to 1.5
Outputs:
- denoised: bfloat16 [88, 8, 4096], P('band', ('row', 'col'))
The draws below stay inside these ranges and needn't reach their ends.
Inputs may be any that keep to these rules, and one draw needn't show every extreme that they name: `shears`: strictly increasing over the bands, the first 0 and the last 348.
All inputs are finite; a program needn't handle non-finite values. No bound on the sum of `aperture` on one device may be relied on, other than what follows from the above.
Results may differ from the reference program's by a relative error of at most 0.0047.
Values may be sent and summed in bfloat16 or wider, within the bound.
No kernel may reach another device: no remote copies, remote signals or barrier semaphores. Data moves between devices by JAX's collectives and lax.ppermute only.
A program may use at most 64 MiB of HBM per device.

```python
import math
import jax
import jax.numpy as jnp
from jax import lax

COLS = 4096
CH = 16
TAPS = 7
BANDS = 88
SHEAR = 348
ROWS = 8


def draw_shears(key, part):
    gaps = BANDS - 1
    base_step = SHEAR // gaps
    extra = SHEAR - base_step * gaps
    quarter = gaps // 4
    ranks = jax.random.permutation(key, gaps)
    change = jnp.where(ranks < quarter, 1, jnp.where(ranks < 2 * quarter, -1, 0))
    last_extra = jnp.where(jnp.arange(gaps) == gaps - 1, extra, 0)
    increments = (base_step + change + last_extra).astype(jnp.int32)
    return jnp.concatenate([jnp.zeros((1,), jnp.int32), jnp.cumsum(increments).astype(jnp.int32)])


def with_ends(result, stream_key, low, high):
    shape = result.shape
    spot = [jax.random.randint(jax.random.fold_in(stream_key, axis), (), 0, shape[axis]) for axis in range(len(shape))]
    result = result.at[tuple(spot)].set(low)
    longest = shape.index(max(shape))
    spot[longest] = (spot[longest] + 1) % shape[longest]
    return result.at[tuple(spot)].set(high)


def steps_of(stream_key, shape, cuts, least, largest):
    def one(position, blocks):
        steps = jax.random.uniform(jax.random.fold_in(jax.random.fold_in(stream_key, 6), position), (blocks,), jnp.float32, least / len(cuts), largest / len(cuts))
        return jnp.repeat(jnp.exp(steps), shape[position] // blocks).reshape((-1,) + (1,) * (len(shape) - position - 1))

    factor_of = one(*cuts[0])
    for cut in cuts[1:]:
        factor_of = factor_of * one(*cut)
    return factor_of


def normal_values(key, dims, spread, reach, cuts=(), kind=jnp.bfloat16):
    entries = spread * jax.random.normal(key, dims, jnp.float32)
    if cuts:
        entries = entries * steps_of(key, dims, cuts, -0.22, 0.18)
    return jnp.clip(entries, -reach, reach).astype(kind)


def setup_inputs(seed: int = 0) -> dict:
    seeds = jax.random.split(jax.random.key(seed), 11)
    return {
        "spectral_cube": normal_values(seeds[0], (BANDS, ROWS, COLS), 1.0, 6.0, ((0, 4), (1, 8))),
        "aperture": with_ends((jax.random.randint(seeds[1], (ROWS, COLS), 0, 2) < 1).astype(jnp.int32), jax.random.fold_in(seeds[1], 1), 0, 1),
        "measurement": normal_values(seeds[2], (ROWS, COLS + SHEAR), 8.0, 48.0, ((0, 8),), jnp.float32),
        "shears": draw_shears(jax.random.fold_in(seeds[10], 71), 0),
        "step_sizes": jnp.clip(jnp.exp(math.log(2.0) - 1.3862944 * jax.random.uniform(seeds[4], (BANDS,), jnp.float32) ** steps_of(seeds[4], (BANDS,), ((0, 4),), -0.2, 0.2)), 0.5, 2.0),
        "spatial_weight": normal_values(seeds[5], (CH, 9), 9 ** -0.5, 2.0),
        "spatial_bias": normal_values(seeds[6], (CH,), 0.5, 3.0, (), jnp.float32),
        "spectral_weight": normal_values(seeds[7], (TAPS, CH, CH), (TAPS * CH) ** -0.5, 0.5),
        "spectral_bias": normal_values(seeds[8], (CH,), 0.5, 3.0, (), jnp.float32),
        "out_weight": normal_values(seeds[9], (CH,), CH ** -0.5, 1.5, (), jnp.float32),
    }


def denoise(padded, band_start, total_bands, block_width, spatial_weight, spatial_bias, spectral_weight, spectral_bias, out_weight):
    bands_in, rows_pad, cols_pad = padded.shape
    row_count = rows_pad - 2
    col_count = cols_pad - 2
    bands_out = bands_in - 6
    across = col_count // block_width
    band_ids = band_start + jnp.arange(bands_in, dtype=jnp.int32)
    band_valid = (band_ids >= 0) & (band_ids < total_bands)
    weight_f = out_weight.astype(jnp.float32)

    def one_block(block_index):
        row_index = block_index // across
        col_start = (block_index % across) * block_width
        window = lax.dynamic_slice(padded, (jnp.int32(0), row_index, col_start), (bands_in, 3, block_width + 2))
        patches = jnp.stack([window[:, i, j:j + block_width] for i in range(3) for j in range(3)])
        spatial_out = jnp.einsum("kq,qbc->kbc", spatial_weight, patches, preferred_element_type=jnp.float32) + spatial_bias[:, None, None]
        active = jnp.where(band_valid[None, :, None], jax.nn.silu(spatial_out), 0.0).astype(jnp.bfloat16)
        second = jnp.zeros((spatial_out.shape[0], bands_out, block_width), jnp.float32) + spectral_bias[:, None, None]
        for d in range(spectral_weight.shape[0]):
            second = second + jnp.einsum("kj,jbc->kbc", spectral_weight[d], active[:, d:d + bands_out], preferred_element_type=jnp.float32)
        update_term = jnp.einsum("k,kbc->bc", weight_f, jax.nn.silu(second), precision=lax.Precision.HIGHEST)
        center = window[3:3 + bands_out, 1, 1:1 + block_width].astype(jnp.float32)
        return (center + update_term).astype(jnp.bfloat16)

    blocks = lax.map(one_block, jnp.arange(row_count * across, dtype=jnp.int32))
    return blocks.reshape(row_count, across, bands_out, block_width).transpose(2, 0, 1, 3).reshape(bands_out, row_count, col_count)


def reference(spectral_cube, aperture, measurement, shears, step_sizes, spatial_weight, spatial_bias, spectral_weight, spectral_bias, out_weight):
    detector_width = COLS + SHEAR
    aperture_f = aperture.astype(jnp.float32)
    masked = spectral_cube.astype(jnp.float32) * aperture_f[None]

    def place(carry, inputs):
        band_layer, offset = inputs
        empty_plane = jnp.zeros((ROWS, detector_width), jnp.float32)
        placed_band = lax.dynamic_update_slice(empty_plane, band_layer, (jnp.int32(0), offset))
        opened = lax.dynamic_update_slice(empty_plane, aperture_f, (jnp.int32(0), offset))
        return (carry[0] + placed_band, carry[1] + opened), None

    start_sums = (jnp.zeros((ROWS, detector_width), jnp.float32), jnp.zeros((ROWS, detector_width), jnp.float32))
    (predicted, counts), _ = lax.scan(place, start_sums, (masked, shears))
    residual = (measurement - predicted) / jnp.maximum(counts, 1.0)

    def adjoint(inputs):
        offset, step_one = inputs
        pulled = lax.dynamic_slice(residual, (jnp.int32(0), offset), (ROWS, COLS))
        return pulled * aperture_f * step_one

    updates = lax.map(adjoint, (shears, step_sizes))
    updated = (spectral_cube.astype(jnp.float32) + updates).astype(jnp.bfloat16)
    padded = jnp.pad(updated, ((3, 3), (1, 1), (1, 1)))
    return denoise(padded, -3, BANDS, COLS, spatial_weight, spatial_bias, spectral_weight, spectral_bias, out_weight)
```

```python
import functools

import jax
import jax.numpy as jnp
from jax import lax
from jax.experimental import pallas as pl
from jax.experimental.pallas import tpu as pltpu
from jax.sharding import PartitionSpec as P

LANES = 128
SUB = 8
F32 = jnp.float32
BF16 = jnp.bfloat16
I32 = jnp.int32


def lanes_of(shape=(SUB, LANES)):
    return lax.broadcasted_iota(I32, shape, 1)


def rows_of(shape=(SUB, LANES)):
    return lax.broadcasted_iota(I32, shape, 0)


def column(row, rows):
    n = row.shape[1]
    eye = rows_of((rows, n)) == lanes_of((rows, n))
    return jnp.sum(jnp.where(eye, jnp.broadcast_to(row, (rows, n)), 0.0), axis=1, keepdims=True)


def turn(chunk, index):
    return jnp.take_along_axis(chunk, index, axis=1, mode="promise_in_bounds")


def choose(delay, options):
    result = options[-1]
    for d in range(len(options) - 2, -1, -1):
        result = jnp.where(delay == d, options[d], result)
    return result


def split3(x):
    hi = x.astype(BF16).astype(F32)
    mid = (x - hi).astype(BF16).astype(F32)
    return hi, mid, x - hi - mid


def project_kernel(reach, cube_ref, ap_ref, shear_ref, step_ref, up_ref, dn_ref, raw):
    bands, cols = cube_ref.shape
    groups = -(-bands // SUB)
    inner = cols // LANES
    outer = up_ref.shape[1] // LANES
    raw[bands // SUB * SUB :, :] = jnp.zeros((raw.shape[0] - bands // SUB * SUB, cols), F32)
    raw[0:bands, :] = cube_ref[...].astype(F32)
    shear_f = column(shear_ref[...].astype(F32), groups * SUB)
    step_f = column(step_ref[...], groups * SUB)
    shear_i = shear_f.astype(I32)
    lane, sub = lanes_of(), rows_of()
    index, delay = [], []
    for g in range(groups):
        s = jnp.broadcast_to(shear_i[g * SUB : (g + 1) * SUB], (SUB, LANES))
        rest = s & (LANES - 1)
        index.append((lane - rest) & (LANES - 1))
        delay.append((s >> 7) + jnp.where(lane < rest, 1, 0))
    zero = jnp.zeros((SUB, LANES), F32)
    turned = [[zero] * (reach - 1) for _ in range(groups)]
    opened = [[zero] * (reach - 1) for _ in range(groups)]
    low_first = (bands - 3) % SUB
    for p in range(outer):
        total = zero
        count = zero
        if p < inner:
            open_p = jnp.broadcast_to(
                ap_ref[:, p * LANES : (p + 1) * LANES].astype(F32), (SUB, LANES)
            )
            layers = [
                raw[g * SUB : (g + 1) * SUB, p * LANES : (p + 1) * LANES] for g in range(groups)
            ]
        for g in range(groups):
            if p < inner:
                here = turn(layers[g] * open_p, index[g])
                here_open = turn(open_p, index[g])
            else:
                here = here_open = zero
            options = [here] + turned[g]
            options_open = [here_open] + opened[g]
            turned[g] = options[:-1]
            opened[g] = options_open[:-1]
            total = total + choose(delay[g], options)
            part = choose(delay[g], options_open)
            if (g + 1) * SUB > bands:
                part = jnp.where(sub < bands - g * SUB, part, 0.0)
            count = count + part
        predicted = jnp.sum(total, axis=0, keepdims=True)
        hi = predicted.astype(BF16).astype(F32)
        lo = predicted - hi
        counts = jnp.sum(count, axis=0, keepdims=True)
        if p < inner:
            first, last = layers[0], layers[-1]
        elif p == inner:
            sides = []
            for g in (0, groups - 1):
                s = shear_i[g * SUB : (g + 1) * SUB]
                parts = [(s >> 1).astype(F32), (s & 1).astype(F32)]
                parts += list(split3(step_f[g * SUB : (g + 1) * SUB]))
                side = zero
                for i, part in enumerate(parts):
                    side = jnp.where(lane == i, part, side)
                sides.append(side)
            first, last = sides
        else:
            first = last = zero
        up = jnp.where((sub >= low_first) & (sub < low_first + 3), last, 0.0)
        dn = jnp.where(sub < 3, first, 0.0)
        for i, value in enumerate((hi, lo, counts)):
            up = jnp.where(sub == i, value, up)
            dn = jnp.where(sub == 3 + i, value, dn)
        up_ref[:, p * LANES : (p + 1) * LANES] = up.astype(BF16)
        dn_ref[:, p * LANES : (p + 1) * LANES] = dn.astype(BF16)


def update_kernel(
    reach,
    fars,
    cube_ref,
    ap_ref,
    meas_ref,
    shear_ref,
    step_ref,
    own_ref,
    below_ref,
    above_ref,
    *rest_refs,
):
    far_refs = rest_refs[:fars]
    out_ref, raw, meas = rest_refs[fars:]
    bands, cols = cube_ref.shape
    groups = -(-bands // SUB)
    inner = cols // LANES
    outer = own_ref.shape[1] // LANES
    raw[bands // SUB * SUB :, :] = jnp.zeros((raw.shape[0] - bands // SUB * SUB, cols), F32)
    raw[0:bands, :] = cube_ref[...].astype(F32)
    meas[:, (outer - 1) * LANES :] = jnp.zeros((1, LANES), F32)
    meas[:, 0 : meas_ref.shape[1]] = meas_ref[...]
    shear_f = column(shear_ref[...].astype(F32), groups * SUB)
    step_f = column(step_ref[...], groups * SUB)
    lane, sub = lanes_of(), rows_of()

    def halo(p):
        where = slice(p * LANES, (p + 1) * LANES)
        return jnp.where(sub < 3, above_ref[:, where].astype(F32), below_ref[:, where].astype(F32))

    side = halo(inner)
    shear_cols = [shear_f[g * SUB : (g + 1) * SUB] for g in range(groups)]
    step_cols = [step_f[g * SUB : (g + 1) * SUB] for g in range(groups)]
    inside = rows_of((SUB, 1)) < 6
    shear_cols.append(jnp.where(inside, 2.0 * side[:, 0:1] + side[:, 1:2], 0.0))
    step_cols.append(jnp.where(inside, side[:, 2:3] + side[:, 3:4] + side[:, 4:5], 0.0))
    index, delay, steps = [], [], []
    for g in range(groups + 1):
        s = jnp.broadcast_to(shear_cols[g].astype(I32), (SUB, LANES))
        rest = s & (LANES - 1)
        index.append((lane + rest) & (LANES - 1))
        delay.append((s >> 7) + jnp.where(lane + rest >= LANES, 1, 0))
        steps.append(jnp.broadcast_to(step_cols[g], (SUB, LANES)))
    turned = [[] for _ in range(groups + 1)]
    for p in range(outer + 1):
        if p < outer:
            where = slice(p * LANES, (p + 1) * LANES)
            up_sum = own_ref[:, where].astype(F32) + below_ref[:, where].astype(F32)
            for far in far_refs:
                up_sum = up_sum + far[:, where].astype(F32)
            dn_sum = above_ref[:, where].astype(F32)
            predicted = up_sum[0:1] + up_sum[1:2] + dn_sum[3:4] + dn_sum[4:5]
            counts = up_sum[2:3] + dn_sum[5:6]
            residual = (meas[:, where] - predicted) / jnp.maximum(counts, 1.0)
            residual = jnp.broadcast_to(residual, (SUB, LANES))
        else:
            residual = jnp.zeros((SUB, LANES), F32)
        for g in range(groups + 1):
            turned[g].append(turn(residual, index[g]) if p < outer else residual)
        q = p - (reach - 1)
        if q < 0 or q >= inner:
            continue
        here = slice(q * LANES, (q + 1) * LANES)
        open_q = jnp.broadcast_to(ap_ref[:, here].astype(F32), (SUB, LANES))
        pieces = []
        for g in range(groups + 1):
            pulled = choose(delay[g], turned[g][q : q + reach])
            base = raw[g * SUB : (g + 1) * SUB, here] if g < groups else halo(q)
            if g == groups:
                base = jnp.where(sub < 6, base, 0.0)
            pieces.append(base + pulled * open_q * steps[g])
        out_ref[:, here] = jnp.concatenate(pieces, axis=0).astype(BF16)


def weights_kernel(edge_ref, sw_ref, sb_ref, cw_ref, cb_ref, main_ref, halo_ref, band_ref):
    ch, taps2 = sw_ref.shape
    taps = cw_ref.shape[0]

    def spread(rows, which):
        return (which(rows_of((rows, ch))) == lanes_of((rows, ch))).astype(F32).astype(BF16)

    def bias_column(row_ref, rows, which):
        pick = which(rows_of((rows, ch))) == lanes_of((rows, ch))
        row = jnp.broadcast_to(row_ref[...], (rows, ch))
        return 0.5 * jnp.sum(jnp.where(pick, row, 0.0), axis=1, keepdims=True)

    def with_bias(matrix, bias, start):
        lane = lanes_of(matrix.shape)
        for i, part in enumerate(split3(bias)):
            matrix = jnp.where(lane == start + i, part, matrix)
        return matrix

    width = main_ref.shape[1]
    slots = 16
    fan = (lanes_of((taps2, width)) // slots == rows_of((taps2, width))).astype(F32).astype(BF16)
    flat = jnp.dot(sw_ref[...], fan, preferred_element_type=F32).astype(BF16)
    for ref, slot_of in (
        (main_ref, lambda b: b),
        (halo_ref, lambda b: jnp.where(b < 3, 11 + b, jnp.where(b < 9, b - 3, b - 1))),
    ):
        rows = ref.shape[0]
        which = lambda r: r % ch
        full = jnp.dot(spread(rows, which), flat, preferred_element_type=F32)
        lane = lanes_of((rows, width))
        band = rows_of((rows, width)) // ch
        keep = (lane % slots == slot_of(band)) & (lane < taps2 * slots)
        matrix = with_bias(
            jnp.where(keep, 0.5 * full, 0.0), bias_column(sb_ref, rows, which), taps2 * slots
        )
        if ref is halo_ref:
            valid = jnp.where(band < 3, edge_ref[0], jnp.where(band >= 9, edge_ref[1], 1))
            matrix = jnp.where(valid > 0, matrix, 0.0)
        ref[...] = matrix.astype(BF16)

    rows, width = band_ref.shape
    per = rows // ch
    used = (per + taps - 1) * ch
    which = lambda r: r // per
    fan = (lanes_of((ch, width)) % ch == rows_of((ch, width))).astype(F32).astype(BF16)
    picks = spread(rows, which)
    lane = lanes_of((rows, width))
    ahead = lane // ch - rows_of((rows, width)) % per
    matrix = jnp.zeros((rows, width), F32)
    for d in range(taps):
        flat = jnp.dot(cw_ref[d], fan, preferred_element_type=F32).astype(BF16)
        full = jnp.dot(picks, flat, preferred_element_type=F32)
        matrix = jnp.where(ahead == d, 0.5 * full, matrix)
    matrix = jnp.where(lane < used, matrix, 0.0)
    matrix = with_bias(matrix, bias_column(cb_ref, rows, which), used)
    band_ref[...] = matrix.astype(BF16)


def denoise_kernel(
    tile, ow_ref, up_ref, mid_ref, dn_ref, main_ref, halo_ref, band_ref, out_ref, act
):
    bands, cols = out_ref.shape
    slots = 16
    ch = ow_ref.shape[0]
    tiles = cols // tile
    wide = tile + 2 * LANES
    rows = act.shape[0]
    act[rows - 2 * slots :, :] = jnp.zeros((2 * slots, tile), BF16)
    ones = jnp.where(rows_of((slots, tile)) < 3, 1.0, 0.0).astype(BF16)

    def silu_twice(half):
        return half + half * jnp.tanh(half)

    def body(t, carry):
        start = pl.multiple_of(t * tile, LANES)
        before = pl.multiple_of(jnp.maximum(start - LANES, 0), LANES)
        after = pl.multiple_of(jnp.minimum(start + tile, cols - LANES), LANES)
        patches = []
        center = None
        for ref in (up_ref, mid_ref, dn_ref):
            left = ref[:, pl.ds(before, LANES)].astype(F32)
            here = ref[:, pl.ds(start, tile)]
            right = ref[:, pl.ds(after, LANES)].astype(F32)
            left = jnp.where(t > 0, left, 0.0)
            right = jnp.where(t < tiles - 1, right, 0.0)
            here_f = here.astype(F32)
            row = jnp.concatenate([left, here_f, right], axis=1)
            back = pltpu.roll(row, 1, 1)[:, LANES : LANES + tile].astype(BF16)
            ahead = pltpu.roll(row, wide - 1, 1)[:, LANES : LANES + tile].astype(BF16)
            patches += [back, here, ahead]
            if ref is mid_ref:
                center = here_f
        for part, w_ref in enumerate((main_ref, halo_ref)):
            x = jnp.concatenate(
                [p[part * slots : (part + 1) * slots] for p in patches] + [ones], axis=0
            )
            half = jnp.dot(w_ref[...], x, preferred_element_type=F32)
            value = silu_twice(half).astype(BF16)
            if part == 0:
                act[3 * ch : 19 * ch, :] = value
            else:
                act[0 : 3 * ch, :] = value[0 : 3 * ch]
                act[19 * ch : 28 * ch, :] = value[3 * ch :]
        weights = band_ref[...]
        per = weights.shape[0] // ch
        used = (per + 6) * ch
        pieces = []
        for i in range(-(-bands // per)):
            x = jnp.concatenate([act[i * per * ch : i * per * ch + used, :], ones], axis=0)
            half = jnp.dot(weights, x, preferred_element_type=F32)
            total = center[i * per : (i + 1) * per]
            for k in range(ch):
                total = total + ow_ref[k] * silu_twice(half[k * per : (k + 1) * per])
            pieces.append(total)
        result = jnp.concatenate(pieces, axis=0)[0:bands]
        out_ref[:, pl.ds(start, tile)] = result.astype(BF16)
        return carry

    lax.fori_loop(0, tiles, body, 0)


def vmem(n):
    return [pl.BlockSpec(memory_space=pltpu.VMEM)] * n


SMEM = pl.BlockSpec(memory_space=pltpu.SMEM)


def on_device(
    spectral_cube,
    aperture,
    measurement,
    shears,
    step_sizes,
    spatial_weight,
    spatial_bias,
    spectral_weight,
    spectral_bias,
    out_weight,
):
    bands, row_count, cols = spectral_cube.shape
    width = measurement.shape[1]
    reach = (width - cols) // LANES + 2
    outer = -(-width // LANES)
    groups = -(-bands // SUB)
    slots = (groups + 1) * SUB
    taps, ch = spectral_weight.shape[:2]
    taps2 = spatial_weight.shape[1]
    count = lax.axis_size("band")
    place = lax.axis_index("band")
    cube = spectral_cube.reshape(bands, cols)
    shear_row = shears.reshape(1, bands)
    step_row = step_sizes.reshape(1, bands)
    params = pltpu.CompilerParams(vmem_limit_bytes=48 * 2**20)

    payload = jax.ShapeDtypeStruct((SUB, outer * LANES), BF16)
    up, dn = pl.pallas_call(
        functools.partial(project_kernel, reach),
        out_shape=(payload, payload),
        in_specs=vmem(4),
        out_specs=tuple(vmem(2)),
        scratch_shapes=[pltpu.VMEM((groups * SUB, cols), F32)],
        compiler_params=params,
        name="project",
    )(cube, aperture, shear_row, step_row)

    def around(x, shift):
        return lax.ppermute(x, "band", [(i, (i + shift) % count) for i in range(count)])

    below = around(up, 1)
    above = around(dn, -1)
    far = [around(up, s) for s in range(2, count - 1)]

    edges = jnp.stack([place > 0, place < count - 1]).astype(I32)
    used = taps2 * 16
    main_w, halo_w, band_w = pl.pallas_call(
        weights_kernel,
        out_shape=(
            jax.ShapeDtypeStruct((16 * ch, used + 16), BF16),
            jax.ShapeDtypeStruct((12 * ch, used + 16), BF16),
            jax.ShapeDtypeStruct((SUB * ch, (SUB + taps - 1) * ch + 16), BF16),
        ),
        in_specs=[SMEM] + vmem(4),
        out_specs=tuple(vmem(3)),
        compiler_params=params,
        name="weights",
    )(
        edges,
        spatial_weight,
        spatial_bias.reshape(1, ch),
        spectral_weight,
        spectral_bias.reshape(1, ch),
    )

    updated = pl.pallas_call(
        functools.partial(update_kernel, reach, len(far)),
        out_shape=jax.ShapeDtypeStruct((slots, cols), BF16),
        in_specs=vmem(8 + len(far)),
        out_specs=vmem(1)[0],
        scratch_shapes=[
            pltpu.VMEM((groups * SUB, cols), F32),
            pltpu.VMEM((1, outer * LANES), F32),
        ],
        compiler_params=params,
        name="update",
    )(cube, aperture, measurement, shear_row, step_row, up, below, above, *far)

    lines = lax.axis_size(("row", "col"))
    over = lax.ppermute(updated, ("row", "col"), [(i, i + 1) for i in range(lines - 1)])
    under = lax.ppermute(updated, ("row", "col"), [(i + 1, i) for i in range(lines - 1)])

    tile = 512
    result = pl.pallas_call(
        functools.partial(denoise_kernel, tile),
        out_shape=jax.ShapeDtypeStruct((bands, cols), BF16),
        in_specs=[SMEM] + vmem(6),
        out_specs=vmem(1)[0],
        scratch_shapes=[pltpu.VMEM((30 * ch, tile), BF16)],
        compiler_params=params,
        name="denoise",
    )(out_weight, over, updated, under, main_w, halo_w, band_w)
    return result.reshape(bands, 1, cols)


def solution(mesh):
    in_specs = (
        P("band", ("row", "col"), None),
        P(("row", "col"), None),
        P(("row", "col"), None),
        P("band"),
        P("band"),
        P(),
        P(),
        P(),
        P(),
        P(),
    )
    out_specs = P("band", ("row", "col"), None)
    return jax.shard_map(
        on_device, mesh=mesh, in_specs=in_specs, out_specs=out_specs, check_vma=False
    )
```

```python
import functools

import jax
import jax.numpy as jnp
from jax import lax
from jax.experimental import pallas as pl
from jax.experimental.pallas import tpu as pltpu
from jax.sharding import PartitionSpec as P

LANES = 128
SUB = 8
F32 = jnp.float32
BF16 = jnp.bfloat16
I32 = jnp.int32


def lanes_of(shape=(SUB, LANES)):
    return lax.broadcasted_iota(I32, shape, 1)


def rows_of(shape=(SUB, LANES)):
    return lax.broadcasted_iota(I32, shape, 0)


def column(row, rows):
    n = row.shape[1]
    eye = rows_of((rows, n)) == lanes_of((rows, n))
    return jnp.sum(jnp.where(eye, jnp.broadcast_to(row, (rows, n)), 0.0), axis=1, keepdims=True)


def turn(chunk, index):
    return jnp.take_along_axis(chunk, index, axis=1, mode="promise_in_bounds")


def choose(delay, options):
    result = options[-1]
    for d in range(len(options) - 2, -1, -1):
        result = jnp.where(delay == d, options[d], result)
    return result


def split3(x):
    hi = x.astype(BF16).astype(F32)
    mid = (x - hi).astype(BF16).astype(F32)
    return hi, mid, x - hi - mid


def fetch(sources, targets, sems):
    copies = [
        pltpu.make_async_copy(src, dst, sems.at[i]) for i, (src, dst) in enumerate(zip(sources, targets))
    ]
    for copy in copies:
        copy.start()
    return copies


def project_kernel(
    reach, cube_in, ap_in, meas_in, shear_in, step_in, up_ref, dn_ref, *rest_refs
):
    kept, (raw, sems) = rest_refs[:5], rest_refs[5:]
    cube_ref, ap_ref, meas_ref, shear_ref, step_ref = kept
    copies = fetch((cube_in, ap_in, meas_in, shear_in, step_in), kept, sems)
    for copy in copies:
        copy.wait()
    bands, cols = cube_ref.shape
    groups = -(-bands // SUB)
    inner = cols // LANES
    outer = up_ref.shape[1] // LANES
    raw[bands // SUB * SUB :, :] = jnp.zeros((raw.shape[0] - bands // SUB * SUB, cols), F32)
    raw[0:bands, :] = cube_ref[...].astype(F32)
    shear_f = column(shear_ref[...].astype(F32), groups * SUB)
    step_f = column(step_ref[...], groups * SUB)
    shear_i = shear_f.astype(I32)
    lane, sub = lanes_of(), rows_of()
    index, delay = [], []
    for g in range(groups):
        s = jnp.broadcast_to(shear_i[g * SUB : (g + 1) * SUB], (SUB, LANES))
        rest = s & (LANES - 1)
        index.append((lane - rest) & (LANES - 1))
        delay.append((s >> 7) + jnp.where(lane < rest, 1, 0))
    zero = jnp.zeros((SUB, LANES), F32)
    turned = [[zero] * (reach - 1) for _ in range(groups)]
    opened = [[zero] * (reach - 1) for _ in range(groups)]
    low_first = (bands - 3) % SUB
    for p in range(outer):
        total = zero
        count = zero
        if p < inner:
            open_p = jnp.broadcast_to(
                ap_ref[:, p * LANES : (p + 1) * LANES].astype(F32), (SUB, LANES)
            )
            layers = [
                raw[g * SUB : (g + 1) * SUB, p * LANES : (p + 1) * LANES] for g in range(groups)
            ]
        for g in range(groups):
            if p < inner:
                here = turn(layers[g] * open_p, index[g])
                here_open = turn(open_p, index[g])
            else:
                here = here_open = zero
            options = [here] + turned[g]
            options_open = [here_open] + opened[g]
            turned[g] = options[:-1]
            opened[g] = options_open[:-1]
            total = total + choose(delay[g], options)
            part = choose(delay[g], options_open)
            if (g + 1) * SUB > bands:
                part = jnp.where(sub < bands - g * SUB, part, 0.0)
            count = count + part
        predicted = jnp.sum(total, axis=0, keepdims=True)
        hi = predicted.astype(BF16).astype(F32)
        lo = predicted - hi
        counts = jnp.sum(count, axis=0, keepdims=True)
        if p < inner:
            first, last = layers[0], layers[-1]
        elif p == inner:
            sides = []
            for g in (0, groups - 1):
                s = shear_i[g * SUB : (g + 1) * SUB]
                parts = [(s >> 1).astype(F32), (s & 1).astype(F32)]
                parts += list(split3(step_f[g * SUB : (g + 1) * SUB]))
                side = zero
                for i, part in enumerate(parts):
                    side = jnp.where(lane == i, part, side)
                sides.append(side)
            first, last = sides
        else:
            first = last = zero
        up = jnp.where((sub >= low_first) & (sub < low_first + 3), last, 0.0)
        dn = jnp.where(sub < 3, first, 0.0)
        for i, value in enumerate((hi, lo, counts)):
            up = jnp.where(sub == i, value, up)
            dn = jnp.where(sub == 3 + i, value, dn)
        up_ref[:, p * LANES : (p + 1) * LANES] = up.astype(BF16)
        dn_ref[:, p * LANES : (p + 1) * LANES] = dn.astype(BF16)


def update_kernel(
    reach,
    fars,
    cube_ref,
    ap_ref,
    meas_ref,
    shear_ref,
    step_ref,
    own_ref,
    below_ref,
    above_ref,
    _,
    *rest_refs,
):
    far_refs = rest_refs[:fars]
    out_ref, raw, meas = rest_refs[fars:]
    bands, cols = cube_ref.shape
    groups = -(-bands // SUB)
    inner = cols // LANES
    outer = own_ref.shape[1] // LANES
    raw[bands // SUB * SUB :, :] = jnp.zeros((raw.shape[0] - bands // SUB * SUB, cols), F32)
    raw[0:bands, :] = cube_ref[...].astype(F32)
    meas[:, (outer - 1) * LANES :] = jnp.zeros((1, LANES), F32)
    meas[:, 0 : meas_ref.shape[1]] = meas_ref[...]
    shear_f = column(shear_ref[...].astype(F32), groups * SUB)
    step_f = column(step_ref[...], groups * SUB)
    lane, sub = lanes_of(), rows_of()

    def halo(p):
        where = slice(p * LANES, (p + 1) * LANES)
        return jnp.where(sub < 3, above_ref[:, where].astype(F32), below_ref[:, where].astype(F32))

    side = halo(inner)
    shear_cols = [shear_f[g * SUB : (g + 1) * SUB] for g in range(groups)]
    step_cols = [step_f[g * SUB : (g + 1) * SUB] for g in range(groups)]
    inside = rows_of((SUB, 1)) < 6
    shear_cols.append(jnp.where(inside, 2.0 * side[:, 0:1] + side[:, 1:2], 0.0))
    step_cols.append(jnp.where(inside, side[:, 2:3] + side[:, 3:4] + side[:, 4:5], 0.0))
    index, delay, steps = [], [], []
    for g in range(groups + 1):
        s = jnp.broadcast_to(shear_cols[g].astype(I32), (SUB, LANES))
        rest = s & (LANES - 1)
        index.append((lane + rest) & (LANES - 1))
        delay.append((s >> 7) + jnp.where(lane + rest >= LANES, 1, 0))
        steps.append(jnp.broadcast_to(step_cols[g], (SUB, LANES)))
    turned = [[] for _ in range(groups + 1)]
    for p in range(outer + 1):
        if p < outer:
            where = slice(p * LANES, (p + 1) * LANES)
            up_sum = own_ref[:, where].astype(F32) + below_ref[:, where].astype(F32)
            for far in far_refs:
                up_sum = up_sum + far[:, where].astype(F32)
            dn_sum = above_ref[:, where].astype(F32)
            predicted = up_sum[0:1] + up_sum[1:2] + dn_sum[3:4] + dn_sum[4:5]
            counts = up_sum[2:3] + dn_sum[5:6]
            residual = (meas[:, where] - predicted) / jnp.maximum(counts, 1.0)
            residual = jnp.broadcast_to(residual, (SUB, LANES))
        else:
            residual = jnp.zeros((SUB, LANES), F32)
        for g in range(groups + 1):
            turned[g].append(turn(residual, index[g]) if p < outer else residual)
        q = p - (reach - 1)
        if q < 0 or q >= inner:
            continue
        here = slice(q * LANES, (q + 1) * LANES)
        open_q = jnp.broadcast_to(ap_ref[:, here].astype(F32), (SUB, LANES))
        pieces = []
        for g in range(groups + 1):
            pulled = choose(delay[g], turned[g][q : q + reach])
            base = raw[g * SUB : (g + 1) * SUB, here] if g < groups else halo(q)
            if g == groups:
                base = jnp.where(sub < 6, base, 0.0)
            pieces.append(base + pulled * open_q * steps[g])
        out_ref[:, here] = jnp.concatenate(pieces, axis=0).astype(BF16)


def weights_kernel(
    _, sw_in, sb_in, cw_in, cb_in, ow_in, main_ref, halo_ref, first_ref, second_ref, out_w_ref, *rest
):
    local, sems = rest[:5], rest[5]
    for copy in fetch((sw_in, sb_in, cw_in, cb_in, ow_in), local, sems):
        copy.wait()
    sw_ref, sb_ref, cw_ref, cb_ref, ow_ref = local
    ch, taps2 = sw_ref.shape
    taps = cw_ref.shape[0]
    place = lax.axis_index("band")
    has_low = jnp.where(place > 0, 1, 0)
    has_high = jnp.where(place < lax.axis_size("band") - 1, 1, 0)

    def spread(rows, which):
        return (which(rows_of((rows, ch))) == lanes_of((rows, ch))).astype(F32).astype(BF16)

    def bias_column(row_ref, rows, which):
        pick = which(rows_of((rows, ch))) == lanes_of((rows, ch))
        row = jnp.broadcast_to(row_ref[...], (rows, ch))
        return 0.5 * jnp.sum(jnp.where(pick, row, 0.0), axis=1, keepdims=True)

    def with_bias(matrix, bias, start):
        lane = lanes_of(matrix.shape)
        for i, part in enumerate(split3(bias)):
            matrix = jnp.where(lane == start + i, part, matrix)
        return matrix

    width = main_ref.shape[1]
    slots = 16
    fan = (lanes_of((taps2, width)) // slots == rows_of((taps2, width))).astype(F32).astype(BF16)
    flat = jnp.dot(sw_ref[...], fan, preferred_element_type=F32).astype(BF16)
    for ref, slot_of in (
        (main_ref, lambda b: b),
        (halo_ref, lambda b: jnp.where(b < 3, 11 + b, jnp.where(b < 9, b - 3, b - 1))),
    ):
        rows = ref.shape[0]
        which = lambda r: r % ch
        full = jnp.dot(spread(rows, which), flat, preferred_element_type=F32)
        lane = lanes_of((rows, width))
        band = rows_of((rows, width)) // ch
        keep = (lane % slots == slot_of(band)) & (lane < taps2 * slots)
        matrix = with_bias(
            jnp.where(keep, 0.5 * full, 0.0), bias_column(sb_ref, rows, which), taps2 * slots
        )
        if ref is halo_ref:
            valid = jnp.where(band < 3, has_low, jnp.where(band >= 9, has_high, 1))
            matrix = jnp.where(valid > 0, matrix, 0.0)
        ref[...] = matrix.astype(BF16)

    per = SUB
    rows = per * ch
    width = first_ref.shape[1]
    used = (per + taps - 1) * ch
    which = lambda r: r // per
    fan = (lanes_of((ch, width)) % ch == rows_of((ch, width))).astype(F32).astype(BF16)
    picks = spread(rows, which)
    lane = lanes_of((rows, width))
    ahead = jnp.where(lane < used, lane // ch - rows_of((rows, width)) % per, -LANES)
    shifts = (0, per, per - (per + taps - 1), 2 * per - (per + taps - 1))
    blocks = [jnp.zeros((rows, width), F32) for _ in shifts]
    for d in range(taps):
        flat = jnp.dot(cw_ref[d], fan, preferred_element_type=F32).astype(BF16)
        full = 0.5 * jnp.dot(picks, flat, preferred_element_type=F32)
        blocks = [jnp.where(ahead == d + s, full, b) for s, b in zip(shifts, blocks)]
    bias = bias_column(cb_ref, rows, which)
    for i, block in enumerate(blocks):
        block = block if i == 2 else with_bias(block, bias, used)
        ref = first_ref if i < 2 else second_ref
        ref[i % 2 * rows : (i % 2 + 1) * rows, :] = block.astype(BF16)
    pick = which(rows_of((rows, ch))) == lanes_of((rows, ch))
    scale = jnp.sum(jnp.where(pick, ow_ref[...], 0.0), axis=1, keepdims=True)
    out_w_ref[...] = jnp.broadcast_to(scale, out_w_ref.shape)


def denoise_kernel(
    tile, ow_ref, up_ref, mid_ref, dn_ref, main_ref, halo_ref, first_ref, second_ref, out_ref, act
):
    bands, cols = out_ref.shape
    slots = 16
    ch = main_ref.shape[0] // slots
    tiles = cols // tile
    wide = tile + 2 * LANES
    split = act.shape[1] // 2
    ones = jnp.where(rows_of((slots, tile)) < 3, 1.0, 0.0).astype(BF16)
    blank = jnp.zeros((32, LANES), F32)

    def silu_twice(half):
        return half + half * jnp.tanh(half)

    def spatial(t):
        start = t * tile
        patches = []
        for ref in (up_ref, mid_ref, dn_ref):
            left = ref[:, start - LANES : start].astype(F32) if t else blank
            here = ref[:, start : start + tile]
            end = start + tile
            right = ref[:, end : end + LANES].astype(F32) if t < tiles - 1 else blank
            row = jnp.concatenate([left, here.astype(F32), right], axis=1)
            back = pltpu.roll(row, 1, 1)[:, LANES : LANES + tile].astype(BF16)
            ahead = pltpu.roll(row, wide - 1, 1)[:, LANES : LANES + tile].astype(BF16)
            patches += [back, here, ahead]
        buf = act.at[t % act.shape[0]]
        for part, w_ref in enumerate((main_ref, halo_ref)):
            x = jnp.concatenate(
                [p[part * slots : (part + 1) * slots] for p in patches] + [ones], axis=0
            )
            half = jnp.dot(w_ref[...], x, preferred_element_type=F32)
            value = silu_twice(half).astype(BF16)
            if part == 0:
                buf[3 * ch : 19 * ch, :] = value
            else:
                buf[0 : 3 * ch, :] = value[0 : 3 * ch]
                buf[19 * ch : 28 * ch, :] = value[3 * ch :]

    def spectral(t):
        start = t * tile
        buf = act.at[t % act.shape[0]]
        halves = []
        for part, w_ref in enumerate((first_ref, second_ref)):
            x = jnp.concatenate([buf[part * split : (part + 1) * split, :], ones], axis=0)
            halves.append(jnp.dot(w_ref[...], x, preferred_element_type=F32))
        rows = SUB * ch
        blocks = [halves[0][0:rows], halves[0][rows:] + halves[1][0:rows], halves[1][rows:]]
        pieces = []
        for half in blocks:
            total = None
            for k in range(ch):
                weight = ow_ref[k * SUB : (k + 1) * SUB, :]
                weight = jnp.concatenate([weight] * (tile // LANES), axis=1)
                term = weight * silu_twice(half[k * SUB : (k + 1) * SUB])
                total = term if total is None else total + term
            pieces.append(total)
        update = jnp.concatenate(pieces, axis=0)[0:bands]
        center = mid_ref[:, start : start + tile].astype(F32)[0:bands]
        out_ref[:, start : start + tile] = (center + update).astype(BF16)

    spatial(0)
    for t in range(tiles):
        if t + 1 < tiles:
            spatial(t + 1)
        spectral(t)


def vmem(n):
    return [pl.BlockSpec(memory_space=pltpu.VMEM)] * n


def hbm(n):
    return [pl.BlockSpec(memory_space=pltpu.HBM)] * n


def in_hbm(arrays):
    return [pltpu.with_memory_space_constraint(x, pltpu.HBM) for x in arrays]


ANY = pl.BlockSpec(memory_space=pl.ANY)


def on_device(
    spectral_cube,
    aperture,
    measurement,
    shears,
    step_sizes,
    spatial_weight,
    spatial_bias,
    spectral_weight,
    spectral_bias,
    out_weight,
):
    bands, row_count, cols = spectral_cube.shape
    width = measurement.shape[1]
    reach = (width - cols) // LANES + 2
    outer = -(-width // LANES)
    groups = -(-bands // SUB)
    slots = (groups + 1) * SUB
    taps, ch = spectral_weight.shape[:2]
    taps2 = spatial_weight.shape[1]
    count = lax.axis_size("band")
    place = lax.axis_index("band")
    cube = spectral_cube.reshape(bands, cols)
    shear_row = shears.reshape(1, bands)
    step_row = step_sizes.reshape(1, bands)
    params = pltpu.CompilerParams(vmem_limit_bytes=48 * 2**20)

    payload = jax.ShapeDtypeStruct((SUB, outer * LANES), BF16)
    inputs = (cube, aperture, measurement, shear_row, step_row)
    up, dn, *kept = pl.pallas_call(
        functools.partial(project_kernel, reach),
        out_shape=(payload, payload)
        + tuple(jax.ShapeDtypeStruct(x.shape, x.dtype) for x in inputs),
        in_specs=hbm(5),
        out_specs=tuple(vmem(7)),
        scratch_shapes=[
            pltpu.VMEM((groups * SUB, cols), F32),
            pltpu.SemaphoreType.DMA((5,)),
        ],
        compiler_params=params,
        name="project",
    )(*in_hbm(inputs))

    def around(x, shift):
        return lax.ppermute(x, "band", [(i, (i + shift) % count) for i in range(count)])

    below = around(up, 1)
    above = around(dn, -1)
    far = [around(up, s) for s in range(2, count - 1)]

    small = (
        spatial_weight,
        spatial_bias.reshape(1, ch),
        spectral_weight,
        spectral_bias.reshape(1, ch),
        out_weight.reshape(1, ch),
    )
    reached = (SUB + taps - 1) * ch
    main_w, halo_w, first_w, second_w, out_w = pl.pallas_call(
        weights_kernel,
        out_shape=(
            jax.ShapeDtypeStruct((16 * ch, taps2 * 16 + 16), BF16),
            jax.ShapeDtypeStruct((12 * ch, taps2 * 16 + 16), BF16),
            jax.ShapeDtypeStruct((2 * SUB * ch, reached + 16), BF16),
            jax.ShapeDtypeStruct((2 * SUB * ch, reached + 16), BF16),
            jax.ShapeDtypeStruct((SUB * ch, LANES), F32),
        ),
        in_specs=[ANY] + hbm(5),
        out_specs=tuple(vmem(5)),
        scratch_shapes=[pltpu.VMEM(x.shape, x.dtype) for x in small]
        + [pltpu.SemaphoreType.DMA((5,))],
        compiler_params=params,
        name="weights",
    )(up, *in_hbm(small))

    updated = pl.pallas_call(
        functools.partial(update_kernel, reach, len(far)),
        out_shape=jax.ShapeDtypeStruct((slots, cols), BF16),
        in_specs=vmem(8) + [ANY] + vmem(len(far)),
        out_specs=vmem(1)[0],
        scratch_shapes=[
            pltpu.VMEM((groups * SUB, cols), F32),
            pltpu.VMEM((1, outer * LANES), F32),
        ],
        compiler_params=params,
        name="update",
    )(*kept, up, below, above, out_w, *far)

    lines = lax.axis_size(("row", "col"))
    over = lax.ppermute(updated, ("row", "col"), [(i, i + 1) for i in range(lines - 1)])
    under = lax.ppermute(updated, ("row", "col"), [(i + 1, i) for i in range(lines - 1)])

    tile = 512
    result = pl.pallas_call(
        functools.partial(denoise_kernel, tile),
        out_shape=jax.ShapeDtypeStruct((bands, cols), BF16),
        in_specs=vmem(8),
        out_specs=vmem(1)[0],
        scratch_shapes=[pltpu.VMEM((4, 28 * ch, tile), BF16)],
        compiler_params=params,
        name="denoise",
    )(out_w, over, updated, under, main_w, halo_w, first_w, second_w)
    return result.reshape(bands, 1, cols)


def solution(mesh):
    in_specs = (
        P("band", ("row", "col"), None),
        P(("row", "col"), None),
        P(("row", "col"), None),
        P("band"),
        P("band"),
        P(),
        P(),
        P(),
        P(),
        P(),
    )
    out_specs = P("band", ("row", "col"), None)
    return jax.shard_map(
        on_device, mesh=mesh, in_specs=in_specs, out_specs=out_specs, check_vma=False
    )
```

```python
import functools

import jax
import jax.numpy as jnp
from jax import lax
from jax.experimental import pallas as pl
from jax.experimental.pallas import tpu as pltpu
from jax.sharding import PartitionSpec as P

LANES = 128
SUB = 8
F32 = jnp.float32
BF16 = jnp.bfloat16
I32 = jnp.int32


def lanes_of(shape=(SUB, LANES)):
    return lax.broadcasted_iota(I32, shape, 1)


def rows_of(shape=(SUB, LANES)):
    return lax.broadcasted_iota(I32, shape, 0)


def column(row, rows):
    n = row.shape[1]
    eye = rows_of((rows, n)) == lanes_of((rows, n))
    return jnp.sum(jnp.where(eye, jnp.broadcast_to(row, (rows, n)), 0.0), axis=1, keepdims=True)


def turn(chunk, index):
    return jnp.take_along_axis(chunk, index, axis=1, mode="promise_in_bounds")


def choose(delay, options):
    result = options[-1]
    for d in range(len(options) - 2, -1, -1):
        result = jnp.where(delay == d, options[d], result)
    return result


def split3(x):
    hi = x.astype(BF16).astype(F32)
    mid = (x - hi).astype(BF16).astype(F32)
    return hi, mid, x - hi - mid


def fetch(sources, targets, sems):
    copies = [
        pltpu.make_async_copy(src, dst, sems.at[i]) for i, (src, dst) in enumerate(zip(sources, targets))
    ]
    for copy in copies:
        copy.start()
    return copies


def project_kernel(
    reach, cube_in, ap_in, meas_in, shear_in, step_in, part_ref, up_ref, dn_ref, *rest_refs
):
    kept, (raw, sems) = rest_refs[:5], rest_refs[5:]
    cube_ref, ap_ref, meas_ref, shear_ref, step_ref = kept
    copies = fetch((cube_in, ap_in, meas_in, shear_in, step_in), kept, sems)
    for copy in copies:
        copy.wait()
    bands, cols = cube_ref.shape
    groups = -(-bands // SUB)
    inner = cols // LANES
    tall = part_ref.shape[0] // 2
    outer = -(-meas_ref.shape[1] // LANES)
    raw[bands // SUB * SUB :, :] = jnp.zeros((raw.shape[0] - bands // SUB * SUB, cols), F32)
    raw[0:bands, :] = cube_ref[...].astype(F32)
    shear_f = column(shear_ref[...].astype(F32), groups * SUB)
    step_f = column(step_ref[...], groups * SUB)
    shear_i = shear_f.astype(I32)
    lane, sub = lanes_of(), rows_of()
    index, delay = [], []
    for g in range(groups):
        s = jnp.broadcast_to(shear_i[g * SUB : (g + 1) * SUB], (SUB, LANES))
        rest = s & (LANES - 1)
        index.append((lane - rest) & (LANES - 1))
        delay.append((s >> 7) + jnp.where(lane < rest, 1, 0))
    zero = jnp.zeros((SUB, LANES), F32)
    turned = [[zero] * (reach - 1) for _ in range(groups)]
    opened = [[zero] * (reach - 1) for _ in range(groups)]
    sums = [zero] * (tall // SUB)
    counts = [zero] * (tall // SUB)
    firsts, lasts = [], []
    for p in range(outer):
        total = zero
        count = zero
        if p < inner:
            open_p = jnp.broadcast_to(
                ap_ref[:, p * LANES : (p + 1) * LANES].astype(F32), (SUB, LANES)
            )
            layers = [
                raw[g * SUB : (g + 1) * SUB, p * LANES : (p + 1) * LANES] for g in range(groups)
            ]
            firsts.append(layers[0])
            lasts.append(layers[-1])
        for g in range(groups):
            if p < inner:
                here = turn(layers[g] * open_p, index[g])
                here_open = turn(open_p, index[g])
            else:
                here = here_open = zero
            options = [here] + turned[g]
            options_open = [here_open] + opened[g]
            turned[g] = options[:-1]
            opened[g] = options_open[:-1]
            total = total + choose(delay[g], options)
            part = choose(delay[g], options_open)
            if (g + 1) * SUB > bands:
                part = jnp.where(sub < bands - g * SUB, part, 0.0)
            count = count + part
        v, at = divmod(p, SUB)
        sums[v] = jnp.where(sub == at, jnp.sum(total, axis=0, keepdims=True), sums[v])
        counts[v] = jnp.where(sub == at, jnp.sum(count, axis=0, keepdims=True), counts[v])
    sides = []
    for g in (0, groups - 1):
        s = shear_i[g * SUB : (g + 1) * SUB]
        parts = [(s >> 1).astype(F32), (s & 1).astype(F32)]
        parts += list(split3(step_f[g * SUB : (g + 1) * SUB]))
        side = zero
        for i, part in enumerate(parts):
            side = jnp.where(lane == i, part, side)
        sides.append(side)
    half = inner // 2
    dn = [
        jnp.where(sub < 3, firsts[q], pltpu.roll(firsts[q + half], 3, 0)) for q in range(half)
    ] + [sides[0], zero]
    up = [
        jnp.where(sub < 3, pltpu.roll(lasts[q + half], SUB - 3, 0), lasts[q]) for q in range(half)
    ] + [sides[1], zero]
    part_ref[...] = jnp.concatenate(sums + counts, axis=0).astype(BF16)
    up_ref[...] = jnp.concatenate(sums + counts + up, axis=0).astype(BF16)
    dn_ref[...] = jnp.concatenate(sums + counts + dn, axis=0).astype(BF16)


def update_kernel(
    reach,
    fars,
    cube_ref,
    ap_ref,
    meas_ref,
    shear_ref,
    step_ref,
    own_ref,
    below_ref,
    above_ref,
    _,
    *rest_refs,
):
    far_refs = rest_refs[:fars]
    out_ref, raw, meas, rest_row = rest_refs[fars:]
    bands, cols = cube_ref.shape
    groups = -(-bands // SUB)
    inner = cols // LANES
    half = inner // 2
    tall = own_ref.shape[0] // 2
    outer = -(-meas_ref.shape[1] // LANES)
    raw[bands // SUB * SUB :, :] = jnp.zeros((raw.shape[0] - bands // SUB * SUB, cols), F32)
    raw[0:bands, :] = cube_ref[...].astype(F32)
    meas[:, (outer - 1) * LANES :] = jnp.zeros((1, LANES), F32)
    meas[:, 0 : meas_ref.shape[1]] = meas_ref[...]
    shear_f = column(shear_ref[...].astype(F32), groups * SUB)
    step_f = column(step_ref[...], groups * SUB)
    lane, sub = lanes_of(), rows_of()
    below = below_ref[...].astype(F32)
    above = above_ref[...].astype(F32)
    sums = own_ref[...].astype(F32) + below[0 : 2 * tall] + above[0 : 2 * tall]
    for far in far_refs:
        sums = sums + far[...].astype(F32)
    measured = []
    for v in range(tall // SUB):
        tile = jnp.zeros((SUB, LANES), F32)
        for at in range(min(SUB, outer - v * SUB)):
            p = v * SUB + at
            tile = jnp.where(sub == at, meas[:, p * LANES : (p + 1) * LANES], tile)
        measured.append(tile)
    measured = jnp.concatenate(measured, axis=0)
    rest_row[...] = (measured - sums[0:tall]) / jnp.maximum(sums[tall:], 1.0)

    def halo(q):
        at = 2 * tall + q % half * SUB
        high, low = above[at : at + SUB], below[at : at + SUB]
        if q // half == 1:
            high, low = pltpu.roll(high, SUB - 3, 0), pltpu.roll(low, 3, 0)
        return jnp.where(sub < 3, high, jnp.where(sub < 6, low, 0.0))

    side = 2 * tall + half * SUB
    side = jnp.where(sub < 3, above[side : side + SUB], below[side : side + SUB])
    shear_cols = [shear_f[g * SUB : (g + 1) * SUB] for g in range(groups)]
    step_cols = [step_f[g * SUB : (g + 1) * SUB] for g in range(groups)]
    inside = rows_of((SUB, 1)) < 6
    shear_cols.append(jnp.where(inside, 2.0 * side[:, 0:1] + side[:, 1:2], 0.0))
    step_cols.append(jnp.where(inside, side[:, 2:3] + side[:, 3:4] + side[:, 4:5], 0.0))
    index, delay, steps = [], [], []
    for g in range(groups + 1):
        s = jnp.broadcast_to(shear_cols[g].astype(I32), (SUB, LANES))
        rest = s & (LANES - 1)
        index.append((lane + rest) & (LANES - 1))
        delay.append((s >> 7) + jnp.where(lane + rest >= LANES, 1, 0))
        steps.append(jnp.broadcast_to(step_cols[g], (SUB, LANES)))
    turned = [[] for _ in range(groups + 1)]
    for p in range(outer + 1):
        if p < outer:
            residual = jnp.broadcast_to(rest_row[p : p + 1, :], (SUB, LANES))
        else:
            residual = jnp.zeros((SUB, LANES), F32)
        for g in range(groups + 1):
            turned[g].append(turn(residual, index[g]) if p < outer else residual)
        q = p - (reach - 1)
        if q < 0 or q >= inner:
            continue
        here = slice(q * LANES, (q + 1) * LANES)
        open_q = jnp.broadcast_to(ap_ref[:, here].astype(F32), (SUB, LANES))
        pieces = []
        for g in range(groups + 1):
            pulled = choose(delay[g], turned[g][q : q + reach])
            base = raw[g * SUB : (g + 1) * SUB, here] if g < groups else halo(q)
            pieces.append(base + pulled * open_q * steps[g])
        out_ref[:, here] = jnp.concatenate(pieces, axis=0).astype(BF16)


def weights_kernel(
    _, sw_in, sb_in, cw_in, cb_in, ow_in, main_ref, halo_ref, first_ref, second_ref, out_w_ref, *rest
):
    local, sems = rest[:5], rest[5]
    for copy in fetch((sw_in, sb_in, cw_in, cb_in, ow_in), local, sems):
        copy.wait()
    sw_ref, sb_ref, cw_ref, cb_ref, ow_ref = local
    ch, taps2 = sw_ref.shape
    taps = cw_ref.shape[0]
    place = lax.axis_index("band")
    has_low = jnp.where(place > 0, 1, 0)
    has_high = jnp.where(place < lax.axis_size("band") - 1, 1, 0)

    def spread(rows, which):
        return (which(rows_of((rows, ch))) == lanes_of((rows, ch))).astype(F32).astype(BF16)

    def bias_column(row_ref, rows, which):
        pick = which(rows_of((rows, ch))) == lanes_of((rows, ch))
        row = jnp.broadcast_to(row_ref[...], (rows, ch))
        return 0.5 * jnp.sum(jnp.where(pick, row, 0.0), axis=1, keepdims=True)

    def with_bias(matrix, bias, start):
        lane = lanes_of(matrix.shape)
        for i, part in enumerate(split3(bias)):
            matrix = jnp.where(lane == start + i, part, matrix)
        return matrix

    width = main_ref.shape[1]
    slots = 16
    line = lax.axis_index("row") * lax.axis_size("col") + lax.axis_index("col")
    lines = lax.axis_size("row") * lax.axis_size("col")
    group = lanes_of((taps2, width)) // slots
    offset = jnp.where(line % 2 == 1, group // 3, 2 - group // 3)
    present = (line + offset >= 1) & (line + offset <= lines)
    fan = (rows_of((taps2, width)) == 3 * offset + group % 3) & present
    fan = fan.astype(F32).astype(BF16)
    flat = jnp.dot(sw_ref[...], fan, preferred_element_type=F32).astype(BF16)
    for ref, slot_of in (
        (main_ref, lambda b: b),
        (halo_ref, lambda b: jnp.where(b < 3, 11 + b, jnp.where(b < 9, b - 3, b - 1))),
    ):
        rows = ref.shape[0]
        which = lambda r: r % ch
        full = jnp.dot(spread(rows, which), flat, preferred_element_type=F32)
        lane = lanes_of((rows, width))
        band = rows_of((rows, width)) // ch
        keep = (lane % slots == slot_of(band)) & (lane < taps2 * slots)
        matrix = with_bias(
            jnp.where(keep, 0.5 * full, 0.0), bias_column(sb_ref, rows, which), taps2 * slots
        )
        if ref is halo_ref:
            valid = jnp.where(band < 3, has_low, jnp.where(band >= 9, has_high, 1))
            matrix = jnp.where(valid > 0, matrix, 0.0)
        ref[...] = matrix.astype(BF16)

    per = SUB
    rows = per * ch
    width = first_ref.shape[1]
    used = (per + taps - 1) * ch
    which = lambda r: r // per
    fan = (lanes_of((ch, width)) % ch == rows_of((ch, width))).astype(F32).astype(BF16)
    picks = spread(rows, which)
    lane = lanes_of((rows, width))
    ahead = jnp.where(lane < used, lane // ch - rows_of((rows, width)) % per, -LANES)
    shifts = (0, per, per - (per + taps - 1), 2 * per - (per + taps - 1))
    blocks = [jnp.zeros((rows, width), F32) for _ in shifts]
    for d in range(taps):
        flat = jnp.dot(cw_ref[d], fan, preferred_element_type=F32).astype(BF16)
        full = 0.5 * jnp.dot(picks, flat, preferred_element_type=F32)
        blocks = [jnp.where(ahead == d + s, full, b) for s, b in zip(shifts, blocks)]
    bias = bias_column(cb_ref, rows, which)
    for i, block in enumerate(blocks):
        block = block if i == 2 else with_bias(block, bias, used)
        ref = first_ref if i < 2 else second_ref
        ref[i % 2 * rows : (i % 2 + 1) * rows, :] = block.astype(BF16)
    pick = which(rows_of((rows, ch))) == lanes_of((rows, ch))
    scale = jnp.sum(jnp.where(pick, ow_ref[...], 0.0), axis=1, keepdims=True)
    out_w_ref[...] = jnp.broadcast_to(scale, out_w_ref.shape)


def denoise_kernel(
    tile, ow_ref, up_ref, mid_ref, dn_ref, main_ref, halo_ref, first_ref, second_ref, out_ref, act
):
    bands, cols = out_ref.shape
    slots = 16
    ch = main_ref.shape[0] // slots
    tiles = cols // tile
    wide = tile + 2 * LANES
    split = act.shape[1] // 2
    ones = jnp.where(rows_of((slots, tile)) < 3, 1.0, 0.0).astype(BF16)
    blank = jnp.zeros((32, LANES), F32)

    def silu_twice(half):
        return half + half * jnp.tanh(half)

    def spatial(t):
        start = t * tile
        patches = []
        for ref in (up_ref, mid_ref, dn_ref):
            left = ref[:, start - LANES : start].astype(F32) if t else blank
            here = ref[:, start : start + tile]
            end = start + tile
            right = ref[:, end : end + LANES].astype(F32) if t < tiles - 1 else blank
            row = jnp.concatenate([left, here.astype(F32), right], axis=1)
            back = pltpu.roll(row, 1, 1)[:, LANES : LANES + tile].astype(BF16)
            ahead = pltpu.roll(row, wide - 1, 1)[:, LANES : LANES + tile].astype(BF16)
            patches += [back, here, ahead]
        buf = act.at[t % act.shape[0]]
        for part, w_ref in enumerate((main_ref, halo_ref)):
            x = jnp.concatenate(
                [p[part * slots : (part + 1) * slots] for p in patches] + [ones], axis=0
            )
            half = jnp.dot(w_ref[...], x, preferred_element_type=F32)
            value = silu_twice(half).astype(BF16)
            if part == 0:
                buf[3 * ch : 19 * ch, :] = value
            else:
                buf[0 : 3 * ch, :] = value[0 : 3 * ch]
                buf[19 * ch : 28 * ch, :] = value[3 * ch :]

    def spectral(t):
        start = t * tile
        buf = act.at[t % act.shape[0]]
        halves = []
        for part, w_ref in enumerate((first_ref, second_ref)):
            x = jnp.concatenate([buf[part * split : (part + 1) * split, :], ones], axis=0)
            halves.append(jnp.dot(w_ref[...], x, preferred_element_type=F32))
        rows = SUB * ch
        blocks = [halves[0][0:rows], halves[0][rows:] + halves[1][0:rows], halves[1][rows:]]
        pieces = []
        for half in blocks:
            total = None
            for k in range(ch):
                weight = ow_ref[k * SUB : (k + 1) * SUB, :]
                weight = jnp.concatenate([weight] * (tile // LANES), axis=1)
                term = weight * silu_twice(half[k * SUB : (k + 1) * SUB])
                total = term if total is None else total + term
            pieces.append(total)
        update = jnp.concatenate(pieces, axis=0)[0:bands]
        center = mid_ref[:, start : start + tile].astype(F32)[0:bands]
        out_ref[:, start : start + tile] = (center + update).astype(BF16)

    spatial(0)
    for t in range(tiles):
        if t + 1 < tiles:
            spatial(t + 1)
        spectral(t)


def vmem(n):
    return [pl.BlockSpec(memory_space=pltpu.VMEM)] * n


def hbm(n):
    return [pl.BlockSpec(memory_space=pltpu.HBM)] * n


def in_hbm(arrays):
    return [pltpu.with_memory_space_constraint(x, pltpu.HBM) for x in arrays]


ANY = pl.BlockSpec(memory_space=pl.ANY)


def on_device(
    spectral_cube,
    aperture,
    measurement,
    shears,
    step_sizes,
    spatial_weight,
    spatial_bias,
    spectral_weight,
    spectral_bias,
    out_weight,
):
    bands, row_count, cols = spectral_cube.shape
    width = measurement.shape[1]
    reach = (width - cols) // LANES + 2
    outer = -(-width // LANES)
    groups = -(-bands // SUB)
    slots = (groups + 1) * SUB
    taps, ch = spectral_weight.shape[:2]
    taps2 = spatial_weight.shape[1]
    count = lax.axis_size("band")
    cube = spectral_cube.reshape(bands, cols)
    shear_row = shears.reshape(1, bands)
    step_row = step_sizes.reshape(1, bands)
    params = pltpu.CompilerParams(vmem_limit_bytes=48 * 2**20)

    tall = -(-outer // SUB) * SUB
    side = (cols // LANES // 2 + 2) * SUB
    inputs = (cube, aperture, measurement, shear_row, step_row)
    part, up, dn, *kept = pl.pallas_call(
        functools.partial(project_kernel, reach),
        out_shape=(
            jax.ShapeDtypeStruct((2 * tall, LANES), BF16),
            jax.ShapeDtypeStruct((2 * tall + side, LANES), BF16),
            jax.ShapeDtypeStruct((2 * tall + side, LANES), BF16),
        )
        + tuple(jax.ShapeDtypeStruct(x.shape, x.dtype) for x in inputs),
        in_specs=hbm(5),
        out_specs=tuple(vmem(8)),
        scratch_shapes=[
            pltpu.VMEM((groups * SUB, cols), F32),
            pltpu.SemaphoreType.DMA((5,)),
        ],
        compiler_params=params,
        name="project",
    )(*in_hbm(inputs))

    def around(x, shift):
        return lax.ppermute(x, "band", [(i, (i + shift) % count) for i in range(count)])

    below = around(up, 1)
    above = around(dn, -1)
    far = [around(part, s) for s in range(2, count - 1)]

    small = (
        spatial_weight,
        spatial_bias.reshape(1, ch),
        spectral_weight,
        spectral_bias.reshape(1, ch),
        out_weight.reshape(1, ch),
    )
    reached = (SUB + taps - 1) * ch
    main_w, halo_w, first_w, second_w, out_w = pl.pallas_call(
        weights_kernel,
        out_shape=(
            jax.ShapeDtypeStruct((16 * ch, taps2 * 16 + 16), BF16),
            jax.ShapeDtypeStruct((12 * ch, taps2 * 16 + 16), BF16),
            jax.ShapeDtypeStruct((2 * SUB * ch, reached + 16), BF16),
            jax.ShapeDtypeStruct((2 * SUB * ch, reached + 16), BF16),
            jax.ShapeDtypeStruct((SUB * ch, LANES), F32),
        ),
        in_specs=[ANY] + hbm(5),
        out_specs=tuple(vmem(5)),
        scratch_shapes=[pltpu.VMEM(x.shape, x.dtype) for x in small]
        + [pltpu.SemaphoreType.DMA((5,))],
        compiler_params=params,
        name="weights",
    )(part, *in_hbm(small))

    updated = pl.pallas_call(
        functools.partial(update_kernel, reach, len(far)),
        out_shape=jax.ShapeDtypeStruct((slots, cols), BF16),
        in_specs=vmem(8) + [ANY] + vmem(len(far)),
        out_specs=vmem(1)[0],
        scratch_shapes=[
            pltpu.VMEM((groups * SUB, cols), F32),
            pltpu.VMEM((1, outer * LANES), F32),
            pltpu.VMEM((tall, LANES), F32),
        ],
        compiler_params=params,
        name="update",
    )(*kept, part, below, above, out_w, *far)

    lines = lax.axis_size(("row", "col"))
    partner = lax.ppermute(updated, ("row", "col"), [(i, i ^ 1) for i in range(lines)])
    other = lax.ppermute(
        updated, ("row", "col"), [(i, (i - 1 + i % 2 * 2) % lines) for i in range(lines)]
    )

    tile = 512
    result = pl.pallas_call(
        functools.partial(denoise_kernel, tile),
        out_shape=jax.ShapeDtypeStruct((bands, cols), BF16),
        in_specs=vmem(8),
        out_specs=vmem(1)[0],
        scratch_shapes=[pltpu.VMEM((4, 28 * ch, tile), BF16)],
        compiler_params=params,
        name="denoise",
    )(out_w, partner, updated, other, main_w, halo_w, first_w, second_w)
    return result.reshape(bands, 1, cols)


def solution(mesh):
    in_specs = (
        P("band", ("row", "col"), None),
        P(("row", "col"), None),
        P(("row", "col"), None),
        P("band"),
        P("band"),
        P(),
        P(),
        P(),
        P(),
        P(),
    )
    out_specs = P("band", ("row", "col"), None)
    return jax.shard_map(
        on_device, mesh=mesh, in_specs=in_specs, out_specs=out_specs, check_vma=False
    )
```

```python
import functools

import jax
import jax.numpy as jnp
from jax import lax
from jax.experimental import pallas as pl
from jax.experimental.pallas import tpu as pltpu
from jax.sharding import PartitionSpec as P

LANES = 128
SUB = 8
F32 = jnp.float32
BF16 = jnp.bfloat16
I32 = jnp.int32


def lanes_of(shape=(SUB, LANES)):
    return lax.broadcasted_iota(I32, shape, 1)


def rows_of(shape=(SUB, LANES)):
    return lax.broadcasted_iota(I32, shape, 0)


def column(row, rows):
    n = row.shape[1]
    eye = rows_of((rows, n)) == lanes_of((rows, n))
    return jnp.sum(jnp.where(eye, jnp.broadcast_to(row, (rows, n)), 0.0), axis=1, keepdims=True)


def turn(chunk, index):
    return jnp.take_along_axis(chunk, index, axis=1, mode="promise_in_bounds")


def choose(delay, options):
    result = options[-1]
    for d in range(len(options) - 2, -1, -1):
        result = jnp.where(delay == d, options[d], result)
    return result


def split3(x):
    hi = x.astype(BF16).astype(F32)
    mid = (x - hi).astype(BF16).astype(F32)
    return hi, mid, x - hi - mid


def fetch(sources, targets, sems):
    copies = [
        pltpu.make_async_copy(src, dst, sems.at[i]) for i, (src, dst) in enumerate(zip(sources, targets))
    ]
    for copy in copies:
        copy.start()
    return copies


def project_kernel(
    reach, cube_in, ap_in, meas_in, shear_in, step_in, part_ref, up_ref, dn_ref, *rest_refs
):
    kept, (raw, sems) = rest_refs[:5], rest_refs[5:]
    cube_ref, ap_ref, meas_ref, shear_ref, step_ref = kept
    copies = fetch((cube_in, ap_in, meas_in, shear_in, step_in), kept, sems)
    for copy in copies:
        copy.wait()
    bands, cols = cube_ref.shape
    groups = -(-bands // SUB)
    inner = cols // LANES
    tall = part_ref.shape[0] // 2
    outer = -(-meas_ref.shape[1] // LANES)
    raw[bands // SUB * SUB :, :] = jnp.zeros((raw.shape[0] - bands // SUB * SUB, cols), F32)
    raw[0:bands, :] = cube_ref[...].astype(F32)
    shear_f = column(shear_ref[...].astype(F32), groups * SUB)
    step_f = column(step_ref[...], groups * SUB)
    shear_i = shear_f.astype(I32)
    lane, sub = lanes_of(), rows_of()
    index, delay = [], []
    for g in range(groups):
        s = jnp.broadcast_to(shear_i[g * SUB : (g + 1) * SUB], (SUB, LANES))
        rest = s & (LANES - 1)
        index.append((lane - rest) & (LANES - 1))
        delay.append((s >> 7) + jnp.where(lane < rest, 1, 0))
    zero = jnp.zeros((SUB, LANES), F32)
    turned = [[zero] * (reach - 1) for _ in range(groups)]
    opened = [[zero] * (reach - 1) for _ in range(groups)]
    sums = [zero] * (tall // SUB)
    counts = [zero] * (tall // SUB)
    firsts, lasts = [], []
    for p in range(outer):
        total = zero
        count = zero
        if p < inner:
            open_p = jnp.broadcast_to(
                ap_ref[:, p * LANES : (p + 1) * LANES].astype(F32), (SUB, LANES)
            )
            layers = [
                raw[g * SUB : (g + 1) * SUB, p * LANES : (p + 1) * LANES] for g in range(groups)
            ]
            firsts.append(layers[0])
            lasts.append(layers[-1])
        for g in range(groups):
            if p < inner:
                here = turn(layers[g] * open_p, index[g])
                here_open = turn(open_p, index[g])
            else:
                here = here_open = zero
            options = [here] + turned[g]
            options_open = [here_open] + opened[g]
            turned[g] = options[:-1]
            opened[g] = options_open[:-1]
            total = total + choose(delay[g], options)
            part = choose(delay[g], options_open)
            if (g + 1) * SUB > bands:
                part = jnp.where(sub < bands - g * SUB, part, 0.0)
            count = count + part
        v, at = divmod(p, SUB)
        sums[v] = jnp.where(sub == at, jnp.sum(total, axis=0, keepdims=True), sums[v])
        counts[v] = jnp.where(sub == at, jnp.sum(count, axis=0, keepdims=True), counts[v])
    sides = []
    for g in (0, groups - 1):
        s = shear_i[g * SUB : (g + 1) * SUB]
        parts = [(s >> 1).astype(F32), (s & 1).astype(F32)]
        parts += list(split3(step_f[g * SUB : (g + 1) * SUB]))
        side = zero
        for i, part in enumerate(parts):
            side = jnp.where(lane == i, part, side)
        sides.append(side)
    half = inner // 2
    dn = [
        jnp.where(sub < 3, firsts[q], pltpu.roll(firsts[q + half], 3, 0)) for q in range(half)
    ] + [sides[0], zero]
    up = [
        jnp.where(sub < 3, pltpu.roll(lasts[q + half], SUB - 3, 0), lasts[q]) for q in range(half)
    ] + [sides[1], zero]
    part_ref[...] = jnp.concatenate(sums + counts, axis=0).astype(BF16)
    up_ref[...] = jnp.concatenate(sums + counts + up, axis=0).astype(BF16)
    dn_ref[...] = jnp.concatenate(sums + counts + dn, axis=0).astype(BF16)


def update_kernel(
    reach,
    fars,
    cube_ref,
    ap_ref,
    meas_ref,
    shear_ref,
    step_ref,
    own_ref,
    below_ref,
    above_ref,
    _,
    *rest_refs,
):
    far_refs = rest_refs[:fars]
    out_ref, msg_ref, raw, meas, rest_row = rest_refs[fars:]
    bands, cols = cube_ref.shape
    groups = -(-bands // SUB)
    inner = cols // LANES
    half = inner // 2
    tall = own_ref.shape[0] // 2
    outer = -(-meas_ref.shape[1] // LANES)
    raw[bands // SUB * SUB :, :] = jnp.zeros((raw.shape[0] - bands // SUB * SUB, cols), F32)
    raw[0:bands, :] = cube_ref[...].astype(F32)
    meas[:, (outer - 1) * LANES :] = jnp.zeros((1, LANES), F32)
    meas[:, 0 : meas_ref.shape[1]] = meas_ref[...]
    shear_f = column(shear_ref[...].astype(F32), groups * SUB)
    step_f = column(step_ref[...], groups * SUB)
    lane, sub = lanes_of(), rows_of()
    below = below_ref[...].astype(F32)
    above = above_ref[...].astype(F32)
    sums = own_ref[...].astype(F32) + below[0 : 2 * tall] + above[0 : 2 * tall]
    for far in far_refs:
        sums = sums + far[...].astype(F32)
    measured = []
    for v in range(tall // SUB):
        tile = jnp.zeros((SUB, LANES), F32)
        for at in range(min(SUB, outer - v * SUB)):
            p = v * SUB + at
            tile = jnp.where(sub == at, meas[:, p * LANES : (p + 1) * LANES], tile)
        measured.append(tile)
    measured = jnp.concatenate(measured, axis=0)
    rest_row[...] = (measured - sums[0:tall]) / jnp.maximum(sums[tall:], 1.0)

    def halo(q):
        at = 2 * tall + q % half * SUB
        high, low = above[at : at + SUB], below[at : at + SUB]
        if q // half == 1:
            high, low = pltpu.roll(high, SUB - 3, 0), pltpu.roll(low, 3, 0)
        return jnp.where(sub < 3, high, jnp.where(sub < 6, low, 0.0))

    side = 2 * tall + half * SUB
    side = jnp.where(sub < 3, above[side : side + SUB], below[side : side + SUB])
    shear_cols = [shear_f[g * SUB : (g + 1) * SUB] for g in range(groups)]
    step_cols = [step_f[g * SUB : (g + 1) * SUB] for g in range(groups)]
    inside = rows_of((SUB, 1)) < 6
    shear_cols.append(jnp.where(inside, 2.0 * side[:, 0:1] + side[:, 1:2], 0.0))
    step_cols.append(jnp.where(inside, side[:, 2:3] + side[:, 3:4] + side[:, 4:5], 0.0))
    index, delay, steps = [], [], []
    for g in range(groups + 1):
        s = jnp.broadcast_to(shear_cols[g].astype(I32), (SUB, LANES))
        rest = s & (LANES - 1)
        index.append((lane + rest) & (LANES - 1))
        delay.append((s >> 7) + jnp.where(lane + rest >= LANES, 1, 0))
        steps.append(jnp.broadcast_to(step_cols[g], (SUB, LANES)))
    tiles = []
    turned = [[] for _ in range(groups + 1)]
    for p in range(outer + 1):
        if p < outer:
            residual = jnp.broadcast_to(rest_row[p : p + 1, :], (SUB, LANES))
        else:
            residual = jnp.zeros((SUB, LANES), F32)
        tiles.append(jnp.where(sub == 6, residual, 0.0))
        for g in range(groups + 1):
            turned[g].append(turn(residual, index[g]) if p < outer else residual)
        q = p - (reach - 1)
        if q < 0 or q >= inner:
            continue
        here = slice(q * LANES, (q + 1) * LANES)
        open_q = jnp.broadcast_to(ap_ref[:, here].astype(F32), (SUB, LANES))
        pieces = []
        for g in range(groups + 1):
            pulled = choose(delay[g], turned[g][q : q + reach])
            base = raw[g * SUB : (g + 1) * SUB, here] if g < groups else halo(q)
            pieces.append(base + pulled * open_q * steps[g])
        out_ref[:, here] = jnp.concatenate(pieces, axis=0).astype(BF16)
        tiles[q] = jnp.where(sub < 6, pieces[-1], jnp.where(sub == 6, tiles[q], open_q))
    lost = rest_row[...]
    lost = lost - lost.astype(BF16).astype(F32)
    msg_ref[...] = jnp.concatenate(tiles + [lost], axis=0).astype(BF16)


def weights_kernel(
    _, sw_in, sb_in, cw_in, cb_in, ow_in, main_ref, halo_ref, first_ref, second_ref, out_w_ref, *rest
):
    local, sems = rest[:5], rest[5]
    for copy in fetch((sw_in, sb_in, cw_in, cb_in, ow_in), local, sems):
        copy.wait()
    sw_ref, sb_ref, cw_ref, cb_ref, ow_ref = local
    ch, taps2 = sw_ref.shape
    taps = cw_ref.shape[0]
    place = lax.axis_index("band")
    has_low = jnp.where(place > 0, 1, 0)
    has_high = jnp.where(place < lax.axis_size("band") - 1, 1, 0)

    def spread(rows, which):
        return (which(rows_of((rows, ch))) == lanes_of((rows, ch))).astype(F32).astype(BF16)

    def bias_column(row_ref, rows, which):
        pick = which(rows_of((rows, ch))) == lanes_of((rows, ch))
        row = jnp.broadcast_to(row_ref[...], (rows, ch))
        return 0.5 * jnp.sum(jnp.where(pick, row, 0.0), axis=1, keepdims=True)

    def with_bias(matrix, bias, start):
        lane = lanes_of(matrix.shape)
        for i, part in enumerate(split3(bias)):
            matrix = jnp.where(lane == start + i, part, matrix)
        return matrix

    width = main_ref.shape[1]
    slots = 16
    line = lax.axis_index("row") * lax.axis_size("col") + lax.axis_index("col")
    lines = lax.axis_size("row") * lax.axis_size("col")
    group = lanes_of((taps2, width)) // slots
    offset = jnp.where(line % 2 == 1, group // 3, 2 - group // 3)
    present = (line + offset >= 1) & (line + offset <= lines)
    fan = (rows_of((taps2, width)) == 3 * offset + group % 3) & present
    fan = fan.astype(F32).astype(BF16)
    flat = jnp.dot(sw_ref[...], fan, preferred_element_type=F32).astype(BF16)
    for ref, slot_of in (
        (main_ref, lambda b: b),
        (halo_ref, lambda b: jnp.where(b < 3, 11 + b, jnp.where(b < 9, b - 3, b - 1))),
    ):
        rows = ref.shape[0]
        which = lambda r: r % ch
        full = jnp.dot(spread(rows, which), flat, preferred_element_type=F32)
        lane = lanes_of((rows, width))
        band = rows_of((rows, width)) // ch
        keep = (lane % slots == slot_of(band)) & (lane < taps2 * slots)
        matrix = with_bias(
            jnp.where(keep, 0.5 * full, 0.0), bias_column(sb_ref, rows, which), taps2 * slots
        )
        if ref is halo_ref:
            valid = jnp.where(band < 3, has_low, jnp.where(band >= 9, has_high, 1))
            matrix = jnp.where(valid > 0, matrix, 0.0)
        ref[...] = matrix.astype(BF16)

    per = SUB
    rows = per * ch
    width = first_ref.shape[1]
    used = (per + taps - 1) * ch
    which = lambda r: r // per
    fan = (lanes_of((ch, width)) % ch == rows_of((ch, width))).astype(F32).astype(BF16)
    picks = spread(rows, which)
    lane = lanes_of((rows, width))
    ahead = jnp.where(lane < used, lane // ch - rows_of((rows, width)) % per, -LANES)
    shifts = (0, per, per - (per + taps - 1), 2 * per - (per + taps - 1))
    blocks = [jnp.zeros((rows, width), F32) for _ in shifts]
    for d in range(taps):
        flat = jnp.dot(cw_ref[d], fan, preferred_element_type=F32).astype(BF16)
        full = 0.5 * jnp.dot(picks, flat, preferred_element_type=F32)
        blocks = [jnp.where(ahead == d + s, full, b) for s, b in zip(shifts, blocks)]
    bias = bias_column(cb_ref, rows, which)
    for i, block in enumerate(blocks):
        block = block if i == 2 else with_bias(block, bias, used)
        ref = first_ref if i < 2 else second_ref
        ref[i % 2 * rows : (i % 2 + 1) * rows, :] = block.astype(BF16)
    pick = which(rows_of((rows, ch))) == lanes_of((rows, ch))
    scale = jnp.sum(jnp.where(pick, ow_ref[...], 0.0), axis=1, keepdims=True)
    out_w_ref[...] = jnp.broadcast_to(scale, out_w_ref.shape)


def denoise_kernel(
    tile,
    reach,
    ow_ref,
    mid_ref,
    shear_ref,
    step_ref,
    raw0_ref,
    msg0_ref,
    raw1_ref,
    msg1_ref,
    main_ref,
    halo_ref,
    first_ref,
    second_ref,
    out_ref,
    act,
    near0,
    near1,
    words,
):
    bands, cols = out_ref.shape
    slots = 16
    ch = main_ref.shape[0] // slots
    tiles = cols // tile
    inner = cols // LANES
    wide = tile + 2 * LANES
    split = act.shape[1] // 2
    groups = -(-bands // SUB)
    ones = jnp.where(rows_of((slots, tile)) < 3, 1.0, 0.0).astype(BF16)
    blank = jnp.zeros((2 * slots, LANES), F32)
    zero = jnp.zeros((SUB, LANES), F32)
    shear_f = column(shear_ref[...].astype(F32), groups * SUB)
    step_f = column(step_ref[...], groups * SUB)
    lane = lanes_of()
    index, delay, steps = [], [], []
    for g in range(groups):
        s = jnp.broadcast_to(shear_f[g * SUB : (g + 1) * SUB].astype(I32), (SUB, LANES))
        rest = s & (LANES - 1)
        index.append((lane + rest) & (LANES - 1))
        delay.append((s >> 7) + jnp.where(lane + rest >= LANES, 1, 0))
        steps.append(jnp.broadcast_to(step_f[g * SUB : (g + 1) * SUB], (SUB, LANES)))
    rows_in = msg0_ref.shape[0]
    chunks = inner + reach - 1
    lost = rows_in - -(-chunks // SUB) * SUB
    for n, msg_ref in enumerate((msg0_ref, msg1_ref)):
        words[n * rows_in : (n + 1) * rows_in, :] = msg_ref[...].astype(F32)
    turned = [[[] for _ in range(groups)] for _ in range(2)]

    def neighbours(q):
        for n, (raw_ref, near) in enumerate(((raw0_ref, near0), (raw1_ref, near1))):
            base = n * rows_in
            while len(turned[n][0]) < q + reach:
                p = len(turned[n][0])
                if p >= chunks:
                    residual = zero
                else:
                    at = base + p * SUB + 6
                    low = base + lost + p
                    residual = jnp.broadcast_to(
                        words[at : at + 1, :] + words[low : low + 1, :], (SUB, LANES)
                    )
                for g in range(groups):
                    turned[n][g].append(turn(residual, index[g]))
            at = base + q * SUB
            open_q = jnp.broadcast_to(words[at + 7 : at + 8, :], (SUB, LANES))
            raw = raw_ref[:, q * LANES : (q + 1) * LANES].astype(F32)
            raw = jnp.concatenate([raw, jnp.zeros((groups * SUB - bands, LANES), F32)], axis=0)
            pieces = [
                raw[g * SUB : (g + 1) * SUB]
                + choose(delay[g], turned[n][g][q : q + reach]) * open_q * steps[g]
                for g in range(groups)
            ]
            pieces.append(words[at : at + SUB, :])
            near[:, q * LANES : (q + 1) * LANES] = jnp.concatenate(pieces, axis=0).astype(BF16)

    def silu_twice(half):
        return half + half * jnp.tanh(half)

    def spatial(t):
        start = t * tile
        end = start + tile
        patches = []
        for ref in (near0, mid_ref, near1):
            left = ref[:, start - LANES : start].astype(F32) if t else blank
            here = ref[:, start:end]
            right = ref[:, end : end + LANES].astype(F32) if t < tiles - 1 else blank
            row = jnp.concatenate([left, here.astype(F32), right], axis=1)
            back = pltpu.roll(row, 1, 1)[:, LANES : LANES + tile].astype(BF16)
            ahead = pltpu.roll(row, wide - 1, 1)[:, LANES : LANES + tile].astype(BF16)
            patches += [back, here, ahead]
        buf = act.at[t % act.shape[0]]
        for part, w_ref in enumerate((main_ref, halo_ref)):
            x = jnp.concatenate(
                [p[part * slots : (part + 1) * slots] for p in patches] + [ones], axis=0
            )
            half = jnp.dot(w_ref[...], x, preferred_element_type=F32)
            value = silu_twice(half).astype(BF16)
            if part == 0:
                buf[3 * ch : 19 * ch, :] = value
            else:
                buf[0 : 3 * ch, :] = value[0 : 3 * ch]
                buf[19 * ch : 28 * ch, :] = value[3 * ch :]

    def spectral(t):
        start = t * tile
        buf = act.at[t % act.shape[0]]
        halves = []
        for part, w_ref in enumerate((first_ref, second_ref)):
            x = jnp.concatenate([buf[part * split : (part + 1) * split, :], ones], axis=0)
            halves.append(jnp.dot(w_ref[...], x, preferred_element_type=F32))
        rows = SUB * ch
        blocks = [halves[0][0:rows], halves[0][rows:] + halves[1][0:rows], halves[1][rows:]]
        pieces = []
        for half in blocks:
            total = None
            for k in range(ch):
                weight = ow_ref[k * SUB : (k + 1) * SUB, :]
                weight = jnp.concatenate([weight] * (tile // LANES), axis=1)
                term = weight * silu_twice(half[k * SUB : (k + 1) * SUB])
                total = term if total is None else total + term
            pieces.append(total)
        update = jnp.concatenate(pieces, axis=0)[0:bands]
        center = mid_ref[:, start : start + tile].astype(F32)[0:bands]
        out_ref[:, start : start + tile] = (center + update).astype(BF16)

    made = 0
    for t in range(tiles + 1):
        while t < tiles and made < min((t + 1) * tile // LANES + 1, inner):
            neighbours(made)
            made += 1
        if t < tiles:
            spatial(t)
        if t:
            spectral(t - 1)


def vmem(n):
    return [pl.BlockSpec(memory_space=pltpu.VMEM)] * n


def hbm(n):
    return [pl.BlockSpec(memory_space=pltpu.HBM)] * n


def in_hbm(arrays):
    return [pltpu.with_memory_space_constraint(x, pltpu.HBM) for x in arrays]


ANY = pl.BlockSpec(memory_space=pl.ANY)


def on_device(
    spectral_cube,
    aperture,
    measurement,
    shears,
    step_sizes,
    spatial_weight,
    spatial_bias,
    spectral_weight,
    spectral_bias,
    out_weight,
):
    bands, row_count, cols = spectral_cube.shape
    width = measurement.shape[1]
    reach = (width - cols) // LANES + 2
    outer = -(-width // LANES)
    groups = -(-bands // SUB)
    slots = (groups + 1) * SUB
    taps, ch = spectral_weight.shape[:2]
    taps2 = spatial_weight.shape[1]
    count = lax.axis_size("band")
    cube = spectral_cube.reshape(bands, cols)
    shear_row = shears.reshape(1, bands)
    step_row = step_sizes.reshape(1, bands)
    params = pltpu.CompilerParams(vmem_limit_bytes=48 * 2**20)

    tall = -(-outer // SUB) * SUB
    side = (cols // LANES // 2 + 2) * SUB
    inputs = (cube, aperture, measurement, shear_row, step_row)
    part, up, dn, *kept = pl.pallas_call(
        functools.partial(project_kernel, reach),
        out_shape=(
            jax.ShapeDtypeStruct((2 * tall, LANES), BF16),
            jax.ShapeDtypeStruct((2 * tall + side, LANES), BF16),
            jax.ShapeDtypeStruct((2 * tall + side, LANES), BF16),
        )
        + tuple(jax.ShapeDtypeStruct(x.shape, x.dtype) for x in inputs),
        in_specs=hbm(5),
        out_specs=tuple(vmem(8)),
        scratch_shapes=[
            pltpu.VMEM((groups * SUB, cols), F32),
            pltpu.SemaphoreType.DMA((5,)),
        ],
        compiler_params=params,
        name="project",
    )(*in_hbm(inputs))

    def around(x, shift):
        return lax.ppermute(x, "band", [(i, (i + shift) % count) for i in range(count)])

    below = around(up, 1)
    above = around(dn, -1)
    far = [around(part, s) for s in range(2, count - 1)]

    lines = lax.axis_size(("row", "col"))
    pairs = [(i, i ^ 1) for i in range(lines)]
    others = [(i, (i - 1 + i % 2 * 2) % lines) for i in range(lines)]
    raw0 = lax.ppermute(kept[0], ("row", "col"), pairs)
    raw1 = lax.ppermute(kept[0], ("row", "col"), others)

    small = (
        spatial_weight,
        spatial_bias.reshape(1, ch),
        spectral_weight,
        spectral_bias.reshape(1, ch),
        out_weight.reshape(1, ch),
    )
    reached = (SUB + taps - 1) * ch
    main_w, halo_w, first_w, second_w, out_w = pl.pallas_call(
        weights_kernel,
        out_shape=(
            jax.ShapeDtypeStruct((16 * ch, taps2 * 16 + 16), BF16),
            jax.ShapeDtypeStruct((12 * ch, taps2 * 16 + 16), BF16),
            jax.ShapeDtypeStruct((2 * SUB * ch, reached + 16), BF16),
            jax.ShapeDtypeStruct((2 * SUB * ch, reached + 16), BF16),
            jax.ShapeDtypeStruct((SUB * ch, LANES), F32),
        ),
        in_specs=[ANY] + hbm(5),
        out_specs=tuple(vmem(5)),
        scratch_shapes=[pltpu.VMEM(x.shape, x.dtype) for x in small]
        + [pltpu.SemaphoreType.DMA((5,))],
        compiler_params=params,
        name="weights",
    )(part, *in_hbm(small))

    words = (outer + 1) * SUB + tall
    updated, message = pl.pallas_call(
        functools.partial(update_kernel, reach, len(far)),
        out_shape=(
            jax.ShapeDtypeStruct((slots, cols), BF16),
            jax.ShapeDtypeStruct((words, LANES), BF16),
        ),
        in_specs=vmem(8) + [ANY] + vmem(len(far)),
        out_specs=tuple(vmem(2)),
        scratch_shapes=[
            pltpu.VMEM((groups * SUB, cols), F32),
            pltpu.VMEM((1, outer * LANES), F32),
            pltpu.VMEM((tall, LANES), F32),
        ],
        compiler_params=params,
        name="update",
    )(*kept, part, below, above, out_w, *far)

    message0 = lax.ppermute(message, ("row", "col"), pairs)
    message1 = lax.ppermute(message, ("row", "col"), others)

    tile = 512
    result = pl.pallas_call(
        functools.partial(denoise_kernel, tile, reach),
        out_shape=jax.ShapeDtypeStruct((bands, cols), BF16),
        in_specs=vmem(12),
        out_specs=vmem(1)[0],
        scratch_shapes=[
            pltpu.VMEM((4, 28 * ch, tile), BF16),
            pltpu.VMEM((slots, cols), BF16),
            pltpu.VMEM((slots, cols), BF16),
            pltpu.VMEM((2 * words, LANES), F32),
        ],
        compiler_params=params,
        name="denoise",
    )(
        out_w,
        updated,
        kept[3],
        kept[4],
        raw0,
        message0,
        raw1,
        message1,
        main_w,
        halo_w,
        first_w,
        second_w,
    )
    return result.reshape(bands, 1, cols)


def solution(mesh):
    in_specs = (
        P("band", ("row", "col"), None),
        P(("row", "col"), None),
        P(("row", "col"), None),
        P("band"),
        P("band"),
        P(),
        P(),
        P(),
        P(),
        P(),
    )
    out_specs = P("band", ("row", "col"), None)
    return jax.shard_map(
        on_device, mesh=mesh, in_specs=in_specs, out_specs=out_specs, check_vma=False
    )
```

```python
import functools

import jax
import jax.numpy as jnp
from jax import lax
from jax.experimental import pallas as pl
from jax.experimental.pallas import tpu as pltpu
from jax.sharding import PartitionSpec as P

LANES = 128
SUB = 8
F32 = jnp.float32
BF16 = jnp.bfloat16
I32 = jnp.int32


def lanes_of(shape=(SUB, LANES)):
    return lax.broadcasted_iota(I32, shape, 1)


def rows_of(shape=(SUB, LANES)):
    return lax.broadcasted_iota(I32, shape, 0)


def column(row, rows):
    n = row.shape[1]
    eye = rows_of((rows, n)) == lanes_of((rows, n))
    return jnp.sum(jnp.where(eye, jnp.broadcast_to(row, (rows, n)), 0.0), axis=1, keepdims=True)


def turn(chunk, index):
    return jnp.take_along_axis(chunk, index, axis=1, mode="promise_in_bounds")


def choose(delay, options):
    result = options[-1]
    for d in range(len(options) - 2, -1, -1):
        result = jnp.where(delay == d, options[d], result)
    return result


def split3(x):
    hi = x.astype(BF16).astype(F32)
    mid = (x - hi).astype(BF16).astype(F32)
    return hi, mid, x - hi - mid


def fetch(sources, targets, sems):
    copies = [
        pltpu.make_async_copy(src, dst, sems.at[i]) for i, (src, dst) in enumerate(zip(sources, targets))
    ]
    for copy in copies:
        copy.start()
    return copies


def project_kernel(
    reach, cube_in, ap_in, meas_in, shear_in, step_in, part_ref, up_ref, dn_ref, *rest_refs
):
    kept, (raw, sems) = rest_refs[:5], rest_refs[5:]
    cube_ref, ap_ref, meas_ref, shear_ref, step_ref = kept
    copies = fetch((cube_in, ap_in, meas_in, shear_in, step_in), kept, sems)
    for copy in copies:
        copy.wait()
    bands, cols = cube_ref.shape
    groups = -(-bands // SUB)
    inner = cols // LANES
    tall = part_ref.shape[0] // 2
    outer = -(-meas_ref.shape[1] // LANES)
    raw[bands // SUB * SUB :, :] = jnp.zeros((raw.shape[0] - bands // SUB * SUB, cols), F32)
    raw[0:bands, :] = cube_ref[...].astype(F32)
    shear_f = column(shear_ref[...].astype(F32), groups * SUB)
    step_f = column(step_ref[...], groups * SUB)
    shear_i = shear_f.astype(I32)
    lane, sub = lanes_of(), rows_of()
    index, delay = [], []
    for g in range(groups):
        s = jnp.broadcast_to(shear_i[g * SUB : (g + 1) * SUB], (SUB, LANES))
        rest = s & (LANES - 1)
        index.append((lane - rest) & (LANES - 1))
        delay.append((s >> 7) + jnp.where(lane < rest, 1, 0))
    zero = jnp.zeros((SUB, LANES), F32)
    turned = [[zero] * (reach - 1) for _ in range(groups)]
    opened = [[zero] * (reach - 1) for _ in range(groups)]
    sums = [zero] * (tall // SUB)
    counts = [zero] * (tall // SUB)
    firsts, lasts = [], []
    for p in range(outer):
        total = zero
        count = zero
        if p < inner:
            open_p = jnp.broadcast_to(
                ap_ref[:, p * LANES : (p + 1) * LANES].astype(F32), (SUB, LANES)
            )
            layers = [
                raw[g * SUB : (g + 1) * SUB, p * LANES : (p + 1) * LANES] for g in range(groups)
            ]
            firsts.append(layers[0])
            lasts.append(layers[-1])
        for g in range(groups):
            if p < inner:
                here = turn(layers[g] * open_p, index[g])
                here_open = turn(open_p, index[g])
            else:
                here = here_open = zero
            options = [here] + turned[g]
            options_open = [here_open] + opened[g]
            turned[g] = options[:-1]
            opened[g] = options_open[:-1]
            total = total + choose(delay[g], options)
            part = choose(delay[g], options_open)
            if (g + 1) * SUB > bands:
                part = jnp.where(sub < bands - g * SUB, part, 0.0)
            count = count + part
        v, at = divmod(p, SUB)
        sums[v] = jnp.where(sub == at, jnp.sum(total, axis=0, keepdims=True), sums[v])
        counts[v] = jnp.where(sub == at, jnp.sum(count, axis=0, keepdims=True), counts[v])
    sides = []
    for g in (0, groups - 1):
        s = shear_i[g * SUB : (g + 1) * SUB]
        parts = [(s >> 1).astype(F32), (s & 1).astype(F32)]
        parts += list(split3(step_f[g * SUB : (g + 1) * SUB]))
        side = zero
        for i, part in enumerate(parts):
            side = jnp.where(lane == i, part, side)
        sides.append(side)
    half = inner // 2
    dn = [
        jnp.where(sub < 3, firsts[q], pltpu.roll(firsts[q + half], 3, 0)) for q in range(half)
    ] + [sides[0], zero]
    up = [
        jnp.where(sub < 3, pltpu.roll(lasts[q + half], SUB - 3, 0), lasts[q]) for q in range(half)
    ] + [sides[1], zero]
    part_ref[...] = jnp.concatenate(sums + counts, axis=0).astype(BF16)
    up_ref[...] = jnp.concatenate(sums + counts + up, axis=0).astype(BF16)
    dn_ref[...] = jnp.concatenate(sums + counts + dn, axis=0).astype(BF16)


def update_kernel(
    reach,
    fars,
    cube_ref,
    ap_ref,
    meas_ref,
    shear_ref,
    step_ref,
    own_ref,
    below_ref,
    above_ref,
    _,
    *rest_refs,
):
    far_refs = rest_refs[:fars]
    out_ref, msg_ref, raw, meas, rest_row = rest_refs[fars:]
    bands, cols = cube_ref.shape
    groups = -(-bands // SUB)
    inner = cols // LANES
    half = inner // 2
    tall = own_ref.shape[0] // 2
    outer = -(-meas_ref.shape[1] // LANES)
    raw[bands // SUB * SUB :, :] = jnp.zeros((raw.shape[0] - bands // SUB * SUB, cols), F32)
    raw[0:bands, :] = cube_ref[...].astype(F32)
    meas[:, (outer - 1) * LANES :] = jnp.zeros((1, LANES), F32)
    meas[:, 0 : meas_ref.shape[1]] = meas_ref[...]
    shear_f = column(shear_ref[...].astype(F32), groups * SUB)
    step_f = column(step_ref[...], groups * SUB)
    lane, sub = lanes_of(), rows_of()
    below = below_ref[...].astype(F32)
    above = above_ref[...].astype(F32)
    sums = own_ref[...].astype(F32) + below[0 : 2 * tall] + above[0 : 2 * tall]
    for far in far_refs:
        sums = sums + far[...].astype(F32)
    measured = []
    for v in range(tall // SUB):
        tile = jnp.zeros((SUB, LANES), F32)
        for at in range(min(SUB, outer - v * SUB)):
            p = v * SUB + at
            tile = jnp.where(sub == at, meas[:, p * LANES : (p + 1) * LANES], tile)
        measured.append(tile)
    measured = jnp.concatenate(measured, axis=0)
    rest_row[...] = (measured - sums[0:tall]) / jnp.maximum(sums[tall:], 1.0)

    def halo(q):
        at = 2 * tall + q % half * SUB
        high, low = above[at : at + SUB], below[at : at + SUB]
        if q // half == 1:
            high, low = pltpu.roll(high, SUB - 3, 0), pltpu.roll(low, 3, 0)
        return jnp.where(sub < 3, high, jnp.where(sub < 6, low, 0.0))

    side = 2 * tall + half * SUB
    side = jnp.where(sub < 3, above[side : side + SUB], below[side : side + SUB])
    shear_cols = [shear_f[g * SUB : (g + 1) * SUB] for g in range(groups)]
    step_cols = [step_f[g * SUB : (g + 1) * SUB] for g in range(groups)]
    inside = rows_of((SUB, 1)) < 6
    shear_cols.append(jnp.where(inside, 2.0 * side[:, 0:1] + side[:, 1:2], 0.0))
    step_cols.append(jnp.where(inside, side[:, 2:3] + side[:, 3:4] + side[:, 4:5], 0.0))
    index, delay, steps = [], [], []
    for g in range(groups + 1):
        s = jnp.broadcast_to(shear_cols[g].astype(I32), (SUB, LANES))
        rest = s & (LANES - 1)
        index.append((lane + rest) & (LANES - 1))
        delay.append((s >> 7) + jnp.where(lane + rest >= LANES, 1, 0))
        steps.append(jnp.broadcast_to(step_cols[g], (SUB, LANES)))
    tiles = []
    turned = [[] for _ in range(groups + 1)]
    for p in range(outer + 1):
        if p < outer:
            residual = jnp.broadcast_to(rest_row[p : p + 1, :], (SUB, LANES))
        else:
            residual = jnp.zeros((SUB, LANES), F32)
        tiles.append(jnp.where(sub == 6, residual, 0.0))
        for g in range(groups + 1):
            turned[g].append(turn(residual, index[g]) if p < outer else residual)
        q = p - (reach - 1)
        if q < 0 or q >= inner:
            continue
        here = slice(q * LANES, (q + 1) * LANES)
        open_q = jnp.broadcast_to(ap_ref[:, here].astype(F32), (SUB, LANES))
        pieces = []
        for g in range(groups + 1):
            pulled = choose(delay[g], turned[g][q : q + reach])
            base = raw[g * SUB : (g + 1) * SUB, here] if g < groups else halo(q)
            pieces.append(base + pulled * open_q * steps[g])
        out_ref[:, here] = jnp.concatenate(pieces, axis=0).astype(BF16)
        tiles[q] = jnp.where(sub < 6, pieces[-1], jnp.where(sub == 6, tiles[q], open_q))
    lost = rest_row[...]
    lost = lost - lost.astype(BF16).astype(F32)
    msg_ref[...] = jnp.concatenate(tiles + [lost], axis=0).astype(BF16)


def spread(rows, ch, which):
    return (which(rows_of((rows, ch))) == lanes_of((rows, ch))).astype(F32).astype(BF16)


def picked(row_ref, rows, which):
    ch = row_ref.shape[1]
    pick = which(rows_of((rows, ch))) == lanes_of((rows, ch))
    row = jnp.broadcast_to(row_ref[...], (rows, ch))
    return jnp.sum(jnp.where(pick, row, 0.0), axis=1, keepdims=True)


def with_bias(matrix, bias, start):
    lane = lanes_of(matrix.shape)
    for i, part in enumerate(split3(0.5 * bias)):
        matrix = jnp.where(lane == start + i, part, matrix)
    return matrix


def spatial_weights_kernel(_, cube_ref, sw_in, sb_in, main_ref, halo_ref, same_ref, *rest):
    local, sems = rest[:2], rest[2]
    for copy in fetch((sw_in, sb_in), local, sems):
        copy.wait()
    sw_ref, sb_ref = local
    ch, taps2 = sw_ref.shape
    place = lax.axis_index("band")
    has_low = jnp.where(place > 0, 1, 0)
    has_high = jnp.where(place < lax.axis_size("band") - 1, 1, 0)
    width = main_ref.shape[1]
    slots = 16
    line = lax.axis_index("row") * lax.axis_size("col") + lax.axis_index("col")
    lines = lax.axis_size("row") * lax.axis_size("col")
    group = lanes_of((taps2, width)) // slots
    offset = jnp.where(line % 2 == 1, group // 3, 2 - group // 3)
    present = (line + offset >= 1) & (line + offset <= lines)
    fan = (rows_of((taps2, width)) == 3 * offset + group % 3) & present
    fan = fan.astype(F32).astype(BF16)
    flat = jnp.dot(sw_ref[...], fan, preferred_element_type=F32).astype(BF16)
    for ref, slot_of in (
        (main_ref, lambda b: b),
        (halo_ref, lambda b: jnp.where(b < 3, 11 + b, jnp.where(b < 9, b - 3, b - 1))),
    ):
        rows = ref.shape[0]
        which = lambda r: r % ch
        full = jnp.dot(spread(rows, ch, which), flat, preferred_element_type=F32)
        lane = lanes_of((rows, width))
        band = rows_of((rows, width)) // ch
        keep = (lane % slots == slot_of(band)) & (lane < taps2 * slots)
        matrix = with_bias(
            jnp.where(keep, 0.5 * full, 0.0), picked(sb_ref, rows, which), taps2 * slots
        )
        if ref is halo_ref:
            valid = jnp.where(band < 3, has_low, jnp.where(band >= 9, has_high, 1))
            matrix = jnp.where(valid > 0, matrix, 0.0)
        ref[...] = matrix.astype(BF16)


def spectral_weights_kernel(_, cw_in, cb_in, ow_in, first_ref, second_ref, out_w_ref, *rest):
    local, sems = rest[:3], rest[3]
    for copy in fetch((cw_in, cb_in, ow_in), local, sems):
        copy.wait()
    cw_ref, cb_ref, ow_ref = local
    taps, ch = cw_ref.shape[:2]
    per = SUB
    rows = per * ch
    width = first_ref.shape[1]
    used = (per + taps - 1) * ch
    which = lambda r: r // per
    fan = (lanes_of((ch, width)) % ch == rows_of((ch, width))).astype(F32).astype(BF16)
    picks = spread(rows, ch, which)
    lane = lanes_of((rows, width))
    ahead = jnp.where(lane < used, lane // ch - rows_of((rows, width)) % per, -LANES)
    shifts = (0, per, per - (per + taps - 1), 2 * per - (per + taps - 1))
    blocks = [jnp.zeros((rows, width), F32) for _ in shifts]
    for d in range(taps):
        flat = jnp.dot(cw_ref[d], fan, preferred_element_type=F32).astype(BF16)
        full = 0.5 * jnp.dot(picks, flat, preferred_element_type=F32)
        blocks = [jnp.where(ahead == d + s, full, b) for s, b in zip(shifts, blocks)]
    bias = picked(cb_ref, rows, which)
    for i, block in enumerate(blocks):
        block = block if i == 2 else with_bias(block, bias, used)
        ref = first_ref if i < 2 else second_ref
        ref[i % 2 * rows : (i % 2 + 1) * rows, :] = block.astype(BF16)
    out_w_ref[...] = jnp.broadcast_to(picked(ow_ref, rows, which), out_w_ref.shape)


def denoise_kernel(
    tile,
    reach,
    ow_ref,
    mid_ref,
    shear_ref,
    step_ref,
    raw0_ref,
    msg0_ref,
    raw1_ref,
    msg1_ref,
    main_ref,
    halo_ref,
    first_ref,
    second_ref,
    out_ref,
    act,
    near0,
    near1,
    words,
):
    bands, cols = out_ref.shape
    slots = 16
    ch = main_ref.shape[0] // slots
    tiles = cols // tile
    inner = cols // LANES
    wide = tile + 2 * LANES
    split = act.shape[1] // 2
    groups = -(-bands // SUB)
    ones = jnp.where(rows_of((slots, tile)) < 3, 1.0, 0.0).astype(BF16)
    blank = jnp.zeros((2 * slots, LANES), F32)
    zero = jnp.zeros((SUB, LANES), F32)
    shear_f = column(shear_ref[...].astype(F32), groups * SUB)
    step_f = column(step_ref[...], groups * SUB)
    lane = lanes_of()
    index, delay, steps = [], [], []
    for g in range(groups):
        s = jnp.broadcast_to(shear_f[g * SUB : (g + 1) * SUB].astype(I32), (SUB, LANES))
        rest = s & (LANES - 1)
        index.append((lane + rest) & (LANES - 1))
        delay.append((s >> 7) + jnp.where(lane + rest >= LANES, 1, 0))
        steps.append(jnp.broadcast_to(step_f[g * SUB : (g + 1) * SUB], (SUB, LANES)))
    rows_in = msg0_ref.shape[0]
    chunks = inner + reach - 1
    lost = rows_in - -(-chunks // SUB) * SUB
    for n, msg_ref in enumerate((msg0_ref, msg1_ref)):
        words[n * rows_in : (n + 1) * rows_in, :] = msg_ref[...].astype(F32)
    turned = [[[] for _ in range(groups)] for _ in range(2)]

    def neighbours(q):
        for n, (raw_ref, near) in enumerate(((raw0_ref, near0), (raw1_ref, near1))):
            base = n * rows_in
            while len(turned[n][0]) < q + reach:
                p = len(turned[n][0])
                if p >= chunks:
                    residual = zero
                else:
                    at = base + p * SUB + 6
                    low = base + lost + p
                    residual = jnp.broadcast_to(
                        words[at : at + 1, :] + words[low : low + 1, :], (SUB, LANES)
                    )
                for g in range(groups):
                    turned[n][g].append(turn(residual, index[g]))
            at = base + q * SUB
            open_q = jnp.broadcast_to(words[at + 7 : at + 8, :], (SUB, LANES))
            raw = raw_ref[:, q * LANES : (q + 1) * LANES].astype(F32)
            raw = jnp.concatenate([raw, jnp.zeros((groups * SUB - bands, LANES), F32)], axis=0)
            pieces = [
                raw[g * SUB : (g + 1) * SUB]
                + choose(delay[g], turned[n][g][q : q + reach]) * open_q * steps[g]
                for g in range(groups)
            ]
            pieces.append(words[at : at + SUB, :])
            near[:, q * LANES : (q + 1) * LANES] = jnp.concatenate(pieces, axis=0).astype(BF16)

    def silu_twice(half):
        return half + half * jnp.tanh(half)

    def spatial(t):
        start = t * tile
        end = start + tile
        patches = []
        for ref in (near0, mid_ref, near1):
            left = ref[:, start - LANES : start].astype(F32) if t else blank
            here = ref[:, start:end]
            right = ref[:, end : end + LANES].astype(F32) if t < tiles - 1 else blank
            row = jnp.concatenate([left, here.astype(F32), right], axis=1)
            back = pltpu.roll(row, 1, 1)[:, LANES : LANES + tile].astype(BF16)
            ahead = pltpu.roll(row, wide - 1, 1)[:, LANES : LANES + tile].astype(BF16)
            patches += [back, here, ahead]
        buf = act.at[t % act.shape[0]]
        for part, w_ref in enumerate((main_ref, halo_ref)):
            x = jnp.concatenate(
                [p[part * slots : (part + 1) * slots] for p in patches] + [ones], axis=0
            )
            half = jnp.dot(w_ref[...], x, preferred_element_type=F32)
            value = silu_twice(half).astype(BF16)
            if part == 0:
                buf[3 * ch : 19 * ch, :] = value
            else:
                buf[0 : 3 * ch, :] = value[0 : 3 * ch]
                buf[19 * ch : 28 * ch, :] = value[3 * ch :]

    def spectral(t):
        start = t * tile
        buf = act.at[t % act.shape[0]]
        halves = []
        for part, w_ref in enumerate((first_ref, second_ref)):
            x = jnp.concatenate([buf[part * split : (part + 1) * split, :], ones], axis=0)
            halves.append(jnp.dot(w_ref[...], x, preferred_element_type=F32))
        rows = SUB * ch
        blocks = [halves[0][0:rows], halves[0][rows:] + halves[1][0:rows], halves[1][rows:]]
        pieces = []
        for half in blocks:
            total = None
            for k in range(ch):
                weight = ow_ref[k * SUB : (k + 1) * SUB, :]
                weight = jnp.concatenate([weight] * (tile // LANES), axis=1)
                term = weight * silu_twice(half[k * SUB : (k + 1) * SUB])
                total = term if total is None else total + term
            pieces.append(total)
        update = jnp.concatenate(pieces, axis=0)[0:bands]
        center = mid_ref[:, start : start + tile].astype(F32)[0:bands]
        out_ref[:, start : start + tile] = (center + update).astype(BF16)

    made = 0
    for t in range(tiles + 1):
        while t < tiles and made < min((t + 1) * tile // LANES + 1, inner):
            neighbours(made)
            made += 1
        if t < tiles:
            spatial(t)
        if t:
            spectral(t - 1)


def vmem(n):
    return [pl.BlockSpec(memory_space=pltpu.VMEM)] * n


def hbm(n):
    return [pl.BlockSpec(memory_space=pltpu.HBM)] * n


def in_hbm(arrays):
    return [pltpu.with_memory_space_constraint(x, pltpu.HBM) for x in arrays]


ANY = pl.BlockSpec(memory_space=pl.ANY)


def on_device(
    spectral_cube,
    aperture,
    measurement,
    shears,
    step_sizes,
    spatial_weight,
    spatial_bias,
    spectral_weight,
    spectral_bias,
    out_weight,
):
    bands, row_count, cols = spectral_cube.shape
    width = measurement.shape[1]
    reach = (width - cols) // LANES + 2
    outer = -(-width // LANES)
    groups = -(-bands // SUB)
    slots = (groups + 1) * SUB
    taps, ch = spectral_weight.shape[:2]
    taps2 = spatial_weight.shape[1]
    count = lax.axis_size("band")
    cube = spectral_cube.reshape(bands, cols)
    shear_row = shears.reshape(1, bands)
    step_row = step_sizes.reshape(1, bands)
    params = pltpu.CompilerParams(vmem_limit_bytes=48 * 2**20)

    tall = -(-outer // SUB) * SUB
    side = (cols // LANES // 2 + 2) * SUB
    inputs = (cube, aperture, measurement, shear_row, step_row)
    part, up, dn, *kept = pl.pallas_call(
        functools.partial(project_kernel, reach),
        out_shape=(
            jax.ShapeDtypeStruct((2 * tall, LANES), BF16),
            jax.ShapeDtypeStruct((2 * tall + side, LANES), BF16),
            jax.ShapeDtypeStruct((2 * tall + side, LANES), BF16),
        )
        + tuple(jax.ShapeDtypeStruct(x.shape, x.dtype) for x in inputs),
        in_specs=hbm(5),
        out_specs=tuple(vmem(8)),
        scratch_shapes=[
            pltpu.VMEM((groups * SUB, cols), F32),
            pltpu.SemaphoreType.DMA((5,)),
        ],
        compiler_params=params,
        name="project",
    )(*in_hbm(inputs))

    def around(x, shift):
        return lax.ppermute(x, "band", [(i, (i + shift) % count) for i in range(count)])

    below = around(up, 1)
    above = around(dn, -1)
    far = [around(part, s) for s in range(2, count - 1)]

    small = (spatial_weight, spatial_bias.reshape(1, ch))
    main_w, halo_w, cube = pl.pallas_call(
        spatial_weights_kernel,
        out_shape=(
            jax.ShapeDtypeStruct((16 * ch, taps2 * 16 + 16), BF16),
            jax.ShapeDtypeStruct((12 * ch, taps2 * 16 + 16), BF16),
            jax.ShapeDtypeStruct(cube.shape, BF16),
        ),
        in_specs=[ANY, ANY] + hbm(2),
        out_specs=(*vmem(2), ANY),
        scratch_shapes=[pltpu.VMEM(x.shape, x.dtype) for x in small]
        + [pltpu.SemaphoreType.DMA((2,))],
        input_output_aliases={1: 2},
        compiler_params=params,
        name="spatial_weights",
    )(part, kept[0], *in_hbm(small))
    kept[0] = cube

    lines = lax.axis_size(("row", "col"))
    pairs = [(i, i ^ 1) for i in range(lines)]
    others = [(i, (i - 1 + i % 2 * 2) % lines) for i in range(lines)]
    raw0 = lax.ppermute(cube, ("row", "col"), pairs)
    raw1 = lax.ppermute(cube, ("row", "col"), others)

    small = (spectral_weight, spectral_bias.reshape(1, ch), out_weight.reshape(1, ch))
    reached = (SUB + taps - 1) * ch
    first_w, second_w, out_w = pl.pallas_call(
        spectral_weights_kernel,
        out_shape=(
            jax.ShapeDtypeStruct((2 * SUB * ch, reached + 16), BF16),
            jax.ShapeDtypeStruct((2 * SUB * ch, reached + 16), BF16),
            jax.ShapeDtypeStruct((SUB * ch, LANES), F32),
        ),
        in_specs=[ANY] + hbm(3),
        out_specs=tuple(vmem(3)),
        scratch_shapes=[pltpu.VMEM(x.shape, x.dtype) for x in small]
        + [pltpu.SemaphoreType.DMA((3,))],
        compiler_params=params,
        name="spectral_weights",
    )(halo_w, *in_hbm(small))

    words = (outer + 1) * SUB + tall
    updated, message = pl.pallas_call(
        functools.partial(update_kernel, reach, len(far)),
        out_shape=(
            jax.ShapeDtypeStruct((slots, cols), BF16),
            jax.ShapeDtypeStruct((words, LANES), BF16),
        ),
        in_specs=vmem(8) + [ANY] + vmem(len(far)),
        out_specs=tuple(vmem(2)),
        scratch_shapes=[
            pltpu.VMEM((groups * SUB, cols), F32),
            pltpu.VMEM((1, outer * LANES), F32),
            pltpu.VMEM((tall, LANES), F32),
        ],
        compiler_params=params,
        cost_estimate=pl.CostEstimate(
            flops=10**10, bytes_accessed=4 * 10**7, transcendentals=0
        ),
        name="update",
    )(*kept, part, below, above, out_w, *far)

    message0 = lax.ppermute(message, ("row", "col"), pairs)
    message1 = lax.ppermute(message, ("row", "col"), others)

    tile = 512
    result = pl.pallas_call(
        functools.partial(denoise_kernel, tile, reach),
        out_shape=jax.ShapeDtypeStruct((bands, cols), BF16),
        in_specs=vmem(12),
        out_specs=vmem(1)[0],
        scratch_shapes=[
            pltpu.VMEM((4, 28 * ch, tile), BF16),
            pltpu.VMEM((slots, cols), BF16),
            pltpu.VMEM((slots, cols), BF16),
            pltpu.VMEM((2 * words, LANES), F32),
        ],
        compiler_params=params,
        name="denoise",
    )(
        out_w,
        updated,
        kept[3],
        kept[4],
        raw0,
        message0,
        raw1,
        message1,
        main_w,
        halo_w,
        first_w,
        second_w,
    )
    return result.reshape(bands, 1, cols)


def solution(mesh):
    in_specs = (
        P("band", ("row", "col"), None),
        P(("row", "col"), None),
        P(("row", "col"), None),
        P("band"),
        P("band"),
        P(),
        P(),
        P(),
        P(),
        P(),
    )
    out_specs = P("band", ("row", "col"), None)
    return jax.shard_map(
        on_device, mesh=mesh, in_specs=in_specs, out_specs=out_specs, check_vma=False
    )
```

```python
import functools

import jax
import jax.numpy as jnp
from jax import lax
from jax.experimental import pallas as pl
from jax.experimental.pallas import tpu as pltpu
from jax.sharding import PartitionSpec as P

LANES = 128
SUB = 8
F32 = jnp.float32
BF16 = jnp.bfloat16
I32 = jnp.int32


def lanes_of(shape=(SUB, LANES)):
    return lax.broadcasted_iota(I32, shape, 1)


def rows_of(shape=(SUB, LANES)):
    return lax.broadcasted_iota(I32, shape, 0)


def column(row, rows):
    n = row.shape[1]
    eye = rows_of((rows, n)) == lanes_of((rows, n))
    return jnp.sum(jnp.where(eye, jnp.broadcast_to(row, (rows, n)), 0.0), axis=1, keepdims=True)


def turn(chunk, index):
    return jnp.take_along_axis(chunk, index, axis=1, mode="promise_in_bounds")


def choose(delay, options):
    result = options[-1]
    for d in range(len(options) - 2, -1, -1):
        result = jnp.where(delay == d, options[d], result)
    return result


def split3(x):
    hi = x.astype(BF16).astype(F32)
    mid = (x - hi).astype(BF16).astype(F32)
    return hi, mid, x - hi - mid


def fetch(sources, targets, sems):
    copies = [
        pltpu.make_async_copy(src, dst, sems.at[i]) for i, (src, dst) in enumerate(zip(sources, targets))
    ]
    for copy in copies:
        copy.start()
    return copies


def project_kernel(
    reach, cube_in, ap_in, meas_in, shear_in, step_in, part_ref, up_ref, dn_ref, *rest_refs
):
    line_ref, *kept = rest_refs[:5]
    cube_ref, raw, sems = rest_refs[5:]
    ap_ref, meas_ref, shear_ref, step_ref = kept
    copies = fetch((cube_in, ap_in, meas_in, shear_in, step_in), (cube_ref, *kept), sems)
    for copy in copies:
        copy.wait()
    bands, cols = cube_ref.shape
    groups = -(-bands // SUB)
    inner = cols // LANES
    tall = part_ref.shape[0] // 2
    outer = -(-meas_ref.shape[1] // LANES)
    raw[bands // SUB * SUB :, :] = jnp.zeros((raw.shape[0] - bands // SUB * SUB, cols), F32)
    raw[0:bands, :] = cube_ref[...].astype(F32)
    shear_f = column(shear_ref[...].astype(F32), groups * SUB)
    step_f = column(step_ref[...], groups * SUB)
    shear_i = shear_f.astype(I32)
    lane, sub = lanes_of(), rows_of()
    index, delay = [], []
    for g in range(groups):
        s = jnp.broadcast_to(shear_i[g * SUB : (g + 1) * SUB], (SUB, LANES))
        rest = s & (LANES - 1)
        index.append((lane - rest) & (LANES - 1))
        delay.append((s >> 7) + jnp.where(lane < rest, 1, 0))
    zero = jnp.zeros((SUB, LANES), F32)
    turned = [[zero] * (reach - 1) for _ in range(groups)]
    opened = [[zero] * (reach - 1) for _ in range(groups)]
    sums = [zero] * (tall // SUB)
    counts = [zero] * (tall // SUB)
    firsts, lasts = [], []
    for p in range(outer):
        total = zero
        count = zero
        if p < inner:
            open_p = jnp.broadcast_to(
                ap_ref[:, p * LANES : (p + 1) * LANES].astype(F32), (SUB, LANES)
            )
            layers = [
                raw[g * SUB : (g + 1) * SUB, p * LANES : (p + 1) * LANES] for g in range(groups)
            ]
            firsts.append(layers[0])
            lasts.append(layers[-1])
            tagged = jnp.where(sub == bands % SUB, open_p, layers[-1])
            line_ref[:, p * LANES : (p + 1) * LANES] = jnp.concatenate(
                layers[:-1] + [tagged], axis=0
            ).astype(BF16)
        for g in range(groups):
            if p < inner:
                here = turn(layers[g] * open_p, index[g])
                here_open = turn(open_p, index[g])
            else:
                here = here_open = zero
            options = [here] + turned[g]
            options_open = [here_open] + opened[g]
            turned[g] = options[:-1]
            opened[g] = options_open[:-1]
            total = total + choose(delay[g], options)
            part = choose(delay[g], options_open)
            if (g + 1) * SUB > bands:
                part = jnp.where(sub < bands - g * SUB, part, 0.0)
            count = count + part
        v, at = divmod(p, SUB)
        sums[v] = jnp.where(sub == at, jnp.sum(total, axis=0, keepdims=True), sums[v])
        counts[v] = jnp.where(sub == at, jnp.sum(count, axis=0, keepdims=True), counts[v])
    sides = []
    for g in (0, groups - 1):
        s = shear_i[g * SUB : (g + 1) * SUB]
        parts = [(s >> 1).astype(F32), (s & 1).astype(F32)]
        parts += list(split3(step_f[g * SUB : (g + 1) * SUB]))
        side = zero
        for i, part in enumerate(parts):
            side = jnp.where(lane == i, part, side)
        sides.append(side)
    half = inner // 2
    dn = [
        jnp.where(sub < 3, firsts[q], pltpu.roll(firsts[q + half], 3, 0)) for q in range(half)
    ] + [sides[0], zero]
    up = [
        jnp.where(sub < 3, pltpu.roll(lasts[q + half], SUB - 3, 0), lasts[q]) for q in range(half)
    ] + [sides[1], zero]
    part_ref[...] = jnp.concatenate(sums + counts, axis=0).astype(BF16)
    up_ref[...] = jnp.concatenate(sums + counts + up, axis=0).astype(BF16)
    dn_ref[...] = jnp.concatenate(sums + counts + dn, axis=0).astype(BF16)


def update_kernel(
    reach,
    fars,
    line_ref,
    ap_ref,
    meas_ref,
    shear_ref,
    step_ref,
    own_ref,
    below_ref,
    above_ref,
    *rest_refs,
):
    far_refs = rest_refs[:fars]
    out_ref, msg_ref, raw, meas, rest_row = rest_refs[fars:]
    groups = line_ref.shape[0] // SUB
    cols = line_ref.shape[1]
    inner = cols // LANES
    half = inner // 2
    tall = own_ref.shape[0] // 2
    outer = -(-meas_ref.shape[1] // LANES)
    raw[...] = line_ref[...].astype(F32)
    meas[:, (outer - 1) * LANES :] = jnp.zeros((1, LANES), F32)
    meas[:, 0 : meas_ref.shape[1]] = meas_ref[...]
    shear_f = column(shear_ref[...].astype(F32), groups * SUB)
    step_f = column(step_ref[...], groups * SUB)
    lane, sub = lanes_of(), rows_of()
    below = below_ref[...].astype(F32)
    above = above_ref[...].astype(F32)
    sums = own_ref[...].astype(F32) + below[0 : 2 * tall] + above[0 : 2 * tall]
    for far in far_refs:
        sums = sums + far[...].astype(F32)
    measured = []
    for v in range(tall // SUB):
        tile = jnp.zeros((SUB, LANES), F32)
        for at in range(min(SUB, outer - v * SUB)):
            p = v * SUB + at
            tile = jnp.where(sub == at, meas[:, p * LANES : (p + 1) * LANES], tile)
        measured.append(tile)
    measured = jnp.concatenate(measured, axis=0)
    rest_row[...] = (measured - sums[0:tall]) / jnp.maximum(sums[tall:], 1.0)

    def halo(q):
        at = 2 * tall + q % half * SUB
        high, low = above[at : at + SUB], below[at : at + SUB]
        if q // half == 1:
            high, low = pltpu.roll(high, SUB - 3, 0), pltpu.roll(low, 3, 0)
        return jnp.where(sub < 3, high, jnp.where(sub < 6, low, 0.0))

    side = 2 * tall + half * SUB
    side = jnp.where(sub < 3, above[side : side + SUB], below[side : side + SUB])
    shear_cols = [shear_f[g * SUB : (g + 1) * SUB] for g in range(groups)]
    step_cols = [step_f[g * SUB : (g + 1) * SUB] for g in range(groups)]
    inside = rows_of((SUB, 1)) < 6
    shear_cols.append(jnp.where(inside, 2.0 * side[:, 0:1] + side[:, 1:2], 0.0))
    step_cols.append(jnp.where(inside, side[:, 2:3] + side[:, 3:4] + side[:, 4:5], 0.0))
    index, delay, steps = [], [], []
    for g in range(groups + 1):
        s = jnp.broadcast_to(shear_cols[g].astype(I32), (SUB, LANES))
        rest = s & (LANES - 1)
        index.append((lane + rest) & (LANES - 1))
        delay.append((s >> 7) + jnp.where(lane + rest >= LANES, 1, 0))
        steps.append(jnp.broadcast_to(step_cols[g], (SUB, LANES)))
    tiles = []
    turned = [[] for _ in range(groups + 1)]
    for p in range(outer + 1):
        if p < outer:
            residual = jnp.broadcast_to(rest_row[p : p + 1, :], (SUB, LANES))
        else:
            residual = jnp.zeros((SUB, LANES), F32)
        lost = residual - residual.astype(BF16).astype(F32)
        tiles.append(jnp.where(sub < 7, residual, lost))
        for g in range(groups + 1):
            turned[g].append(turn(residual, index[g]) if p < outer else residual)
        q = p - (reach - 1)
        if q < 0 or q >= inner:
            continue
        here = slice(q * LANES, (q + 1) * LANES)
        open_q = jnp.broadcast_to(ap_ref[:, here].astype(F32), (SUB, LANES))
        pieces = []
        for g in range(groups + 1):
            pulled = choose(delay[g], turned[g][q : q + reach])
            base = raw[g * SUB : (g + 1) * SUB, here] if g < groups else halo(q)
            pieces.append(base + pulled * open_q * steps[g])
        out_ref[:, here] = jnp.concatenate(pieces, axis=0).astype(BF16)
        tiles[q] = jnp.where(sub < 6, pieces[-1], tiles[q])
    msg_ref[...] = jnp.concatenate(tiles, axis=0).astype(BF16)


def spread(rows, ch, which):
    return (which(rows_of((rows, ch))) == lanes_of((rows, ch))).astype(F32).astype(BF16)


def picked(row_ref, rows, which):
    ch = row_ref.shape[1]
    pick = which(rows_of((rows, ch))) == lanes_of((rows, ch))
    row = jnp.broadcast_to(row_ref[...], (rows, ch))
    return jnp.sum(jnp.where(pick, row, 0.0), axis=1, keepdims=True)


def with_bias(matrix, bias, start):
    lane = lanes_of(matrix.shape)
    for i, part in enumerate(split3(0.5 * bias)):
        matrix = jnp.where(lane == start + i, part, matrix)
    return matrix


def gate_kernel(_, line_ref, same_ref):
    pass


def weights_kernel(
    _, sw_in, sb_in, cw_in, cb_in, ow_in, main_ref, halo_ref, first_ref, second_ref, out_w_ref, *rest
):
    local, sems = rest[:5], rest[5]
    for copy in fetch((sw_in, sb_in, cw_in, cb_in, ow_in), local, sems):
        copy.wait()
    sw_ref, sb_ref, cw_ref, cb_ref, ow_ref = local
    ch, taps2 = sw_ref.shape
    taps = cw_ref.shape[0]
    place = lax.axis_index("band")
    has_low = jnp.where(place > 0, 1, 0)
    has_high = jnp.where(place < lax.axis_size("band") - 1, 1, 0)
    width = main_ref.shape[1]
    slots = 16
    line = lax.axis_index("row") * lax.axis_size("col") + lax.axis_index("col")
    lines = lax.axis_size("row") * lax.axis_size("col")
    group = lanes_of((taps2, width)) // slots
    offset = jnp.where(line % 2 == 1, group // 3, 2 - group // 3)
    present = (line + offset >= 1) & (line + offset <= lines)
    fan = (rows_of((taps2, width)) == 3 * offset + group % 3) & present
    fan = fan.astype(F32).astype(BF16)
    flat = jnp.dot(sw_ref[...], fan, preferred_element_type=F32).astype(BF16)
    for ref, slot_of in (
        (main_ref, lambda b: b),
        (halo_ref, lambda b: jnp.where(b < 3, 11 + b, jnp.where(b < 9, b - 3, b - 1))),
    ):
        rows = ref.shape[0]
        which = lambda r: r % ch
        full = jnp.dot(spread(rows, ch, which), flat, preferred_element_type=F32)
        lane = lanes_of((rows, width))
        band = rows_of((rows, width)) // ch
        keep = (lane % slots == slot_of(band)) & (lane < taps2 * slots)
        matrix = with_bias(
            jnp.where(keep, 0.5 * full, 0.0), picked(sb_ref, rows, which), taps2 * slots
        )
        if ref is halo_ref:
            valid = jnp.where(band < 3, has_low, jnp.where(band >= 9, has_high, 1))
            matrix = jnp.where(valid > 0, matrix, 0.0)
        ref[...] = matrix.astype(BF16)

    per = SUB
    rows = per * ch
    width = first_ref.shape[1]
    used = (per + taps - 1) * ch
    which = lambda r: r // per
    fan = (lanes_of((ch, width)) % ch == rows_of((ch, width))).astype(F32).astype(BF16)
    picks = spread(rows, ch, which)
    lane = lanes_of((rows, width))
    ahead = jnp.where(lane < used, lane // ch - rows_of((rows, width)) % per, -LANES)
    shifts = (0, per, per - (per + taps - 1), 2 * per - (per + taps - 1))
    blocks = [jnp.zeros((rows, width), F32) for _ in shifts]
    for d in range(taps):
        flat = jnp.dot(cw_ref[d], fan, preferred_element_type=F32).astype(BF16)
        full = 0.5 * jnp.dot(picks, flat, preferred_element_type=F32)
        blocks = [jnp.where(ahead == d + s, full, b) for s, b in zip(shifts, blocks)]
    bias = picked(cb_ref, rows, which)
    for i, block in enumerate(blocks):
        block = block if i == 2 else with_bias(block, bias, used)
        ref = first_ref if i < 2 else second_ref
        ref[i % 2 * rows : (i % 2 + 1) * rows, :] = block.astype(BF16)
    out_w_ref[...] = jnp.broadcast_to(picked(ow_ref, rows, which), out_w_ref.shape)


def denoise_kernel(
    tile,
    reach,
    ow_ref,
    mid_ref,
    shear_ref,
    step_ref,
    raw0_ref,
    msg0_ref,
    raw1_ref,
    msg1_ref,
    main_ref,
    halo_ref,
    first_ref,
    second_ref,
    out_ref,
    act,
    near0,
    near1,
    words,
):
    bands, cols = out_ref.shape
    slots = 16
    ch = main_ref.shape[0] // slots
    tiles = cols // tile
    inner = cols // LANES
    wide = tile + 2 * LANES
    split = act.shape[1] // 2
    groups = -(-bands // SUB)
    ones = jnp.where(rows_of((slots, tile)) < 3, 1.0, 0.0).astype(BF16)
    blank = jnp.zeros((2 * slots, LANES), BF16)
    zero = jnp.zeros((SUB, LANES), F32)
    shear_f = column(shear_ref[...].astype(F32), groups * SUB)
    step_f = column(step_ref[...], groups * SUB)
    lane = lanes_of()
    index, delay, steps = [], [], []
    for g in range(groups):
        s = jnp.broadcast_to(shear_f[g * SUB : (g + 1) * SUB].astype(I32), (SUB, LANES))
        rest = s & (LANES - 1)
        index.append((lane + rest) & (LANES - 1))
        delay.append((s >> 7) + jnp.where(lane + rest >= LANES, 1, 0))
        steps.append(jnp.broadcast_to(step_f[g * SUB : (g + 1) * SUB], (SUB, LANES)))
    rows_in = msg0_ref.shape[0]
    chunks = inner + reach - 1
    for n, msg_ref in enumerate((msg0_ref, msg1_ref)):
        words[n * rows_in : (n + 1) * rows_in, :] = msg_ref[...].astype(F32)
    turned = [[[] for _ in range(groups)] for _ in range(2)]

    def neighbours(q):
        for n, (raw_ref, near) in enumerate(((raw0_ref, near0), (raw1_ref, near1))):
            base = n * rows_in
            while len(turned[n][0]) < q + reach:
                p = len(turned[n][0])
                if p >= chunks:
                    residual = zero
                else:
                    at = base + p * SUB + 6
                    residual = words[at : at + 1, :] + words[at + 1 : at + 2, :]
                    residual = jnp.broadcast_to(residual, (SUB, LANES))
                for g in range(groups):
                    turned[n][g].append(turn(residual, index[g]))
            at = base + q * SUB
            raw = raw_ref[:, q * LANES : (q + 1) * LANES].astype(F32)
            open_q = jnp.broadcast_to(raw[bands : bands + 1], (SUB, LANES))
            pieces = [
                raw[g * SUB : (g + 1) * SUB]
                + choose(delay[g], turned[n][g][q : q + reach]) * open_q * steps[g]
                for g in range(groups)
            ]
            pieces.append(words[at : at + SUB, :])
            near[:, q * LANES : (q + 1) * LANES] = jnp.concatenate(pieces, axis=0).astype(BF16)

    def silu_twice(half):
        return half + half * jnp.tanh(half)

    def spatial(t):
        start = t * tile
        end = start + tile
        patches = []
        for ref in (near0, mid_ref, near1):
            left = ref[:, start - LANES : start] if t else blank
            here = ref[:, start:end]
            right = ref[:, end : end + LANES] if t < tiles - 1 else blank
            row = jnp.concatenate([left, here, right], axis=1)
            back = pltpu.roll(row, 1, 1)[:, LANES : LANES + tile]
            ahead = pltpu.roll(row, wide - 1, 1)[:, LANES : LANES + tile]
            patches += [back, here, ahead]
        buf = act.at[t % act.shape[0]]
        for part, w_ref in enumerate((main_ref, halo_ref)):
            x = jnp.concatenate(
                [p[part * slots : (part + 1) * slots] for p in patches] + [ones], axis=0
            )
            half = jnp.dot(w_ref[...], x, preferred_element_type=F32)
            value = silu_twice(half).astype(BF16)
            if part == 0:
                buf[3 * ch : 19 * ch, :] = value
            else:
                buf[0 : 3 * ch, :] = value[0 : 3 * ch]
                buf[19 * ch : 28 * ch, :] = value[3 * ch :]

    def spectral(t):
        start = t * tile
        buf = act.at[t % act.shape[0]]
        halves = []
        for part, w_ref in enumerate((first_ref, second_ref)):
            x = jnp.concatenate([buf[part * split : (part + 1) * split, :], ones], axis=0)
            halves.append(jnp.dot(w_ref[...], x, preferred_element_type=F32))
        rows = SUB * ch
        blocks = [halves[0][0:rows], halves[0][rows:] + halves[1][0:rows], halves[1][rows:]]
        pieces = []
        for half in blocks:
            total = None
            for k in range(ch):
                weight = ow_ref[k * SUB : (k + 1) * SUB, :]
                weight = jnp.concatenate([weight] * (tile // LANES), axis=1)
                term = weight * silu_twice(half[k * SUB : (k + 1) * SUB])
                total = term if total is None else total + term
            pieces.append(total)
        update = jnp.concatenate(pieces, axis=0)[0:bands]
        center = mid_ref[:, start : start + tile].astype(F32)[0:bands]
        out_ref[:, start : start + tile] = (center + update).astype(BF16)

    made = 0
    for t in range(tiles + 1):
        while t < tiles and made < min((t + 1) * tile // LANES + 1, inner):
            neighbours(made)
            made += 1
        if t < tiles:
            spatial(t)
        if t:
            spectral(t - 1)


def vmem(n):
    return [pl.BlockSpec(memory_space=pltpu.VMEM)] * n


def hbm(n):
    return [pl.BlockSpec(memory_space=pltpu.HBM)] * n


def in_hbm(arrays):
    return [pltpu.with_memory_space_constraint(x, pltpu.HBM) for x in arrays]


ANY = pl.BlockSpec(memory_space=pl.ANY)


def on_device(
    spectral_cube,
    aperture,
    measurement,
    shears,
    step_sizes,
    spatial_weight,
    spatial_bias,
    spectral_weight,
    spectral_bias,
    out_weight,
):
    bands, row_count, cols = spectral_cube.shape
    width = measurement.shape[1]
    reach = (width - cols) // LANES + 2
    outer = -(-width // LANES)
    groups = -(-bands // SUB)
    slots = (groups + 1) * SUB
    taps, ch = spectral_weight.shape[:2]
    taps2 = spatial_weight.shape[1]
    count = lax.axis_size("band")
    cube = spectral_cube.reshape(bands, cols)
    shear_row = shears.reshape(1, bands)
    step_row = step_sizes.reshape(1, bands)
    params = pltpu.CompilerParams(vmem_limit_bytes=48 * 2**20)

    tall = -(-outer // SUB) * SUB
    side = (cols // LANES // 2 + 2) * SUB
    inputs = (cube, aperture, measurement, shear_row, step_row)
    part, up, dn, *kept = pl.pallas_call(
        functools.partial(project_kernel, reach),
        out_shape=(
            jax.ShapeDtypeStruct((2 * tall, LANES), BF16),
            jax.ShapeDtypeStruct((2 * tall + side, LANES), BF16),
            jax.ShapeDtypeStruct((2 * tall + side, LANES), BF16),
        )
        + (jax.ShapeDtypeStruct((groups * SUB, cols), BF16),)
        + tuple(jax.ShapeDtypeStruct(x.shape, x.dtype) for x in inputs[1:]),
        in_specs=hbm(5),
        out_specs=tuple(vmem(8)),
        scratch_shapes=[
            pltpu.VMEM((bands, cols), BF16),
            pltpu.VMEM((groups * SUB, cols), F32),
            pltpu.SemaphoreType.DMA((5,)),
        ],
        compiler_params=params,
        name="project",
    )(*in_hbm(inputs))

    def around(x, shift):
        return lax.ppermute(x, "band", [(i, (i + shift) % count) for i in range(count)])

    below = around(up, 1)
    above = around(dn, -1)
    far = [around(part, s) for s in range(2, count - 1)]

    line = pl.pallas_call(
        gate_kernel,
        out_shape=jax.ShapeDtypeStruct(kept[0].shape, BF16),
        in_specs=[ANY, ANY],
        out_specs=ANY,
        input_output_aliases={1: 0},
        name="gate",
    )(part, kept[0])
    kept[0] = line

    lines = lax.axis_size(("row", "col"))
    pairs = [(i, i ^ 1) for i in range(lines)]
    others = [(i, (i - 1 + i % 2 * 2) % lines) for i in range(lines)]
    raw0 = lax.ppermute(line, ("row", "col"), pairs)
    raw1 = lax.ppermute(line, ("row", "col"), others)

    words = (outer + 1) * SUB
    updated, message = pl.pallas_call(
        functools.partial(update_kernel, reach, len(far)),
        out_shape=(
            jax.ShapeDtypeStruct((slots, cols), BF16),
            jax.ShapeDtypeStruct((words, LANES), BF16),
        ),
        in_specs=vmem(8 + len(far)),
        out_specs=tuple(vmem(2)),
        scratch_shapes=[
            pltpu.VMEM((groups * SUB, cols), F32),
            pltpu.VMEM((1, outer * LANES), F32),
            pltpu.VMEM((tall, LANES), F32),
        ],
        compiler_params=params,
        cost_estimate=pl.CostEstimate(
            flops=10**10, bytes_accessed=4 * 10**7, transcendentals=0
        ),
        name="update",
    )(*kept, part, below, above, *far)

    message0 = lax.ppermute(message, ("row", "col"), pairs)
    message1 = lax.ppermute(message, ("row", "col"), others)

    small = (
        spatial_weight,
        spatial_bias.reshape(1, ch),
        spectral_weight,
        spectral_bias.reshape(1, ch),
        out_weight.reshape(1, ch),
    )
    reached = (SUB + taps - 1) * ch
    main_w, halo_w, first_w, second_w, out_w = pl.pallas_call(
        weights_kernel,
        out_shape=(
            jax.ShapeDtypeStruct((16 * ch, taps2 * 16 + 16), BF16),
            jax.ShapeDtypeStruct((12 * ch, taps2 * 16 + 16), BF16),
            jax.ShapeDtypeStruct((2 * SUB * ch, reached + 16), BF16),
            jax.ShapeDtypeStruct((2 * SUB * ch, reached + 16), BF16),
            jax.ShapeDtypeStruct((SUB * ch, LANES), F32),
        ),
        in_specs=[ANY] + hbm(5),
        out_specs=tuple(vmem(5)),
        scratch_shapes=[pltpu.VMEM(x.shape, x.dtype) for x in small]
        + [pltpu.SemaphoreType.DMA((5,))],
        compiler_params=params,
        name="weights",
    )(message, *in_hbm(small))

    tile = 512
    result = pl.pallas_call(
        functools.partial(denoise_kernel, tile, reach),
        out_shape=jax.ShapeDtypeStruct((bands, cols), BF16),
        in_specs=vmem(12),
        out_specs=vmem(1)[0],
        scratch_shapes=[
            pltpu.VMEM((4, 28 * ch, tile), BF16),
            pltpu.VMEM((slots, cols), BF16),
            pltpu.VMEM((slots, cols), BF16),
            pltpu.VMEM((2 * words, LANES), F32),
        ],
        compiler_params=params,
        name="denoise",
    )(
        out_w,
        updated,
        kept[3],
        kept[4],
        raw0,
        message0,
        raw1,
        message1,
        main_w,
        halo_w,
        first_w,
        second_w,
    )
    return result.reshape(bands, 1, cols)


def solution(mesh):
    in_specs = (
        P("band", ("row", "col"), None),
        P(("row", "col"), None),
        P(("row", "col"), None),
        P("band"),
        P("band"),
        P(),
        P(),
        P(),
        P(),
        P(),
    )
    out_specs = P("band", ("row", "col"), None)
    return jax.shard_map(
        on_device, mesh=mesh, in_specs=in_specs, out_specs=out_specs, check_vma=False
    )
```

```python
import functools

import jax
import jax.numpy as jnp
from jax import lax
from jax.experimental import pallas as pl
from jax.experimental.pallas import tpu as pltpu
from jax.sharding import PartitionSpec as P

LANES = 128
SUB = 8
F32 = jnp.float32
BF16 = jnp.bfloat16
I32 = jnp.int32


def lanes_of(shape=(SUB, LANES)):
    return lax.broadcasted_iota(I32, shape, 1)


def rows_of(shape=(SUB, LANES)):
    return lax.broadcasted_iota(I32, shape, 0)


def column(row, rows):
    n = row.shape[1]
    eye = rows_of((rows, n)) == lanes_of((rows, n))
    return jnp.sum(jnp.where(eye, jnp.broadcast_to(row, (rows, n)), 0.0), axis=1, keepdims=True)


def turn(chunk, index):
    return jnp.take_along_axis(chunk, index, axis=1, mode="promise_in_bounds")


def choose(delay, options):
    result = options[-1]
    for d in range(len(options) - 2, -1, -1):
        result = jnp.where(delay == d, options[d], result)
    return result


def split3(x):
    hi = x.astype(BF16).astype(F32)
    mid = (x - hi).astype(BF16).astype(F32)
    return hi, mid, x - hi - mid


def fetch(sources, targets, sems):
    copies = [
        pltpu.make_async_copy(src, dst, sems.at[i]) for i, (src, dst) in enumerate(zip(sources, targets))
    ]
    for copy in copies:
        copy.start()
    return copies


def project_kernel(
    reach, cube_in, ap_in, meas_in, shear_in, step_in, part_ref, up_ref, dn_ref, *rest_refs
):
    line_ref, *kept = rest_refs[:5]
    cube_ref, raw, sems = rest_refs[5:]
    ap_ref, meas_ref, shear_ref, step_ref = kept
    copies = fetch((cube_in, ap_in, meas_in, shear_in, step_in), (cube_ref, *kept), sems)
    for copy in copies:
        copy.wait()
    bands, cols = cube_ref.shape
    groups = -(-bands // SUB)
    inner = cols // LANES
    tall = part_ref.shape[0] // 2
    outer = -(-meas_ref.shape[1] // LANES)
    raw[bands // SUB * SUB :, :] = jnp.zeros((raw.shape[0] - bands // SUB * SUB, cols), F32)
    raw[0:bands, :] = cube_ref[...].astype(F32)
    shear_f = column(shear_ref[...].astype(F32), groups * SUB)
    step_f = column(step_ref[...], groups * SUB)
    shear_i = shear_f.astype(I32)
    lane, sub = lanes_of(), rows_of()
    index, delay = [], []
    for g in range(groups):
        s = jnp.broadcast_to(shear_i[g * SUB : (g + 1) * SUB], (SUB, LANES))
        rest = s & (LANES - 1)
        index.append((lane - rest) & (LANES - 1))
        delay.append((s >> 7) + jnp.where(lane < rest, 1, 0))
    zero = jnp.zeros((SUB, LANES), F32)
    turned = [[zero] * (reach - 1) for _ in range(groups)]
    opened = [[zero] * (reach - 1) for _ in range(groups)]
    sums = [zero] * (tall // SUB)
    counts = [zero] * (tall // SUB)
    firsts, lasts = [], []
    for p in range(outer):
        total = zero
        count = zero
        if p < inner:
            open_p = jnp.broadcast_to(
                ap_ref[:, p * LANES : (p + 1) * LANES].astype(F32), (SUB, LANES)
            )
            layers = [
                raw[g * SUB : (g + 1) * SUB, p * LANES : (p + 1) * LANES] for g in range(groups)
            ]
            firsts.append(layers[0])
            lasts.append(layers[-1])
            tagged = jnp.where(sub == bands % SUB, open_p, layers[-1])
            line_ref[:, p * LANES : (p + 1) * LANES] = jnp.concatenate(
                layers[:-1] + [tagged], axis=0
            ).astype(BF16)
        for g in range(groups):
            if p < inner:
                here = turn(layers[g] * open_p, index[g])
                here_open = turn(open_p, index[g])
            else:
                here = here_open = zero
            options = [here] + turned[g]
            options_open = [here_open] + opened[g]
            turned[g] = options[:-1]
            opened[g] = options_open[:-1]
            total = total + choose(delay[g], options)
            part = choose(delay[g], options_open)
            if (g + 1) * SUB > bands:
                part = jnp.where(sub < bands - g * SUB, part, 0.0)
            count = count + part
        v, at = divmod(p, SUB)
        sums[v] = jnp.where(sub == at, jnp.sum(total, axis=0, keepdims=True), sums[v])
        counts[v] = jnp.where(sub == at, jnp.sum(count, axis=0, keepdims=True), counts[v])
    sides = []
    for g in (0, groups - 1):
        s = shear_i[g * SUB : (g + 1) * SUB]
        parts = [(s >> 1).astype(F32), (s & 1).astype(F32)]
        parts += list(split3(step_f[g * SUB : (g + 1) * SUB]))
        side = zero
        for i, part in enumerate(parts):
            side = jnp.where(lane == i, part, side)
        sides.append(side)
    half = inner // 2
    dn = [
        jnp.where(sub < 3, firsts[q], pltpu.roll(firsts[q + half], 3, 0)) for q in range(half)
    ] + [sides[0], zero]
    up = [
        jnp.where(sub < 3, pltpu.roll(lasts[q + half], SUB - 3, 0), lasts[q]) for q in range(half)
    ] + [sides[1], zero]
    part_ref[...] = jnp.concatenate(sums + counts, axis=0).astype(BF16)
    up_ref[...] = jnp.concatenate(sums + counts + up, axis=0).astype(BF16)
    dn_ref[...] = jnp.concatenate(sums + counts + dn, axis=0).astype(BF16)


def update_kernel(
    reach,
    fars,
    line_ref,
    ap_ref,
    meas_ref,
    shear_ref,
    step_ref,
    own_ref,
    below_ref,
    above_ref,
    *rest_refs,
):
    far_refs = rest_refs[:fars]
    out_ref, msg_ref, raw, meas, rest_row = rest_refs[fars:]
    groups = line_ref.shape[0] // SUB
    cols = line_ref.shape[1]
    inner = cols // LANES
    half = inner // 2
    tall = own_ref.shape[0] // 2
    outer = -(-meas_ref.shape[1] // LANES)
    raw[...] = line_ref[...].astype(F32)
    meas[:, (outer - 1) * LANES :] = jnp.zeros((1, LANES), F32)
    meas[:, 0 : meas_ref.shape[1]] = meas_ref[...]
    shear_f = column(shear_ref[...].astype(F32), groups * SUB)
    step_f = column(step_ref[...], groups * SUB)
    lane, sub = lanes_of(), rows_of()
    below = below_ref[...].astype(F32)
    above = above_ref[...].astype(F32)
    sums = own_ref[...].astype(F32) + below[0 : 2 * tall] + above[0 : 2 * tall]
    for far in far_refs:
        sums = sums + far[...].astype(F32)
    measured = []
    for v in range(tall // SUB):
        tile = jnp.zeros((SUB, LANES), F32)
        for at in range(min(SUB, outer - v * SUB)):
            p = v * SUB + at
            tile = jnp.where(sub == at, meas[:, p * LANES : (p + 1) * LANES], tile)
        measured.append(tile)
    measured = jnp.concatenate(measured, axis=0)
    rest_row[...] = (measured - sums[0:tall]) / jnp.maximum(sums[tall:], 1.0)

    def halo(q):
        at = 2 * tall + q % half * SUB
        high, low = above[at : at + SUB], below[at : at + SUB]
        if q // half == 1:
            high, low = pltpu.roll(high, SUB - 3, 0), pltpu.roll(low, 3, 0)
        return jnp.where(sub < 3, high, jnp.where(sub < 6, low, 0.0))

    side = 2 * tall + half * SUB
    side = jnp.where(sub < 3, above[side : side + SUB], below[side : side + SUB])
    shear_cols = [shear_f[g * SUB : (g + 1) * SUB] for g in range(groups)]
    step_cols = [step_f[g * SUB : (g + 1) * SUB] for g in range(groups)]
    inside = rows_of((SUB, 1)) < 6
    shear_cols.append(jnp.where(inside, 2.0 * side[:, 0:1] + side[:, 1:2], 0.0))
    step_cols.append(jnp.where(inside, side[:, 2:3] + side[:, 3:4] + side[:, 4:5], 0.0))
    index, delay, steps = [], [], []
    for g in range(groups + 1):
        s = jnp.broadcast_to(shear_cols[g].astype(I32), (SUB, LANES))
        rest = s & (LANES - 1)
        index.append((lane + rest) & (LANES - 1))
        delay.append((s >> 7) + jnp.where(lane + rest >= LANES, 1, 0))
        steps.append(jnp.broadcast_to(step_cols[g], (SUB, LANES)))
    tiles = []
    turned = [[] for _ in range(groups + 1)]
    for p in range(outer + 1):
        if p < outer:
            residual = jnp.broadcast_to(rest_row[p : p + 1, :], (SUB, LANES))
        else:
            residual = jnp.zeros((SUB, LANES), F32)
        lost = residual - residual.astype(BF16).astype(F32)
        tiles.append(jnp.where(sub < 7, residual, lost))
        for g in range(groups + 1):
            turned[g].append(turn(residual, index[g]) if p < outer else residual)
        q = p - (reach - 1)
        if q < 0 or q >= inner:
            continue
        here = slice(q * LANES, (q + 1) * LANES)
        open_q = jnp.broadcast_to(ap_ref[:, here].astype(F32), (SUB, LANES))
        pieces = []
        for g in range(groups + 1):
            pulled = choose(delay[g], turned[g][q : q + reach])
            base = raw[g * SUB : (g + 1) * SUB, here] if g < groups else halo(q)
            pieces.append(base + pulled * open_q * steps[g])
        out_ref[:, here] = jnp.concatenate(pieces, axis=0).astype(BF16)
        tiles[q] = jnp.where(sub < 6, pieces[-1], tiles[q])
    msg_ref[...] = jnp.concatenate(tiles, axis=0).astype(BF16)


def spread(rows, ch, which):
    return (which(rows_of((rows, ch))) == lanes_of((rows, ch))).astype(F32).astype(BF16)


def picked(row_ref, rows, which):
    ch = row_ref.shape[1]
    pick = which(rows_of((rows, ch))) == lanes_of((rows, ch))
    row = jnp.broadcast_to(row_ref[...], (rows, ch))
    return jnp.sum(jnp.where(pick, row, 0.0), axis=1, keepdims=True)


def with_bias(matrix, bias, start):
    lane = lanes_of(matrix.shape)
    for i, part in enumerate(split3(0.5 * bias)):
        matrix = jnp.where(lane == start + i, part, matrix)
    return matrix


def gate_kernel(_, line_ref, same_ref):
    pass


def weights_kernel(
    _, sw_in, sb_in, cw_in, cb_in, ow_in, main_ref, halo_ref, first_ref, second_ref, out_w_ref, *rest
):
    local, sems = rest[:5], rest[5]
    for copy in fetch((sw_in, sb_in, cw_in, cb_in, ow_in), local, sems):
        copy.wait()
    sw_ref, sb_ref, cw_ref, cb_ref, ow_ref = local
    ch, taps2 = sw_ref.shape
    taps = cw_ref.shape[0]
    place = lax.axis_index("band")
    has_low = jnp.where(place > 0, 1, 0)
    has_high = jnp.where(place < lax.axis_size("band") - 1, 1, 0)
    width = main_ref.shape[1]
    slots = 16
    line = lax.axis_index("row") * lax.axis_size("col") + lax.axis_index("col")
    lines = lax.axis_size("row") * lax.axis_size("col")
    group = lanes_of((taps2, width)) // slots
    offset = jnp.where(line % 2 == 1, group // 3, 2 - group // 3)
    present = (line + offset >= 1) & (line + offset <= lines)
    fan = (rows_of((taps2, width)) == 3 * offset + group % 3) & present
    fan = fan.astype(F32).astype(BF16)
    flat = jnp.dot(sw_ref[...], fan, preferred_element_type=F32).astype(BF16)
    for ref, slot_of in (
        (main_ref, lambda b: b),
        (halo_ref, lambda b: jnp.where(b < 3, 11 + b, jnp.where(b < 9, b - 3, b - 1))),
    ):
        rows = ref.shape[0]
        which = lambda r: r % ch
        full = jnp.dot(spread(rows, ch, which), flat, preferred_element_type=F32)
        lane = lanes_of((rows, width))
        band = rows_of((rows, width)) // ch
        keep = (lane % slots == slot_of(band)) & (lane < taps2 * slots)
        matrix = with_bias(
            jnp.where(keep, 0.5 * full, 0.0), picked(sb_ref, rows, which), taps2 * slots
        )
        if ref is halo_ref:
            valid = jnp.where(band < 3, has_low, jnp.where(band >= 9, has_high, 1))
            matrix = jnp.where(valid > 0, matrix, 0.0)
        ref[...] = matrix.astype(BF16)

    per = SUB
    rows = per * ch
    width = first_ref.shape[1]
    used = (per + taps - 1) * ch
    which = lambda r: r // per
    fan = (lanes_of((ch, width)) % ch == rows_of((ch, width))).astype(F32).astype(BF16)
    picks = spread(rows, ch, which)
    lane = lanes_of((rows, width))
    ahead = jnp.where(lane < used, lane // ch - rows_of((rows, width)) % per, -LANES)
    shifts = (0, per, per - (per + taps - 1), 2 * per - (per + taps - 1))
    blocks = [jnp.zeros((rows, width), F32) for _ in shifts]
    for d in range(taps):
        flat = jnp.dot(cw_ref[d], fan, preferred_element_type=F32).astype(BF16)
        full = 0.5 * jnp.dot(picks, flat, preferred_element_type=F32)
        blocks = [jnp.where(ahead == d + s, full, b) for s, b in zip(shifts, blocks)]
    bias = picked(cb_ref, rows, which)
    for i, block in enumerate(blocks):
        block = block if i == 2 else with_bias(block, bias, used)
        ref = first_ref if i < 2 else second_ref
        ref[i % 2 * rows : (i % 2 + 1) * rows, :] = block.astype(BF16)
    out_w_ref[...] = jnp.broadcast_to(picked(ow_ref, rows, which), out_w_ref.shape)


def denoise_kernel(
    tile,
    reach,
    ow_ref,
    mid_ref,
    shear_ref,
    step_ref,
    raw0_ref,
    msg0_ref,
    raw1_ref,
    msg1_ref,
    main_ref,
    halo_ref,
    first_ref,
    second_ref,
    out_ref,
    act,
    near0,
    near1,
    words,
):
    bands, cols = out_ref.shape
    slots = 16
    ch = main_ref.shape[0] // slots
    tiles = cols // tile
    inner = cols // LANES
    wide = tile + 2 * LANES
    split = act.shape[1] // 2
    groups = -(-bands // SUB)
    ones = jnp.where(rows_of((slots, tile)) < 3, 1.0, 0.0).astype(BF16)
    blank = jnp.zeros((2 * slots, LANES), BF16)
    zero = jnp.zeros((SUB, LANES), F32)
    shear_f = column(shear_ref[...].astype(F32), groups * SUB)
    step_f = column(step_ref[...], groups * SUB)
    lane = lanes_of()
    index, delay, steps = [], [], []
    for g in range(groups):
        s = jnp.broadcast_to(shear_f[g * SUB : (g + 1) * SUB].astype(I32), (SUB, LANES))
        rest = s & (LANES - 1)
        index.append((lane + rest) & (LANES - 1))
        delay.append((s >> 7) + jnp.where(lane + rest >= LANES, 1, 0))
        steps.append(jnp.broadcast_to(step_f[g * SUB : (g + 1) * SUB], (SUB, LANES)))
    rows_in = msg0_ref.shape[0]
    chunks = inner + reach - 1
    for n, msg_ref in enumerate((msg0_ref, msg1_ref)):
        words[n * rows_in : (n + 1) * rows_in, :] = msg_ref[...].astype(F32)
    turned = [[[] for _ in range(groups)] for _ in range(2)]

    def neighbours(q):
        for n, (raw_ref, near) in enumerate(((raw0_ref, near0), (raw1_ref, near1))):
            base = n * rows_in
            while len(turned[n][0]) < q + reach:
                p = len(turned[n][0])
                if p >= chunks:
                    residual = zero
                else:
                    at = base + p * SUB + 6
                    residual = words[at : at + 1, :] + words[at + 1 : at + 2, :]
                    residual = jnp.broadcast_to(residual, (SUB, LANES))
                for g in range(groups):
                    turned[n][g].append(turn(residual, index[g]))
            at = base + q * SUB
            raw = raw_ref[:, q * LANES : (q + 1) * LANES].astype(F32)
            open_q = jnp.broadcast_to(raw[bands : bands + 1], (SUB, LANES))
            pieces = [
                raw[g * SUB : (g + 1) * SUB]
                + choose(delay[g], turned[n][g][q : q + reach]) * open_q * steps[g]
                for g in range(groups)
            ]
            pieces.append(words[at : at + SUB, :])
            near[:, q * LANES : (q + 1) * LANES] = jnp.concatenate(pieces, axis=0).astype(BF16)

    def silu_twice(half):
        return half + half * jnp.tanh(half)

    def spatial(t):
        start = t * tile
        end = start + tile
        patches = []
        for ref in (near0, mid_ref, near1):
            left = ref[:, start - LANES : start] if t else blank
            here = ref[:, start:end]
            right = ref[:, end : end + LANES] if t < tiles - 1 else blank
            row = jnp.concatenate([left, here, right], axis=1)
            back = pltpu.roll(row, 1, 1)[:, LANES : LANES + tile]
            ahead = pltpu.roll(row, wide - 1, 1)[:, LANES : LANES + tile]
            patches += [back, here, ahead]
        buf = act.at[t % act.shape[0]]
        for part, w_ref in enumerate((main_ref, halo_ref)):
            x = jnp.concatenate(
                [p[part * slots : (part + 1) * slots] for p in patches] + [ones], axis=0
            )
            half = jnp.dot(w_ref[...], x, preferred_element_type=F32)
            value = silu_twice(half).astype(BF16)
            if part == 0:
                buf[3 * ch : 19 * ch, :] = value
            else:
                buf[0 : 3 * ch, :] = value[0 : 3 * ch]
                buf[19 * ch : 28 * ch, :] = value[3 * ch :]

    def spectral(t):
        start = t * tile
        buf = act.at[t % act.shape[0]]
        halves = []
        for part, w_ref in enumerate((first_ref, second_ref)):
            x = jnp.concatenate([buf[part * split : (part + 1) * split, :], ones], axis=0)
            halves.append(jnp.dot(w_ref[...], x, preferred_element_type=F32))
        rows = SUB * ch
        blocks = [halves[0][0:rows], halves[0][rows:] + halves[1][0:rows], halves[1][rows:]]
        pieces = []
        for half in blocks:
            total = None
            for k in range(ch):
                weight = ow_ref[k * SUB : (k + 1) * SUB, :]
                weight = jnp.concatenate([weight] * (tile // LANES), axis=1)
                term = weight * silu_twice(half[k * SUB : (k + 1) * SUB])
                total = term if total is None else total + term
            pieces.append(total)
        update = jnp.concatenate(pieces, axis=0)[0:bands]
        center = mid_ref[:, start : start + tile].astype(F32)[0:bands]
        out_ref[:, start : start + tile] = (center + update).astype(BF16)

    made = 0
    for t in range(tiles + 1):
        while t < tiles and made < min((t + 1) * tile // LANES + 1, inner):
            neighbours(made)
            made += 1
        if t < tiles:
            spatial(t)
        if t:
            spectral(t - 1)


def vmem(n):
    return [pl.BlockSpec(memory_space=pltpu.VMEM)] * n


def hbm(n):
    return [pl.BlockSpec(memory_space=pltpu.HBM)] * n


def in_hbm(arrays):
    return [pltpu.with_memory_space_constraint(x, pltpu.HBM) for x in arrays]


ANY = pl.BlockSpec(memory_space=pl.ANY)


def on_device(
    spectral_cube,
    aperture,
    measurement,
    shears,
    step_sizes,
    spatial_weight,
    spatial_bias,
    spectral_weight,
    spectral_bias,
    out_weight,
):
    bands, row_count, cols = spectral_cube.shape
    width = measurement.shape[1]
    reach = (width - cols) // LANES + 2
    outer = -(-width // LANES)
    groups = -(-bands // SUB)
    slots = (groups + 1) * SUB
    taps, ch = spectral_weight.shape[:2]
    taps2 = spatial_weight.shape[1]
    count = lax.axis_size("band")
    cube = spectral_cube.reshape(bands, cols)
    shear_row = shears.reshape(1, bands)
    step_row = step_sizes.reshape(1, bands)
    params = pltpu.CompilerParams(vmem_limit_bytes=48 * 2**20)

    tall = -(-outer // SUB) * SUB
    side = (cols // LANES // 2 + 2) * SUB
    inputs = (cube, aperture, measurement, shear_row, step_row)
    part, up, dn, *kept = pl.pallas_call(
        functools.partial(project_kernel, reach),
        out_shape=(
            jax.ShapeDtypeStruct((2 * tall, LANES), BF16),
            jax.ShapeDtypeStruct((2 * tall + side, LANES), BF16),
            jax.ShapeDtypeStruct((2 * tall + side, LANES), BF16),
        )
        + (jax.ShapeDtypeStruct((groups * SUB, cols), BF16),)
        + tuple(jax.ShapeDtypeStruct(x.shape, x.dtype) for x in inputs[1:]),
        in_specs=hbm(5),
        out_specs=tuple(vmem(8)),
        scratch_shapes=[
            pltpu.VMEM((bands, cols), BF16),
            pltpu.VMEM((groups * SUB, cols), F32),
            pltpu.SemaphoreType.DMA((5,)),
        ],
        compiler_params=params,
        name="project",
    )(*in_hbm(inputs))

    def around(x, shift):
        return lax.ppermute(x, "band", [(i, (i + shift) % count) for i in range(count)])

    below = around(up, 1)
    above = around(dn, -1)
    far = [around(part, s) for s in range(2, count - 1)]

    line = pl.pallas_call(
        gate_kernel,
        out_shape=jax.ShapeDtypeStruct(kept[0].shape, BF16),
        in_specs=[ANY, ANY],
        out_specs=ANY,
        input_output_aliases={1: 0},
        compiler_params=pltpu.CompilerParams(vmem_limit_bytes=2**20),
        name="gate",
    )(part, kept[0])
    kept[0] = line

    lines = lax.axis_size(("row", "col"))
    pairs = [(i, i ^ 1) for i in range(lines)]
    others = [(i, (i - 1 + i % 2 * 2) % lines) for i in range(lines)]
    raw0 = lax.ppermute(line, ("row", "col"), pairs)
    raw1 = lax.ppermute(line, ("row", "col"), others)

    words = (outer + 1) * SUB
    updated, message = pl.pallas_call(
        functools.partial(update_kernel, reach, len(far)),
        out_shape=(
            jax.ShapeDtypeStruct((slots, cols), BF16),
            jax.ShapeDtypeStruct((words, LANES), BF16),
        ),
        in_specs=vmem(8 + len(far)),
        out_specs=tuple(vmem(2)),
        scratch_shapes=[
            pltpu.VMEM((groups * SUB, cols), F32),
            pltpu.VMEM((1, outer * LANES), F32),
            pltpu.VMEM((tall, LANES), F32),
        ],
        compiler_params=params,
        cost_estimate=pl.CostEstimate(
            flops=10**10, bytes_accessed=4 * 10**7, transcendentals=0
        ),
        name="update",
    )(*kept, part, below, above, *far)

    message0 = lax.ppermute(message, ("row", "col"), pairs)
    message1 = lax.ppermute(message, ("row", "col"), others)

    small = (
        spatial_weight,
        spatial_bias.reshape(1, ch),
        spectral_weight,
        spectral_bias.reshape(1, ch),
        out_weight.reshape(1, ch),
    )
    reached = (SUB + taps - 1) * ch
    main_w, halo_w, first_w, second_w, out_w = pl.pallas_call(
        weights_kernel,
        out_shape=(
            jax.ShapeDtypeStruct((16 * ch, taps2 * 16 + 16), BF16),
            jax.ShapeDtypeStruct((12 * ch, taps2 * 16 + 16), BF16),
            jax.ShapeDtypeStruct((2 * SUB * ch, reached + 16), BF16),
            jax.ShapeDtypeStruct((2 * SUB * ch, reached + 16), BF16),
            jax.ShapeDtypeStruct((SUB * ch, LANES), F32),
        ),
        in_specs=[ANY] + hbm(5),
        out_specs=tuple(vmem(5)),
        scratch_shapes=[pltpu.VMEM(x.shape, x.dtype) for x in small]
        + [pltpu.SemaphoreType.DMA((5,))],
        compiler_params=params,
        name="weights",
    )(message, *in_hbm(small))

    tile = 512
    result = pl.pallas_call(
        functools.partial(denoise_kernel, tile, reach),
        out_shape=jax.ShapeDtypeStruct((bands, cols), BF16),
        in_specs=vmem(12),
        out_specs=vmem(1)[0],
        scratch_shapes=[
            pltpu.VMEM((4, 28 * ch, tile), BF16),
            pltpu.VMEM((slots, cols), BF16),
            pltpu.VMEM((slots, cols), BF16),
            pltpu.VMEM((2 * words, LANES), F32),
        ],
        compiler_params=params,
        name="denoise",
    )(
        out_w,
        updated,
        kept[3],
        kept[4],
        raw0,
        message0,
        raw1,
        message1,
        main_w,
        halo_w,
        first_w,
        second_w,
    )
    return result.reshape(bands, 1, cols)


def solution(mesh):
    in_specs = (
        P("band", ("row", "col"), None),
        P(("row", "col"), None),
        P(("row", "col"), None),
        P("band"),
        P("band"),
        P(),
        P(),
        P(),
        P(),
        P(),
    )
    out_specs = P("band", ("row", "col"), None)
    return jax.shard_map(
        on_device, mesh=mesh, in_specs=in_specs, out_specs=out_specs, check_vma=False
    )
```

```python
import functools

import jax
import jax.numpy as jnp
from jax import lax
from jax.experimental import pallas as pl
from jax.experimental.pallas import tpu as pltpu
from jax.sharding import PartitionSpec as P

LANES = 128
SUB = 8
F32 = jnp.float32
BF16 = jnp.bfloat16
I32 = jnp.int32


def lanes_of(shape=(SUB, LANES)):
    return lax.broadcasted_iota(I32, shape, 1)


def rows_of(shape=(SUB, LANES)):
    return lax.broadcasted_iota(I32, shape, 0)


def column(row, rows):
    n = row.shape[1]
    eye = rows_of((rows, n)) == lanes_of((rows, n))
    return jnp.sum(jnp.where(eye, jnp.broadcast_to(row, (rows, n)), 0.0), axis=1, keepdims=True)


def turn(chunk, index):
    return jnp.take_along_axis(chunk, index, axis=1, mode="promise_in_bounds")


def choose(delay, options):
    result = options[-1]
    for d in range(len(options) - 2, -1, -1):
        result = jnp.where(delay == d, options[d], result)
    return result


def split3(x):
    hi = x.astype(BF16).astype(F32)
    mid = (x - hi).astype(BF16).astype(F32)
    return hi, mid, x - hi - mid


def fetch(sources, targets, sems):
    copies = [
        pltpu.make_async_copy(src, dst, sems.at[i]) for i, (src, dst) in enumerate(zip(sources, targets))
    ]
    for copy in copies:
        copy.start()
    return copies


def project_kernel(
    reach, cube_in, ap_in, meas_in, shear_in, step_in, part_ref, up_ref, dn_ref, *rest_refs
):
    line_ref, *kept = rest_refs[:5]
    cube_ref, raw, sems = rest_refs[5:]
    ap_ref, meas_ref, shear_ref, step_ref = kept
    copies = fetch((cube_in, ap_in, meas_in, shear_in, step_in), (cube_ref, *kept), sems)
    for copy in copies:
        copy.wait()
    bands, cols = cube_ref.shape
    groups = -(-bands // SUB)
    inner = cols // LANES
    tall = part_ref.shape[0] // 2
    outer = -(-meas_ref.shape[1] // LANES)
    raw[bands // SUB * SUB :, :] = jnp.zeros((raw.shape[0] - bands // SUB * SUB, cols), F32)
    raw[0:bands, :] = cube_ref[...].astype(F32)
    shear_f = column(shear_ref[...].astype(F32), groups * SUB)
    step_f = column(step_ref[...], groups * SUB)
    shear_i = shear_f.astype(I32)
    lane, sub = lanes_of(), rows_of()
    index, delay = [], []
    for g in range(groups):
        s = jnp.broadcast_to(shear_i[g * SUB : (g + 1) * SUB], (SUB, LANES))
        rest = s & (LANES - 1)
        index.append((lane - rest) & (LANES - 1))
        delay.append((s >> 7) + jnp.where(lane < rest, 1, 0))
    zero = jnp.zeros((SUB, LANES), F32)
    turned = [[zero] * (reach - 1) for _ in range(groups)]
    opened = [[zero] * (reach - 1) for _ in range(groups)]
    sums = [zero] * (tall // SUB)
    counts = [zero] * (tall // SUB)
    firsts, lasts = [], []
    for p in range(outer):
        total = zero
        count = zero
        if p < inner:
            open_p = jnp.broadcast_to(
                ap_ref[:, p * LANES : (p + 1) * LANES].astype(F32), (SUB, LANES)
            )
            layers = [
                raw[g * SUB : (g + 1) * SUB, p * LANES : (p + 1) * LANES] for g in range(groups)
            ]
            firsts.append(layers[0])
            lasts.append(layers[-1])
            tagged = jnp.where(sub == bands % SUB, open_p, layers[-1])
            line_ref[:, p * LANES : (p + 1) * LANES] = jnp.concatenate(
                layers[:-1] + [tagged], axis=0
            ).astype(BF16)
        for g in range(groups):
            if p < inner:
                here = turn(layers[g] * open_p, index[g])
                here_open = turn(open_p, index[g])
            else:
                here = here_open = zero
            options = [here] + turned[g]
            options_open = [here_open] + opened[g]
            turned[g] = options[:-1]
            opened[g] = options_open[:-1]
            total = total + choose(delay[g], options)
            part = choose(delay[g], options_open)
            if (g + 1) * SUB > bands:
                part = jnp.where(sub < bands - g * SUB, part, 0.0)
            count = count + part
        v, at = divmod(p, SUB)
        sums[v] = jnp.where(sub == at, jnp.sum(total, axis=0, keepdims=True), sums[v])
        counts[v] = jnp.where(sub == at, jnp.sum(count, axis=0, keepdims=True), counts[v])
    sides = []
    for g in (0, groups - 1):
        s = shear_i[g * SUB : (g + 1) * SUB]
        parts = [(s >> 1).astype(F32), (s & 1).astype(F32)]
        parts += list(split3(step_f[g * SUB : (g + 1) * SUB]))
        side = zero
        for i, part in enumerate(parts):
            side = jnp.where(lane == i, part, side)
        sides.append(side)
    half = inner // 2
    dn = [
        jnp.where(sub < 3, firsts[q], pltpu.roll(firsts[q + half], 3, 0)) for q in range(half)
    ] + [sides[0], zero]
    up = [
        jnp.where(sub < 3, pltpu.roll(lasts[q + half], SUB - 3, 0), lasts[q]) for q in range(half)
    ] + [sides[1], zero]
    part_ref[...] = jnp.concatenate(sums + counts, axis=0).astype(BF16)
    up_ref[...] = jnp.concatenate(sums + counts + up, axis=0).astype(BF16)
    dn_ref[...] = jnp.concatenate(sums + counts + dn, axis=0).astype(BF16)


def update_kernel(
    reach,
    fars,
    line_ref,
    ap_ref,
    meas_ref,
    shear_ref,
    step_ref,
    own_ref,
    below_ref,
    above_ref,
    *rest_refs,
):
    far_refs = rest_refs[:fars]
    out_ref, msg_ref, raw, meas, rest_row = rest_refs[fars:]
    groups = line_ref.shape[0] // SUB
    cols = line_ref.shape[1]
    inner = cols // LANES
    half = inner // 2
    tall = own_ref.shape[0] // 2
    outer = -(-meas_ref.shape[1] // LANES)
    raw[...] = line_ref[...].astype(F32)
    meas[:, (outer - 1) * LANES :] = jnp.zeros((1, LANES), F32)
    meas[:, 0 : meas_ref.shape[1]] = meas_ref[...]
    shear_f = column(shear_ref[...].astype(F32), groups * SUB)
    step_f = column(step_ref[...], groups * SUB)
    lane, sub = lanes_of(), rows_of()
    below = below_ref[...].astype(F32)
    above = above_ref[...].astype(F32)
    sums = own_ref[...].astype(F32) + below[0 : 2 * tall] + above[0 : 2 * tall]
    for far in far_refs:
        sums = sums + far[...].astype(F32)
    measured = []
    for v in range(tall // SUB):
        tile = jnp.zeros((SUB, LANES), F32)
        for at in range(min(SUB, outer - v * SUB)):
            p = v * SUB + at
            tile = jnp.where(sub == at, meas[:, p * LANES : (p + 1) * LANES], tile)
        measured.append(tile)
    measured = jnp.concatenate(measured, axis=0)
    rest_row[...] = (measured - sums[0:tall]) / jnp.maximum(sums[tall:], 1.0)

    def halo(q):
        at = 2 * tall + q % half * SUB
        high, low = above[at : at + SUB], below[at : at + SUB]
        if q // half == 1:
            high, low = pltpu.roll(high, SUB - 3, 0), pltpu.roll(low, 3, 0)
        return jnp.where(sub < 3, high, jnp.where(sub < 6, low, 0.0))

    side = 2 * tall + half * SUB
    side = jnp.where(sub < 3, above[side : side + SUB], below[side : side + SUB])
    shear_cols = [shear_f[g * SUB : (g + 1) * SUB] for g in range(groups)]
    step_cols = [step_f[g * SUB : (g + 1) * SUB] for g in range(groups)]
    inside = rows_of((SUB, 1)) < 6
    shear_cols.append(jnp.where(inside, 2.0 * side[:, 0:1] + side[:, 1:2], 0.0))
    step_cols.append(jnp.where(inside, side[:, 2:3] + side[:, 3:4] + side[:, 4:5], 0.0))
    index, delay, steps = [], [], []
    for g in range(groups + 1):
        s = jnp.broadcast_to(shear_cols[g].astype(I32), (SUB, LANES))
        rest = s & (LANES - 1)
        index.append((lane + rest) & (LANES - 1))
        delay.append((s >> 7) + jnp.where(lane + rest >= LANES, 1, 0))
        steps.append(jnp.broadcast_to(step_cols[g], (SUB, LANES)))
    tiles = []
    turned = [[] for _ in range(groups + 1)]
    for p in range(outer + 1):
        if p < outer:
            residual = jnp.broadcast_to(rest_row[p : p + 1, :], (SUB, LANES))
        else:
            residual = jnp.zeros((SUB, LANES), F32)
        lost = residual - residual.astype(BF16).astype(F32)
        tiles.append(jnp.where(sub < 7, residual, lost))
        for g in range(groups + 1):
            turned[g].append(turn(residual, index[g]) if p < outer else residual)
        q = p - (reach - 1)
        if q < 0 or q >= inner:
            continue
        here = slice(q * LANES, (q + 1) * LANES)
        open_q = jnp.broadcast_to(ap_ref[:, here].astype(F32), (SUB, LANES))
        pieces = []
        for g in range(groups + 1):
            pulled = choose(delay[g], turned[g][q : q + reach])
            base = raw[g * SUB : (g + 1) * SUB, here] if g < groups else halo(q)
            pieces.append(base + pulled * open_q * steps[g])
        out_ref[:, here] = jnp.concatenate(pieces, axis=0).astype(BF16)
        tiles[q] = jnp.where(sub < 6, pieces[-1], tiles[q])
    msg_ref[...] = jnp.concatenate(tiles, axis=0).astype(BF16)


def spread(rows, ch, which):
    return (which(rows_of((rows, ch))) == lanes_of((rows, ch))).astype(F32).astype(BF16)


def picked(row_ref, rows, which):
    ch = row_ref.shape[1]
    pick = which(rows_of((rows, ch))) == lanes_of((rows, ch))
    row = jnp.broadcast_to(row_ref[...], (rows, ch))
    return jnp.sum(jnp.where(pick, row, 0.0), axis=1, keepdims=True)


def with_bias(matrix, bias, start):
    lane = lanes_of(matrix.shape)
    for i, part in enumerate(split3(0.5 * bias)):
        matrix = jnp.where(lane == start + i, part, matrix)
    return matrix


def gate_kernel(_, line_ref, same_ref):
    pass


def weights_kernel(
    _, sw_in, sb_in, cw_in, cb_in, ow_in, main_ref, halo_ref, first_ref, second_ref, out_w_ref, *rest
):
    local, sems = rest[:5], rest[5]
    for copy in fetch((sw_in, sb_in, cw_in, cb_in, ow_in), local, sems):
        copy.wait()
    sw_ref, sb_ref, cw_ref, cb_ref, ow_ref = local
    ch, taps2 = sw_ref.shape
    taps = cw_ref.shape[0]
    place = lax.axis_index("band")
    has_low = jnp.where(place > 0, 1, 0)
    has_high = jnp.where(place < lax.axis_size("band") - 1, 1, 0)
    width = main_ref.shape[1]
    slots = 16
    line = lax.axis_index("row") * lax.axis_size("col") + lax.axis_index("col")
    lines = lax.axis_size("row") * lax.axis_size("col")
    group = lanes_of((taps2, width)) // slots
    offset = jnp.where(line % 2 == 1, group // 3, 2 - group // 3)
    present = (line + offset >= 1) & (line + offset <= lines)
    fan = (rows_of((taps2, width)) == 3 * offset + group % 3) & present
    fan = fan.astype(F32).astype(BF16)
    flat = jnp.dot(sw_ref[...], fan, preferred_element_type=F32).astype(BF16)
    for ref, slot_of in (
        (main_ref, lambda b: b),
        (halo_ref, lambda b: jnp.where(b < 3, 11 + b, jnp.where(b < 9, b - 3, b - 1))),
    ):
        rows = ref.shape[0]
        which = lambda r: r % ch
        full = jnp.dot(spread(rows, ch, which), flat, preferred_element_type=F32)
        lane = lanes_of((rows, width))
        band = rows_of((rows, width)) // ch
        keep = (lane % slots == slot_of(band)) & (lane < taps2 * slots)
        matrix = with_bias(
            jnp.where(keep, 0.5 * full, 0.0), picked(sb_ref, rows, which), taps2 * slots
        )
        if ref is halo_ref:
            valid = jnp.where(band < 3, has_low, jnp.where(band >= 9, has_high, 1))
            matrix = jnp.where(valid > 0, matrix, 0.0)
        ref[...] = matrix.astype(BF16)

    per = SUB
    rows = per * ch
    width = first_ref.shape[1]
    used = (per + taps - 1) * ch
    which = lambda r: r // per
    fan = (lanes_of((ch, width)) % ch == rows_of((ch, width))).astype(F32).astype(BF16)
    picks = spread(rows, ch, which)
    lane = lanes_of((rows, width))
    ahead = jnp.where(lane < used, lane // ch - rows_of((rows, width)) % per, -LANES)
    shifts = (0, per, per - (per + taps - 1), 2 * per - (per + taps - 1))
    blocks = [jnp.zeros((rows, width), F32) for _ in shifts]
    for d in range(taps):
        flat = jnp.dot(cw_ref[d], fan, preferred_element_type=F32).astype(BF16)
        full = 0.5 * jnp.dot(picks, flat, preferred_element_type=F32)
        blocks = [jnp.where(ahead == d + s, full, b) for s, b in zip(shifts, blocks)]
    bias = picked(cb_ref, rows, which)
    for i, block in enumerate(blocks):
        block = block if i == 2 else with_bias(block, bias, used)
        ref = first_ref if i < 2 else second_ref
        ref[i % 2 * rows : (i % 2 + 1) * rows, :] = block.astype(BF16)
    out_w_ref[...] = jnp.broadcast_to(picked(ow_ref, rows, which), out_w_ref.shape)


def denoise_kernel(
    tile,
    reach,
    ow_ref,
    mid_ref,
    shear_ref,
    step_ref,
    raw0_ref,
    msg0_ref,
    raw1_ref,
    msg1_ref,
    main_ref,
    halo_ref,
    first_ref,
    second_ref,
    out_ref,
    act,
    near0,
    near1,
    words,
):
    bands, cols = out_ref.shape
    slots = 16
    ch = main_ref.shape[0] // slots
    tiles = cols // tile
    inner = cols // LANES
    wide = tile + 2 * LANES
    split = act.shape[1] // 2
    groups = -(-bands // SUB)
    ones = jnp.where(rows_of((slots, tile)) < 3, 1.0, 0.0).astype(BF16)
    blank = jnp.zeros((2 * slots, LANES), BF16)
    zero = jnp.zeros((SUB, LANES), F32)
    shear_f = column(shear_ref[...].astype(F32), groups * SUB)
    step_f = column(step_ref[...], groups * SUB)
    lane = lanes_of()
    index, delay, steps = [], [], []
    for g in range(groups):
        s = jnp.broadcast_to(shear_f[g * SUB : (g + 1) * SUB].astype(I32), (SUB, LANES))
        rest = s & (LANES - 1)
        index.append((lane + rest) & (LANES - 1))
        delay.append((s >> 7) + jnp.where(lane + rest >= LANES, 1, 0))
        steps.append(jnp.broadcast_to(step_f[g * SUB : (g + 1) * SUB], (SUB, LANES)))
    rows_in = msg0_ref.shape[0]
    chunks = inner + reach - 1
    for n, msg_ref in enumerate((msg0_ref, msg1_ref)):
        words[n * rows_in : (n + 1) * rows_in, :] = msg_ref[...].astype(F32)
    turned = [[[] for _ in range(groups)] for _ in range(2)]

    def neighbours(q):
        for n, (raw_ref, near) in enumerate(((raw0_ref, near0), (raw1_ref, near1))):
            base = n * rows_in
            while len(turned[n][0]) < q + reach:
                p = len(turned[n][0])
                if p >= chunks:
                    residual = zero
                else:
                    at = base + p * SUB + 6
                    residual = words[at : at + 1, :] + words[at + 1 : at + 2, :]
                    residual = jnp.broadcast_to(residual, (SUB, LANES))
                for g in range(groups):
                    turned[n][g].append(turn(residual, index[g]))
            at = base + q * SUB
            raw = raw_ref[:, q * LANES : (q + 1) * LANES].astype(F32)
            open_q = jnp.broadcast_to(raw[bands : bands + 1], (SUB, LANES))
            pieces = [
                raw[g * SUB : (g + 1) * SUB]
                + choose(delay[g], turned[n][g][q : q + reach]) * open_q * steps[g]
                for g in range(groups)
            ]
            pieces.append(words[at : at + SUB, :])
            near[:, q * LANES : (q + 1) * LANES] = jnp.concatenate(pieces, axis=0).astype(BF16)

    def silu_twice(half):
        return half + half * jnp.tanh(half)

    def spatial(t):
        start = t * tile
        end = start + tile
        patches = []
        for ref in (near0, mid_ref, near1):
            left = ref[:, start - LANES : start] if t else blank
            here = ref[:, start:end]
            right = ref[:, end : end + LANES] if t < tiles - 1 else blank
            row = jnp.concatenate([left, here, right], axis=1)
            back = pltpu.roll(row, 1, 1)[:, LANES : LANES + tile]
            ahead = pltpu.roll(row, wide - 1, 1)[:, LANES : LANES + tile]
            patches += [back, here, ahead]
        buf = act.at[t % act.shape[0]]
        for part, w_ref in enumerate((main_ref, halo_ref)):
            x = jnp.concatenate(
                [p[part * slots : (part + 1) * slots] for p in patches] + [ones], axis=0
            )
            half = jnp.dot(w_ref[...], x, preferred_element_type=F32)
            value = silu_twice(half).astype(BF16)
            if part == 0:
                buf[3 * ch : 19 * ch, :] = value
            else:
                buf[0 : 3 * ch, :] = value[0 : 3 * ch]
                buf[19 * ch : 28 * ch, :] = value[3 * ch :]

    def spectral(t):
        start = t * tile
        buf = act.at[t % act.shape[0]]
        halves = []
        for part, w_ref in enumerate((first_ref, second_ref)):
            x = jnp.concatenate([buf[part * split : (part + 1) * split, :], ones], axis=0)
            halves.append(jnp.dot(w_ref[...], x, preferred_element_type=F32))
        rows = SUB * ch
        blocks = [halves[0][0:rows], halves[0][rows:] + halves[1][0:rows], halves[1][rows:]]
        pieces = []
        for half in blocks:
            total = None
            for k in range(ch):
                weight = ow_ref[k * SUB : (k + 1) * SUB, :]
                weight = jnp.concatenate([weight] * (tile // LANES), axis=1)
                term = weight * silu_twice(half[k * SUB : (k + 1) * SUB])
                total = term if total is None else total + term
            pieces.append(total)
        update = jnp.concatenate(pieces, axis=0)[0:bands]
        center = mid_ref[:, start : start + tile].astype(F32)[0:bands]
        out_ref[:, start : start + tile] = (center + update).astype(BF16)

    made = 0
    for t in range(tiles + 1):
        while t < tiles and made < min((t + 1) * tile // LANES + 1, inner):
            neighbours(made)
            made += 1
        if t < tiles:
            spatial(t)
        if t:
            spectral(t - 1)


def vmem(n):
    return [pl.BlockSpec(memory_space=pltpu.VMEM)] * n


def hbm(n):
    return [pl.BlockSpec(memory_space=pltpu.HBM)] * n


def in_hbm(arrays):
    return [pltpu.with_memory_space_constraint(x, pltpu.HBM) for x in arrays]


ANY = pl.BlockSpec(memory_space=pl.ANY)


def on_device(
    spectral_cube,
    aperture,
    measurement,
    shears,
    step_sizes,
    spatial_weight,
    spatial_bias,
    spectral_weight,
    spectral_bias,
    out_weight,
):
    bands, row_count, cols = spectral_cube.shape
    width = measurement.shape[1]
    reach = (width - cols) // LANES + 2
    outer = -(-width // LANES)
    groups = -(-bands // SUB)
    slots = (groups + 1) * SUB
    taps, ch = spectral_weight.shape[:2]
    taps2 = spatial_weight.shape[1]
    count = lax.axis_size("band")
    cube = spectral_cube.reshape(bands, cols)
    shear_row = shears.reshape(1, bands)
    step_row = step_sizes.reshape(1, bands)
    params = pltpu.CompilerParams(vmem_limit_bytes=48 * 2**20)

    tall = -(-outer // SUB) * SUB
    side = (cols // LANES // 2 + 2) * SUB
    inputs = (cube, aperture, measurement, shear_row, step_row)
    part, up, dn, *kept = pl.pallas_call(
        functools.partial(project_kernel, reach),
        out_shape=(
            jax.ShapeDtypeStruct((2 * tall, LANES), BF16),
            jax.ShapeDtypeStruct((2 * tall + side, LANES), BF16),
            jax.ShapeDtypeStruct((2 * tall + side, LANES), BF16),
        )
        + (jax.ShapeDtypeStruct((groups * SUB, cols), BF16),)
        + tuple(jax.ShapeDtypeStruct(x.shape, x.dtype) for x in inputs[1:]),
        in_specs=hbm(5),
        out_specs=tuple(vmem(8)),
        scratch_shapes=[
            pltpu.VMEM((bands, cols), BF16),
            pltpu.VMEM((groups * SUB, cols), F32),
            pltpu.SemaphoreType.DMA((5,)),
        ],
        compiler_params=params,
        name="project",
    )(*in_hbm(inputs))

    def around(x, shift):
        return lax.ppermute(x, "band", [(i, (i + shift) % count) for i in range(count)])

    below = around(up, 1)
    above = around(dn, -1)
    far = [around(part, s) for s in range(2, count - 1)]

    line = pl.pallas_call(
        gate_kernel,
        out_shape=jax.ShapeDtypeStruct(kept[0].shape, BF16),
        in_specs=[ANY, ANY],
        out_specs=ANY,
        input_output_aliases={1: 0},
        compiler_params=pltpu.CompilerParams(vmem_limit_bytes=2**20),
        name="gate",
    )(part, kept[0])
    kept[0] = line

    lines = lax.axis_size(("row", "col"))
    pairs = [(i, i ^ 1) for i in range(lines)]
    others = [(i, min(max(i - 1 + i % 2 * 2, 0), lines - 1)) for i in range(lines)]
    raw0 = lax.ppermute(line, ("row", "col"), pairs)
    raw1 = lax.ppermute(line, ("row", "col"), others)

    words = (outer + 1) * SUB
    updated, message = pl.pallas_call(
        functools.partial(update_kernel, reach, len(far)),
        out_shape=(
            jax.ShapeDtypeStruct((slots, cols), BF16),
            jax.ShapeDtypeStruct((words, LANES), BF16),
        ),
        in_specs=vmem(8 + len(far)),
        out_specs=tuple(vmem(2)),
        scratch_shapes=[
            pltpu.VMEM((groups * SUB, cols), F32),
            pltpu.VMEM((1, outer * LANES), F32),
            pltpu.VMEM((tall, LANES), F32),
        ],
        compiler_params=params,
        cost_estimate=pl.CostEstimate(
            flops=10**10, bytes_accessed=4 * 10**7, transcendentals=0
        ),
        name="update",
    )(*kept, part, below, above, *far)

    message0 = lax.ppermute(message, ("row", "col"), pairs)
    message1 = lax.ppermute(message, ("row", "col"), others)

    small = (
        spatial_weight,
        spatial_bias.reshape(1, ch),
        spectral_weight,
        spectral_bias.reshape(1, ch),
        out_weight.reshape(1, ch),
    )
    reached = (SUB + taps - 1) * ch
    main_w, halo_w, first_w, second_w, out_w = pl.pallas_call(
        weights_kernel,
        out_shape=(
            jax.ShapeDtypeStruct((16 * ch, taps2 * 16 + 16), BF16),
            jax.ShapeDtypeStruct((12 * ch, taps2 * 16 + 16), BF16),
            jax.ShapeDtypeStruct((2 * SUB * ch, reached + 16), BF16),
            jax.ShapeDtypeStruct((2 * SUB * ch, reached + 16), BF16),
            jax.ShapeDtypeStruct((SUB * ch, LANES), F32),
        ),
        in_specs=[ANY] + hbm(5),
        out_specs=tuple(vmem(5)),
        scratch_shapes=[pltpu.VMEM(x.shape, x.dtype) for x in small]
        + [pltpu.SemaphoreType.DMA((5,))],
        compiler_params=params,
        name="weights",
    )(message, *in_hbm(small))

    tile = 256
    result = pl.pallas_call(
        functools.partial(denoise_kernel, tile, reach),
        out_shape=jax.ShapeDtypeStruct((bands, cols), BF16),
        in_specs=vmem(12),
        out_specs=vmem(1)[0],
        scratch_shapes=[
            pltpu.VMEM((4, 28 * ch, tile), BF16),
            pltpu.VMEM((slots, cols), BF16),
            pltpu.VMEM((slots, cols), BF16),
            pltpu.VMEM((2 * words, LANES), F32),
        ],
        compiler_params=params,
        name="denoise",
    )(
        out_w,
        updated,
        kept[3],
        kept[4],
        raw0,
        message0,
        raw1,
        message1,
        main_w,
        halo_w,
        first_w,
        second_w,
    )
    return result.reshape(bands, 1, cols)


def solution(mesh):
    in_specs = (
        P("band", ("row", "col"), None),
        P(("row", "col"), None),
        P(("row", "col"), None),
        P("band"),
        P("band"),
        P(),
        P(),
        P(),
        P(),
        P(),
    )
    out_specs = P("band", ("row", "col"), None)
    return jax.shard_map(
        on_device, mesh=mesh, in_specs=in_specs, out_specs=out_specs, check_vma=False
    )
```

```python
import functools

import jax
import jax.numpy as jnp
from jax import lax
from jax.experimental import pallas as pl
from jax.experimental.pallas import tpu as pltpu
from jax.sharding import PartitionSpec as P

LANES = 128
SUB = 8
F32 = jnp.float32
BF16 = jnp.bfloat16
I32 = jnp.int32


def lanes_of(shape=(SUB, LANES)):
    return lax.broadcasted_iota(I32, shape, 1)


def rows_of(shape=(SUB, LANES)):
    return lax.broadcasted_iota(I32, shape, 0)


def column(row, rows):
    n = row.shape[1]
    eye = rows_of((rows, n)) == lanes_of((rows, n))
    return jnp.sum(jnp.where(eye, jnp.broadcast_to(row, (rows, n)), 0.0), axis=1, keepdims=True)


def turn(chunk, index):
    return jnp.take_along_axis(chunk, index, axis=1, mode="promise_in_bounds")


def choose(delay, options):
    result = options[-1]
    for d in range(len(options) - 2, -1, -1):
        result = jnp.where(delay == d, options[d], result)
    return result


def split3(x):
    hi = x.astype(BF16).astype(F32)
    mid = (x - hi).astype(BF16).astype(F32)
    return hi, mid, x - hi - mid


def fetch(sources, targets, sems):
    copies = [
        pltpu.make_async_copy(src, dst, sems.at[i]) for i, (src, dst) in enumerate(zip(sources, targets))
    ]
    for copy in copies:
        copy.start()
    return copies


def project_kernel(
    reach, cube_in, ap_in, meas_in, shear_in, step_in, part_ref, up_ref, dn_ref, *rest_refs
):
    line_ref, *kept = rest_refs[:5]
    cube_ref, raw, sems = rest_refs[5:]
    ap_ref, meas_ref, shear_ref, step_ref = kept
    copies = fetch((cube_in, ap_in, meas_in, shear_in, step_in), (cube_ref, *kept), sems)
    for copy in copies:
        copy.wait()
    bands, cols = cube_ref.shape
    groups = -(-bands // SUB)
    inner = cols // LANES
    tall = part_ref.shape[0] // 2
    outer = -(-meas_ref.shape[1] // LANES)
    raw[bands // SUB * SUB :, :] = jnp.zeros((raw.shape[0] - bands // SUB * SUB, cols), F32)
    raw[0:bands, :] = cube_ref[...].astype(F32)
    shear_f = column(shear_ref[...].astype(F32), groups * SUB)
    step_f = column(step_ref[...], groups * SUB)
    shear_i = shear_f.astype(I32)
    lane, sub = lanes_of(), rows_of()
    index, delay = [], []
    for g in range(groups):
        s = jnp.broadcast_to(shear_i[g * SUB : (g + 1) * SUB], (SUB, LANES))
        rest = s & (LANES - 1)
        index.append((lane - rest) & (LANES - 1))
        delay.append((s >> 7) + jnp.where(lane < rest, 1, 0))
    zero = jnp.zeros((SUB, LANES), F32)
    turned = [[zero] * (reach - 1) for _ in range(groups)]
    opened = [[zero] * (reach - 1) for _ in range(groups)]
    sums = [zero] * (tall // SUB)
    counts = [zero] * (tall // SUB)
    firsts, lasts = [], []
    for p in range(outer):
        total = zero
        count = zero
        if p < inner:
            open_p = jnp.broadcast_to(
                ap_ref[:, p * LANES : (p + 1) * LANES].astype(F32), (SUB, LANES)
            )
            layers = [
                raw[g * SUB : (g + 1) * SUB, p * LANES : (p + 1) * LANES] for g in range(groups)
            ]
            firsts.append(layers[0])
            lasts.append(layers[-1])
            tagged = jnp.where(sub == bands % SUB, open_p, layers[-1])
            line_ref[:, p * LANES : (p + 1) * LANES] = jnp.concatenate(
                layers[:-1] + [tagged], axis=0
            ).astype(BF16)
        for g in range(groups):
            if p < inner:
                here = turn(layers[g] * open_p, index[g])
                here_open = turn(open_p, index[g])
            else:
                here = here_open = zero
            options = [here] + turned[g]
            options_open = [here_open] + opened[g]
            turned[g] = options[:-1]
            opened[g] = options_open[:-1]
            total = total + choose(delay[g], options)
            part = choose(delay[g], options_open)
            if (g + 1) * SUB > bands:
                part = jnp.where(sub < bands - g * SUB, part, 0.0)
            count = count + part
        v, at = divmod(p, SUB)
        sums[v] = jnp.where(sub == at, jnp.sum(total, axis=0, keepdims=True), sums[v])
        counts[v] = jnp.where(sub == at, jnp.sum(count, axis=0, keepdims=True), counts[v])
    sides = []
    for g in (0, groups - 1):
        s = shear_i[g * SUB : (g + 1) * SUB]
        parts = [(s >> 1).astype(F32), (s & 1).astype(F32)]
        parts += list(split3(step_f[g * SUB : (g + 1) * SUB]))
        side = zero
        for i, part in enumerate(parts):
            side = jnp.where(lane == i, part, side)
        sides.append(side)
    half = inner // 2
    dn = [
        jnp.where(sub < 3, firsts[q], pltpu.roll(firsts[q + half], 3, 0)) for q in range(half)
    ] + [sides[0], zero]
    up = [
        jnp.where(sub < 3, pltpu.roll(lasts[q + half], SUB - 3, 0), lasts[q]) for q in range(half)
    ] + [sides[1], zero]
    part_ref[...] = jnp.concatenate(sums + counts, axis=0).astype(BF16)
    up_ref[...] = jnp.concatenate(sums + counts + up, axis=0).astype(BF16)
    dn_ref[...] = jnp.concatenate(sums + counts + dn, axis=0).astype(BF16)


def update_kernel(
    reach,
    fars,
    line_ref,
    ap_ref,
    meas_ref,
    shear_ref,
    step_ref,
    own_ref,
    below_ref,
    above_ref,
    *rest_refs,
):
    far_refs = rest_refs[:fars]
    out_ref, msg_ref, raw, meas, rest_row = rest_refs[fars:]
    groups = line_ref.shape[0] // SUB
    cols = line_ref.shape[1]
    inner = cols // LANES
    half = inner // 2
    tall = own_ref.shape[0] // 2
    outer = -(-meas_ref.shape[1] // LANES)
    raw[...] = line_ref[...].astype(F32)
    meas[:, (outer - 1) * LANES :] = jnp.zeros((1, LANES), F32)
    meas[:, 0 : meas_ref.shape[1]] = meas_ref[...]
    shear_f = column(shear_ref[...].astype(F32), groups * SUB)
    step_f = column(step_ref[...], groups * SUB)
    lane, sub = lanes_of(), rows_of()
    below = below_ref[...].astype(F32)
    above = above_ref[...].astype(F32)
    sums = own_ref[...].astype(F32) + below[0 : 2 * tall] + above[0 : 2 * tall]
    for far in far_refs:
        sums = sums + far[...].astype(F32)
    measured = []
    for v in range(tall // SUB):
        tile = jnp.zeros((SUB, LANES), F32)
        for at in range(min(SUB, outer - v * SUB)):
            p = v * SUB + at
            tile = jnp.where(sub == at, meas[:, p * LANES : (p + 1) * LANES], tile)
        measured.append(tile)
    measured = jnp.concatenate(measured, axis=0)
    rest_row[...] = (measured - sums[0:tall]) / jnp.maximum(sums[tall:], 1.0)

    def halo(q):
        at = 2 * tall + q % half * SUB
        high, low = above[at : at + SUB], below[at : at + SUB]
        if q // half == 1:
            high, low = pltpu.roll(high, SUB - 3, 0), pltpu.roll(low, 3, 0)
        return jnp.where(sub < 3, high, jnp.where(sub < 6, low, 0.0))

    side = 2 * tall + half * SUB
    side = jnp.where(sub < 3, above[side : side + SUB], below[side : side + SUB])
    shear_cols = [shear_f[g * SUB : (g + 1) * SUB] for g in range(groups)]
    step_cols = [step_f[g * SUB : (g + 1) * SUB] for g in range(groups)]
    inside = rows_of((SUB, 1)) < 6
    shear_cols.append(jnp.where(inside, 2.0 * side[:, 0:1] + side[:, 1:2], 0.0))
    step_cols.append(jnp.where(inside, side[:, 2:3] + side[:, 3:4] + side[:, 4:5], 0.0))
    index, delay, steps = [], [], []
    for g in range(groups + 1):
        s = jnp.broadcast_to(shear_cols[g].astype(I32), (SUB, LANES))
        rest = s & (LANES - 1)
        index.append((lane + rest) & (LANES - 1))
        delay.append((s >> 7) + jnp.where(lane + rest >= LANES, 1, 0))
        steps.append(jnp.broadcast_to(step_cols[g], (SUB, LANES)))
    tiles = []
    turned = [[] for _ in range(groups + 1)]
    for p in range(outer + 1):
        if p < outer:
            residual = jnp.broadcast_to(rest_row[p : p + 1, :], (SUB, LANES))
        else:
            residual = jnp.zeros((SUB, LANES), F32)
        lost = residual - residual.astype(BF16).astype(F32)
        tiles.append(jnp.where(sub < 7, residual, lost))
        for g in range(groups + 1):
            turned[g].append(turn(residual, index[g]) if p < outer else residual)
        q = p - (reach - 1)
        if q < 0 or q >= inner:
            continue
        here = slice(q * LANES, (q + 1) * LANES)
        open_q = jnp.broadcast_to(ap_ref[:, here].astype(F32), (SUB, LANES))
        pieces = []
        for g in range(groups + 1):
            pulled = choose(delay[g], turned[g][q : q + reach])
            base = raw[g * SUB : (g + 1) * SUB, here] if g < groups else halo(q)
            pieces.append(base + pulled * open_q * steps[g])
        out_ref[:, here] = jnp.concatenate(pieces, axis=0).astype(BF16)
        tiles[q] = jnp.where(sub < 6, pieces[-1], tiles[q])
    msg_ref[...] = jnp.concatenate(tiles, axis=0).astype(BF16)


def spread(rows, ch, which):
    return (which(rows_of((rows, ch))) == lanes_of((rows, ch))).astype(F32).astype(BF16)


def picked(row_ref, rows, which):
    ch = row_ref.shape[1]
    pick = which(rows_of((rows, ch))) == lanes_of((rows, ch))
    row = jnp.broadcast_to(row_ref[...], (rows, ch))
    return jnp.sum(jnp.where(pick, row, 0.0), axis=1, keepdims=True)


def with_bias(matrix, bias, start):
    lane = lanes_of(matrix.shape)
    for i, part in enumerate(split3(0.5 * bias)):
        matrix = jnp.where(lane == start + i, part, matrix)
    return matrix


def gate_kernel(_, line_ref, same_ref):
    pass


def weights_kernel(
    _, sw_in, sb_in, cw_in, cb_in, ow_in, main_ref, halo_ref, first_ref, second_ref, out_w_ref, *rest
):
    local, sems = rest[:5], rest[5]
    for copy in fetch((sw_in, sb_in, cw_in, cb_in, ow_in), local, sems):
        copy.wait()
    sw_ref, sb_ref, cw_ref, cb_ref, ow_ref = local
    ch, taps2 = sw_ref.shape
    taps = cw_ref.shape[0]
    place = lax.axis_index("band")
    has_low = jnp.where(place > 0, 1, 0)
    has_high = jnp.where(place < lax.axis_size("band") - 1, 1, 0)
    width = main_ref.shape[1]
    slots = 16
    line = lax.axis_index("row") * lax.axis_size("col") + lax.axis_index("col")
    lines = lax.axis_size("row") * lax.axis_size("col")
    group = lanes_of((taps2, width)) // slots
    offset = jnp.where(line % 2 == 1, group // 3, 2 - group // 3)
    present = (line + offset >= 1) & (line + offset <= lines)
    fan = (rows_of((taps2, width)) == 3 * offset + group % 3) & present
    fan = fan.astype(F32).astype(BF16)
    flat = jnp.dot(sw_ref[...], fan, preferred_element_type=F32).astype(BF16)
    for ref, slot_of in (
        (main_ref, lambda b: b),
        (halo_ref, lambda b: jnp.where(b < 3, 11 + b, jnp.where(b < 9, b - 3, b - 1))),
    ):
        rows = ref.shape[0]
        which = lambda r: r % ch
        full = jnp.dot(spread(rows, ch, which), flat, preferred_element_type=F32)
        lane = lanes_of((rows, width))
        band = rows_of((rows, width)) // ch
        keep = (lane % slots == slot_of(band)) & (lane < taps2 * slots)
        matrix = with_bias(
            jnp.where(keep, 0.5 * full, 0.0), picked(sb_ref, rows, which), taps2 * slots
        )
        if ref is halo_ref:
            valid = jnp.where(band < 3, has_low, jnp.where(band >= 9, has_high, 1))
            matrix = jnp.where(valid > 0, matrix, 0.0)
        ref[...] = matrix.astype(BF16)

    per = SUB
    rows = per * ch
    width = first_ref.shape[1]
    used = (per + taps - 1) * ch
    which = lambda r: r // per
    fan = (lanes_of((ch, width)) % ch == rows_of((ch, width))).astype(F32).astype(BF16)
    picks = spread(rows, ch, which)
    lane = lanes_of((rows, width))
    ahead = jnp.where(lane < used, lane // ch - rows_of((rows, width)) % per, -LANES)
    matrix = jnp.zeros((rows, width), F32)
    for d in range(taps):
        flat = jnp.dot(cw_ref[d], fan, preferred_element_type=F32).astype(BF16)
        full = 0.5 * jnp.dot(picks, flat, preferred_element_type=F32)
        matrix = jnp.where(ahead == d, full, matrix)
    bias = picked(cb_ref, rows, which)
    first_ref[...] = with_bias(matrix, bias, used).astype(BF16)
    short = second_ref.shape[1]
    start = short - 16
    matrix = jnp.where(lanes_of((rows, short)) < start, matrix[:, 0:short], 0.0)
    second_ref[...] = with_bias(matrix, bias, start).astype(BF16)
    out_w_ref[...] = jnp.broadcast_to(picked(ow_ref, rows, which), out_w_ref.shape)


def denoise_kernel(
    tile,
    reach,
    ow_ref,
    mid_ref,
    shear_ref,
    step_ref,
    raw0_ref,
    msg0_ref,
    raw1_ref,
    msg1_ref,
    main_ref,
    halo_ref,
    first_ref,
    second_ref,
    out_ref,
    act,
    near0,
    near1,
    words,
):
    bands, cols = out_ref.shape
    slots = 16
    ch = main_ref.shape[0] // slots
    tiles = cols // tile
    inner = cols // LANES
    wide = tile + 2 * LANES
    groups = -(-bands // SUB)
    ones = jnp.where(rows_of((slots, tile)) < 3, 1.0, 0.0).astype(BF16)
    blank = jnp.zeros((2 * slots, LANES), BF16)
    zero = jnp.zeros((SUB, LANES), F32)
    shear_f = column(shear_ref[...].astype(F32), groups * SUB)
    step_f = column(step_ref[...], groups * SUB)
    lane = lanes_of()
    index, delay, steps = [], [], []
    for g in range(groups):
        s = jnp.broadcast_to(shear_f[g * SUB : (g + 1) * SUB].astype(I32), (SUB, LANES))
        rest = s & (LANES - 1)
        index.append((lane + rest) & (LANES - 1))
        delay.append((s >> 7) + jnp.where(lane + rest >= LANES, 1, 0))
        steps.append(jnp.broadcast_to(step_f[g * SUB : (g + 1) * SUB], (SUB, LANES)))
    rows_in = msg0_ref.shape[0]
    chunks = inner + reach - 1
    for n, msg_ref in enumerate((msg0_ref, msg1_ref)):
        words[n * rows_in : (n + 1) * rows_in, :] = msg_ref[...].astype(F32)
    turned = [[[] for _ in range(groups)] for _ in range(2)]

    def neighbours(q):
        for n, (raw_ref, near) in enumerate(((raw0_ref, near0), (raw1_ref, near1))):
            base = n * rows_in
            while len(turned[n][0]) < q + reach:
                p = len(turned[n][0])
                if p >= chunks:
                    residual = zero
                else:
                    at = base + p * SUB + 6
                    residual = words[at : at + 1, :] + words[at + 1 : at + 2, :]
                    residual = jnp.broadcast_to(residual, (SUB, LANES))
                for g in range(groups):
                    turned[n][g].append(turn(residual, index[g]))
            at = base + q * SUB
            raw = raw_ref[:, q * LANES : (q + 1) * LANES].astype(F32)
            open_q = jnp.broadcast_to(raw[bands : bands + 1], (SUB, LANES))
            pieces = [
                raw[g * SUB : (g + 1) * SUB]
                + choose(delay[g], turned[n][g][q : q + reach]) * open_q * steps[g]
                for g in range(groups)
            ]
            pieces.append(words[at : at + SUB, :])
            near[:, q * LANES : (q + 1) * LANES] = jnp.concatenate(pieces, axis=0).astype(BF16)

    def silu_twice(half):
        return half + half * jnp.tanh(half)

    def spatial(t):
        start = t * tile
        end = start + tile
        patches = []
        for ref in (near0, mid_ref, near1):
            left = ref[:, start - LANES : start] if t else blank
            here = ref[:, start:end]
            right = ref[:, end : end + LANES] if t < tiles - 1 else blank
            row = jnp.concatenate([left, here, right], axis=1)
            back = pltpu.roll(row, 1, 1)[:, LANES : LANES + tile]
            ahead = pltpu.roll(row, wide - 1, 1)[:, LANES : LANES + tile]
            patches += [back, here, ahead]
        buf = act.at[t % act.shape[0]]
        for part, w_ref in enumerate((main_ref, halo_ref)):
            x = jnp.concatenate(
                [p[part * slots : (part + 1) * slots] for p in patches] + [ones], axis=0
            )
            half = jnp.dot(w_ref[...], x, preferred_element_type=F32)
            value = silu_twice(half).astype(BF16)
            if part == 0:
                buf[3 * ch : 19 * ch, :] = value
            else:
                buf[0 : 3 * ch, :] = value[0 : 3 * ch]
                buf[19 * ch : 28 * ch, :] = value[3 * ch :]

    def spectral(t):
        start = t * tile
        buf = act.at[t % act.shape[0]]
        blocks = []
        for i in range(groups):
            w_ref = second_ref if i == groups - 1 else first_ref
            first = i * SUB * ch
            x = jnp.concatenate([buf[first : first + w_ref.shape[1] - slots, :], ones], axis=0)
            blocks.append(jnp.dot(w_ref[...], x, preferred_element_type=F32))
        pieces = []
        for half in blocks:
            total = None
            for k in range(ch):
                weight = ow_ref[k * SUB : (k + 1) * SUB, :]
                weight = jnp.concatenate([weight] * (tile // LANES), axis=1)
                term = weight * silu_twice(half[k * SUB : (k + 1) * SUB])
                total = term if total is None else total + term
            pieces.append(total)
        update = jnp.concatenate(pieces, axis=0)[0:bands]
        center = mid_ref[:, start : start + tile].astype(F32)[0:bands]
        out_ref[:, start : start + tile] = (center + update).astype(BF16)

    made = 0
    for t in range(tiles + 1):
        while t < tiles and made < min((t + 1) * tile // LANES + 1, inner):
            neighbours(made)
            made += 1
        if t < tiles:
            spatial(t)
        if t:
            spectral(t - 1)


def vmem(n):
    return [pl.BlockSpec(memory_space=pltpu.VMEM)] * n


def hbm(n):
    return [pl.BlockSpec(memory_space=pltpu.HBM)] * n


def in_hbm(arrays):
    return [pltpu.with_memory_space_constraint(x, pltpu.HBM) for x in arrays]


ANY = pl.BlockSpec(memory_space=pl.ANY)


def on_device(
    spectral_cube,
    aperture,
    measurement,
    shears,
    step_sizes,
    spatial_weight,
    spatial_bias,
    spectral_weight,
    spectral_bias,
    out_weight,
):
    bands, row_count, cols = spectral_cube.shape
    width = measurement.shape[1]
    reach = (width - cols) // LANES + 2
    outer = -(-width // LANES)
    groups = -(-bands // SUB)
    slots = (groups + 1) * SUB
    taps, ch = spectral_weight.shape[:2]
    taps2 = spatial_weight.shape[1]
    count = lax.axis_size("band")
    cube = spectral_cube.reshape(bands, cols)
    shear_row = shears.reshape(1, bands)
    step_row = step_sizes.reshape(1, bands)
    params = pltpu.CompilerParams(vmem_limit_bytes=48 * 2**20)

    tall = -(-outer // SUB) * SUB
    side = (cols // LANES // 2 + 2) * SUB
    inputs = (cube, aperture, measurement, shear_row, step_row)
    part, up, dn, *kept = pl.pallas_call(
        functools.partial(project_kernel, reach),
        out_shape=(
            jax.ShapeDtypeStruct((2 * tall, LANES), BF16),
            jax.ShapeDtypeStruct((2 * tall + side, LANES), BF16),
            jax.ShapeDtypeStruct((2 * tall + side, LANES), BF16),
        )
        + (jax.ShapeDtypeStruct((groups * SUB, cols), BF16),)
        + tuple(jax.ShapeDtypeStruct(x.shape, x.dtype) for x in inputs[1:]),
        in_specs=hbm(5),
        out_specs=tuple(vmem(8)),
        scratch_shapes=[
            pltpu.VMEM((bands, cols), BF16),
            pltpu.VMEM((groups * SUB, cols), F32),
            pltpu.SemaphoreType.DMA((5,)),
        ],
        compiler_params=params,
        name="project",
    )(*in_hbm(inputs))

    def around(x, shift):
        return lax.ppermute(x, "band", [(i, (i + shift) % count) for i in range(count)])

    below = around(up, 1)
    above = around(dn, -1)
    far = [around(part, s) for s in range(2, count - 1)]

    line = pl.pallas_call(
        gate_kernel,
        out_shape=jax.ShapeDtypeStruct(kept[0].shape, BF16),
        in_specs=[ANY, ANY],
        out_specs=ANY,
        input_output_aliases={1: 0},
        compiler_params=pltpu.CompilerParams(vmem_limit_bytes=2**20),
        name="gate",
    )(part, kept[0])
    kept[0] = line

    lines = lax.axis_size(("row", "col"))
    pairs = [(i, i ^ 1) for i in range(lines)]
    others = [(i, (i - 1 + i % 2 * 2) % lines) for i in range(lines)]
    raw0 = lax.ppermute(line, ("row", "col"), pairs)
    raw1 = lax.ppermute(line, ("row", "col"), others)

    words = (outer + 1) * SUB
    updated, message = pl.pallas_call(
        functools.partial(update_kernel, reach, len(far)),
        out_shape=(
            jax.ShapeDtypeStruct((slots, cols), BF16),
            jax.ShapeDtypeStruct((words, LANES), BF16),
        ),
        in_specs=vmem(8 + len(far)),
        out_specs=tuple(vmem(2)),
        scratch_shapes=[
            pltpu.VMEM((groups * SUB, cols), F32),
            pltpu.VMEM((1, outer * LANES), F32),
            pltpu.VMEM((tall, LANES), F32),
        ],
        compiler_params=params,
        cost_estimate=pl.CostEstimate(
            flops=10**10, bytes_accessed=4 * 10**7, transcendentals=0
        ),
        name="update",
    )(*kept, part, below, above, *far)

    message0 = lax.ppermute(message, ("row", "col"), pairs)
    message1 = lax.ppermute(message, ("row", "col"), others)

    small = (
        spatial_weight,
        spatial_bias.reshape(1, ch),
        spectral_weight,
        spectral_bias.reshape(1, ch),
        out_weight.reshape(1, ch),
    )
    reached = (SUB + taps - 1) * ch
    last = (bands - (groups - 1) * SUB + taps - 1) * ch
    main_w, halo_w, first_w, second_w, out_w = pl.pallas_call(
        weights_kernel,
        out_shape=(
            jax.ShapeDtypeStruct((16 * ch, taps2 * 16 + 16), BF16),
            jax.ShapeDtypeStruct((12 * ch, taps2 * 16 + 16), BF16),
            jax.ShapeDtypeStruct((SUB * ch, reached + 16), BF16),
            jax.ShapeDtypeStruct((SUB * ch, last + 16), BF16),
            jax.ShapeDtypeStruct((SUB * ch, LANES), F32),
        ),
        in_specs=[ANY] + hbm(5),
        out_specs=tuple(vmem(5)),
        scratch_shapes=[pltpu.VMEM(x.shape, x.dtype) for x in small]
        + [pltpu.SemaphoreType.DMA((5,))],
        compiler_params=params,
        name="weights",
    )(message, *in_hbm(small))

    tile = 512
    result = pl.pallas_call(
        functools.partial(denoise_kernel, tile, reach),
        out_shape=jax.ShapeDtypeStruct((bands, cols), BF16),
        in_specs=vmem(12),
        out_specs=vmem(1)[0],
        scratch_shapes=[
            pltpu.VMEM((4, 28 * ch, tile), BF16),
            pltpu.VMEM((slots, cols), BF16),
            pltpu.VMEM((slots, cols), BF16),
            pltpu.VMEM((2 * words, LANES), F32),
        ],
        compiler_params=params,
        name="denoise",
    )(
        out_w,
        updated,
        kept[3],
        kept[4],
        raw0,
        message0,
        raw1,
        message1,
        main_w,
        halo_w,
        first_w,
        second_w,
    )
    return result.reshape(bands, 1, cols)


def solution(mesh):
    in_specs = (
        P("band", ("row", "col"), None),
        P(("row", "col"), None),
        P(("row", "col"), None),
        P("band"),
        P("band"),
        P(),
        P(),
        P(),
        P(),
        P(),
    )
    out_specs = P("band", ("row", "col"), None)
    return jax.shard_map(
        on_device, mesh=mesh, in_specs=in_specs, out_specs=out_specs, check_vma=False
    )
```

```python
import functools

import jax
import jax.numpy as jnp
from jax import lax
from jax.experimental import pallas as pl
from jax.experimental.pallas import tpu as pltpu
from jax.sharding import PartitionSpec as P

LANES = 128
SUB = 8
F32 = jnp.float32
BF16 = jnp.bfloat16
I32 = jnp.int32


def lanes_of(shape=(SUB, LANES)):
    return lax.broadcasted_iota(I32, shape, 1)


def rows_of(shape=(SUB, LANES)):
    return lax.broadcasted_iota(I32, shape, 0)


def column(row, rows):
    n = row.shape[1]
    eye = rows_of((rows, n)) == lanes_of((rows, n))
    return jnp.sum(jnp.where(eye, jnp.broadcast_to(row, (rows, n)), 0.0), axis=1, keepdims=True)


def turn(chunk, index):
    return jnp.take_along_axis(chunk, index, axis=1, mode="promise_in_bounds")


def choose(delay, options):
    result = options[-1]
    for d in range(len(options) - 2, -1, -1):
        result = jnp.where(delay == d, options[d], result)
    return result


def split3(x):
    hi = x.astype(BF16).astype(F32)
    mid = (x - hi).astype(BF16).astype(F32)
    return hi, mid, x - hi - mid


def fetch(sources, targets, sems):
    copies = [
        pltpu.make_async_copy(src, dst, sems.at[i]) for i, (src, dst) in enumerate(zip(sources, targets))
    ]
    for copy in copies:
        copy.start()
    return copies


def project_kernel(
    reach, cube_in, ap_in, meas_in, shear_in, step_in, part_ref, up_ref, dn_ref, *rest_refs
):
    line_ref, *kept = rest_refs[:5]
    cube_ref, raw, sems = rest_refs[5:]
    ap_ref, meas_ref, shear_ref, step_ref = kept
    copies = fetch((cube_in, ap_in, meas_in, shear_in, step_in), (cube_ref, *kept), sems)
    for copy in copies:
        copy.wait()
    bands, cols = cube_ref.shape
    groups = -(-bands // SUB)
    inner = cols // LANES
    tall = part_ref.shape[0] // 2
    outer = -(-meas_ref.shape[1] // LANES)
    raw[bands // SUB * SUB :, :] = jnp.zeros((raw.shape[0] - bands // SUB * SUB, cols), F32)
    raw[0:bands, :] = cube_ref[...].astype(F32)
    shear_f = column(shear_ref[...].astype(F32), groups * SUB)
    step_f = column(step_ref[...], groups * SUB)
    shear_i = shear_f.astype(I32)
    lane, sub = lanes_of(), rows_of()
    index, delay = [], []
    for g in range(groups):
        s = jnp.broadcast_to(shear_i[g * SUB : (g + 1) * SUB], (SUB, LANES))
        rest = s & (LANES - 1)
        index.append((lane - rest) & (LANES - 1))
        delay.append((s >> 7) + jnp.where(lane < rest, 1, 0))
    zero = jnp.zeros((SUB, LANES), F32)
    turned = [[zero] * (reach - 1) for _ in range(groups)]
    opened = [[zero] * (reach - 1) for _ in range(groups)]
    sums = [zero] * (tall // SUB)
    counts = [zero] * (tall // SUB)
    firsts, lasts = [], []
    for p in range(outer):
        total = zero
        count = zero
        if p < inner:
            open_p = jnp.broadcast_to(
                ap_ref[:, p * LANES : (p + 1) * LANES].astype(F32), (SUB, LANES)
            )
            layers = [
                raw[g * SUB : (g + 1) * SUB, p * LANES : (p + 1) * LANES] for g in range(groups)
            ]
            firsts.append(layers[0])
            lasts.append(layers[-1])
            tagged = jnp.where(sub == bands % SUB, open_p, layers[-1])
            line_ref[:, p * LANES : (p + 1) * LANES] = jnp.concatenate(
                layers[:-1] + [tagged], axis=0
            ).astype(BF16)
        for g in range(groups):
            if p < inner:
                here = turn(layers[g] * open_p, index[g])
                here_open = turn(open_p, index[g])
            else:
                here = here_open = zero
            options = [here] + turned[g]
            options_open = [here_open] + opened[g]
            turned[g] = options[:-1]
            opened[g] = options_open[:-1]
            total = total + choose(delay[g], options)
            part = choose(delay[g], options_open)
            if (g + 1) * SUB > bands:
                part = jnp.where(sub < bands - g * SUB, part, 0.0)
            count = count + part
        v, at = divmod(p, SUB)
        sums[v] = jnp.where(sub == at, jnp.sum(total, axis=0, keepdims=True), sums[v])
        counts[v] = jnp.where(sub == at, jnp.sum(count, axis=0, keepdims=True), counts[v])
    sides = []
    for g in (0, groups - 1):
        s = shear_i[g * SUB : (g + 1) * SUB]
        parts = [(s >> 1).astype(F32), (s & 1).astype(F32)]
        parts += list(split3(step_f[g * SUB : (g + 1) * SUB]))
        side = zero
        for i, part in enumerate(parts):
            side = jnp.where(lane == i, part, side)
        sides.append(side)
    half = inner // 2
    dn = [
        jnp.where(sub < 3, firsts[q], pltpu.roll(firsts[q + half], 3, 0)) for q in range(half)
    ] + [sides[0], zero]
    up = [
        jnp.where(sub < 3, pltpu.roll(lasts[q + half], SUB - 3, 0), lasts[q]) for q in range(half)
    ] + [sides[1], zero]
    part_ref[...] = jnp.concatenate(sums + counts, axis=0).astype(BF16)
    up_ref[...] = jnp.concatenate(sums + counts + up, axis=0).astype(BF16)
    dn_ref[...] = jnp.concatenate(sums + counts + dn, axis=0).astype(BF16)


def update_kernel(
    reach,
    fars,
    line_ref,
    ap_ref,
    meas_ref,
    shear_ref,
    step_ref,
    own_ref,
    below_ref,
    above_ref,
    *rest_refs,
):
    far_refs = rest_refs[:fars]
    out_ref, msg_ref, raw, meas, rest_row = rest_refs[fars:]
    groups = line_ref.shape[0] // SUB
    cols = line_ref.shape[1]
    inner = cols // LANES
    half = inner // 2
    tall = own_ref.shape[0] // 2
    outer = -(-meas_ref.shape[1] // LANES)
    raw[...] = line_ref[...].astype(F32)
    meas[:, (outer - 1) * LANES :] = jnp.zeros((1, LANES), F32)
    meas[:, 0 : meas_ref.shape[1]] = meas_ref[...]
    shear_f = column(shear_ref[...].astype(F32), groups * SUB)
    step_f = column(step_ref[...], groups * SUB)
    lane, sub = lanes_of(), rows_of()
    below = below_ref[...].astype(F32)
    above = above_ref[...].astype(F32)
    sums = own_ref[...].astype(F32) + below[0 : 2 * tall] + above[0 : 2 * tall]
    for far in far_refs:
        sums = sums + far[...].astype(F32)
    measured = []
    for v in range(tall // SUB):
        tile = jnp.zeros((SUB, LANES), F32)
        for at in range(min(SUB, outer - v * SUB)):
            p = v * SUB + at
            tile = jnp.where(sub == at, meas[:, p * LANES : (p + 1) * LANES], tile)
        measured.append(tile)
    measured = jnp.concatenate(measured, axis=0)
    rest_row[...] = (measured - sums[0:tall]) / jnp.maximum(sums[tall:], 1.0)

    def halo(q):
        at = 2 * tall + q % half * SUB
        high, low = above[at : at + SUB], below[at : at + SUB]
        if q // half == 1:
            high, low = pltpu.roll(high, SUB - 3, 0), pltpu.roll(low, 3, 0)
        return jnp.where(sub < 3, high, jnp.where(sub < 6, low, 0.0))

    side = 2 * tall + half * SUB
    side = jnp.where(sub < 3, above[side : side + SUB], below[side : side + SUB])
    shear_cols = [shear_f[g * SUB : (g + 1) * SUB] for g in range(groups)]
    step_cols = [step_f[g * SUB : (g + 1) * SUB] for g in range(groups)]
    inside = rows_of((SUB, 1)) < 6
    shear_cols.append(jnp.where(inside, 2.0 * side[:, 0:1] + side[:, 1:2], 0.0))
    step_cols.append(jnp.where(inside, side[:, 2:3] + side[:, 3:4] + side[:, 4:5], 0.0))
    index, delay, steps = [], [], []
    for g in range(groups + 1):
        s = jnp.broadcast_to(shear_cols[g].astype(I32), (SUB, LANES))
        rest = s & (LANES - 1)
        index.append((lane + rest) & (LANES - 1))
        delay.append((s >> 7) + jnp.where(lane + rest >= LANES, 1, 0))
        steps.append(jnp.broadcast_to(step_cols[g], (SUB, LANES)))
    tiles = []
    turned = [[] for _ in range(groups + 1)]
    for p in range(outer + 1):
        if p < outer:
            residual = jnp.broadcast_to(rest_row[p : p + 1, :], (SUB, LANES))
        else:
            residual = jnp.zeros((SUB, LANES), F32)
        lost = residual - residual.astype(BF16).astype(F32)
        tiles.append(jnp.where(sub < 7, residual, lost))
        for g in range(groups + 1):
            turned[g].append(turn(residual, index[g]) if p < outer else residual)
        q = p - (reach - 1)
        if q < 0 or q >= inner:
            continue
        here = slice(q * LANES, (q + 1) * LANES)
        open_q = jnp.broadcast_to(ap_ref[:, here].astype(F32), (SUB, LANES))
        pieces = []
        for g in range(groups + 1):
            pulled = choose(delay[g], turned[g][q : q + reach])
            base = raw[g * SUB : (g + 1) * SUB, here] if g < groups else halo(q)
            pieces.append(base + pulled * open_q * steps[g])
        out_ref[:, here] = jnp.concatenate(pieces, axis=0).astype(BF16)
        tiles[q] = jnp.where(sub < 6, pieces[-1], tiles[q])
    msg_ref[...] = jnp.concatenate(tiles, axis=0).astype(BF16)


def spread(rows, ch, which):
    return (which(rows_of((rows, ch))) == lanes_of((rows, ch))).astype(F32).astype(BF16)


def picked(row_ref, rows, which):
    ch = row_ref.shape[1]
    pick = which(rows_of((rows, ch))) == lanes_of((rows, ch))
    row = jnp.broadcast_to(row_ref[...], (rows, ch))
    return jnp.sum(jnp.where(pick, row, 0.0), axis=1, keepdims=True)


def with_bias(matrix, bias, start):
    lane = lanes_of(matrix.shape)
    for i, part in enumerate(split3(0.5 * bias)):
        matrix = jnp.where(lane == start + i, part, matrix)
    return matrix


def gate_kernel(_, line_ref, same_ref):
    pass


def weights_kernel(
    _, sw_in, sb_in, cw_in, cb_in, ow_in, main_ref, halo_ref, first_ref, second_ref, out_w_ref, *rest
):
    local, sems = rest[:5], rest[5]
    for copy in fetch((sw_in, sb_in, cw_in, cb_in, ow_in), local, sems):
        copy.wait()
    sw_ref, sb_ref, cw_ref, cb_ref, ow_ref = local
    ch, taps2 = sw_ref.shape
    taps = cw_ref.shape[0]
    place = lax.axis_index("band")
    has_low = jnp.where(place > 0, 1, 0)
    has_high = jnp.where(place < lax.axis_size("band") - 1, 1, 0)
    width = main_ref.shape[1]
    slots = 16
    line = lax.axis_index("row") * lax.axis_size("col") + lax.axis_index("col")
    lines = lax.axis_size("row") * lax.axis_size("col")
    group = lanes_of((taps2, width)) // slots
    offset = jnp.where(line % 2 == 1, group // 3, 2 - group // 3)
    present = (line + offset >= 1) & (line + offset <= lines)
    fan = (rows_of((taps2, width)) == 3 * offset + group % 3) & present
    fan = fan.astype(F32).astype(BF16)
    flat = jnp.dot(sw_ref[...], fan, preferred_element_type=F32).astype(BF16)
    for ref, slot_of in (
        (main_ref, lambda b: b),
        (halo_ref, lambda b: jnp.where(b < 3, 11 + b, jnp.where(b < 9, b - 3, b - 1))),
    ):
        rows = ref.shape[0]
        which = lambda r: r % ch
        full = jnp.dot(spread(rows, ch, which), flat, preferred_element_type=F32)
        lane = lanes_of((rows, width))
        band = rows_of((rows, width)) // ch
        keep = (lane % slots == slot_of(band)) & (lane < taps2 * slots)
        matrix = with_bias(
            jnp.where(keep, 0.5 * full, 0.0), picked(sb_ref, rows, which), taps2 * slots
        )
        if ref is halo_ref:
            valid = jnp.where(band < 3, has_low, jnp.where(band >= 9, has_high, 1))
            matrix = jnp.where(valid > 0, matrix, 0.0)
        ref[...] = matrix.astype(BF16)

    per = SUB
    rows = per * ch
    width = first_ref.shape[1]
    used = (per + taps - 1) * ch
    which = lambda r: r // per
    fan = (lanes_of((ch, width)) % ch == rows_of((ch, width))).astype(F32).astype(BF16)
    picks = spread(rows, ch, which)
    lane = lanes_of((rows, width))
    ahead = jnp.where(lane < used, lane // ch - rows_of((rows, width)) % per, -LANES)
    matrix = jnp.zeros((rows, width), F32)
    for d in range(taps):
        flat = jnp.dot(cw_ref[d], fan, preferred_element_type=F32).astype(BF16)
        full = 0.5 * jnp.dot(picks, flat, preferred_element_type=F32)
        matrix = jnp.where(ahead == d, full, matrix)
    bias = picked(cb_ref, rows, which)
    first_ref[...] = with_bias(matrix, bias, used).astype(BF16)
    short = second_ref.shape[1]
    start = short - 16
    matrix = jnp.where(lanes_of((rows, short)) < start, matrix[:, 0:short], 0.0)
    second_ref[...] = with_bias(matrix, bias, start).astype(BF16)
    out_w_ref[...] = jnp.broadcast_to(picked(ow_ref, rows, which), out_w_ref.shape)


def denoise_kernel(
    tile,
    reach,
    ow_ref,
    mid_ref,
    shear_ref,
    step_ref,
    raw0_ref,
    msg0_ref,
    raw1_ref,
    msg1_ref,
    main_ref,
    halo_ref,
    first_ref,
    second_ref,
    out_ref,
    act,
    near0,
    near1,
    words,
):
    bands, cols = out_ref.shape
    slots = 16
    ch = main_ref.shape[0] // slots
    tiles = cols // tile
    inner = cols // LANES
    wide = tile + 2 * LANES
    groups = -(-bands // SUB)
    ones = jnp.where(rows_of((slots, tile)) < 3, 1.0, 0.0).astype(BF16)
    blank = jnp.zeros((2 * slots, LANES), BF16)
    zero = jnp.zeros((SUB, LANES), F32)
    shear_f = column(shear_ref[...].astype(F32), groups * SUB)
    step_f = column(step_ref[...], groups * SUB)
    lane = lanes_of()
    index, delay, steps = [], [], []
    for g in range(groups):
        s = jnp.broadcast_to(shear_f[g * SUB : (g + 1) * SUB].astype(I32), (SUB, LANES))
        rest = s & (LANES - 1)
        index.append((lane + rest) & (LANES - 1))
        delay.append((s >> 7) + jnp.where(lane + rest >= LANES, 1, 0))
        steps.append(jnp.broadcast_to(step_f[g * SUB : (g + 1) * SUB], (SUB, LANES)))
    rows_in = msg0_ref.shape[0]
    chunks = inner + reach - 1
    for n, msg_ref in enumerate((msg0_ref, msg1_ref)):
        words[n * rows_in : (n + 1) * rows_in, :] = msg_ref[...].astype(F32)
    turned = [[[] for _ in range(groups)] for _ in range(2)]

    def neighbours(q):
        for n, (raw_ref, near) in enumerate(((raw0_ref, near0), (raw1_ref, near1))):
            base = n * rows_in
            while len(turned[n][0]) < q + reach:
                p = len(turned[n][0])
                if p >= chunks:
                    residual = zero
                else:
                    at = base + p * SUB + 6
                    residual = words[at : at + 1, :] + words[at + 1 : at + 2, :]
                    residual = jnp.broadcast_to(residual, (SUB, LANES))
                for g in range(groups):
                    turned[n][g].append(turn(residual, index[g]))
            at = base + q * SUB
            raw = raw_ref[:, q * LANES : (q + 1) * LANES].astype(F32)
            open_q = jnp.broadcast_to(raw[bands : bands + 1], (SUB, LANES))
            pieces = [
                raw[g * SUB : (g + 1) * SUB]
                + choose(delay[g], turned[n][g][q : q + reach]) * open_q * steps[g]
                for g in range(groups)
            ]
            pieces.append(words[at : at + SUB, :])
            near[:, q * LANES : (q + 1) * LANES] = jnp.concatenate(pieces, axis=0).astype(BF16)

    def silu_twice(half):
        return half + half * jnp.tanh(half)

    inputs, halves, blocks, sums = {}, {}, {}, {}
    made = 0

    def update_up_to(t):
        nonlocal made
        while made < min((t + 1) * tile // LANES + 1, inner):
            neighbours(made)
            made += 1

    def patches(t):
        start = t * tile
        end = start + tile
        parts = []
        for ref in (near0, mid_ref, near1):
            left = ref[:, start - LANES : start] if t else blank
            here = ref[:, start:end]
            right = ref[:, end : end + LANES] if t < tiles - 1 else blank
            row = jnp.concatenate([left, here, right], axis=1)
            back = pltpu.roll(row, 1, 1)[:, LANES : LANES + tile]
            ahead = pltpu.roll(row, wide - 1, 1)[:, LANES : LANES + tile]
            parts += [back, here, ahead]
        for part in range(2):
            inputs[t, part] = jnp.concatenate(
                [p[part * slots : (part + 1) * slots] for p in parts] + [ones], axis=0
            )

    def spatial(t, part):
        w_ref = halo_ref if part else main_ref
        halves[t, part] = jnp.dot(
            w_ref[...], inputs.pop((t, part)), preferred_element_type=F32
        )

    def activate(t, part):
        buf = act.at[t % act.shape[0]]
        value = silu_twice(halves.pop((t, part))).astype(BF16)
        if part == 0:
            buf[3 * ch : 19 * ch, :] = value
        else:
            buf[0 : 3 * ch, :] = value[0 : 3 * ch]
            buf[19 * ch : 28 * ch, :] = value[3 * ch :]

    def spectral(t, i):
        buf = act.at[t % act.shape[0]]
        w_ref = second_ref if i == groups - 1 else first_ref
        first = i * SUB * ch
        x = jnp.concatenate([buf[first : first + w_ref.shape[1] - slots, :], ones], axis=0)
        blocks[t, i] = jnp.dot(w_ref[...], x, preferred_element_type=F32)

    def project(t, i):
        half = blocks.pop((t, i))
        total = None
        for k in range(ch):
            weight = ow_ref[k * SUB : (k + 1) * SUB, :]
            weight = jnp.concatenate([weight] * (tile // LANES), axis=1)
            term = weight * silu_twice(half[k * SUB : (k + 1) * SUB])
            total = term if total is None else total + term
        sums[t, i] = total
        if i == groups - 1:
            start = t * tile
            update = jnp.concatenate([sums.pop((t, n)) for n in range(groups)], axis=0)[0:bands]
            center = mid_ref[:, start : start + tile].astype(F32)[0:bands]
            out_ref[:, start : start + tile] = (center + update).astype(BF16)

    update_up_to(0)
    patches(0)
    spatial(0, 0)
    spatial(0, 1)
    update_up_to(1)
    activate(0, 0)
    patches(1)
    activate(0, 1)
    for t in range(tiles):
        if t + 1 < tiles:
            spatial(t + 1, 0)
        if t:
            project(t - 1, groups - 1)
        if t + 2 < tiles:
            update_up_to(t + 2)
        if t + 1 < tiles:
            spatial(t + 1, 1)
            activate(t + 1, 0)
        spectral(t, 0)
        if t + 1 < tiles:
            activate(t + 1, 1)
        for i in range(1, groups):
            spectral(t, i)
            project(t, i - 1)
        if t + 2 < tiles:
            patches(t + 2)
    project(tiles - 1, groups - 1)


def vmem(n):
    return [pl.BlockSpec(memory_space=pltpu.VMEM)] * n


def hbm(n):
    return [pl.BlockSpec(memory_space=pltpu.HBM)] * n


def in_hbm(arrays):
    return [pltpu.with_memory_space_constraint(x, pltpu.HBM) for x in arrays]


ANY = pl.BlockSpec(memory_space=pl.ANY)


def on_device(
    spectral_cube,
    aperture,
    measurement,
    shears,
    step_sizes,
    spatial_weight,
    spatial_bias,
    spectral_weight,
    spectral_bias,
    out_weight,
):
    bands, row_count, cols = spectral_cube.shape
    width = measurement.shape[1]
    reach = (width - cols) // LANES + 2
    outer = -(-width // LANES)
    groups = -(-bands // SUB)
    slots = (groups + 1) * SUB
    taps, ch = spectral_weight.shape[:2]
    taps2 = spatial_weight.shape[1]
    count = lax.axis_size("band")
    cube = spectral_cube.reshape(bands, cols)
    shear_row = shears.reshape(1, bands)
    step_row = step_sizes.reshape(1, bands)
    params = pltpu.CompilerParams(vmem_limit_bytes=48 * 2**20)

    tall = -(-outer // SUB) * SUB
    side = (cols // LANES // 2 + 2) * SUB
    inputs = (cube, aperture, measurement, shear_row, step_row)
    part, up, dn, *kept = pl.pallas_call(
        functools.partial(project_kernel, reach),
        out_shape=(
            jax.ShapeDtypeStruct((2 * tall, LANES), BF16),
            jax.ShapeDtypeStruct((2 * tall + side, LANES), BF16),
            jax.ShapeDtypeStruct((2 * tall + side, LANES), BF16),
        )
        + (jax.ShapeDtypeStruct((groups * SUB, cols), BF16),)
        + tuple(jax.ShapeDtypeStruct(x.shape, x.dtype) for x in inputs[1:]),
        in_specs=hbm(5),
        out_specs=tuple(vmem(8)),
        scratch_shapes=[
            pltpu.VMEM((bands, cols), BF16),
            pltpu.VMEM((groups * SUB, cols), F32),
            pltpu.SemaphoreType.DMA((5,)),
        ],
        compiler_params=params,
        name="project",
    )(*in_hbm(inputs))

    def around(x, shift):
        return lax.ppermute(x, "band", [(i, (i + shift) % count) for i in range(count)])

    below = around(up, 1)
    above = around(dn, -1)
    far = [around(part, s) for s in range(2, count - 1)]

    line = pl.pallas_call(
        gate_kernel,
        out_shape=jax.ShapeDtypeStruct(kept[0].shape, BF16),
        in_specs=[ANY, ANY],
        out_specs=ANY,
        input_output_aliases={1: 0},
        compiler_params=pltpu.CompilerParams(vmem_limit_bytes=2**20),
        name="gate",
    )(part, kept[0])
    kept[0] = line

    lines = lax.axis_size(("row", "col"))
    pairs = [(i, i ^ 1) for i in range(lines)]
    others = [(i, (i - 1 + i % 2 * 2) % lines) for i in range(lines)]
    raw0 = lax.ppermute(line, ("row", "col"), pairs)
    raw1 = lax.ppermute(line, ("row", "col"), others)

    words = (outer + 1) * SUB
    updated, message = pl.pallas_call(
        functools.partial(update_kernel, reach, len(far)),
        out_shape=(
            jax.ShapeDtypeStruct((slots, cols), BF16),
            jax.ShapeDtypeStruct((words, LANES), BF16),
        ),
        in_specs=vmem(8 + len(far)),
        out_specs=tuple(vmem(2)),
        scratch_shapes=[
            pltpu.VMEM((groups * SUB, cols), F32),
            pltpu.VMEM((1, outer * LANES), F32),
            pltpu.VMEM((tall, LANES), F32),
        ],
        compiler_params=params,
        cost_estimate=pl.CostEstimate(
            flops=10**10, bytes_accessed=4 * 10**7, transcendentals=0
        ),
        name="update",
    )(*kept, part, below, above, *far)

    message0 = lax.ppermute(message, ("row", "col"), pairs)
    message1 = lax.ppermute(message, ("row", "col"), others)

    small = (
        spatial_weight,
        spatial_bias.reshape(1, ch),
        spectral_weight,
        spectral_bias.reshape(1, ch),
        out_weight.reshape(1, ch),
    )
    reached = (SUB + taps - 1) * ch
    last = (bands - (groups - 1) * SUB + taps - 1) * ch
    main_w, halo_w, first_w, second_w, out_w = pl.pallas_call(
        weights_kernel,
        out_shape=(
            jax.ShapeDtypeStruct((16 * ch, taps2 * 16 + 16), BF16),
            jax.ShapeDtypeStruct((12 * ch, taps2 * 16 + 16), BF16),
            jax.ShapeDtypeStruct((SUB * ch, reached + 16), BF16),
            jax.ShapeDtypeStruct((SUB * ch, last + 16), BF16),
            jax.ShapeDtypeStruct((SUB * ch, LANES), F32),
        ),
        in_specs=[ANY] + hbm(5),
        out_specs=tuple(vmem(5)),
        scratch_shapes=[pltpu.VMEM(x.shape, x.dtype) for x in small]
        + [pltpu.SemaphoreType.DMA((5,))],
        compiler_params=params,
        name="weights",
    )(message, *in_hbm(small))

    tile = 512
    result = pl.pallas_call(
        functools.partial(denoise_kernel, tile, reach),
        out_shape=jax.ShapeDtypeStruct((bands, cols), BF16),
        in_specs=vmem(12),
        out_specs=vmem(1)[0],
        scratch_shapes=[
            pltpu.VMEM((4, 28 * ch, tile), BF16),
            pltpu.VMEM((slots, cols), BF16),
            pltpu.VMEM((slots, cols), BF16),
            pltpu.VMEM((2 * words, LANES), F32),
        ],
        compiler_params=params,
        name="denoise",
    )(
        out_w,
        updated,
        kept[3],
        kept[4],
        raw0,
        message0,
        raw1,
        message1,
        main_w,
        halo_w,
        first_w,
        second_w,
    )
    return result.reshape(bands, 1, cols)


def solution(mesh):
    in_specs = (
        P("band", ("row", "col"), None),
        P(("row", "col"), None),
        P(("row", "col"), None),
        P("band"),
        P("band"),
        P(),
        P(),
        P(),
        P(),
        P(),
    )
    out_specs = P("band", ("row", "col"), None)
    return jax.shard_map(
        on_device, mesh=mesh, in_specs=in_specs, out_specs=out_specs, check_vma=False
    )
```

```python
import functools

import jax
import jax.numpy as jnp
from jax import lax
from jax.experimental import pallas as pl
from jax.experimental.pallas import tpu as pltpu
from jax.sharding import PartitionSpec as P

LANES = 128
SUB = 8
F32 = jnp.float32
BF16 = jnp.bfloat16
I32 = jnp.int32


def lanes_of(shape=(SUB, LANES)):
    return lax.broadcasted_iota(I32, shape, 1)


def rows_of(shape=(SUB, LANES)):
    return lax.broadcasted_iota(I32, shape, 0)


def column(row, rows):
    n = row.shape[1]
    eye = rows_of((rows, n)) == lanes_of((rows, n))
    return jnp.sum(jnp.where(eye, jnp.broadcast_to(row, (rows, n)), 0.0), axis=1, keepdims=True)


def turn(chunk, index):
    return jnp.take_along_axis(chunk, index, axis=1, mode="promise_in_bounds")


def choose(delay, options):
    result = options[-1]
    for d in range(len(options) - 2, -1, -1):
        result = jnp.where(delay == d, options[d], result)
    return result


def split3(x):
    hi = x.astype(BF16).astype(F32)
    mid = (x - hi).astype(BF16).astype(F32)
    return hi, mid, x - hi - mid


def fetch(sources, targets, sems):
    copies = [
        pltpu.make_async_copy(src, dst, sems.at[i]) for i, (src, dst) in enumerate(zip(sources, targets))
    ]
    for copy in copies:
        copy.start()
    return copies


def project_kernel(
    reach, cube_in, ap_in, meas_in, shear_in, step_in, part_ref, up_ref, dn_ref, *rest_refs
):
    line_ref, *kept = rest_refs[:5]
    cube_ref, raw, sems = rest_refs[5:]
    ap_ref, meas_ref, shear_ref, step_ref = kept
    copies = fetch((cube_in, ap_in, meas_in, shear_in, step_in), (cube_ref, *kept), sems)
    for copy in copies:
        copy.wait()
    bands, cols = cube_ref.shape
    groups = -(-bands // SUB)
    inner = cols // LANES
    tall = part_ref.shape[0] // 2
    outer = -(-meas_ref.shape[1] // LANES)
    raw[bands // SUB * SUB :, :] = jnp.zeros((raw.shape[0] - bands // SUB * SUB, cols), F32)
    raw[0:bands, :] = cube_ref[...].astype(F32)
    shear_f = column(shear_ref[...].astype(F32), groups * SUB)
    step_f = column(step_ref[...], groups * SUB)
    shear_i = shear_f.astype(I32)
    lane, sub = lanes_of(), rows_of()
    index, delay = [], []
    for g in range(groups):
        s = jnp.broadcast_to(shear_i[g * SUB : (g + 1) * SUB], (SUB, LANES))
        rest = s & (LANES - 1)
        index.append((lane - rest) & (LANES - 1))
        delay.append((s >> 7) + jnp.where(lane < rest, 1, 0))
    zero = jnp.zeros((SUB, LANES), F32)
    turned = [[zero] * (reach - 1) for _ in range(groups)]
    opened = [[zero] * (reach - 1) for _ in range(groups)]
    sums = [zero] * (tall // SUB)
    counts = [zero] * (tall // SUB)
    firsts, lasts = [], []
    for p in range(outer):
        total = zero
        count = zero
        if p < inner:
            open_p = jnp.broadcast_to(
                ap_ref[:, p * LANES : (p + 1) * LANES].astype(F32), (SUB, LANES)
            )
            layers = [
                raw[g * SUB : (g + 1) * SUB, p * LANES : (p + 1) * LANES] for g in range(groups)
            ]
            firsts.append(layers[0])
            lasts.append(layers[-1])
            tagged = jnp.where(sub == bands % SUB, open_p, layers[-1])
            line_ref[:, p * LANES : (p + 1) * LANES] = jnp.concatenate(
                layers[:-1] + [tagged], axis=0
            ).astype(BF16)
        for g in range(groups):
            if p < inner:
                here = turn(layers[g] * open_p, index[g])
                here_open = turn(open_p, index[g])
            else:
                here = here_open = zero
            options = [here] + turned[g]
            options_open = [here_open] + opened[g]
            turned[g] = options[:-1]
            opened[g] = options_open[:-1]
            total = total + choose(delay[g], options)
            part = choose(delay[g], options_open)
            if (g + 1) * SUB > bands:
                part = jnp.where(sub < bands - g * SUB, part, 0.0)
            count = count + part
        v, at = divmod(p, SUB)
        sums[v] = jnp.where(sub == at, jnp.sum(total, axis=0, keepdims=True), sums[v])
        counts[v] = jnp.where(sub == at, jnp.sum(count, axis=0, keepdims=True), counts[v])
    sides = []
    for g in (0, groups - 1):
        s = shear_i[g * SUB : (g + 1) * SUB]
        parts = [(s >> 1).astype(F32), (s & 1).astype(F32)]
        parts += list(split3(step_f[g * SUB : (g + 1) * SUB]))
        side = zero
        for i, part in enumerate(parts):
            side = jnp.where(lane == i, part, side)
        sides.append(side)
    half = inner // 2
    dn = [
        jnp.where(sub < 3, firsts[q], pltpu.roll(firsts[q + half], 3, 0)) for q in range(half)
    ] + [sides[0], zero]
    up = [
        jnp.where(sub < 3, pltpu.roll(lasts[q + half], SUB - 3, 0), lasts[q]) for q in range(half)
    ] + [sides[1], zero]
    part_ref[...] = jnp.concatenate(sums + counts, axis=0).astype(BF16)
    up_ref[...] = jnp.concatenate(sums + counts + up, axis=0).astype(BF16)
    dn_ref[...] = jnp.concatenate(sums + counts + dn, axis=0).astype(BF16)


def update_kernel(
    reach,
    fars,
    line_ref,
    ap_ref,
    meas_ref,
    shear_ref,
    step_ref,
    own_ref,
    below_ref,
    above_ref,
    *rest_refs,
):
    far_refs = rest_refs[:fars]
    out_ref, msg_ref, raw, meas, rest_row = rest_refs[fars:]
    groups = line_ref.shape[0] // SUB
    cols = line_ref.shape[1]
    inner = cols // LANES
    half = inner // 2
    tall = own_ref.shape[0] // 2
    outer = -(-meas_ref.shape[1] // LANES)
    raw[...] = line_ref[...].astype(F32)
    blank = jnp.zeros((out_ref.shape[0], LANES), BF16)
    out_ref[:, 0:LANES] = blank
    out_ref[:, cols + LANES :] = blank
    meas[:, (outer - 1) * LANES :] = jnp.zeros((1, LANES), F32)
    meas[:, 0 : meas_ref.shape[1]] = meas_ref[...]
    shear_f = column(shear_ref[...].astype(F32), groups * SUB)
    step_f = column(step_ref[...], groups * SUB)
    lane, sub = lanes_of(), rows_of()
    below = below_ref[...].astype(F32)
    above = above_ref[...].astype(F32)
    sums = own_ref[...].astype(F32) + below[0 : 2 * tall] + above[0 : 2 * tall]
    for far in far_refs:
        sums = sums + far[...].astype(F32)
    measured = []
    for v in range(tall // SUB):
        tile = jnp.zeros((SUB, LANES), F32)
        for at in range(min(SUB, outer - v * SUB)):
            p = v * SUB + at
            tile = jnp.where(sub == at, meas[:, p * LANES : (p + 1) * LANES], tile)
        measured.append(tile)
    measured = jnp.concatenate(measured, axis=0)
    rest_row[...] = (measured - sums[0:tall]) / jnp.maximum(sums[tall:], 1.0)

    def halo(q):
        at = 2 * tall + q % half * SUB
        high, low = above[at : at + SUB], below[at : at + SUB]
        if q // half == 1:
            high, low = pltpu.roll(high, SUB - 3, 0), pltpu.roll(low, 3, 0)
        return jnp.where(sub < 3, high, jnp.where(sub < 6, low, 0.0))

    side = 2 * tall + half * SUB
    side = jnp.where(sub < 3, above[side : side + SUB], below[side : side + SUB])
    shear_cols = [shear_f[g * SUB : (g + 1) * SUB] for g in range(groups)]
    step_cols = [step_f[g * SUB : (g + 1) * SUB] for g in range(groups)]
    inside = rows_of((SUB, 1)) < 6
    shear_cols.append(jnp.where(inside, 2.0 * side[:, 0:1] + side[:, 1:2], 0.0))
    step_cols.append(jnp.where(inside, side[:, 2:3] + side[:, 3:4] + side[:, 4:5], 0.0))
    index, delay, steps = [], [], []
    for g in range(groups + 1):
        s = jnp.broadcast_to(shear_cols[g].astype(I32), (SUB, LANES))
        rest = s & (LANES - 1)
        index.append((lane + rest) & (LANES - 1))
        delay.append((s >> 7) + jnp.where(lane + rest >= LANES, 1, 0))
        steps.append(jnp.broadcast_to(step_cols[g], (SUB, LANES)))
    tiles = []
    turned = [[] for _ in range(groups + 1)]
    for p in range(outer + 1):
        if p < outer:
            residual = jnp.broadcast_to(rest_row[p : p + 1, :], (SUB, LANES))
        else:
            residual = jnp.zeros((SUB, LANES), F32)
        lost = residual - residual.astype(BF16).astype(F32)
        tiles.append(jnp.where(sub < 7, residual, lost))
        for g in range(groups + 1):
            turned[g].append(turn(residual, index[g]) if p < outer else residual)
        q = p - (reach - 1)
        if q < 0 or q >= inner:
            continue
        here = slice(q * LANES, (q + 1) * LANES)
        open_q = jnp.broadcast_to(ap_ref[:, here].astype(F32), (SUB, LANES))
        pieces = []
        for g in range(groups + 1):
            pulled = choose(delay[g], turned[g][q : q + reach])
            base = raw[g * SUB : (g + 1) * SUB, here] if g < groups else halo(q)
            pieces.append(base + pulled * open_q * steps[g])
        out_ref[:, (q + 1) * LANES : (q + 2) * LANES] = jnp.concatenate(pieces, axis=0).astype(
            BF16
        )
        tiles[q] = jnp.where(sub < 6, pieces[-1], tiles[q])
    msg_ref[...] = jnp.concatenate(tiles, axis=0).astype(BF16)


def spread(rows, ch, which):
    return (which(rows_of((rows, ch))) == lanes_of((rows, ch))).astype(F32).astype(BF16)


def picked(row_ref, rows, which):
    ch = row_ref.shape[1]
    pick = which(rows_of((rows, ch))) == lanes_of((rows, ch))
    row = jnp.broadcast_to(row_ref[...], (rows, ch))
    return jnp.sum(jnp.where(pick, row, 0.0), axis=1, keepdims=True)


def with_bias(matrix, bias, start):
    lane = lanes_of(matrix.shape)
    for i, part in enumerate(split3(0.5 * bias)):
        matrix = jnp.where(lane == start + i, part, matrix)
    return matrix


def gate_kernel(_, line_ref, same_ref):
    pass


def weights_kernel(
    _, sw_in, sb_in, cw_in, cb_in, ow_in, main_ref, halo_ref, first_ref, second_ref, out_w_ref, *rest
):
    local, sems = rest[:5], rest[5]
    for copy in fetch((sw_in, sb_in, cw_in, cb_in, ow_in), local, sems):
        copy.wait()
    sw_ref, sb_ref, cw_ref, cb_ref, ow_ref = local
    ch, taps2 = sw_ref.shape
    taps = cw_ref.shape[0]
    place = lax.axis_index("band")
    has_low = jnp.where(place > 0, 1, 0)
    has_high = jnp.where(place < lax.axis_size("band") - 1, 1, 0)
    width = main_ref.shape[1]
    slots = 16
    line = lax.axis_index("row") * lax.axis_size("col") + lax.axis_index("col")
    lines = lax.axis_size("row") * lax.axis_size("col")
    group = lanes_of((taps2, width)) // slots
    offset = jnp.where(line % 2 == 1, group // 3, 2 - group // 3)
    present = (line + offset >= 1) & (line + offset <= lines)
    fan = (rows_of((taps2, width)) == 3 * offset + group % 3) & present
    fan = fan.astype(F32).astype(BF16)
    flat = jnp.dot(sw_ref[...], fan, preferred_element_type=F32).astype(BF16)
    for ref, slot_of in (
        (main_ref, lambda b: b),
        (halo_ref, lambda b: jnp.where(b < 3, 11 + b, jnp.where(b < 9, b - 3, b - 1))),
    ):
        rows = ref.shape[0]
        which = lambda r: r % ch
        full = jnp.dot(spread(rows, ch, which), flat, preferred_element_type=F32)
        lane = lanes_of((rows, width))
        band = rows_of((rows, width)) // ch
        keep = (lane % slots == slot_of(band)) & (lane < taps2 * slots)
        matrix = with_bias(
            jnp.where(keep, 0.5 * full, 0.0), picked(sb_ref, rows, which), taps2 * slots
        )
        if ref is halo_ref:
            valid = jnp.where(band < 3, has_low, jnp.where(band >= 9, has_high, 1))
            matrix = jnp.where(valid > 0, matrix, 0.0)
        ref[...] = matrix.astype(BF16)

    per = SUB
    rows = per * ch
    width = first_ref.shape[1]
    used = (per + taps - 1) * ch
    which = lambda r: r // per
    fan = (lanes_of((ch, width)) % ch == rows_of((ch, width))).astype(F32).astype(BF16)
    picks = spread(rows, ch, which)
    lane = lanes_of((rows, width))
    ahead = jnp.where(lane < used, lane // ch - rows_of((rows, width)) % per, -LANES)
    matrix = jnp.zeros((rows, width), F32)
    for d in range(taps):
        flat = jnp.dot(cw_ref[d], fan, preferred_element_type=F32).astype(BF16)
        full = 0.5 * jnp.dot(picks, flat, preferred_element_type=F32)
        matrix = jnp.where(ahead == d, full, matrix)
    bias = picked(cb_ref, rows, which)
    first_ref[...] = with_bias(matrix, bias, used).astype(BF16)
    short = second_ref.shape[1]
    start = short - 16
    matrix = jnp.where(lanes_of((rows, short)) < start, matrix[:, 0:short], 0.0)
    second_ref[...] = with_bias(matrix, bias, start).astype(BF16)
    out_w_ref[...] = jnp.broadcast_to(picked(ow_ref, rows, which), out_w_ref.shape)


def denoise_kernel(
    tile,
    reach,
    ow_ref,
    mid_ref,
    shear_ref,
    step_ref,
    raw0_ref,
    msg0_ref,
    raw1_ref,
    msg1_ref,
    main_ref,
    halo_ref,
    first_ref,
    second_ref,
    out_ref,
    act,
    near0,
    near1,
    words,
):
    bands, cols = out_ref.shape
    slots = 16
    ch = main_ref.shape[0] // slots
    tiles = cols // tile
    inner = cols // LANES
    wide = tile + 2 * LANES
    groups = -(-bands // SUB)
    ones = jnp.where(rows_of((slots, tile)) < 3, 1.0, 0.0).astype(BF16)
    blank = jnp.zeros((2 * slots, LANES), BF16)
    for near in (near0, near1):
        near[:, 0:LANES] = blank
        near[:, cols + LANES :] = blank
    shear_f = column(shear_ref[...].astype(F32), groups * SUB)
    step_f = column(step_ref[...], groups * SUB)
    lane = lanes_of()
    index, delay, steps = [], [], []
    for g in range(groups):
        s = jnp.broadcast_to(shear_f[g * SUB : (g + 1) * SUB].astype(I32), (SUB, LANES))
        rest = s & (LANES - 1)
        index.append((lane + rest) & (LANES - 1))
        delay.append((s >> 7) + jnp.where(lane + rest >= LANES, 1, 0))
        steps.append(jnp.broadcast_to(step_f[g * SUB : (g + 1) * SUB], (SUB, LANES)))
    rows_in = msg0_ref.shape[0]
    for n, msg_ref in enumerate((msg0_ref, msg1_ref)):
        words[n * rows_in : (n + 1) * rows_in, :] = msg_ref[...].astype(F32)
    step = tile // LANES

    def neighbours(t):
        for n, (raw_ref, near) in enumerate(((raw0_ref, near0), (raw1_ref, near1))):
            base = n * rows_in
            turned = [[] for _ in range(groups)]
            edges = []
            for p in range(step + reach - 1):
                at = pl.multiple_of(base + (t * step + p) * SUB, SUB)
                word = words[pl.ds(at, SUB), :]
                edges.append(word)
                residual = jnp.broadcast_to(word[6:7] + word[7:8], (SUB, LANES))
                for g in range(groups):
                    turned[g].append(turn(residual, index[g]))
            start = pl.multiple_of(t * tile, LANES)
            raw = raw_ref[:, pl.ds(start, tile)].astype(F32)
            made = []
            for q in range(step):
                here = raw[:, q * LANES : (q + 1) * LANES]
                open_q = jnp.broadcast_to(here[bands : bands + 1], (SUB, LANES))
                pieces = [
                    here[g * SUB : (g + 1) * SUB]
                    + choose(delay[g], turned[g][q : q + reach]) * open_q * steps[g]
                    for g in range(groups)
                ]
                made.append(jnp.concatenate(pieces + [edges[q]], axis=0).astype(BF16))
            start = pl.multiple_of(t * tile + LANES, LANES)
            near[:, pl.ds(start, tile)] = jnp.concatenate(made, axis=1)

    def silu_twice(half):
        return half + half * jnp.tanh(half)

    def patches(t):
        parts = []
        for ref in (near0, mid_ref, near1):
            row = ref[:, pl.ds(pl.multiple_of(t * tile, LANES), wide)]
            back = pltpu.roll(row, 1, 1)[:, LANES : LANES + tile]
            ahead = pltpu.roll(row, wide - 1, 1)[:, LANES : LANES + tile]
            parts += [back, row[:, LANES : LANES + tile], ahead]
        return [
            jnp.concatenate([p[at : at + slots] for p in parts] + [ones], axis=0)
            for at in (0, slots)
        ]

    def activate(part, half):
        value = silu_twice(half).astype(BF16)
        if part == 0:
            act[3 * ch : 19 * ch, :] = value
        else:
            act[0 : 3 * ch, :] = value[0 : 3 * ch]
            act[19 * ch : 28 * ch, :] = value[3 * ch :]

    def spatial(part, inputs):
        w_ref = halo_ref if part else main_ref
        return jnp.dot(w_ref[...], inputs[part], preferred_element_type=F32)

    def spectral(i):
        w_ref = second_ref if i == groups - 1 else first_ref
        first = i * SUB * ch
        x = jnp.concatenate([act[first : first + w_ref.shape[1] - slots, :], ones], axis=0)
        return jnp.dot(w_ref[...], x, preferred_element_type=F32)

    def project(half):
        total = None
        for k in range(ch):
            weight = ow_ref[k * SUB : (k + 1) * SUB, :]
            weight = jnp.concatenate([weight] * (tile // LANES), axis=1)
            term = weight * silu_twice(half[k * SUB : (k + 1) * SUB])
            total = term if total is None else total + term
        return total

    def finish(t, sums):
        update = jnp.concatenate(sums, axis=0)[0:bands]
        center = mid_ref[:, pl.ds(pl.multiple_of(t * tile + LANES, LANES), tile)]
        result = center.astype(F32)[0:bands] + update
        out_ref[:, pl.ds(pl.multiple_of(t * tile, LANES), tile)] = result.astype(BF16)

    ahead_by = 3

    def prepare(t, carry):
        neighbours(t)
        return carry

    lax.fori_loop(0, min(ahead_by, tiles), prepare, 0)
    start_inputs = patches(0)
    for part in range(2):
        activate(part, spatial(part, start_inputs))

    def body(t, carry):
        blocks = [spectral(0)]
        inputs = patches(t + 1)
        sums = []
        for i in range(1, groups):
            blocks.append(spectral(i))
            sums.append(project(blocks[i - 1]))
        half0 = spatial(0, inputs)
        sums.append(project(blocks[groups - 1]))
        half1 = spatial(1, inputs)
        finish(t, sums)
        activate(0, half0)
        neighbours(jnp.minimum(t + ahead_by, tiles - 1))
        activate(1, half1)
        return carry

    lax.fori_loop(0, tiles - 1, body, 0)
    finish(tiles - 1, [project(spectral(i)) for i in range(groups)])


def vmem(n):
    return [pl.BlockSpec(memory_space=pltpu.VMEM)] * n


def hbm(n):
    return [pl.BlockSpec(memory_space=pltpu.HBM)] * n


def in_hbm(arrays):
    return [pltpu.with_memory_space_constraint(x, pltpu.HBM) for x in arrays]


ANY = pl.BlockSpec(memory_space=pl.ANY)


def on_device(
    spectral_cube,
    aperture,
    measurement,
    shears,
    step_sizes,
    spatial_weight,
    spatial_bias,
    spectral_weight,
    spectral_bias,
    out_weight,
):
    bands, row_count, cols = spectral_cube.shape
    width = measurement.shape[1]
    reach = (width - cols) // LANES + 2
    outer = -(-width // LANES)
    groups = -(-bands // SUB)
    slots = (groups + 1) * SUB
    taps, ch = spectral_weight.shape[:2]
    taps2 = spatial_weight.shape[1]
    count = lax.axis_size("band")
    cube = spectral_cube.reshape(bands, cols)
    shear_row = shears.reshape(1, bands)
    step_row = step_sizes.reshape(1, bands)
    params = pltpu.CompilerParams(vmem_limit_bytes=48 * 2**20)

    tall = -(-outer // SUB) * SUB
    side = (cols // LANES // 2 + 2) * SUB
    inputs = (cube, aperture, measurement, shear_row, step_row)
    part, up, dn, *kept = pl.pallas_call(
        functools.partial(project_kernel, reach),
        out_shape=(
            jax.ShapeDtypeStruct((2 * tall, LANES), BF16),
            jax.ShapeDtypeStruct((2 * tall + side, LANES), BF16),
            jax.ShapeDtypeStruct((2 * tall + side, LANES), BF16),
        )
        + (jax.ShapeDtypeStruct((groups * SUB, cols), BF16),)
        + tuple(jax.ShapeDtypeStruct(x.shape, x.dtype) for x in inputs[1:]),
        in_specs=hbm(5),
        out_specs=tuple(vmem(8)),
        scratch_shapes=[
            pltpu.VMEM((bands, cols), BF16),
            pltpu.VMEM((groups * SUB, cols), F32),
            pltpu.SemaphoreType.DMA((5,)),
        ],
        compiler_params=params,
        name="project",
    )(*in_hbm(inputs))

    def around(x, shift):
        return lax.ppermute(x, "band", [(i, (i + shift) % count) for i in range(count)])

    below = around(up, 1)
    above = around(dn, -1)
    far = [around(part, s) for s in range(2, count - 1)]

    line = pl.pallas_call(
        gate_kernel,
        out_shape=jax.ShapeDtypeStruct(kept[0].shape, BF16),
        in_specs=[ANY, ANY],
        out_specs=ANY,
        input_output_aliases={1: 0},
        compiler_params=pltpu.CompilerParams(vmem_limit_bytes=2**20),
        name="gate",
    )(part, kept[0])
    kept[0] = line

    lines = lax.axis_size(("row", "col"))
    pairs = [(i, i ^ 1) for i in range(lines)]
    others = [(i, (i - 1 + i % 2 * 2) % lines) for i in range(lines)]
    raw0 = lax.ppermute(line, ("row", "col"), pairs)
    raw1 = lax.ppermute(line, ("row", "col"), others)

    words = (outer + 1) * SUB
    updated, message = pl.pallas_call(
        functools.partial(update_kernel, reach, len(far)),
        out_shape=(
            jax.ShapeDtypeStruct((slots, cols + 2 * LANES), BF16),
            jax.ShapeDtypeStruct((words, LANES), BF16),
        ),
        in_specs=vmem(8 + len(far)),
        out_specs=tuple(vmem(2)),
        scratch_shapes=[
            pltpu.VMEM((groups * SUB, cols), F32),
            pltpu.VMEM((1, outer * LANES), F32),
            pltpu.VMEM((tall, LANES), F32),
        ],
        compiler_params=params,
        cost_estimate=pl.CostEstimate(
            flops=10**10, bytes_accessed=4 * 10**7, transcendentals=0
        ),
        name="update",
    )(*kept, part, below, above, *far)

    message0 = lax.ppermute(message, ("row", "col"), pairs)
    message1 = lax.ppermute(message, ("row", "col"), others)

    small = (
        spatial_weight,
        spatial_bias.reshape(1, ch),
        spectral_weight,
        spectral_bias.reshape(1, ch),
        out_weight.reshape(1, ch),
    )
    reached = (SUB + taps - 1) * ch
    last = (bands - (groups - 1) * SUB + taps - 1) * ch
    main_w, halo_w, first_w, second_w, out_w = pl.pallas_call(
        weights_kernel,
        out_shape=(
            jax.ShapeDtypeStruct((16 * ch, taps2 * 16 + 16), BF16),
            jax.ShapeDtypeStruct((12 * ch, taps2 * 16 + 16), BF16),
            jax.ShapeDtypeStruct((SUB * ch, reached + 16), BF16),
            jax.ShapeDtypeStruct((SUB * ch, last + 16), BF16),
            jax.ShapeDtypeStruct((SUB * ch, LANES), F32),
        ),
        in_specs=[ANY] + hbm(5),
        out_specs=tuple(vmem(5)),
        scratch_shapes=[pltpu.VMEM(x.shape, x.dtype) for x in small]
        + [pltpu.SemaphoreType.DMA((5,))],
        compiler_params=params,
        name="weights",
    )(message, *in_hbm(small))

    tile = 512
    result = pl.pallas_call(
        functools.partial(denoise_kernel, tile, reach),
        out_shape=jax.ShapeDtypeStruct((bands, cols), BF16),
        in_specs=vmem(12),
        out_specs=vmem(1)[0],
        scratch_shapes=[
            pltpu.VMEM((28 * ch, tile), BF16),
            pltpu.VMEM((slots, cols + 2 * LANES), BF16),
            pltpu.VMEM((slots, cols + 2 * LANES), BF16),
            pltpu.VMEM((2 * words, LANES), F32),
        ],
        compiler_params=params,
        name="denoise",
    )(
        out_w,
        updated,
        kept[3],
        kept[4],
        raw0,
        message0,
        raw1,
        message1,
        main_w,
        halo_w,
        first_w,
        second_w,
    )
    return result.reshape(bands, 1, cols)


def solution(mesh):
    in_specs = (
        P("band", ("row", "col"), None),
        P(("row", "col"), None),
        P(("row", "col"), None),
        P("band"),
        P("band"),
        P(),
        P(),
        P(),
        P(),
        P(),
    )
    out_specs = P("band", ("row", "col"), None)
    return jax.shard_map(
        on_device, mesh=mesh, in_specs=in_specs, out_specs=out_specs, check_vma=False
    )
```

```python
import functools

import jax
import jax.numpy as jnp
from jax import lax
from jax.experimental import pallas as pl
from jax.experimental.pallas import tpu as pltpu
from jax.sharding import PartitionSpec as P

LANES = 128
SUB = 8
F32 = jnp.float32
BF16 = jnp.bfloat16
I32 = jnp.int32
COUNTER = 512.0
EXTRA = 16


def lanes_of(shape=(SUB, LANES)):
    return lax.broadcasted_iota(I32, shape, 1)


def rows_of(shape=(SUB, LANES)):
    return lax.broadcasted_iota(I32, shape, 0)


def column(row, rows):
    n = row.shape[1]
    eye = rows_of((rows, n)) == lanes_of((rows, n))
    return jnp.sum(jnp.where(eye, jnp.broadcast_to(row, (rows, n)), 0.0), axis=1, keepdims=True)


def turn(chunk, index):
    return jnp.take_along_axis(chunk, index, axis=1, mode="promise_in_bounds")


def choose(delay, options):
    result = options[-1]
    for d in range(len(options) - 2, -1, -1):
        result = jnp.where(delay == d, options[d], result)
    return result


def split3(x):
    hi = x.astype(BF16).astype(F32)
    mid = (x - hi).astype(BF16).astype(F32)
    return hi, mid, x - hi - mid


def fetch(sources, targets, sems):
    copies = [
        pltpu.make_async_copy(src, dst, sems.at[i]) for i, (src, dst) in enumerate(zip(sources, targets))
    ]
    for copy in copies:
        copy.start()
    return copies


def project_kernel(
    reach, cube_in, ap_in, meas_in, shear_in, step_in, part_ref, up_ref, dn_ref, *rest_refs
):
    line_ref, *kept = rest_refs[:5]
    cube_ref, raw, sems = rest_refs[5:]
    ap_ref, meas_ref, shear_ref, step_ref = kept
    copies = fetch((cube_in, ap_in, meas_in, shear_in, step_in), (cube_ref, *kept), sems)
    for copy in copies:
        copy.wait()
    bands, cols = cube_ref.shape
    groups = -(-bands // SUB)
    inner = cols // LANES
    tall = part_ref.shape[0] // 2
    outer = -(-meas_ref.shape[1] // LANES)
    raw[bands // SUB * SUB :, :] = jnp.zeros((raw.shape[0] - bands // SUB * SUB, cols), F32)
    raw[0:bands, :] = cube_ref[...].astype(F32)
    shear_f = column(shear_ref[...].astype(F32), groups * SUB)
    step_f = column(step_ref[...], groups * SUB)
    shear_i = shear_f.astype(I32)
    lane, sub = lanes_of(), rows_of()
    index, delay = [], []
    for g in range(groups):
        s = jnp.broadcast_to(shear_i[g * SUB : (g + 1) * SUB], (SUB, LANES))
        rest = s & (LANES - 1)
        index.append((lane - rest) & (LANES - 1))
        delay.append((s >> 7) + jnp.where(lane < rest, 1, 0))
    zero = jnp.zeros((SUB, LANES), F32)
    turned = [[zero] * (reach - 1) for _ in range(groups)]
    sums = [zero] * (tall // SUB)
    firsts, lasts = [], []
    for p in range(outer):
        total = zero
        if p < inner:
            open_p = jnp.broadcast_to(
                ap_ref[:, p * LANES : (p + 1) * LANES].astype(F32), (SUB, LANES)
            )
            layers = [
                raw[g * SUB : (g + 1) * SUB, p * LANES : (p + 1) * LANES] for g in range(groups)
            ]
            firsts.append(layers[0])
            lasts.append(layers[-1])
            tagged = jnp.where(sub == bands % SUB, open_p, layers[-1])
            line_ref[:, p * LANES : (p + 1) * LANES] = jnp.concatenate(
                layers[:-1] + [tagged], axis=0
            ).astype(BF16)
        for g in range(groups):
            if p < inner:
                here = (layers[g] + COUNTER) * open_p
                if (g + 1) * SUB > bands:
                    here = jnp.where(sub < bands - g * SUB, here, 0.0)
                here = turn(here, index[g])
            else:
                here = zero
            options = [here] + turned[g]
            turned[g] = options[:-1]
            total = total + choose(delay[g], options)
        v, at = divmod(p, SUB)
        sums[v] = jnp.where(sub == at, jnp.sum(total, axis=0, keepdims=True), sums[v])
    counts = [jnp.floor(x * (1.0 / COUNTER) + 0.5) for x in sums]
    sums = [x - COUNTER * n for x, n in zip(sums, counts)]
    sides = []
    for g in (0, groups - 1):
        s = shear_i[g * SUB : (g + 1) * SUB]
        parts = [(s >> 1).astype(F32), (s & 1).astype(F32)]
        parts += list(split3(step_f[g * SUB : (g + 1) * SUB]))
        side = zero
        for i, part in enumerate(parts):
            side = jnp.where(lane == i, part, side)
        sides.append(side)
    half = inner // 2
    dn = [
        jnp.where(sub < 3, firsts[q], pltpu.roll(firsts[q + half], 3, 0)) for q in range(half)
    ] + [sides[0], zero]
    up = [
        jnp.where(sub < 3, pltpu.roll(lasts[q + half], SUB - 3, 0), lasts[q]) for q in range(half)
    ] + [sides[1], zero]
    part_ref[...] = jnp.concatenate(sums + counts, axis=0).astype(BF16)
    up_ref[...] = jnp.concatenate(sums + counts + up, axis=0).astype(BF16)
    dn_ref[...] = jnp.concatenate(sums + counts + dn, axis=0).astype(BF16)


def update_kernel(
    reach,
    fars,
    line_ref,
    ap_ref,
    meas_ref,
    shear_ref,
    step_ref,
    own_ref,
    below_ref,
    above_ref,
    _,
    *rest_refs,
):
    far_refs = rest_refs[:fars]
    out_ref, msg_ref, long_ref, raw, meas, rest_row = rest_refs[fars:]
    groups = line_ref.shape[0] // SUB
    cols = line_ref.shape[1]
    inner = cols // LANES
    half = inner // 2
    tall = own_ref.shape[0] // 2
    outer = -(-meas_ref.shape[1] // LANES)
    raw[...] = line_ref[...].astype(F32)
    meas[:, (outer - 1) * LANES :] = jnp.zeros((1, LANES), F32)
    meas[:, 0 : meas_ref.shape[1]] = meas_ref[...]
    shear_f = column(shear_ref[...].astype(F32), groups * SUB)
    step_f = column(step_ref[...], groups * SUB)
    lane, sub = lanes_of(), rows_of()
    below = below_ref[...].astype(F32)
    above = above_ref[...].astype(F32)
    sums = own_ref[...].astype(F32) + below[0 : 2 * tall] + above[0 : 2 * tall]
    for far in far_refs:
        sums = sums + far[...].astype(F32)
    measured = []
    for v in range(tall // SUB):
        tile = jnp.zeros((SUB, LANES), F32)
        for at in range(min(SUB, outer - v * SUB)):
            p = v * SUB + at
            tile = jnp.where(sub == at, meas[:, p * LANES : (p + 1) * LANES], tile)
        measured.append(tile)
    measured = jnp.concatenate(measured, axis=0)
    rest_row[...] = (measured - sums[0:tall]) / jnp.maximum(sums[tall:], 1.0)

    def halo(q):
        at = 2 * tall + q % half * SUB
        high, low = above[at : at + SUB], below[at : at + SUB]
        if q // half == 1:
            high, low = pltpu.roll(high, SUB - 3, 0), pltpu.roll(low, 3, 0)
        return jnp.where(sub < 3, high, jnp.where(sub < 6, low, 0.0))

    side = 2 * tall + half * SUB
    side = jnp.where(sub < 3, above[side : side + SUB], below[side : side + SUB])
    shear_cols = [shear_f[g * SUB : (g + 1) * SUB] for g in range(groups)]
    step_cols = [step_f[g * SUB : (g + 1) * SUB] for g in range(groups)]
    inside = rows_of((SUB, 1)) < 6
    shear_cols.append(jnp.where(inside, 2.0 * side[:, 0:1] + side[:, 1:2], 0.0))
    step_cols.append(jnp.where(inside, side[:, 2:3] + side[:, 3:4] + side[:, 4:5], 0.0))
    index, delay, steps = [], [], []
    for g in range(groups + 1):
        s = jnp.broadcast_to(shear_cols[g].astype(I32), (SUB, LANES))
        rest = s & (LANES - 1)
        index.append((lane + rest) & (LANES - 1))
        delay.append((s >> 7) + jnp.where(lane + rest >= LANES, 1, 0))
        steps.append(jnp.broadcast_to(step_cols[g], (SUB, LANES)))
    tiles = []
    turned = [[] for _ in range(groups + 1)]
    for p in range(outer + 1):
        if p < outer:
            residual = jnp.broadcast_to(rest_row[p : p + 1, :], (SUB, LANES))
        else:
            residual = jnp.zeros((SUB, LANES), F32)
        lost = residual - residual.astype(BF16).astype(F32)
        tiles.append(jnp.where(sub < 7, residual, lost))
        for g in range(groups + 1):
            turned[g].append(turn(residual, index[g]) if p < outer else residual)
        q = p - (reach - 1)
        if q < 0 or q >= inner:
            continue
        here = slice(q * LANES, (q + 1) * LANES)
        open_q = jnp.broadcast_to(ap_ref[:, here].astype(F32), (SUB, LANES))
        pieces = []
        for g in range(groups + 1):
            pulled = choose(delay[g], turned[g][q : q + reach])
            base = raw[g * SUB : (g + 1) * SUB, here] if g < groups else halo(q)
            pieces.append(base + pulled * open_q * steps[g])
        out_ref[:, here] = jnp.concatenate(pieces, axis=0).astype(BF16)
        tiles[q] = jnp.where(sub < 6, pieces[-1], tiles[q])
    words = jnp.concatenate(tiles, axis=0).astype(BF16)
    msg_ref[...] = words
    long_ref[0 : words.shape[0], :] = words
    rest = (long_ref.shape[0] - words.shape[0], LANES)
    long_ref[words.shape[0] :, :] = jnp.zeros(rest, BF16)


def spread(rows, ch, which):
    return (which(rows_of((rows, ch))) == lanes_of((rows, ch))).astype(F32).astype(BF16)


def picked(row_ref, rows, which):
    ch = row_ref.shape[1]
    pick = which(rows_of((rows, ch))) == lanes_of((rows, ch))
    row = jnp.broadcast_to(row_ref[...], (rows, ch))
    return jnp.sum(jnp.where(pick, row, 0.0), axis=1, keepdims=True)


def with_bias(matrix, bias, start):
    lane = lanes_of(matrix.shape)
    for i, part in enumerate(split3(0.5 * bias)):
        matrix = jnp.where(lane == start + i, part, matrix)
    return matrix


def gate_kernel(_, line_ref, same_ref):
    pass


def weights_kernel(
    _, sw_in, sb_in, cw_in, cb_in, ow_in, main_ref, halo_ref, first_ref, second_ref, out_w_ref, *rest
):
    local, sems = rest[:5], rest[5]
    for copy in fetch((sw_in, sb_in, cw_in, cb_in, ow_in), local, sems):
        copy.wait()
    sw_ref, sb_ref, cw_ref, cb_ref, ow_ref = local
    ch, taps2 = sw_ref.shape
    taps = cw_ref.shape[0]
    place = lax.axis_index("band")
    has_low = jnp.where(place > 0, 1, 0)
    has_high = jnp.where(place < lax.axis_size("band") - 1, 1, 0)
    width = main_ref.shape[1]
    slots = 16
    line = lax.axis_index("row") * lax.axis_size("col") + lax.axis_index("col")
    lines = lax.axis_size("row") * lax.axis_size("col")
    group = lanes_of((taps2, width)) // slots
    offset = jnp.where(line % 2 == 1, group // 3, 2 - group // 3)
    present = (line + offset >= 1) & (line + offset <= lines)
    fan = (rows_of((taps2, width)) == 3 * offset + group % 3) & present
    fan = fan.astype(F32).astype(BF16)
    flat = jnp.dot(sw_ref[...], fan, preferred_element_type=F32).astype(BF16)
    for ref, slot_of in (
        (main_ref, lambda b: b),
        (halo_ref, lambda b: jnp.where(b < 3, 11 + b, jnp.where(b < 9, b - 3, b - 1))),
    ):
        rows = ref.shape[0]
        which = lambda r: r % ch
        full = jnp.dot(spread(rows, ch, which), flat, preferred_element_type=F32)
        lane = lanes_of((rows, width))
        band = rows_of((rows, width)) // ch
        keep = (lane % slots == slot_of(band)) & (lane < taps2 * slots)
        matrix = with_bias(
            jnp.where(keep, 0.5 * full, 0.0), picked(sb_ref, rows, which), taps2 * slots
        )
        if ref is halo_ref:
            valid = jnp.where(band < 3, has_low, jnp.where(band >= 9, has_high, 1))
            matrix = jnp.where(valid > 0, matrix, 0.0)
        ref[...] = matrix.astype(BF16)

    per = SUB
    rows = per * ch
    width = first_ref.shape[1]
    used = (per + taps - 1) * ch
    which = lambda r: r // per
    fan = (lanes_of((ch, width)) % ch == rows_of((ch, width))).astype(F32).astype(BF16)
    picks = spread(rows, ch, which)
    lane = lanes_of((rows, width))
    ahead = jnp.where(lane < used, lane // ch - rows_of((rows, width)) % per, -LANES)
    matrix = jnp.zeros((rows, width), F32)
    for d in range(taps):
        flat = jnp.dot(cw_ref[d], fan, preferred_element_type=F32).astype(BF16)
        full = 0.5 * jnp.dot(picks, flat, preferred_element_type=F32)
        matrix = jnp.where(ahead == d, full, matrix)
    bias = picked(cb_ref, rows, which)
    first_ref[...] = with_bias(matrix, bias, used).astype(BF16)
    short = second_ref.shape[1]
    start = short - 16
    matrix = jnp.where(lanes_of((rows, short)) < start, matrix[:, 0:short], 0.0)
    second_ref[...] = with_bias(matrix, bias, start).astype(BF16)
    out_w_ref[...] = jnp.broadcast_to(picked(ow_ref, rows, which), out_w_ref.shape)


def neighbour_chunks(reach, bands, shear_ref, step_ref, raw_ref, msg_ref, near, words):
    inner = raw_ref.shape[1] // LANES
    groups = -(-bands // SUB)
    zero = jnp.zeros((SUB, LANES), F32)
    shear_f = column(shear_ref[...].astype(F32), groups * SUB)
    step_f = column(step_ref[...], groups * SUB)
    lane = lanes_of()
    index, delay, steps = [], [], []
    for g in range(groups):
        s = jnp.broadcast_to(shear_f[g * SUB : (g + 1) * SUB].astype(I32), (SUB, LANES))
        rest = s & (LANES - 1)
        index.append((lane + rest) & (LANES - 1))
        delay.append((s >> 7) + jnp.where(lane + rest >= LANES, 1, 0))
        steps.append(jnp.broadcast_to(step_f[g * SUB : (g + 1) * SUB], (SUB, LANES)))
    chunks = inner + reach - 1
    words[...] = msg_ref[0 : words.shape[0], :].astype(F32)
    turned = [[] for _ in range(groups)]

    def make(q):
        while len(turned[0]) < q + reach:
            p = len(turned[0])
            if p >= chunks:
                residual = zero
            else:
                at = p * SUB + 6
                residual = words[at : at + 1, :] + words[at + 1 : at + 2, :]
                residual = jnp.broadcast_to(residual, (SUB, LANES))
            for g in range(groups):
                turned[g].append(turn(residual, index[g]))
        raw = raw_ref[:, q * LANES : (q + 1) * LANES].astype(F32)
        open_q = jnp.broadcast_to(raw[bands : bands + 1], (SUB, LANES))
        pieces = [
            raw[g * SUB : (g + 1) * SUB]
            + choose(delay[g], turned[g][q : q + reach]) * open_q * steps[g]
            for g in range(groups)
        ]
        pieces.append(words[q * SUB : (q + 1) * SUB, :])
        near[:, q * LANES : (q + 1) * LANES] = jnp.concatenate(pieces, axis=0).astype(BF16)

    return make


def neighbour_kernel(reach, shear_ref, step_ref, raw_ref, msg_ref, _, near, words):
    bands = shear_ref.shape[1]
    make = neighbour_chunks(reach, bands, shear_ref, step_ref, raw_ref, msg_ref, near, words)
    for q in range(near.shape[1] // LANES):
        make(q)


def denoise_kernel(
    tile,
    reach,
    ow_ref,
    mid_ref,
    shear_ref,
    step_ref,
    near0,
    raw_ref,
    msg_ref,
    main_ref,
    halo_ref,
    first_ref,
    second_ref,
    out_ref,
    act,
    near1,
    words,
):
    bands, cols = out_ref.shape
    slots = 16
    ch = main_ref.shape[0] // slots
    tiles = cols // tile
    inner = cols // LANES
    wide = tile + 2 * LANES
    groups = -(-bands // SUB)
    ones = jnp.where(rows_of((slots, tile)) < 3, 1.0, 0.0).astype(BF16)
    blank = jnp.zeros((2 * slots, LANES), BF16)
    neighbours = neighbour_chunks(
        reach, bands, shear_ref, step_ref, raw_ref, msg_ref, near1, words
    )

    def silu_twice(half):
        return half + half * jnp.tanh(half)

    inputs, halves, blocks, sums = {}, {}, {}, {}
    made = 0

    def update_up_to(t):
        nonlocal made
        while made < min((t + 1) * tile // LANES + 1, inner):
            neighbours(made)
            made += 1

    def patches(t):
        start = t * tile
        end = start + tile
        parts = []
        for ref in (near0, mid_ref, near1):
            left = ref[:, start - LANES : start] if t else blank
            here = ref[:, start:end]
            right = ref[:, end : end + LANES] if t < tiles - 1 else blank
            row = jnp.concatenate([left, here, right], axis=1)
            back = pltpu.roll(row, 1, 1)[:, LANES : LANES + tile]
            ahead = pltpu.roll(row, wide - 1, 1)[:, LANES : LANES + tile]
            parts += [back, here, ahead]
        for part in range(2):
            inputs[t, part] = jnp.concatenate(
                [p[part * slots : (part + 1) * slots] for p in parts] + [ones], axis=0
            )

    def spatial(t, part):
        w_ref = halo_ref if part else main_ref
        halves[t, part] = jnp.dot(
            w_ref[...], inputs.pop((t, part)), preferred_element_type=F32
        )

    def activate(t, part):
        buf = act.at[t % act.shape[0]]
        value = silu_twice(halves.pop((t, part))).astype(BF16)
        if part == 0:
            buf[3 * ch : 19 * ch, :] = value
        else:
            buf[0 : 3 * ch, :] = value[0 : 3 * ch]
            buf[19 * ch : 28 * ch, :] = value[3 * ch :]

    def spectral(t, i):
        buf = act.at[t % act.shape[0]]
        w_ref = second_ref if i == groups - 1 else first_ref
        first = i * SUB * ch
        x = jnp.concatenate([buf[first : first + w_ref.shape[1] - slots, :], ones], axis=0)
        blocks[t, i] = jnp.dot(w_ref[...], x, preferred_element_type=F32)

    def project(t, i):
        half = blocks.pop((t, i))
        total = None
        for k in range(ch):
            weight = ow_ref[k * SUB : (k + 1) * SUB, :]
            weight = jnp.concatenate([weight] * (tile // LANES), axis=1)
            term = weight * silu_twice(half[k * SUB : (k + 1) * SUB])
            total = term if total is None else total + term
        sums[t, i] = total
        if i == groups - 1:
            start = t * tile
            update = jnp.concatenate([sums.pop((t, n)) for n in range(groups)], axis=0)[0:bands]
            center = mid_ref[:, start : start + tile].astype(F32)[0:bands]
            out_ref[:, start : start + tile] = (center + update).astype(BF16)

    update_up_to(0)
    patches(0)
    spatial(0, 0)
    spatial(0, 1)
    update_up_to(1)
    activate(0, 0)
    patches(1)
    activate(0, 1)
    for t in range(tiles):
        if t + 1 < tiles:
            spatial(t + 1, 0)
        if t:
            project(t - 1, groups - 1)
        if t + 2 < tiles:
            update_up_to(t + 2)
        if t + 1 < tiles:
            spatial(t + 1, 1)
            activate(t + 1, 0)
        spectral(t, 0)
        if t + 1 < tiles:
            activate(t + 1, 1)
        for i in range(1, groups):
            spectral(t, i)
            project(t, i - 1)
        if t + 2 < tiles:
            patches(t + 2)
    project(tiles - 1, groups - 1)


def vmem(n):
    return [pl.BlockSpec(memory_space=pltpu.VMEM)] * n


def hbm(n):
    return [pl.BlockSpec(memory_space=pltpu.HBM)] * n


def in_hbm(arrays):
    return [pltpu.with_memory_space_constraint(x, pltpu.HBM) for x in arrays]


ANY = pl.BlockSpec(memory_space=pl.ANY)


def on_device(
    spectral_cube,
    aperture,
    measurement,
    shears,
    step_sizes,
    spatial_weight,
    spatial_bias,
    spectral_weight,
    spectral_bias,
    out_weight,
):
    bands, row_count, cols = spectral_cube.shape
    width = measurement.shape[1]
    reach = (width - cols) // LANES + 2
    outer = -(-width // LANES)
    groups = -(-bands // SUB)
    slots = (groups + 1) * SUB
    taps, ch = spectral_weight.shape[:2]
    taps2 = spatial_weight.shape[1]
    count = lax.axis_size("band")
    cube = spectral_cube.reshape(bands, cols)
    shear_row = shears.reshape(1, bands)
    step_row = step_sizes.reshape(1, bands)
    params = pltpu.CompilerParams(vmem_limit_bytes=48 * 2**20)

    tall = -(-outer // SUB) * SUB
    side = (cols // LANES // 2 + 2) * SUB
    inputs = (cube, aperture, measurement, shear_row, step_row)
    part, up, dn, *kept = pl.pallas_call(
        functools.partial(project_kernel, reach),
        out_shape=(
            jax.ShapeDtypeStruct((2 * tall, LANES), BF16),
            jax.ShapeDtypeStruct((2 * tall + side, LANES), BF16),
            jax.ShapeDtypeStruct((2 * tall + side, LANES), BF16),
        )
        + (jax.ShapeDtypeStruct((groups * SUB, cols), BF16),)
        + tuple(jax.ShapeDtypeStruct(x.shape, x.dtype) for x in inputs[1:]),
        in_specs=hbm(5),
        out_specs=tuple(vmem(8)),
        scratch_shapes=[
            pltpu.VMEM((bands, cols), BF16),
            pltpu.VMEM((groups * SUB, cols), F32),
            pltpu.SemaphoreType.DMA((5,)),
        ],
        compiler_params=params,
        name="project",
    )(*in_hbm(inputs))

    def around(x, shift):
        return lax.ppermute(x, "band", [(i, (i + shift) % count) for i in range(count)])

    below = around(up, 1)
    above = around(dn, -1)
    far = [around(part, s) for s in range(2, count - 1)]

    line = pl.pallas_call(
        gate_kernel,
        out_shape=jax.ShapeDtypeStruct(kept[0].shape, BF16),
        in_specs=[ANY, ANY],
        out_specs=ANY,
        input_output_aliases={1: 0},
        compiler_params=pltpu.CompilerParams(vmem_limit_bytes=2**20),
        name="gate",
    )(part, kept[0])
    kept[0] = line

    lines = lax.axis_size(("row", "col"))
    pairs = [(i, i ^ 1) for i in range(lines)]
    others = [(i, (i - 1 + i % 2 * 2) % lines) for i in range(lines)]
    raw0 = lax.ppermute(line, ("row", "col"), pairs)
    raw1 = lax.ppermute(line, ("row", "col"), others)

    small = (
        spatial_weight,
        spatial_bias.reshape(1, ch),
        spectral_weight,
        spectral_bias.reshape(1, ch),
        out_weight.reshape(1, ch),
    )
    reached = (SUB + taps - 1) * ch
    last = (bands - (groups - 1) * SUB + taps - 1) * ch
    main_w, halo_w, first_w, second_w, out_w = pl.pallas_call(
        weights_kernel,
        out_shape=(
            jax.ShapeDtypeStruct((16 * ch, taps2 * 16 + 16), BF16),
            jax.ShapeDtypeStruct((12 * ch, taps2 * 16 + 16), BF16),
            jax.ShapeDtypeStruct((SUB * ch, reached + 16), BF16),
            jax.ShapeDtypeStruct((SUB * ch, last + 16), BF16),
            jax.ShapeDtypeStruct((SUB * ch, LANES), F32),
        ),
        in_specs=[ANY] + hbm(5),
        out_specs=tuple(vmem(5)),
        scratch_shapes=[pltpu.VMEM(x.shape, x.dtype) for x in small]
        + [pltpu.SemaphoreType.DMA((5,))],
        compiler_params=params,
        name="weights",
    )(line, *in_hbm(small))

    words = (outer + 1) * SUB
    updated, message, longer = pl.pallas_call(
        functools.partial(update_kernel, reach, len(far)),
        out_shape=(
            jax.ShapeDtypeStruct((slots, cols), BF16),
            jax.ShapeDtypeStruct((words, LANES), BF16),
            jax.ShapeDtypeStruct((words + EXTRA, LANES), BF16),
        ),
        in_specs=vmem(8) + [ANY] + vmem(len(far)),
        out_specs=tuple(vmem(3)),
        scratch_shapes=[
            pltpu.VMEM((groups * SUB, cols), F32),
            pltpu.VMEM((1, outer * LANES), F32),
            pltpu.VMEM((tall, LANES), F32),
        ],
        compiler_params=params,
        cost_estimate=pl.CostEstimate(
            flops=10**10, bytes_accessed=4 * 10**7, transcendentals=0
        ),
        name="update",
    )(*kept, part, below, above, out_w, *far)

    message0 = lax.ppermute(message, ("row", "col"), pairs)
    message1 = lax.ppermute(longer, ("row", "col"), others)

    near0 = pl.pallas_call(
        functools.partial(neighbour_kernel, reach),
        out_shape=jax.ShapeDtypeStruct((slots, cols), BF16),
        in_specs=vmem(4) + [ANY],
        out_specs=vmem(1)[0],
        scratch_shapes=[pltpu.VMEM((words, LANES), F32)],
        compiler_params=params,
        cost_estimate=pl.CostEstimate(flops=1, bytes_accessed=1, transcendentals=0),
        name="partner",
    )(kept[3], kept[4], raw0, message0, message)

    tile = 512
    result = pl.pallas_call(
        functools.partial(denoise_kernel, tile, reach),
        out_shape=jax.ShapeDtypeStruct((bands, cols), BF16),
        in_specs=vmem(11),
        out_specs=vmem(1)[0],
        scratch_shapes=[
            pltpu.VMEM((4, 28 * ch, tile), BF16),
            pltpu.VMEM((slots, cols), BF16),
            pltpu.VMEM((words, LANES), F32),
        ],
        compiler_params=params,
        name="denoise",
    )(
        out_w,
        updated,
        kept[3],
        kept[4],
        near0,
        raw1,
        message1,
        main_w,
        halo_w,
        first_w,
        second_w,
    )
    return result.reshape(bands, 1, cols)


def solution(mesh):
    in_specs = (
        P("band", ("row", "col"), None),
        P(("row", "col"), None),
        P(("row", "col"), None),
        P("band"),
        P("band"),
        P(),
        P(),
        P(),
        P(),
        P(),
    )
    out_specs = P("band", ("row", "col"), None)
    return jax.shard_map(
        on_device, mesh=mesh, in_specs=in_specs, out_specs=out_specs, check_vma=False
    )
```

```python
import functools

import jax
import jax.numpy as jnp
from jax import lax
from jax.experimental import pallas as pl
from jax.experimental.pallas import tpu as pltpu
from jax.sharding import PartitionSpec as P

LANES = 128
SUB = 8
F32 = jnp.float32
BF16 = jnp.bfloat16
I32 = jnp.int32
COUNTER = 512.0
EXTRA = 16


def lanes_of(shape=(SUB, LANES)):
    return lax.broadcasted_iota(I32, shape, 1)


def rows_of(shape=(SUB, LANES)):
    return lax.broadcasted_iota(I32, shape, 0)


def column(row, rows):
    n = row.shape[1]
    eye = rows_of((rows, n)) == lanes_of((rows, n))
    return jnp.sum(jnp.where(eye, jnp.broadcast_to(row, (rows, n)), 0.0), axis=1, keepdims=True)


def turn(chunk, index):
    return jnp.take_along_axis(chunk, index, axis=1, mode="promise_in_bounds")


def choose(delay, options):
    result = options[-1]
    for d in range(len(options) - 2, -1, -1):
        result = jnp.where(delay == d, options[d], result)
    return result


def split3(x):
    hi = x.astype(BF16).astype(F32)
    mid = (x - hi).astype(BF16).astype(F32)
    return hi, mid, x - hi - mid


def fetch(sources, targets, sems):
    copies = [
        pltpu.make_async_copy(src, dst, sems.at[i]) for i, (src, dst) in enumerate(zip(sources, targets))
    ]
    for copy in copies:
        copy.start()
    return copies


def project_kernel(
    reach, cube_in, ap_in, meas_in, shear_in, step_in, part_ref, up_ref, dn_ref, *rest_refs
):
    line_ref, *kept = rest_refs[:5]
    cube_ref, raw, sems = rest_refs[5:]
    ap_ref, meas_ref, shear_ref, step_ref = kept
    copies = fetch((cube_in, ap_in, meas_in, shear_in, step_in), (cube_ref, *kept), sems)
    for copy in copies:
        copy.wait()
    bands, cols = cube_ref.shape
    groups = -(-bands // SUB)
    inner = cols // LANES
    tall = part_ref.shape[0] // 2
    outer = -(-meas_ref.shape[1] // LANES)
    raw[bands // SUB * SUB :, :] = jnp.zeros((raw.shape[0] - bands // SUB * SUB, cols), F32)
    raw[0:bands, :] = cube_ref[...].astype(F32)
    shear_f = column(shear_ref[...].astype(F32), groups * SUB)
    step_f = column(step_ref[...], groups * SUB)
    shear_i = shear_f.astype(I32)
    lane, sub = lanes_of(), rows_of()
    index, delay = [], []
    for g in range(groups):
        s = jnp.broadcast_to(shear_i[g * SUB : (g + 1) * SUB], (SUB, LANES))
        rest = s & (LANES - 1)
        index.append((lane - rest) & (LANES - 1))
        delay.append((s >> 7) + jnp.where(lane < rest, 1, 0))
    zero = jnp.zeros((SUB, LANES), F32)
    turned = [[zero] * (reach - 1) for _ in range(groups)]
    sums = [zero] * (tall // SUB)
    firsts, lasts = [], []
    for p in range(outer):
        total = zero
        if p < inner:
            open_p = jnp.broadcast_to(
                ap_ref[:, p * LANES : (p + 1) * LANES].astype(F32), (SUB, LANES)
            )
            layers = [
                raw[g * SUB : (g + 1) * SUB, p * LANES : (p + 1) * LANES] for g in range(groups)
            ]
            firsts.append(layers[0])
            lasts.append(layers[-1])
            tagged = jnp.where(sub == bands % SUB, open_p, layers[-1])
            line_ref[:, p * LANES : (p + 1) * LANES] = jnp.concatenate(
                layers[:-1] + [tagged], axis=0
            ).astype(BF16)
        for g in range(groups):
            if p < inner:
                here = (layers[g] + COUNTER) * open_p
                if (g + 1) * SUB > bands:
                    here = jnp.where(sub < bands - g * SUB, here, 0.0)
                here = turn(here, index[g])
            else:
                here = zero
            options = [here] + turned[g]
            turned[g] = options[:-1]
            total = total + choose(delay[g], options)
        v, at = divmod(p, SUB)
        sums[v] = jnp.where(sub == at, jnp.sum(total, axis=0, keepdims=True), sums[v])
    counts = [jnp.floor(x * (1.0 / COUNTER) + 0.5) for x in sums]
    sums = [x - COUNTER * n for x, n in zip(sums, counts)]
    sides = []
    for g in (0, groups - 1):
        s = shear_i[g * SUB : (g + 1) * SUB]
        parts = [(s >> 1).astype(F32), (s & 1).astype(F32)]
        parts += list(split3(step_f[g * SUB : (g + 1) * SUB]))
        side = zero
        for i, part in enumerate(parts):
            side = jnp.where(lane == i, part, side)
        sides.append(side)
    half = inner // 2
    dn = [
        jnp.where(sub < 3, firsts[q], pltpu.roll(firsts[q + half], 3, 0)) for q in range(half)
    ] + [sides[0], zero]
    up = [
        jnp.where(sub < 3, pltpu.roll(lasts[q + half], SUB - 3, 0), lasts[q]) for q in range(half)
    ] + [sides[1], zero]
    part_ref[...] = jnp.concatenate(sums + counts, axis=0).astype(BF16)
    up_ref[...] = jnp.concatenate(sums + counts + up, axis=0).astype(BF16)
    dn_ref[...] = jnp.concatenate(sums + counts + dn, axis=0).astype(BF16)


def update_kernel(
    reach,
    fars,
    line_ref,
    ap_ref,
    meas_ref,
    shear_ref,
    step_ref,
    own_ref,
    below_ref,
    above_ref,
    _,
    *rest_refs,
):
    far_refs = rest_refs[:fars]
    out_ref, msg_ref, long_ref, raw, meas, rest_row = rest_refs[fars:]
    groups = line_ref.shape[0] // SUB
    cols = line_ref.shape[1]
    inner = cols // LANES
    half = inner // 2
    tall = own_ref.shape[0] // 2
    outer = -(-meas_ref.shape[1] // LANES)
    raw[...] = line_ref[...].astype(F32)
    meas[:, (outer - 1) * LANES :] = jnp.zeros((1, LANES), F32)
    meas[:, 0 : meas_ref.shape[1]] = meas_ref[...]
    shear_f = column(shear_ref[...].astype(F32), groups * SUB)
    step_f = column(step_ref[...], groups * SUB)
    lane, sub = lanes_of(), rows_of()
    below = below_ref[...].astype(F32)
    above = above_ref[...].astype(F32)
    sums = own_ref[...].astype(F32) + below[0 : 2 * tall] + above[0 : 2 * tall]
    for far in far_refs:
        sums = sums + far[...].astype(F32)
    measured = []
    for v in range(tall // SUB):
        tile = jnp.zeros((SUB, LANES), F32)
        for at in range(min(SUB, outer - v * SUB)):
            p = v * SUB + at
            tile = jnp.where(sub == at, meas[:, p * LANES : (p + 1) * LANES], tile)
        measured.append(tile)
    measured = jnp.concatenate(measured, axis=0)
    rest_row[...] = (measured - sums[0:tall]) / jnp.maximum(sums[tall:], 1.0)

    def halo(q):
        at = 2 * tall + q % half * SUB
        high, low = above[at : at + SUB], below[at : at + SUB]
        if q // half == 1:
            high, low = pltpu.roll(high, SUB - 3, 0), pltpu.roll(low, 3, 0)
        return jnp.where(sub < 3, high, jnp.where(sub < 6, low, 0.0))

    side = 2 * tall + half * SUB
    side = jnp.where(sub < 3, above[side : side + SUB], below[side : side + SUB])
    shear_cols = [shear_f[g * SUB : (g + 1) * SUB] for g in range(groups)]
    step_cols = [step_f[g * SUB : (g + 1) * SUB] for g in range(groups)]
    inside = rows_of((SUB, 1)) < 6
    shear_cols.append(jnp.where(inside, 2.0 * side[:, 0:1] + side[:, 1:2], 0.0))
    step_cols.append(jnp.where(inside, side[:, 2:3] + side[:, 3:4] + side[:, 4:5], 0.0))
    index, delay, steps = [], [], []
    for g in range(groups + 1):
        s = jnp.broadcast_to(shear_cols[g].astype(I32), (SUB, LANES))
        rest = s & (LANES - 1)
        index.append((lane + rest) & (LANES - 1))
        delay.append((s >> 7) + jnp.where(lane + rest >= LANES, 1, 0))
        steps.append(jnp.broadcast_to(step_cols[g], (SUB, LANES)))
    tiles = []
    turned = [[] for _ in range(groups + 1)]
    for p in range(outer + 1):
        if p < outer:
            residual = jnp.broadcast_to(rest_row[p : p + 1, :], (SUB, LANES))
        else:
            residual = jnp.zeros((SUB, LANES), F32)
        lost = residual - residual.astype(BF16).astype(F32)
        tiles.append(jnp.where(sub < 7, residual, lost))
        for g in range(groups + 1):
            turned[g].append(turn(residual, index[g]) if p < outer else residual)
        q = p - (reach - 1)
        if q < 0 or q >= inner:
            continue
        here = slice(q * LANES, (q + 1) * LANES)
        open_q = jnp.broadcast_to(ap_ref[:, here].astype(F32), (SUB, LANES))
        pieces = []
        for g in range(groups + 1):
            pulled = choose(delay[g], turned[g][q : q + reach])
            base = raw[g * SUB : (g + 1) * SUB, here] if g < groups else halo(q)
            pieces.append(base + pulled * open_q * steps[g])
        out_ref[:, here] = jnp.concatenate(pieces, axis=0).astype(BF16)
        tiles[q] = jnp.where(sub < 6, pieces[-1], tiles[q])
    words = jnp.concatenate(tiles, axis=0).astype(BF16)
    msg_ref[...] = words
    long_ref[0 : words.shape[0], :] = words
    rest = (long_ref.shape[0] - words.shape[0], LANES)
    long_ref[words.shape[0] :, :] = jnp.zeros(rest, BF16)


def spread(rows, ch, which):
    return (which(rows_of((rows, ch))) == lanes_of((rows, ch))).astype(F32).astype(BF16)


def picked(row_ref, rows, which):
    ch = row_ref.shape[1]
    pick = which(rows_of((rows, ch))) == lanes_of((rows, ch))
    row = jnp.broadcast_to(row_ref[...], (rows, ch))
    return jnp.sum(jnp.where(pick, row, 0.0), axis=1, keepdims=True)


def with_bias(matrix, bias, start):
    lane = lanes_of(matrix.shape)
    for i, part in enumerate(split3(0.5 * bias)):
        matrix = jnp.where(lane == start + i, part, matrix)
    return matrix


def gate_kernel(_, line_ref, same_ref):
    pass


def weights_kernel(
    _, sw_in, sb_in, cw_in, cb_in, ow_in, main_ref, halo_ref, first_ref, second_ref, out_w_ref, *rest
):
    local, sems = rest[:5], rest[5]
    for copy in fetch((sw_in, sb_in, cw_in, cb_in, ow_in), local, sems):
        copy.wait()
    sw_ref, sb_ref, cw_ref, cb_ref, ow_ref = local
    ch, taps2 = sw_ref.shape
    taps = cw_ref.shape[0]
    place = lax.axis_index("band")
    has_low = jnp.where(place > 0, 1, 0)
    has_high = jnp.where(place < lax.axis_size("band") - 1, 1, 0)
    width = main_ref.shape[1]
    slots = 16
    line = lax.axis_index("row") * lax.axis_size("col") + lax.axis_index("col")
    lines = lax.axis_size("row") * lax.axis_size("col")
    group = lanes_of((taps2, width)) // slots
    offset = jnp.where(line % 2 == 1, group // 3, 2 - group // 3)
    present = (line + offset >= 1) & (line + offset <= lines)
    fan = (rows_of((taps2, width)) == 3 * offset + group % 3) & present
    fan = fan.astype(F32).astype(BF16)
    flat = jnp.dot(sw_ref[...], fan, preferred_element_type=F32).astype(BF16)
    for ref, slot_of in (
        (main_ref, lambda b: b),
        (halo_ref, lambda b: jnp.where(b < 3, 11 + b, jnp.where(b < 9, b - 3, b - 1))),
    ):
        rows = ref.shape[0]
        which = lambda r: r % ch
        full = jnp.dot(spread(rows, ch, which), flat, preferred_element_type=F32)
        lane = lanes_of((rows, width))
        band = rows_of((rows, width)) // ch
        keep = (lane % slots == slot_of(band)) & (lane < taps2 * slots)
        matrix = with_bias(
            jnp.where(keep, 0.5 * full, 0.0), picked(sb_ref, rows, which), taps2 * slots
        )
        if ref is halo_ref:
            valid = jnp.where(band < 3, has_low, jnp.where(band >= 9, has_high, 1))
            matrix = jnp.where(valid > 0, matrix, 0.0)
        ref[...] = matrix.astype(BF16)

    per = SUB
    rows = per * ch
    width = first_ref.shape[1]
    used = (per + taps - 1) * ch
    which = lambda r: r // per
    fan = (lanes_of((ch, width)) % ch == rows_of((ch, width))).astype(F32).astype(BF16)
    picks = spread(rows, ch, which)
    lane = lanes_of((rows, width))
    ahead = jnp.where(lane < used, lane // ch - rows_of((rows, width)) % per, -LANES)
    matrix = jnp.zeros((rows, width), F32)
    for d in range(taps):
        flat = jnp.dot(cw_ref[d], fan, preferred_element_type=F32).astype(BF16)
        full = 0.5 * jnp.dot(picks, flat, preferred_element_type=F32)
        matrix = jnp.where(ahead == d, full, matrix)
    bias = picked(cb_ref, rows, which)
    first_ref[...] = with_bias(matrix, bias, used).astype(BF16)
    short = second_ref.shape[1]
    start = short - 16
    matrix = jnp.where(lanes_of((rows, short)) < start, matrix[:, 0:short], 0.0)
    second_ref[...] = with_bias(matrix, bias, start).astype(BF16)
    out_w_ref[...] = jnp.broadcast_to(picked(ow_ref, rows, which), out_w_ref.shape)


def neighbour_chunks(reach, bands, shear_ref, step_ref, raw_ref, msg_ref, near, words):
    inner = raw_ref.shape[1] // LANES
    groups = -(-bands // SUB)
    zero = jnp.zeros((SUB, LANES), F32)
    shear_f = column(shear_ref[...].astype(F32), groups * SUB)
    step_f = column(step_ref[...], groups * SUB)
    lane = lanes_of()
    index, delay, steps = [], [], []
    for g in range(groups):
        s = jnp.broadcast_to(shear_f[g * SUB : (g + 1) * SUB].astype(I32), (SUB, LANES))
        rest = s & (LANES - 1)
        index.append((lane + rest) & (LANES - 1))
        delay.append((s >> 7) + jnp.where(lane + rest >= LANES, 1, 0))
        steps.append(jnp.broadcast_to(step_f[g * SUB : (g + 1) * SUB], (SUB, LANES)))
    chunks = inner + reach - 1
    words[...] = msg_ref[0 : words.shape[0], :].astype(F32)
    turned = [[] for _ in range(groups)]

    def make(q):
        while len(turned[0]) < q + reach:
            p = len(turned[0])
            if p >= chunks:
                residual = zero
            else:
                at = p * SUB + 6
                residual = words[at : at + 1, :] + words[at + 1 : at + 2, :]
                residual = jnp.broadcast_to(residual, (SUB, LANES))
            for g in range(groups):
                turned[g].append(turn(residual, index[g]))
        raw = raw_ref[:, q * LANES : (q + 1) * LANES].astype(F32)
        open_q = jnp.broadcast_to(raw[bands : bands + 1], (SUB, LANES))
        pieces = [
            raw[g * SUB : (g + 1) * SUB]
            + choose(delay[g], turned[g][q : q + reach]) * open_q * steps[g]
            for g in range(groups)
        ]
        pieces.append(words[q * SUB : (q + 1) * SUB, :])
        near[:, q * LANES : (q + 1) * LANES] = jnp.concatenate(pieces, axis=0).astype(BF16)

    return make


def neighbour_kernel(reach, shear_ref, step_ref, raw_ref, msg_ref, _, near, words):
    bands = shear_ref.shape[1]
    make = neighbour_chunks(reach, bands, shear_ref, step_ref, raw_ref, msg_ref, near, words)
    for q in range(near.shape[1] // LANES):
        make(q)


def denoise_kernel(
    tile,
    reach,
    ow_ref,
    mid_ref,
    shear_ref,
    step_ref,
    near0,
    raw_ref,
    msg_ref,
    main_ref,
    halo_ref,
    first_ref,
    second_ref,
    out_ref,
    act,
    near1,
    words,
):
    bands, cols = out_ref.shape
    slots = 16
    ch = main_ref.shape[0] // slots
    tiles = cols // tile
    inner = cols // LANES
    wide = tile + 2 * LANES
    groups = -(-bands // SUB)
    ones = jnp.where(rows_of((slots, tile)) < 3, 1.0, 0.0).astype(BF16)
    blank = jnp.zeros((2 * slots, LANES), BF16)
    neighbours = neighbour_chunks(
        reach, bands, shear_ref, step_ref, raw_ref, msg_ref, near1, words
    )

    def silu_twice(half):
        return half + half * jnp.tanh(half)

    inputs, halves, blocks, sums = {}, {}, {}, {}
    made = 0

    def update_up_to(t):
        nonlocal made
        while made < min((t + 1) * tile // LANES + 1, inner):
            neighbours(made)
            made += 1

    def patches(t):
        start = t * tile
        end = start + tile
        parts = []
        for ref in (near0, mid_ref, near1):
            left = ref[:, start - LANES : start] if t else blank
            here = ref[:, start:end]
            right = ref[:, end : end + LANES] if t < tiles - 1 else blank
            row = jnp.concatenate([left, here, right], axis=1)
            back = pltpu.roll(row, 1, 1)[:, LANES : LANES + tile]
            ahead = pltpu.roll(row, wide - 1, 1)[:, LANES : LANES + tile]
            parts += [back, here, ahead]
        for part in range(2):
            inputs[t, part] = jnp.concatenate(
                [p[part * slots : (part + 1) * slots] for p in parts] + [ones], axis=0
            )

    def spatial(t, part):
        w_ref = halo_ref if part else main_ref
        halves[t, part] = jnp.dot(
            w_ref[...], inputs.pop((t, part)), preferred_element_type=F32
        )

    def activate(t, part):
        buf = act.at[t % act.shape[0]]
        value = silu_twice(halves.pop((t, part))).astype(BF16)
        if part == 0:
            buf[3 * ch : 19 * ch, :] = value
        else:
            buf[0 : 3 * ch, :] = value[0 : 3 * ch]
            buf[19 * ch : 28 * ch, :] = value[3 * ch :]

    def spectral(t, i):
        buf = act.at[t % act.shape[0]]
        w_ref = second_ref if i == groups - 1 else first_ref
        first = i * SUB * ch
        x = jnp.concatenate([buf[first : first + w_ref.shape[1] - slots, :], ones], axis=0)
        blocks[t, i] = jnp.dot(w_ref[...], x, preferred_element_type=F32)

    def project(t, i):
        half = blocks.pop((t, i))
        total = None
        for k in range(ch):
            weight = ow_ref[k * SUB : (k + 1) * SUB, :]
            weight = jnp.concatenate([weight] * (tile // LANES), axis=1)
            term = weight * silu_twice(half[k * SUB : (k + 1) * SUB])
            total = term if total is None else total + term
        sums[t, i] = total
        if i == groups - 1:
            start = t * tile
            update = jnp.concatenate([sums.pop((t, n)) for n in range(groups)], axis=0)[0:bands]
            center = mid_ref[:, start : start + tile].astype(F32)[0:bands]
            out_ref[:, start : start + tile] = (center + update).astype(BF16)

    update_up_to(0)
    patches(0)
    spatial(0, 0)
    spatial(0, 1)
    update_up_to(1)
    activate(0, 0)
    patches(1)
    activate(0, 1)
    for t in range(tiles):
        if t + 1 < tiles:
            spatial(t + 1, 0)
        if t:
            project(t - 1, groups - 1)
        if t + 2 < tiles:
            update_up_to(t + 2)
        if t + 1 < tiles:
            spatial(t + 1, 1)
            activate(t + 1, 0)
        spectral(t, 0)
        if t + 1 < tiles:
            activate(t + 1, 1)
        for i in range(1, groups):
            spectral(t, i)
            project(t, i - 1)
        if t + 2 < tiles:
            patches(t + 2)
    project(tiles - 1, groups - 1)


def vmem(n):
    return [pl.BlockSpec(memory_space=pltpu.VMEM)] * n


def hbm(n):
    return [pl.BlockSpec(memory_space=pltpu.HBM)] * n


def in_hbm(arrays):
    return [pltpu.with_memory_space_constraint(x, pltpu.HBM) for x in arrays]


ANY = pl.BlockSpec(memory_space=pl.ANY)


def on_device(
    spectral_cube,
    aperture,
    measurement,
    shears,
    step_sizes,
    spatial_weight,
    spatial_bias,
    spectral_weight,
    spectral_bias,
    out_weight,
):
    bands, row_count, cols = spectral_cube.shape
    width = measurement.shape[1]
    reach = (width - cols) // LANES + 2
    outer = -(-width // LANES)
    groups = -(-bands // SUB)
    slots = (groups + 1) * SUB
    taps, ch = spectral_weight.shape[:2]
    taps2 = spatial_weight.shape[1]
    count = lax.axis_size("band")
    cube = spectral_cube.reshape(bands, cols)
    shear_row = shears.reshape(1, bands)
    step_row = step_sizes.reshape(1, bands)
    params = pltpu.CompilerParams(vmem_limit_bytes=48 * 2**20)

    tall = -(-outer // SUB) * SUB
    side = (cols // LANES // 2 + 2) * SUB
    inputs = (cube, aperture, measurement, shear_row, step_row)
    part, up, dn, *kept = pl.pallas_call(
        functools.partial(project_kernel, reach),
        out_shape=(
            jax.ShapeDtypeStruct((2 * tall, LANES), BF16),
            jax.ShapeDtypeStruct((2 * tall + side, LANES), BF16),
            jax.ShapeDtypeStruct((2 * tall + side, LANES), BF16),
        )
        + (jax.ShapeDtypeStruct((groups * SUB, cols), BF16),)
        + tuple(jax.ShapeDtypeStruct(x.shape, x.dtype) for x in inputs[1:]),
        in_specs=hbm(5),
        out_specs=tuple(vmem(8)),
        scratch_shapes=[
            pltpu.VMEM((bands, cols), BF16),
            pltpu.VMEM((groups * SUB, cols), F32),
            pltpu.SemaphoreType.DMA((5,)),
        ],
        compiler_params=params,
        name="project",
    )(*in_hbm(inputs))

    def around(x, shift):
        return lax.ppermute(x, "band", [(i, (i + shift) % count) for i in range(count)])

    below = around(up, 1)
    above = around(dn, -1)
    far = [around(part, s) for s in range(2, count - 1)]

    line = pl.pallas_call(
        gate_kernel,
        out_shape=jax.ShapeDtypeStruct(kept[0].shape, BF16),
        in_specs=[ANY, ANY],
        out_specs=ANY,
        input_output_aliases={1: 0},
        compiler_params=pltpu.CompilerParams(vmem_limit_bytes=2**20),
        name="gate",
    )(part, kept[0])

    lines = lax.axis_size(("row", "col"))
    pairs = [(i, i ^ 1) for i in range(lines)]
    others = [(i, (i - 1 + i % 2 * 2) % lines) for i in range(lines)]
    raw1 = lax.ppermute(kept[0], ("row", "col"), others)
    raw0 = lax.ppermute(line, ("row", "col"), pairs)

    small = (
        spatial_weight,
        spatial_bias.reshape(1, ch),
        spectral_weight,
        spectral_bias.reshape(1, ch),
        out_weight.reshape(1, ch),
    )
    reached = (SUB + taps - 1) * ch
    last = (bands - (groups - 1) * SUB + taps - 1) * ch
    main_w, halo_w, first_w, second_w, out_w = pl.pallas_call(
        weights_kernel,
        out_shape=(
            jax.ShapeDtypeStruct((16 * ch, taps2 * 16 + 16), BF16),
            jax.ShapeDtypeStruct((12 * ch, taps2 * 16 + 16), BF16),
            jax.ShapeDtypeStruct((SUB * ch, reached + 16), BF16),
            jax.ShapeDtypeStruct((SUB * ch, last + 16), BF16),
            jax.ShapeDtypeStruct((SUB * ch, LANES), F32),
        ),
        in_specs=[ANY] + hbm(5),
        out_specs=tuple(vmem(5)),
        scratch_shapes=[pltpu.VMEM(x.shape, x.dtype) for x in small]
        + [pltpu.SemaphoreType.DMA((5,))],
        compiler_params=params,
        name="weights",
    )(line, *in_hbm(small))

    words = (outer + 1) * SUB
    updated, message, longer = pl.pallas_call(
        functools.partial(update_kernel, reach, len(far)),
        out_shape=(
            jax.ShapeDtypeStruct((slots, cols), BF16),
            jax.ShapeDtypeStruct((words, LANES), BF16),
            jax.ShapeDtypeStruct((words + EXTRA, LANES), BF16),
        ),
        in_specs=vmem(8) + [ANY] + vmem(len(far)),
        out_specs=tuple(vmem(3)),
        scratch_shapes=[
            pltpu.VMEM((groups * SUB, cols), F32),
            pltpu.VMEM((1, outer * LANES), F32),
            pltpu.VMEM((tall, LANES), F32),
        ],
        compiler_params=params,
        cost_estimate=pl.CostEstimate(
            flops=10**10, bytes_accessed=4 * 10**7, transcendentals=0
        ),
        name="update",
    )(*kept, part, below, above, out_w, *far)

    message0 = lax.ppermute(message, ("row", "col"), pairs)
    message1 = lax.ppermute(longer, ("row", "col"), others)

    near0 = pl.pallas_call(
        functools.partial(neighbour_kernel, reach),
        out_shape=jax.ShapeDtypeStruct((slots, cols), BF16),
        in_specs=vmem(4) + [ANY],
        out_specs=vmem(1)[0],
        scratch_shapes=[pltpu.VMEM((words, LANES), F32)],
        compiler_params=params,
        cost_estimate=pl.CostEstimate(flops=1, bytes_accessed=1, transcendentals=0),
        name="partner",
    )(kept[3], kept[4], raw0, message0, message)

    tile = 512
    result = pl.pallas_call(
        functools.partial(denoise_kernel, tile, reach),
        out_shape=jax.ShapeDtypeStruct((bands, cols), BF16),
        in_specs=vmem(11),
        out_specs=vmem(1)[0],
        scratch_shapes=[
            pltpu.VMEM((4, 28 * ch, tile), BF16),
            pltpu.VMEM((slots, cols), BF16),
            pltpu.VMEM((words, LANES), F32),
        ],
        compiler_params=params,
        name="denoise",
    )(
        out_w,
        updated,
        kept[3],
        kept[4],
        near0,
        raw1,
        message1,
        main_w,
        halo_w,
        first_w,
        second_w,
    )
    return result.reshape(bands, 1, cols)


def solution(mesh):
    in_specs = (
        P("band", ("row", "col"), None),
        P(("row", "col"), None),
        P(("row", "col"), None),
        P("band"),
        P("band"),
        P(),
        P(),
        P(),
        P(),
        P(),
    )
    out_specs = P("band", ("row", "col"), None)
    return jax.shard_map(
        on_device, mesh=mesh, in_specs=in_specs, out_specs=out_specs, check_vma=False
    )
```

```python
import functools

import jax
import jax.numpy as jnp
from jax import lax
from jax.experimental import pallas as pl
from jax.experimental.pallas import tpu as pltpu
from jax.sharding import PartitionSpec as P

LANES = 128
SUB = 8
F32 = jnp.float32
BF16 = jnp.bfloat16
I32 = jnp.int32
COUNTER = 512.0
EXTRA = 16


def lanes_of(shape=(SUB, LANES)):
    return lax.broadcasted_iota(I32, shape, 1)


def rows_of(shape=(SUB, LANES)):
    return lax.broadcasted_iota(I32, shape, 0)


def column(row, rows):
    n = row.shape[1]
    eye = rows_of((rows, n)) == lanes_of((rows, n))
    return jnp.sum(jnp.where(eye, jnp.broadcast_to(row, (rows, n)), 0.0), axis=1, keepdims=True)


def turn(chunk, index):
    return jnp.take_along_axis(chunk, index, axis=1, mode="promise_in_bounds")


def choose(delay, options):
    result = options[-1]
    for d in range(len(options) - 2, -1, -1):
        result = jnp.where(delay == d, options[d], result)
    return result


def split3(x):
    hi = x.astype(BF16).astype(F32)
    mid = (x - hi).astype(BF16).astype(F32)
    return hi, mid, x - hi - mid


def fetch(sources, targets, sems):
    copies = [
        pltpu.make_async_copy(src, dst, sems.at[i]) for i, (src, dst) in enumerate(zip(sources, targets))
    ]
    for copy in copies:
        copy.start()
    return copies


def project_kernel(
    reach, cube_in, ap_in, meas_in, shear_in, step_in, part_ref, up_ref, dn_ref, *rest_refs
):
    line_ref, *kept = rest_refs[:5]
    cube_ref, raw, sems = rest_refs[5:]
    ap_ref, meas_ref, shear_ref, step_ref = kept
    copies = fetch((cube_in, ap_in, meas_in, shear_in, step_in), (cube_ref, *kept), sems)
    for copy in copies:
        copy.wait()
    bands, cols = cube_ref.shape
    groups = -(-bands // SUB)
    inner = cols // LANES
    tall = part_ref.shape[0] // 2
    outer = -(-meas_ref.shape[1] // LANES)
    raw[bands // SUB * SUB :, :] = jnp.zeros((raw.shape[0] - bands // SUB * SUB, cols), F32)
    raw[0:bands, :] = cube_ref[...].astype(F32)
    shear_f = column(shear_ref[...].astype(F32), groups * SUB)
    step_f = column(step_ref[...], groups * SUB)
    shear_i = shear_f.astype(I32)
    lane, sub = lanes_of(), rows_of()
    index, delay = [], []
    for g in range(groups):
        s = jnp.broadcast_to(shear_i[g * SUB : (g + 1) * SUB], (SUB, LANES))
        rest = s & (LANES - 1)
        index.append((lane - rest) & (LANES - 1))
        delay.append((s >> 7) + jnp.where(lane < rest, 1, 0))
    zero = jnp.zeros((SUB, LANES), F32)
    turned = [[zero] * (reach - 1) for _ in range(groups)]
    sums = [zero] * (tall // SUB)
    firsts, lasts = [], []
    for p in range(outer):
        total = zero
        if p < inner:
            open_p = jnp.broadcast_to(
                ap_ref[:, p * LANES : (p + 1) * LANES].astype(F32), (SUB, LANES)
            )
            layers = [
                raw[g * SUB : (g + 1) * SUB, p * LANES : (p + 1) * LANES] for g in range(groups)
            ]
            firsts.append(layers[0])
            lasts.append(layers[-1])
            tagged = jnp.where(sub == bands % SUB, open_p, layers[-1])
            line_ref[:, p * LANES : (p + 1) * LANES] = jnp.concatenate(
                layers[:-1] + [tagged], axis=0
            ).astype(BF16)
        for g in range(groups):
            if p < inner:
                here = (layers[g] + COUNTER) * open_p
                if (g + 1) * SUB > bands:
                    here = jnp.where(sub < bands - g * SUB, here, 0.0)
                here = turn(here, index[g])
            else:
                here = zero
            options = [here] + turned[g]
            turned[g] = options[:-1]
            total = total + choose(delay[g], options)
        v, at = divmod(p, SUB)
        sums[v] = jnp.where(sub == at, jnp.sum(total, axis=0, keepdims=True), sums[v])
    counts = [jnp.floor(x * (1.0 / COUNTER) + 0.5) for x in sums]
    sums = [x - COUNTER * n for x, n in zip(sums, counts)]
    sides = []
    for g in (0, groups - 1):
        s = shear_i[g * SUB : (g + 1) * SUB]
        parts = [(s >> 1).astype(F32), (s & 1).astype(F32)]
        parts += list(split3(step_f[g * SUB : (g + 1) * SUB]))
        side = zero
        for i, part in enumerate(parts):
            side = jnp.where(lane == i, part, side)
        sides.append(side)
    half = inner // 2
    dn = [
        jnp.where(sub < 3, firsts[q], pltpu.roll(firsts[q + half], 3, 0)) for q in range(half)
    ] + [sides[0], zero]
    up = [
        jnp.where(sub < 3, pltpu.roll(lasts[q + half], SUB - 3, 0), lasts[q]) for q in range(half)
    ] + [sides[1], zero]
    part_ref[...] = jnp.concatenate(sums + counts, axis=0).astype(BF16)
    up_ref[...] = jnp.concatenate(sums + counts + up, axis=0).astype(BF16)
    dn_ref[...] = jnp.concatenate(sums + counts + dn, axis=0).astype(BF16)


def update_kernel(
    reach, fars, ap_ref, meas_ref, own_ref, below_ref, above_ref, _, *rest_refs
):
    far_refs = rest_refs[:fars]
    msg_ref, long_ref, meas, rest_row = rest_refs[fars:]
    cols = ap_ref.shape[1]
    inner = cols // LANES
    half = inner // 2
    tall = own_ref.shape[0] // 2
    outer = -(-meas_ref.shape[1] // LANES)
    meas[:, (outer - 1) * LANES :] = jnp.zeros((1, LANES), F32)
    meas[:, 0 : meas_ref.shape[1]] = meas_ref[...]
    lane, sub = lanes_of(), rows_of()
    below = below_ref[...].astype(F32)
    above = above_ref[...].astype(F32)
    sums = own_ref[...].astype(F32) + below[0 : 2 * tall] + above[0 : 2 * tall]
    for far in far_refs:
        sums = sums + far[...].astype(F32)
    measured = []
    for v in range(tall // SUB):
        tile = jnp.zeros((SUB, LANES), F32)
        for at in range(min(SUB, outer - v * SUB)):
            p = v * SUB + at
            tile = jnp.where(sub == at, meas[:, p * LANES : (p + 1) * LANES], tile)
        measured.append(tile)
    measured = jnp.concatenate(measured, axis=0)
    rest_row[...] = (measured - sums[0:tall]) / jnp.maximum(sums[tall:], 1.0)

    def halo(q):
        at = 2 * tall + q % half * SUB
        high, low = above[at : at + SUB], below[at : at + SUB]
        if q // half == 1:
            high, low = pltpu.roll(high, SUB - 3, 0), pltpu.roll(low, 3, 0)
        return jnp.where(sub < 3, high, jnp.where(sub < 6, low, 0.0))

    side = 2 * tall + half * SUB
    side = jnp.where(sub < 3, above[side : side + SUB], below[side : side + SUB])
    inside = rows_of((SUB, 1)) < 6
    shear = jnp.where(inside, 2.0 * side[:, 0:1] + side[:, 1:2], 0.0)
    step = jnp.where(inside, side[:, 2:3] + side[:, 3:4] + side[:, 4:5], 0.0)
    shear = jnp.broadcast_to(shear.astype(I32), (SUB, LANES))
    step = jnp.broadcast_to(step, (SUB, LANES))
    rest = shear & (LANES - 1)
    index = (lane + rest) & (LANES - 1)
    delay = (shear >> 7) + jnp.where(lane + rest >= LANES, 1, 0)
    tiles = []
    turned = []
    for p in range(outer + 1):
        if p < outer:
            residual = jnp.broadcast_to(rest_row[p : p + 1, :], (SUB, LANES))
            turned.append(turn(residual, index))
        else:
            residual = jnp.zeros((SUB, LANES), F32)
            turned.append(residual)
        lost = residual - residual.astype(BF16).astype(F32)
        tiles.append(jnp.where(sub < 7, residual, lost))
        q = p - (reach - 1)
        if q < 0 or q >= inner:
            continue
        here = slice(q * LANES, (q + 1) * LANES)
        open_q = jnp.broadcast_to(ap_ref[:, here].astype(F32), (SUB, LANES))
        value = halo(q) + choose(delay, turned[q : q + reach]) * open_q * step
        tiles[q] = jnp.where(sub < 6, value, tiles[q])
    words = jnp.concatenate(tiles, axis=0).astype(BF16)
    msg_ref[...] = words
    long_ref[0 : words.shape[0], :] = words
    rest = (long_ref.shape[0] - words.shape[0], LANES)
    long_ref[words.shape[0] :, :] = jnp.zeros(rest, BF16)


def spread(rows, ch, which):
    return (which(rows_of((rows, ch))) == lanes_of((rows, ch))).astype(F32).astype(BF16)


def picked(row_ref, rows, which):
    ch = row_ref.shape[1]
    pick = which(rows_of((rows, ch))) == lanes_of((rows, ch))
    row = jnp.broadcast_to(row_ref[...], (rows, ch))
    return jnp.sum(jnp.where(pick, row, 0.0), axis=1, keepdims=True)


def with_bias(matrix, bias, start):
    lane = lanes_of(matrix.shape)
    for i, part in enumerate(split3(0.5 * bias)):
        matrix = jnp.where(lane == start + i, part, matrix)
    return matrix


def gate_kernel(_, line_ref, same_ref):
    pass


def weights_kernel(
    _, sw_in, sb_in, cw_in, cb_in, ow_in, main_ref, halo_ref, first_ref, second_ref, out_w_ref, *rest
):
    local, sems = rest[:5], rest[5]
    for copy in fetch((sw_in, sb_in, cw_in, cb_in, ow_in), local, sems):
        copy.wait()
    sw_ref, sb_ref, cw_ref, cb_ref, ow_ref = local
    ch, taps2 = sw_ref.shape
    taps = cw_ref.shape[0]
    place = lax.axis_index("band")
    has_low = jnp.where(place > 0, 1, 0)
    has_high = jnp.where(place < lax.axis_size("band") - 1, 1, 0)
    width = main_ref.shape[1]
    slots = 16
    line = lax.axis_index("row") * lax.axis_size("col") + lax.axis_index("col")
    lines = lax.axis_size("row") * lax.axis_size("col")
    group = lanes_of((taps2, width)) // slots
    offset = jnp.where(line % 2 == 1, group // 3, 2 - group // 3)
    present = (line + offset >= 1) & (line + offset <= lines)
    fan = (rows_of((taps2, width)) == 3 * offset + group % 3) & present
    fan = fan.astype(F32).astype(BF16)
    flat = jnp.dot(sw_ref[...], fan, preferred_element_type=F32).astype(BF16)
    for ref, slot_of in (
        (main_ref, lambda b: b),
        (halo_ref, lambda b: jnp.where(b < 3, 11 + b, jnp.where(b < 9, b - 3, b - 1))),
    ):
        rows = ref.shape[0]
        which = lambda r: r % ch
        full = jnp.dot(spread(rows, ch, which), flat, preferred_element_type=F32)
        lane = lanes_of((rows, width))
        band = rows_of((rows, width)) // ch
        keep = (lane % slots == slot_of(band)) & (lane < taps2 * slots)
        matrix = with_bias(
            jnp.where(keep, 0.5 * full, 0.0), picked(sb_ref, rows, which), taps2 * slots
        )
        if ref is halo_ref:
            valid = jnp.where(band < 3, has_low, jnp.where(band >= 9, has_high, 1))
            matrix = jnp.where(valid > 0, matrix, 0.0)
        ref[...] = matrix.astype(BF16)

    per = SUB
    rows = per * ch
    width = first_ref.shape[1]
    used = (per + taps - 1) * ch
    which = lambda r: r // per
    fan = (lanes_of((ch, width)) % ch == rows_of((ch, width))).astype(F32).astype(BF16)
    picks = spread(rows, ch, which)
    lane = lanes_of((rows, width))
    ahead = jnp.where(lane < used, lane // ch - rows_of((rows, width)) % per, -LANES)
    matrix = jnp.zeros((rows, width), F32)
    for d in range(taps):
        flat = jnp.dot(cw_ref[d], fan, preferred_element_type=F32).astype(BF16)
        full = 0.5 * jnp.dot(picks, flat, preferred_element_type=F32)
        matrix = jnp.where(ahead == d, full, matrix)
    bias = picked(cb_ref, rows, which)
    first_ref[...] = with_bias(matrix, bias, used).astype(BF16)
    short = second_ref.shape[1]
    start = short - 16
    matrix = jnp.where(lanes_of((rows, short)) < start, matrix[:, 0:short], 0.0)
    second_ref[...] = with_bias(matrix, bias, start).astype(BF16)
    out_w_ref[...] = jnp.broadcast_to(picked(ow_ref, rows, which), out_w_ref.shape)


def neighbour_chunks(reach, bands, shear_ref, step_ref, raw_ref, msg_ref, near, words):
    inner = raw_ref.shape[1] // LANES
    groups = -(-bands // SUB)
    zero = jnp.zeros((SUB, LANES), F32)
    shear_f = column(shear_ref[...].astype(F32), groups * SUB)
    step_f = column(step_ref[...], groups * SUB)
    lane = lanes_of()
    index, delay, steps = [], [], []
    for g in range(groups):
        s = jnp.broadcast_to(shear_f[g * SUB : (g + 1) * SUB].astype(I32), (SUB, LANES))
        rest = s & (LANES - 1)
        index.append((lane + rest) & (LANES - 1))
        delay.append((s >> 7) + jnp.where(lane + rest >= LANES, 1, 0))
        steps.append(jnp.broadcast_to(step_f[g * SUB : (g + 1) * SUB], (SUB, LANES)))
    chunks = inner + reach - 1
    words[...] = msg_ref[0 : words.shape[0], :].astype(F32)
    turned = [[] for _ in range(groups)]

    def make(q):
        while len(turned[0]) < q + reach:
            p = len(turned[0])
            if p >= chunks:
                residual = zero
            else:
                at = p * SUB + 6
                residual = words[at : at + 1, :] + words[at + 1 : at + 2, :]
                residual = jnp.broadcast_to(residual, (SUB, LANES))
            for g in range(groups):
                turned[g].append(turn(residual, index[g]))
        raw = raw_ref[:, q * LANES : (q + 1) * LANES].astype(F32)
        open_q = jnp.broadcast_to(raw[bands : bands + 1], (SUB, LANES))
        pieces = [
            raw[g * SUB : (g + 1) * SUB]
            + choose(delay[g], turned[g][q : q + reach]) * open_q * steps[g]
            for g in range(groups)
        ]
        pieces.append(words[q * SUB : (q + 1) * SUB, :])
        near[:, q * LANES : (q + 1) * LANES] = jnp.concatenate(pieces, axis=0).astype(BF16)

    return make


def neighbour_kernel(reach, shear_ref, step_ref, raw_ref, msg_ref, _, near, words):
    bands = shear_ref.shape[1]
    make = neighbour_chunks(reach, bands, shear_ref, step_ref, raw_ref, msg_ref, near, words)
    for q in range(near.shape[1] // LANES):
        make(q)


def denoise_kernel(
    tile,
    reach,
    ow_ref,
    mid_ref,
    shear_ref,
    step_ref,
    near0,
    raw_ref,
    msg_ref,
    main_ref,
    halo_ref,
    first_ref,
    second_ref,
    out_ref,
    act,
    near1,
    words,
):
    bands, cols = out_ref.shape
    slots = 16
    ch = main_ref.shape[0] // slots
    tiles = cols // tile
    inner = cols // LANES
    wide = tile + 2 * LANES
    groups = -(-bands // SUB)
    ones = jnp.where(rows_of((slots, tile)) < 3, 1.0, 0.0).astype(BF16)
    blank = jnp.zeros((2 * slots, LANES), BF16)
    neighbours = neighbour_chunks(
        reach, bands, shear_ref, step_ref, raw_ref, msg_ref, near1, words
    )

    def silu_twice(half):
        return half + half * jnp.tanh(half)

    inputs, halves, blocks, sums = {}, {}, {}, {}
    made = 0

    def update_up_to(t):
        nonlocal made
        while made < min((t + 1) * tile // LANES + 1, inner):
            neighbours(made)
            made += 1

    def patches(t):
        start = t * tile
        end = start + tile
        parts = []
        for ref in (near0, mid_ref, near1):
            left = ref[:, start - LANES : start] if t else blank
            here = ref[:, start:end]
            right = ref[:, end : end + LANES] if t < tiles - 1 else blank
            row = jnp.concatenate([left, here, right], axis=1)
            back = pltpu.roll(row, 1, 1)[:, LANES : LANES + tile]
            ahead = pltpu.roll(row, wide - 1, 1)[:, LANES : LANES + tile]
            parts += [back, here, ahead]
        for part in range(2):
            inputs[t, part] = jnp.concatenate(
                [p[part * slots : (part + 1) * slots] for p in parts] + [ones], axis=0
            )

    def spatial(t, part):
        w_ref = halo_ref if part else main_ref
        halves[t, part] = jnp.dot(
            w_ref[...], inputs.pop((t, part)), preferred_element_type=F32
        )

    def activate(t, part):
        buf = act.at[t % act.shape[0]]
        value = silu_twice(halves.pop((t, part))).astype(BF16)
        if part == 0:
            buf[3 * ch : 19 * ch, :] = value
        else:
            buf[0 : 3 * ch, :] = value[0 : 3 * ch]
            buf[19 * ch : 28 * ch, :] = value[3 * ch :]

    def spectral(t, i):
        buf = act.at[t % act.shape[0]]
        w_ref = second_ref if i == groups - 1 else first_ref
        first = i * SUB * ch
        x = jnp.concatenate([buf[first : first + w_ref.shape[1] - slots, :], ones], axis=0)
        blocks[t, i] = jnp.dot(w_ref[...], x, preferred_element_type=F32)

    def project(t, i):
        half = blocks.pop((t, i))
        total = None
        for k in range(ch):
            weight = ow_ref[k * SUB : (k + 1) * SUB, :]
            weight = jnp.concatenate([weight] * (tile // LANES), axis=1)
            term = weight * silu_twice(half[k * SUB : (k + 1) * SUB])
            total = term if total is None else total + term
        sums[t, i] = total
        if i == groups - 1:
            start = t * tile
            update = jnp.concatenate([sums.pop((t, n)) for n in range(groups)], axis=0)[0:bands]
            center = mid_ref[:, start : start + tile].astype(F32)[0:bands]
            out_ref[:, start : start + tile] = (center + update).astype(BF16)

    update_up_to(0)
    patches(0)
    spatial(0, 0)
    spatial(0, 1)
    update_up_to(1)
    activate(0, 0)
    patches(1)
    activate(0, 1)
    for t in range(tiles):
        if t + 1 < tiles:
            spatial(t + 1, 0)
        if t:
            project(t - 1, groups - 1)
        if t + 2 < tiles:
            update_up_to(t + 2)
        if t + 1 < tiles:
            spatial(t + 1, 1)
            activate(t + 1, 0)
        spectral(t, 0)
        if t + 1 < tiles:
            activate(t + 1, 1)
        for i in range(1, groups):
            spectral(t, i)
            project(t, i - 1)
        if t + 2 < tiles:
            patches(t + 2)
    project(tiles - 1, groups - 1)


def vmem(n):
    return [pl.BlockSpec(memory_space=pltpu.VMEM)] * n


def hbm(n):
    return [pl.BlockSpec(memory_space=pltpu.HBM)] * n


def in_hbm(arrays):
    return [pltpu.with_memory_space_constraint(x, pltpu.HBM) for x in arrays]


ANY = pl.BlockSpec(memory_space=pl.ANY)


def on_device(
    spectral_cube,
    aperture,
    measurement,
    shears,
    step_sizes,
    spatial_weight,
    spatial_bias,
    spectral_weight,
    spectral_bias,
    out_weight,
):
    bands, row_count, cols = spectral_cube.shape
    width = measurement.shape[1]
    reach = (width - cols) // LANES + 2
    outer = -(-width // LANES)
    groups = -(-bands // SUB)
    slots = (groups + 1) * SUB
    taps, ch = spectral_weight.shape[:2]
    taps2 = spatial_weight.shape[1]
    count = lax.axis_size("band")
    cube = spectral_cube.reshape(bands, cols)
    shear_row = shears.reshape(1, bands)
    step_row = step_sizes.reshape(1, bands)
    params = pltpu.CompilerParams(vmem_limit_bytes=48 * 2**20)

    tall = -(-outer // SUB) * SUB
    side = (cols // LANES // 2 + 2) * SUB
    inputs = (cube, aperture, measurement, shear_row, step_row)
    part, up, dn, *kept = pl.pallas_call(
        functools.partial(project_kernel, reach),
        out_shape=(
            jax.ShapeDtypeStruct((2 * tall, LANES), BF16),
            jax.ShapeDtypeStruct((2 * tall + side, LANES), BF16),
            jax.ShapeDtypeStruct((2 * tall + side, LANES), BF16),
        )
        + (jax.ShapeDtypeStruct((groups * SUB, cols), BF16),)
        + tuple(jax.ShapeDtypeStruct(x.shape, x.dtype) for x in inputs[1:]),
        in_specs=hbm(5),
        out_specs=tuple(vmem(8)),
        scratch_shapes=[
            pltpu.VMEM((bands, cols), BF16),
            pltpu.VMEM((groups * SUB, cols), F32),
            pltpu.SemaphoreType.DMA((5,)),
        ],
        compiler_params=params,
        name="project",
    )(*in_hbm(inputs))

    def around(x, shift):
        return lax.ppermute(x, "band", [(i, (i + shift) % count) for i in range(count)])

    below = around(up, 1)
    above = around(dn, -1)
    far = [around(part, s) for s in range(2, count - 1)]

    line = pl.pallas_call(
        gate_kernel,
        out_shape=jax.ShapeDtypeStruct(kept[0].shape, BF16),
        in_specs=[ANY, ANY],
        out_specs=ANY,
        input_output_aliases={1: 0},
        compiler_params=pltpu.CompilerParams(vmem_limit_bytes=2**20),
        name="gate",
    )(part, kept[0])

    lines = lax.axis_size(("row", "col"))
    pairs = [(i, i ^ 1) for i in range(lines)]
    others = [(i, (i - 1 + i % 2 * 2) % lines) for i in range(lines)]
    raw1 = lax.ppermute(kept[0], ("row", "col"), others)
    raw0 = lax.ppermute(line, ("row", "col"), pairs)

    small = (
        spatial_weight,
        spatial_bias.reshape(1, ch),
        spectral_weight,
        spectral_bias.reshape(1, ch),
        out_weight.reshape(1, ch),
    )
    reached = (SUB + taps - 1) * ch
    last = (bands - (groups - 1) * SUB + taps - 1) * ch
    main_w, halo_w, first_w, second_w, out_w = pl.pallas_call(
        weights_kernel,
        out_shape=(
            jax.ShapeDtypeStruct((16 * ch, taps2 * 16 + 16), BF16),
            jax.ShapeDtypeStruct((12 * ch, taps2 * 16 + 16), BF16),
            jax.ShapeDtypeStruct((SUB * ch, reached + 16), BF16),
            jax.ShapeDtypeStruct((SUB * ch, last + 16), BF16),
            jax.ShapeDtypeStruct((SUB * ch, LANES), F32),
        ),
        in_specs=[ANY] + hbm(5),
        out_specs=tuple(vmem(5)),
        scratch_shapes=[pltpu.VMEM(x.shape, x.dtype) for x in small]
        + [pltpu.SemaphoreType.DMA((5,))],
        compiler_params=params,
        name="weights",
    )(line, *in_hbm(small))

    words = (outer + 1) * SUB
    message, longer = pl.pallas_call(
        functools.partial(update_kernel, reach, len(far)),
        out_shape=(
            jax.ShapeDtypeStruct((words, LANES), BF16),
            jax.ShapeDtypeStruct((words + EXTRA, LANES), BF16),
        ),
        in_specs=vmem(5) + [ANY] + vmem(len(far)),
        out_specs=tuple(vmem(2)),
        scratch_shapes=[
            pltpu.VMEM((1, outer * LANES), F32),
            pltpu.VMEM((tall, LANES), F32),
        ],
        compiler_params=params,
        cost_estimate=pl.CostEstimate(
            flops=10**10, bytes_accessed=4 * 10**7, transcendentals=0
        ),
        name="update",
    )(*kept[1:3], part, below, above, out_w, *far)

    message0 = lax.ppermute(message, ("row", "col"), pairs)
    message1 = lax.ppermute(longer, ("row", "col"), others)

    def renewed(raw, words_of, after, name):
        return pl.pallas_call(
            functools.partial(neighbour_kernel, reach),
            out_shape=jax.ShapeDtypeStruct((slots, cols), BF16),
            in_specs=vmem(4) + [ANY],
            out_specs=vmem(1)[0],
            scratch_shapes=[pltpu.VMEM((words, LANES), F32)],
            compiler_params=params,
            cost_estimate=pl.CostEstimate(flops=1, bytes_accessed=1, transcendentals=0),
            name=name,
        )(kept[3], kept[4], raw, words_of, after)

    updated = renewed(kept[0], message, message, "own")
    near0 = renewed(raw0, message0, updated, "partner")

    tile = 512
    result = pl.pallas_call(
        functools.partial(denoise_kernel, tile, reach),
        out_shape=jax.ShapeDtypeStruct((bands, cols), BF16),
        in_specs=vmem(11),
        out_specs=vmem(1)[0],
        scratch_shapes=[
            pltpu.VMEM((4, 28 * ch, tile), BF16),
            pltpu.VMEM((slots, cols), BF16),
            pltpu.VMEM((words, LANES), F32),
        ],
        compiler_params=params,
        name="denoise",
    )(
        out_w,
        updated,
        kept[3],
        kept[4],
        near0,
        raw1,
        message1,
        main_w,
        halo_w,
        first_w,
        second_w,
    )
    return result.reshape(bands, 1, cols)


def solution(mesh):
    in_specs = (
        P("band", ("row", "col"), None),
        P(("row", "col"), None),
        P(("row", "col"), None),
        P("band"),
        P("band"),
        P(),
        P(),
        P(),
        P(),
        P(),
    )
    out_specs = P("band", ("row", "col"), None)
    return jax.shard_map(
        on_device, mesh=mesh, in_specs=in_specs, out_specs=out_specs, check_vma=False
    )
```

```python
import functools

import jax
import jax.numpy as jnp
from jax import lax
from jax.experimental import pallas as pl
from jax.experimental.pallas import tpu as pltpu
from jax.sharding import PartitionSpec as P

LANES = 128
SUB = 8
F32 = jnp.float32
BF16 = jnp.bfloat16
I32 = jnp.int32
COUNTER = 512.0
EXTRA = 16


def lanes_of(shape=(SUB, LANES)):
    return lax.broadcasted_iota(I32, shape, 1)


def rows_of(shape=(SUB, LANES)):
    return lax.broadcasted_iota(I32, shape, 0)


def column(row, rows):
    n = row.shape[1]
    eye = rows_of((rows, n)) == lanes_of((rows, n))
    return jnp.sum(jnp.where(eye, jnp.broadcast_to(row, (rows, n)), 0.0), axis=1, keepdims=True)


def turn(chunk, index):
    return jnp.take_along_axis(chunk, index, axis=1, mode="promise_in_bounds")


def choose(delay, options):
    result = options[-1]
    for d in range(len(options) - 2, -1, -1):
        result = jnp.where(delay == d, options[d], result)
    return result


def split3(x):
    hi = x.astype(BF16).astype(F32)
    mid = (x - hi).astype(BF16).astype(F32)
    return hi, mid, x - hi - mid


def fetch(sources, targets, sems):
    copies = [
        pltpu.make_async_copy(src, dst, sems.at[i]) for i, (src, dst) in enumerate(zip(sources, targets))
    ]
    for copy in copies:
        copy.start()
    return copies


def project_kernel(
    reach, cube_in, ap_in, meas_in, shear_in, step_in, part_ref, up_ref, dn_ref, *rest_refs
):
    line_ref, *kept = rest_refs[:5]
    cube_ref, raw, sems = rest_refs[5:]
    ap_ref, meas_ref, shear_ref, step_ref = kept
    copies = fetch((cube_in, ap_in, meas_in, shear_in, step_in), (cube_ref, *kept), sems)
    for copy in copies:
        copy.wait()
    bands, cols = cube_ref.shape
    groups = -(-bands // SUB)
    inner = cols // LANES
    tall = part_ref.shape[0] // 2
    outer = -(-meas_ref.shape[1] // LANES)
    raw[bands // SUB * SUB :, :] = jnp.zeros((raw.shape[0] - bands // SUB * SUB, cols), F32)
    raw[0:bands, :] = cube_ref[...].astype(F32)
    shear_f = column(shear_ref[...].astype(F32), groups * SUB)
    step_f = column(step_ref[...], groups * SUB)
    shear_i = shear_f.astype(I32)
    lane, sub = lanes_of(), rows_of()
    index, delay = [], []
    for g in range(groups):
        s = jnp.broadcast_to(shear_i[g * SUB : (g + 1) * SUB], (SUB, LANES))
        rest = s & (LANES - 1)
        index.append((lane - rest) & (LANES - 1))
        delay.append((s >> 7) + jnp.where(lane < rest, 1, 0))
    zero = jnp.zeros((SUB, LANES), F32)
    turned = [[zero] * (reach - 1) for _ in range(groups)]
    sums = [zero] * (tall // SUB)
    firsts, lasts = [], []
    for p in range(outer):
        total = zero
        if p < inner:
            open_p = jnp.broadcast_to(
                ap_ref[:, p * LANES : (p + 1) * LANES].astype(F32), (SUB, LANES)
            )
            layers = [
                raw[g * SUB : (g + 1) * SUB, p * LANES : (p + 1) * LANES] for g in range(groups)
            ]
            firsts.append(layers[0])
            lasts.append(layers[-1])
            tagged = jnp.where(sub == bands % SUB, open_p, layers[-1])
            line_ref[:, p * LANES : (p + 1) * LANES] = jnp.concatenate(
                layers[:-1] + [tagged], axis=0
            ).astype(BF16)
        for g in range(groups):
            if p < inner:
                here = (layers[g] + COUNTER) * open_p
                if (g + 1) * SUB > bands:
                    here = jnp.where(sub < bands - g * SUB, here, 0.0)
                here = turn(here, index[g])
            else:
                here = zero
            options = [here] + turned[g]
            turned[g] = options[:-1]
            total = total + choose(delay[g], options)
        v, at = divmod(p, SUB)
        sums[v] = jnp.where(sub == at, jnp.sum(total, axis=0, keepdims=True), sums[v])
    counts = [jnp.floor(x * (1.0 / COUNTER) + 0.5) for x in sums]
    sums = [x - COUNTER * n for x, n in zip(sums, counts)]
    sides = []
    for g in (0, groups - 1):
        s = shear_i[g * SUB : (g + 1) * SUB]
        parts = [(s >> 1).astype(F32), (s & 1).astype(F32)]
        parts += list(split3(step_f[g * SUB : (g + 1) * SUB]))
        side = zero
        for i, part in enumerate(parts):
            side = jnp.where(lane == i, part, side)
        sides.append(side)
    half = inner // 2
    dn = [
        jnp.where(sub < 3, firsts[q], pltpu.roll(firsts[q + half], 3, 0)) for q in range(half)
    ] + [sides[0], zero]
    up = [
        jnp.where(sub < 3, pltpu.roll(lasts[q + half], SUB - 3, 0), lasts[q]) for q in range(half)
    ] + [sides[1], zero]
    part_ref[...] = jnp.concatenate(sums + counts, axis=0).astype(BF16)
    up_ref[...] = jnp.concatenate(sums + counts + up, axis=0).astype(BF16)
    dn_ref[...] = jnp.concatenate(sums + counts + dn, axis=0).astype(BF16)


def update_kernel(
    reach, fars, ap_ref, meas_ref, own_ref, below_ref, above_ref, _, *rest_refs
):
    far_refs = rest_refs[:fars]
    msg_ref, long_ref, meas, rest_row = rest_refs[fars:]
    cols = ap_ref.shape[1]
    inner = cols // LANES
    half = inner // 2
    tall = own_ref.shape[0] // 2
    outer = -(-meas_ref.shape[1] // LANES)
    meas[:, (outer - 1) * LANES :] = jnp.zeros((1, LANES), F32)
    meas[:, 0 : meas_ref.shape[1]] = meas_ref[...]
    lane, sub = lanes_of(), rows_of()
    below = below_ref[...].astype(F32)
    above = above_ref[...].astype(F32)
    sums = own_ref[...].astype(F32) + below[0 : 2 * tall] + above[0 : 2 * tall]
    for far in far_refs:
        sums = sums + far[...].astype(F32)
    measured = []
    for v in range(tall // SUB):
        tile = jnp.zeros((SUB, LANES), F32)
        for at in range(min(SUB, outer - v * SUB)):
            p = v * SUB + at
            tile = jnp.where(sub == at, meas[:, p * LANES : (p + 1) * LANES], tile)
        measured.append(tile)
    measured = jnp.concatenate(measured, axis=0)
    rest_row[...] = (measured - sums[0:tall]) / jnp.maximum(sums[tall:], 1.0)

    def halo(q):
        at = 2 * tall + q % half * SUB
        high, low = above[at : at + SUB], below[at : at + SUB]
        if q // half == 1:
            high, low = pltpu.roll(high, SUB - 3, 0), pltpu.roll(low, 3, 0)
        return jnp.where(sub < 3, high, jnp.where(sub < 6, low, 0.0))

    side = 2 * tall + half * SUB
    side = jnp.where(sub < 3, above[side : side + SUB], below[side : side + SUB])
    inside = rows_of((SUB, 1)) < 6
    shear = jnp.where(inside, 2.0 * side[:, 0:1] + side[:, 1:2], 0.0)
    step = jnp.where(inside, side[:, 2:3] + side[:, 3:4] + side[:, 4:5], 0.0)
    shear = jnp.broadcast_to(shear.astype(I32), (SUB, LANES))
    step = jnp.broadcast_to(step, (SUB, LANES))
    rest = shear & (LANES - 1)
    index = (lane + rest) & (LANES - 1)
    delay = (shear >> 7) + jnp.where(lane + rest >= LANES, 1, 0)
    tiles = []
    turned = []
    for p in range(outer + 1):
        if p < outer:
            residual = jnp.broadcast_to(rest_row[p : p + 1, :], (SUB, LANES))
            turned.append(turn(residual, index))
        else:
            residual = jnp.zeros((SUB, LANES), F32)
            turned.append(residual)
        lost = residual - residual.astype(BF16).astype(F32)
        tiles.append(jnp.where(sub < 7, residual, lost))
        q = p - (reach - 1)
        if q < 0 or q >= inner:
            continue
        here = slice(q * LANES, (q + 1) * LANES)
        open_q = jnp.broadcast_to(ap_ref[:, here].astype(F32), (SUB, LANES))
        value = halo(q) + choose(delay, turned[q : q + reach]) * open_q * step
        tiles[q] = jnp.where(sub < 6, value, tiles[q])
    words = jnp.concatenate(tiles, axis=0).astype(BF16)
    msg_ref[...] = words
    long_ref[0 : words.shape[0], :] = words
    rest = (long_ref.shape[0] - words.shape[0], LANES)
    long_ref[words.shape[0] :, :] = jnp.zeros(rest, BF16)


def spread(rows, ch, which):
    return (which(rows_of((rows, ch))) == lanes_of((rows, ch))).astype(F32).astype(BF16)


def picked(row_ref, rows, which):
    ch = row_ref.shape[1]
    pick = which(rows_of((rows, ch))) == lanes_of((rows, ch))
    row = jnp.broadcast_to(row_ref[...], (rows, ch))
    return jnp.sum(jnp.where(pick, row, 0.0), axis=1, keepdims=True)


def with_bias(matrix, bias, start):
    lane = lanes_of(matrix.shape)
    for i, part in enumerate(split3(0.5 * bias)):
        matrix = jnp.where(lane == start + i, part, matrix)
    return matrix


def gate_kernel(_, line_ref, same_ref):
    pass


def weights_kernel(
    _, sw_in, sb_in, cw_in, cb_in, ow_in, main_ref, halo_ref, first_ref, second_ref, out_w_ref, *rest
):
    local, sems = rest[:5], rest[5]
    for copy in fetch((sw_in, sb_in, cw_in, cb_in, ow_in), local, sems):
        copy.wait()
    sw_ref, sb_ref, cw_ref, cb_ref, ow_ref = local
    ch, taps2 = sw_ref.shape
    taps = cw_ref.shape[0]
    place = lax.axis_index("band")
    has_low = jnp.where(place > 0, 1, 0)
    has_high = jnp.where(place < lax.axis_size("band") - 1, 1, 0)
    width = main_ref.shape[1]
    slots = 16
    line = lax.axis_index("row") * lax.axis_size("col") + lax.axis_index("col")
    lines = lax.axis_size("row") * lax.axis_size("col")
    group = lanes_of((taps2, width)) // slots
    offset = jnp.where(line % 2 == 1, group // 3, 2 - group // 3)
    present = (line + offset >= 1) & (line + offset <= lines)
    fan = (rows_of((taps2, width)) == 3 * offset + group % 3) & present
    fan = fan.astype(F32).astype(BF16)
    flat = jnp.dot(sw_ref[...], fan, preferred_element_type=F32).astype(BF16)
    for ref, slot_of in (
        (main_ref, lambda b: b),
        (halo_ref, lambda b: jnp.where(b < 3, 11 + b, jnp.where(b < 9, b - 3, b - 1))),
    ):
        rows = ref.shape[0]
        which = lambda r: r % ch
        full = jnp.dot(spread(rows, ch, which), flat, preferred_element_type=F32)
        lane = lanes_of((rows, width))
        band = rows_of((rows, width)) // ch
        keep = (lane % slots == slot_of(band)) & (lane < taps2 * slots)
        matrix = with_bias(
            jnp.where(keep, 0.5 * full, 0.0), picked(sb_ref, rows, which), taps2 * slots
        )
        if ref is halo_ref:
            valid = jnp.where(band < 3, has_low, jnp.where(band >= 9, has_high, 1))
            matrix = jnp.where(valid > 0, matrix, 0.0)
        ref[...] = matrix.astype(BF16)

    per = SUB
    rows = per * ch
    width = first_ref.shape[1]
    used = (per + taps - 1) * ch
    which = lambda r: r // per
    fan = (lanes_of((ch, width)) % ch == rows_of((ch, width))).astype(F32).astype(BF16)
    picks = spread(rows, ch, which)
    lane = lanes_of((rows, width))
    ahead = jnp.where(lane < used, lane // ch - rows_of((rows, width)) % per, -LANES)
    matrix = jnp.zeros((rows, width), F32)
    for d in range(taps):
        flat = jnp.dot(cw_ref[d], fan, preferred_element_type=F32).astype(BF16)
        full = 0.5 * jnp.dot(picks, flat, preferred_element_type=F32)
        matrix = jnp.where(ahead == d, full, matrix)
    bias = picked(cb_ref, rows, which)
    first_ref[...] = with_bias(matrix, bias, used).astype(BF16)
    short = second_ref.shape[1]
    start = short - 16
    matrix = jnp.where(lanes_of((rows, short)) < start, matrix[:, 0:short], 0.0)
    second_ref[...] = with_bias(matrix, bias, start).astype(BF16)
    out_w_ref[...] = jnp.broadcast_to(picked(ow_ref, rows, which), out_w_ref.shape)


def neighbour_chunks(reach, bands, shear_ref, step_ref, raw_ref, msg_ref, near, words):
    inner = raw_ref.shape[1] // LANES
    groups = -(-bands // SUB)
    zero = jnp.zeros((SUB, LANES), F32)
    shear_f = column(shear_ref[...].astype(F32), groups * SUB)
    step_f = column(step_ref[...], groups * SUB)
    lane = lanes_of()
    index, delay, steps = [], [], []
    for g in range(groups):
        s = jnp.broadcast_to(shear_f[g * SUB : (g + 1) * SUB].astype(I32), (SUB, LANES))
        rest = s & (LANES - 1)
        index.append((lane + rest) & (LANES - 1))
        delay.append((s >> 7) + jnp.where(lane + rest >= LANES, 1, 0))
        steps.append(jnp.broadcast_to(step_f[g * SUB : (g + 1) * SUB], (SUB, LANES)))
    chunks = inner + reach - 1
    words[...] = msg_ref[0 : words.shape[0], :].astype(F32)
    turned = [[] for _ in range(groups)]

    def make(q):
        while len(turned[0]) < q + reach:
            p = len(turned[0])
            if p >= chunks:
                residual = zero
            else:
                at = p * SUB + 6
                residual = words[at : at + 1, :] + words[at + 1 : at + 2, :]
                residual = jnp.broadcast_to(residual, (SUB, LANES))
            for g in range(groups):
                turned[g].append(turn(residual, index[g]))
        raw = raw_ref[:, q * LANES : (q + 1) * LANES].astype(F32)
        open_q = jnp.broadcast_to(raw[bands : bands + 1], (SUB, LANES))
        pieces = [
            raw[g * SUB : (g + 1) * SUB]
            + choose(delay[g], turned[g][q : q + reach]) * open_q * steps[g]
            for g in range(groups)
        ]
        pieces.append(words[q * SUB : (q + 1) * SUB, :])
        near[:, q * LANES : (q + 1) * LANES] = jnp.concatenate(pieces, axis=0).astype(BF16)

    return make


def shifted(ref, start, end):
    rows, cols = ref.shape
    blank = jnp.zeros((rows, LANES), BF16)
    left = ref[:, start - LANES : start] if start else blank
    here = ref[:, start:end]
    right = ref[:, end : end + LANES] if end < cols else blank
    row = jnp.concatenate([left, here, right], axis=1)
    width = end - start
    back = pltpu.roll(row, 1, 1)[:, LANES : LANES + width]
    ahead = pltpu.roll(row, row.shape[1] - 1, 1)[:, LANES : LANES + width]
    return back, here, ahead


def neighbour_kernel(tile, reach, shear_ref, step_ref, raw_ref, msg_ref, _, out_ref, near, words):
    bands = shear_ref.shape[1]
    make = neighbour_chunks(reach, bands, shear_ref, step_ref, raw_ref, msg_ref, near, words)
    cols = near.shape[1]
    slots = near.shape[0] // 2
    made = 0
    for start in range(0, cols, tile):
        while made < min((start + tile) // LANES + 1, cols // LANES):
            make(made)
            made += 1
        three = shifted(near, start, start + tile)
        for part in range(2):
            rows = [x[part * slots : (part + 1) * slots] for x in three]
            out_ref[part * 3 * slots : (part + 1) * 3 * slots, start : start + tile] = (
                jnp.concatenate(rows, axis=0)
            )


def denoise_kernel(
    tile,
    reach,
    ow_ref,
    mid_ref,
    shear_ref,
    step_ref,
    near0,
    raw_ref,
    msg_ref,
    main_ref,
    halo_ref,
    first_ref,
    second_ref,
    out_ref,
    act,
    near1,
    words,
):
    bands, cols = out_ref.shape
    slots = 16
    ch = main_ref.shape[0] // slots
    tiles = cols // tile
    inner = cols // LANES
    groups = -(-bands // SUB)
    ones = jnp.where(rows_of((slots, tile)) < 3, 1.0, 0.0).astype(BF16)
    neighbours = neighbour_chunks(
        reach, bands, shear_ref, step_ref, raw_ref, msg_ref, near1, words
    )

    def silu_twice(half):
        return half + half * jnp.tanh(half)

    inputs, halves, blocks, sums = {}, {}, {}, {}
    made = 0

    def update_up_to(t):
        nonlocal made
        while made < min((t + 1) * tile // LANES + 1, inner):
            neighbours(made)
            made += 1

    def patches(t):
        start = t * tile
        end = start + tile
        three = shifted(near1, start, end)
        for part in range(2):
            rows = slice(part * 3 * slots, (part + 1) * 3 * slots)
            x = [near0[rows, start:end], mid_ref[rows, start:end]]
            x += [p[part * slots : (part + 1) * slots] for p in three]
            inputs[t, part] = jnp.concatenate(x + [ones], axis=0)

    def spatial(t, part):
        w_ref = halo_ref if part else main_ref
        halves[t, part] = jnp.dot(
            w_ref[...], inputs.pop((t, part)), preferred_element_type=F32
        )

    def activate(t, part):
        buf = act.at[t % act.shape[0]]
        value = silu_twice(halves.pop((t, part))).astype(BF16)
        if part == 0:
            buf[3 * ch : 19 * ch, :] = value
        else:
            buf[0 : 3 * ch, :] = value[0 : 3 * ch]
            buf[19 * ch : 28 * ch, :] = value[3 * ch :]

    def spectral(t, i):
        buf = act.at[t % act.shape[0]]
        w_ref = second_ref if i == groups - 1 else first_ref
        first = i * SUB * ch
        x = jnp.concatenate([buf[first : first + w_ref.shape[1] - slots, :], ones], axis=0)
        blocks[t, i] = jnp.dot(w_ref[...], x, preferred_element_type=F32)

    def project(t, i):
        half = blocks.pop((t, i))
        total = None
        for k in range(ch):
            weight = ow_ref[k * SUB : (k + 1) * SUB, :]
            weight = jnp.concatenate([weight] * (tile // LANES), axis=1)
            term = weight * silu_twice(half[k * SUB : (k + 1) * SUB])
            total = term if total is None else total + term
        sums[t, i] = total
        if i == groups - 1:
            start = t * tile
            update = jnp.concatenate([sums.pop((t, n)) for n in range(groups)], axis=0)[0:bands]
            center = [
                mid_ref[at : at + slots, start : start + tile].astype(F32)
                for at in (slots, 4 * slots)
            ]
            center = jnp.concatenate(center, axis=0)[0:bands]
            out_ref[:, start : start + tile] = (center + update).astype(BF16)

    update_up_to(0)
    patches(0)
    spatial(0, 0)
    spatial(0, 1)
    update_up_to(1)
    activate(0, 0)
    patches(1)
    activate(0, 1)
    for t in range(tiles):
        if t + 1 < tiles:
            spatial(t + 1, 0)
        if t:
            project(t - 1, groups - 1)
        if t + 2 < tiles:
            update_up_to(t + 2)
        if t + 1 < tiles:
            spatial(t + 1, 1)
            activate(t + 1, 0)
        spectral(t, 0)
        if t + 1 < tiles:
            activate(t + 1, 1)
        for i in range(1, groups):
            spectral(t, i)
            project(t, i - 1)
        if t + 2 < tiles:
            patches(t + 2)
    project(tiles - 1, groups - 1)


def vmem(n):
    return [pl.BlockSpec(memory_space=pltpu.VMEM)] * n


def hbm(n):
    return [pl.BlockSpec(memory_space=pltpu.HBM)] * n


def in_hbm(arrays):
    return [pltpu.with_memory_space_constraint(x, pltpu.HBM) for x in arrays]


ANY = pl.BlockSpec(memory_space=pl.ANY)


def on_device(
    spectral_cube,
    aperture,
    measurement,
    shears,
    step_sizes,
    spatial_weight,
    spatial_bias,
    spectral_weight,
    spectral_bias,
    out_weight,
):
    bands, row_count, cols = spectral_cube.shape
    width = measurement.shape[1]
    reach = (width - cols) // LANES + 2
    outer = -(-width // LANES)
    groups = -(-bands // SUB)
    slots = (groups + 1) * SUB
    taps, ch = spectral_weight.shape[:2]
    taps2 = spatial_weight.shape[1]
    count = lax.axis_size("band")
    cube = spectral_cube.reshape(bands, cols)
    shear_row = shears.reshape(1, bands)
    step_row = step_sizes.reshape(1, bands)
    params = pltpu.CompilerParams(vmem_limit_bytes=48 * 2**20)

    tall = -(-outer // SUB) * SUB
    side = (cols // LANES // 2 + 2) * SUB
    inputs = (cube, aperture, measurement, shear_row, step_row)
    part, up, dn, *kept = pl.pallas_call(
        functools.partial(project_kernel, reach),
        out_shape=(
            jax.ShapeDtypeStruct((2 * tall, LANES), BF16),
            jax.ShapeDtypeStruct((2 * tall + side, LANES), BF16),
            jax.ShapeDtypeStruct((2 * tall + side, LANES), BF16),
        )
        + (jax.ShapeDtypeStruct((groups * SUB, cols), BF16),)
        + tuple(jax.ShapeDtypeStruct(x.shape, x.dtype) for x in inputs[1:]),
        in_specs=hbm(5),
        out_specs=tuple(vmem(8)),
        scratch_shapes=[
            pltpu.VMEM((bands, cols), BF16),
            pltpu.VMEM((groups * SUB, cols), F32),
            pltpu.SemaphoreType.DMA((5,)),
        ],
        compiler_params=params,
        name="project",
    )(*in_hbm(inputs))

    def around(x, shift):
        return lax.ppermute(x, "band", [(i, (i + shift) % count) for i in range(count)])

    below = around(up, 1)
    above = around(dn, -1)
    far = [around(part, s) for s in range(2, count - 1)]

    line = pl.pallas_call(
        gate_kernel,
        out_shape=jax.ShapeDtypeStruct(kept[0].shape, BF16),
        in_specs=[ANY, ANY],
        out_specs=ANY,
        input_output_aliases={1: 0},
        compiler_params=pltpu.CompilerParams(vmem_limit_bytes=2**20),
        name="gate",
    )(part, kept[0])

    lines = lax.axis_size(("row", "col"))
    pairs = [(i, i ^ 1) for i in range(lines)]
    others = [(i, (i - 1 + i % 2 * 2) % lines) for i in range(lines)]
    raw1 = lax.ppermute(kept[0], ("row", "col"), others)
    raw0 = lax.ppermute(line, ("row", "col"), pairs)

    small = (
        spatial_weight,
        spatial_bias.reshape(1, ch),
        spectral_weight,
        spectral_bias.reshape(1, ch),
        out_weight.reshape(1, ch),
    )
    reached = (SUB + taps - 1) * ch
    last = (bands - (groups - 1) * SUB + taps - 1) * ch
    main_w, halo_w, first_w, second_w, out_w = pl.pallas_call(
        weights_kernel,
        out_shape=(
            jax.ShapeDtypeStruct((16 * ch, taps2 * 16 + 16), BF16),
            jax.ShapeDtypeStruct((12 * ch, taps2 * 16 + 16), BF16),
            jax.ShapeDtypeStruct((SUB * ch, reached + 16), BF16),
            jax.ShapeDtypeStruct((SUB * ch, last + 16), BF16),
            jax.ShapeDtypeStruct((SUB * ch, LANES), F32),
        ),
        in_specs=[ANY] + hbm(5),
        out_specs=tuple(vmem(5)),
        scratch_shapes=[pltpu.VMEM(x.shape, x.dtype) for x in small]
        + [pltpu.SemaphoreType.DMA((5,))],
        compiler_params=params,
        name="weights",
    )(line, *in_hbm(small))

    words = (outer + 1) * SUB
    message, longer = pl.pallas_call(
        functools.partial(update_kernel, reach, len(far)),
        out_shape=(
            jax.ShapeDtypeStruct((words, LANES), BF16),
            jax.ShapeDtypeStruct((words + EXTRA, LANES), BF16),
        ),
        in_specs=vmem(5) + [ANY] + vmem(len(far)),
        out_specs=tuple(vmem(2)),
        scratch_shapes=[
            pltpu.VMEM((1, outer * LANES), F32),
            pltpu.VMEM((tall, LANES), F32),
        ],
        compiler_params=params,
        cost_estimate=pl.CostEstimate(
            flops=10**10, bytes_accessed=4 * 10**7, transcendentals=0
        ),
        name="update",
    )(*kept[1:3], part, below, above, out_w, *far)

    message0 = lax.ppermute(message, ("row", "col"), pairs)
    message1 = lax.ppermute(longer, ("row", "col"), others)

    tile = 512

    def renewed(raw, words_of, after, name):
        return pl.pallas_call(
            functools.partial(neighbour_kernel, tile, reach),
            out_shape=jax.ShapeDtypeStruct((3 * slots, cols), BF16),
            in_specs=vmem(4) + [ANY],
            out_specs=vmem(1)[0],
            scratch_shapes=[pltpu.VMEM((slots, cols), BF16), pltpu.VMEM((words, LANES), F32)],
            compiler_params=params,
            cost_estimate=pl.CostEstimate(flops=1, bytes_accessed=1, transcendentals=0),
            name=name,
        )(kept[3], kept[4], raw, words_of, after)

    updated = renewed(kept[0], message, message, "own")
    near0 = renewed(raw0, message0, updated, "partner")

    result = pl.pallas_call(
        functools.partial(denoise_kernel, tile, reach),
        out_shape=jax.ShapeDtypeStruct((bands, cols), BF16),
        in_specs=vmem(11),
        out_specs=vmem(1)[0],
        scratch_shapes=[
            pltpu.VMEM((4, 28 * ch, tile), BF16),
            pltpu.VMEM((slots, cols), BF16),
            pltpu.VMEM((words, LANES), F32),
        ],
        compiler_params=params,
        name="denoise",
    )(
        out_w,
        updated,
        kept[3],
        kept[4],
        near0,
        raw1,
        message1,
        main_w,
        halo_w,
        first_w,
        second_w,
    )
    return result.reshape(bands, 1, cols)


def solution(mesh):
    in_specs = (
        P("band", ("row", "col"), None),
        P(("row", "col"), None),
        P(("row", "col"), None),
        P("band"),
        P("band"),
        P(),
        P(),
        P(),
        P(),
        P(),
    )
    out_specs = P("band", ("row", "col"), None)
    return jax.shard_map(
        on_device, mesh=mesh, in_specs=in_specs, out_specs=out_specs, check_vma=False
    )
```

```python
import functools

import jax
import jax.numpy as jnp
from jax import lax
from jax.experimental import pallas as pl
from jax.experimental.pallas import tpu as pltpu
from jax.sharding import PartitionSpec as P

LANES = 128
SUB = 8
F32 = jnp.float32
BF16 = jnp.bfloat16
I32 = jnp.int32
COUNTER = 512.0
EXTRA = 16


def lanes_of(shape=(SUB, LANES)):
    return lax.broadcasted_iota(I32, shape, 1)


def rows_of(shape=(SUB, LANES)):
    return lax.broadcasted_iota(I32, shape, 0)


def column(row, rows):
    n = row.shape[1]
    eye = rows_of((rows, n)) == lanes_of((rows, n))
    return jnp.sum(jnp.where(eye, jnp.broadcast_to(row, (rows, n)), 0.0), axis=1, keepdims=True)


def turn(chunk, index):
    return jnp.take_along_axis(chunk, index, axis=1, mode="promise_in_bounds")


def choose(delay, options):
    result = options[-1]
    for d in range(len(options) - 2, -1, -1):
        result = jnp.where(delay == d, options[d], result)
    return result


def split3(x):
    hi = x.astype(BF16).astype(F32)
    mid = (x - hi).astype(BF16).astype(F32)
    return hi, mid, x - hi - mid


def fetch(sources, targets, sems):
    copies = [
        pltpu.make_async_copy(src, dst, sems.at[i]) for i, (src, dst) in enumerate(zip(sources, targets))
    ]
    for copy in copies:
        copy.start()
    return copies


def project_kernel(
    reach, cube_in, ap_in, meas_in, shear_in, step_in, part_ref, up_ref, dn_ref, *rest_refs
):
    line_ref, *kept = rest_refs[:5]
    cube_ref, raw, sems = rest_refs[5:]
    ap_ref, meas_ref, shear_ref, step_ref = kept
    copies = fetch((cube_in, ap_in, meas_in, shear_in, step_in), (cube_ref, *kept), sems)
    for copy in copies:
        copy.wait()
    bands, cols = cube_ref.shape
    groups = -(-bands // SUB)
    inner = cols // LANES
    tall = part_ref.shape[0] // 2
    outer = -(-meas_ref.shape[1] // LANES)
    raw[bands // SUB * SUB :, :] = jnp.zeros((raw.shape[0] - bands // SUB * SUB, cols), F32)
    raw[0:bands, :] = cube_ref[...].astype(F32)
    shear_f = column(shear_ref[...].astype(F32), groups * SUB)
    step_f = column(step_ref[...], groups * SUB)
    shear_i = shear_f.astype(I32)
    lane, sub = lanes_of(), rows_of()
    index, delay = [], []
    for g in range(groups):
        s = jnp.broadcast_to(shear_i[g * SUB : (g + 1) * SUB], (SUB, LANES))
        rest = s & (LANES - 1)
        index.append((lane - rest) & (LANES - 1))
        delay.append((s >> 7) + jnp.where(lane < rest, 1, 0))
    zero = jnp.zeros((SUB, LANES), F32)
    turned = [[zero] * (reach - 1) for _ in range(groups)]
    sums = [zero] * (tall // SUB)
    firsts, lasts = [], []
    for p in range(outer):
        total = zero
        if p < inner:
            open_p = jnp.broadcast_to(
                ap_ref[:, p * LANES : (p + 1) * LANES].astype(F32), (SUB, LANES)
            )
            layers = [
                raw[g * SUB : (g + 1) * SUB, p * LANES : (p + 1) * LANES] for g in range(groups)
            ]
            firsts.append(layers[0])
            lasts.append(layers[-1])
            tagged = jnp.where(sub == bands % SUB, open_p, layers[-1])
            line_ref[:, p * LANES : (p + 1) * LANES] = jnp.concatenate(
                layers[:-1] + [tagged], axis=0
            ).astype(BF16)
        for g in range(groups):
            if p < inner:
                here = (layers[g] + COUNTER) * open_p
                if (g + 1) * SUB > bands:
                    here = jnp.where(sub < bands - g * SUB, here, 0.0)
                here = turn(here, index[g])
            else:
                here = zero
            options = [here] + turned[g]
            turned[g] = options[:-1]
            total = total + choose(delay[g], options)
        v, at = divmod(p, SUB)
        sums[v] = jnp.where(sub == at, jnp.sum(total, axis=0, keepdims=True), sums[v])
    counts = [jnp.floor(x * (1.0 / COUNTER) + 0.5) for x in sums]
    sums = [x - COUNTER * n for x, n in zip(sums, counts)]
    sides = []
    for g in (0, groups - 1):
        s = shear_i[g * SUB : (g + 1) * SUB]
        parts = [(s >> 1).astype(F32), (s & 1).astype(F32)]
        parts += list(split3(step_f[g * SUB : (g + 1) * SUB]))
        side = zero
        for i, part in enumerate(parts):
            side = jnp.where(lane == i, part, side)
        sides.append(side)
    half = inner // 2
    dn = [
        jnp.where(sub < 3, firsts[q], pltpu.roll(firsts[q + half], 3, 0)) for q in range(half)
    ] + [sides[0], zero]
    up = [
        jnp.where(sub < 3, pltpu.roll(lasts[q + half], SUB - 3, 0), lasts[q]) for q in range(half)
    ] + [sides[1], zero]
    part_ref[...] = jnp.concatenate(sums + counts, axis=0).astype(BF16)
    up_ref[...] = jnp.concatenate(sums + counts + up, axis=0).astype(BF16)
    dn_ref[...] = jnp.concatenate(sums + counts + dn, axis=0).astype(BF16)


def update_kernel(
    reach, fars, ap_ref, meas_ref, own_ref, below_ref, above_ref, _, *rest_refs
):
    far_refs = rest_refs[:fars]
    msg_ref, long_ref, meas, rest_row = rest_refs[fars:]
    cols = ap_ref.shape[1]
    inner = cols // LANES
    half = inner // 2
    tall = own_ref.shape[0] // 2
    outer = -(-meas_ref.shape[1] // LANES)
    meas[:, (outer - 1) * LANES :] = jnp.zeros((1, LANES), F32)
    meas[:, 0 : meas_ref.shape[1]] = meas_ref[...]
    lane, sub = lanes_of(), rows_of()
    below = below_ref[...].astype(F32)
    above = above_ref[...].astype(F32)
    sums = own_ref[...].astype(F32) + below[0 : 2 * tall] + above[0 : 2 * tall]
    for far in far_refs:
        sums = sums + far[...].astype(F32)
    measured = []
    for v in range(tall // SUB):
        tile = jnp.zeros((SUB, LANES), F32)
        for at in range(min(SUB, outer - v * SUB)):
            p = v * SUB + at
            tile = jnp.where(sub == at, meas[:, p * LANES : (p + 1) * LANES], tile)
        measured.append(tile)
    measured = jnp.concatenate(measured, axis=0)
    rest_row[...] = (measured - sums[0:tall]) / jnp.maximum(sums[tall:], 1.0)

    def halo(q):
        at = 2 * tall + q % half * SUB
        high, low = above[at : at + SUB], below[at : at + SUB]
        if q // half == 1:
            high, low = pltpu.roll(high, SUB - 3, 0), pltpu.roll(low, 3, 0)
        return jnp.where(sub < 3, high, jnp.where(sub < 6, low, 0.0))

    side = 2 * tall + half * SUB
    side = jnp.where(sub < 3, above[side : side + SUB], below[side : side + SUB])
    inside = rows_of((SUB, 1)) < 6
    shear = jnp.where(inside, 2.0 * side[:, 0:1] + side[:, 1:2], 0.0)
    step = jnp.where(inside, side[:, 2:3] + side[:, 3:4] + side[:, 4:5], 0.0)
    shear = jnp.broadcast_to(shear.astype(I32), (SUB, LANES))
    step = jnp.broadcast_to(step, (SUB, LANES))
    rest = shear & (LANES - 1)
    index = (lane + rest) & (LANES - 1)
    delay = (shear >> 7) + jnp.where(lane + rest >= LANES, 1, 0)
    tiles = []
    turned = []
    for p in range(outer + 1):
        if p < outer:
            residual = jnp.broadcast_to(rest_row[p : p + 1, :], (SUB, LANES))
            turned.append(turn(residual, index))
        else:
            residual = jnp.zeros((SUB, LANES), F32)
            turned.append(residual)
        lost = residual - residual.astype(BF16).astype(F32)
        tiles.append(jnp.where(sub < 7, residual, lost))
        q = p - (reach - 1)
        if q < 0 or q >= inner:
            continue
        here = slice(q * LANES, (q + 1) * LANES)
        open_q = jnp.broadcast_to(ap_ref[:, here].astype(F32), (SUB, LANES))
        value = halo(q) + choose(delay, turned[q : q + reach]) * open_q * step
        tiles[q] = jnp.where(sub < 6, value, tiles[q])
    words = jnp.concatenate(tiles, axis=0).astype(BF16)
    msg_ref[...] = words
    long_ref[0 : words.shape[0], :] = words
    rest = (long_ref.shape[0] - words.shape[0], LANES)
    long_ref[words.shape[0] :, :] = jnp.zeros(rest, BF16)


def spread(rows, ch, which):
    return (which(rows_of((rows, ch))) == lanes_of((rows, ch))).astype(F32).astype(BF16)


def picked(row_ref, rows, which):
    ch = row_ref.shape[1]
    pick = which(rows_of((rows, ch))) == lanes_of((rows, ch))
    row = jnp.broadcast_to(row_ref[...], (rows, ch))
    return jnp.sum(jnp.where(pick, row, 0.0), axis=1, keepdims=True)


def with_bias(matrix, bias, start):
    lane = lanes_of(matrix.shape)
    for i, part in enumerate(split3(0.5 * bias)):
        matrix = jnp.where(lane == start + i, part, matrix)
    return matrix


def gate_kernel(_, line_ref, same_ref):
    pass


def weights_kernel(
    _, sw_in, sb_in, cw_in, cb_in, ow_in, main_ref, halo_ref, first_ref, second_ref, out_w_ref, *rest
):
    local, sems = rest[:5], rest[5]
    for copy in fetch((sw_in, sb_in, cw_in, cb_in, ow_in), local, sems):
        copy.wait()
    sw_ref, sb_ref, cw_ref, cb_ref, ow_ref = local
    ch, taps2 = sw_ref.shape
    taps = cw_ref.shape[0]
    place = lax.axis_index("band")
    has_low = jnp.where(place > 0, 1, 0)
    has_high = jnp.where(place < lax.axis_size("band") - 1, 1, 0)
    width = main_ref.shape[1]
    slots = 16
    line = lax.axis_index("row") * lax.axis_size("col") + lax.axis_index("col")
    lines = lax.axis_size("row") * lax.axis_size("col")
    group = lanes_of((taps2, width)) // slots
    offset = jnp.where(line % 2 == 1, group // 3, 2 - group // 3)
    present = (line + offset >= 1) & (line + offset <= lines)
    fan = (rows_of((taps2, width)) == 3 * offset + group % 3) & present
    fan = fan.astype(F32).astype(BF16)
    flat = jnp.dot(sw_ref[...], fan, preferred_element_type=F32).astype(BF16)
    for ref, slot_of in (
        (main_ref, lambda b: b),
        (halo_ref, lambda b: jnp.where(b < 3, 11 + b, jnp.where(b < 9, b - 3, b - 1))),
    ):
        rows = ref.shape[0]
        which = lambda r: r % ch
        full = jnp.dot(spread(rows, ch, which), flat, preferred_element_type=F32)
        lane = lanes_of((rows, width))
        band = rows_of((rows, width)) // ch
        keep = (lane % slots == slot_of(band)) & (lane < taps2 * slots)
        matrix = with_bias(
            jnp.where(keep, 0.5 * full, 0.0), picked(sb_ref, rows, which), taps2 * slots
        )
        if ref is halo_ref:
            valid = jnp.where(band < 3, has_low, jnp.where(band >= 9, has_high, 1))
            matrix = jnp.where(valid > 0, matrix, 0.0)
        ref[...] = matrix.astype(BF16)

    per = SUB
    rows = per * ch
    width = first_ref.shape[1]
    used = (per + taps - 1) * ch
    which = lambda r: r // per
    fan = (lanes_of((ch, width)) % ch == rows_of((ch, width))).astype(F32).astype(BF16)
    picks = spread(rows, ch, which)
    lane = lanes_of((rows, width))
    ahead = jnp.where(lane < used, lane // ch - rows_of((rows, width)) % per, -LANES)
    matrix = jnp.zeros((rows, width), F32)
    for d in range(taps):
        flat = jnp.dot(cw_ref[d], fan, preferred_element_type=F32).astype(BF16)
        full = 0.5 * jnp.dot(picks, flat, preferred_element_type=F32)
        matrix = jnp.where(ahead == d, full, matrix)
    bias = picked(cb_ref, rows, which)
    first_ref[...] = with_bias(matrix, bias, used).astype(BF16)
    short = second_ref.shape[1]
    start = short - 16
    matrix = jnp.where(lanes_of((rows, short)) < start, matrix[:, 0:short], 0.0)
    second_ref[...] = with_bias(matrix, bias, start).astype(BF16)
    out_w_ref[...] = jnp.broadcast_to(picked(ow_ref, rows, which), out_w_ref.shape)


def neighbour_chunks(reach, bands, shear_ref, step_ref, raw_ref, msg_ref, near, words):
    inner = raw_ref.shape[1] // LANES
    groups = -(-bands // SUB)
    zero = jnp.zeros((SUB, LANES), F32)
    shear_f = column(shear_ref[...].astype(F32), groups * SUB)
    step_f = column(step_ref[...], groups * SUB)
    lane = lanes_of()
    index, delay, steps = [], [], []
    for g in range(groups):
        s = jnp.broadcast_to(shear_f[g * SUB : (g + 1) * SUB].astype(I32), (SUB, LANES))
        rest = s & (LANES - 1)
        index.append((lane + rest) & (LANES - 1))
        delay.append((s >> 7) + jnp.where(lane + rest >= LANES, 1, 0))
        steps.append(jnp.broadcast_to(step_f[g * SUB : (g + 1) * SUB], (SUB, LANES)))
    chunks = inner + reach - 1
    words[...] = msg_ref[0 : words.shape[0], :].astype(F32)
    turned = [[] for _ in range(groups)]

    def make(q):
        while len(turned[0]) < q + reach:
            p = len(turned[0])
            if p >= chunks:
                residual = zero
            else:
                at = p * SUB + 6
                residual = words[at : at + 1, :] + words[at + 1 : at + 2, :]
                residual = jnp.broadcast_to(residual, (SUB, LANES))
            for g in range(groups):
                turned[g].append(turn(residual, index[g]))
        raw = raw_ref[:, q * LANES : (q + 1) * LANES].astype(F32)
        open_q = jnp.broadcast_to(raw[bands : bands + 1], (SUB, LANES))
        pieces = [
            raw[g * SUB : (g + 1) * SUB]
            + choose(delay[g], turned[g][q : q + reach]) * open_q * steps[g]
            for g in range(groups)
        ]
        pieces.append(words[q * SUB : (q + 1) * SUB, :])
        near[:, q * LANES : (q + 1) * LANES] = jnp.concatenate(pieces, axis=0).astype(BF16)

    return make


def shifted(ref, start, end):
    rows, cols = ref.shape
    blank = jnp.zeros((rows, LANES), BF16)
    left = ref[:, start - LANES : start] if start else blank
    here = ref[:, start:end]
    right = ref[:, end : end + LANES] if end < cols else blank
    row = jnp.concatenate([left, here, right], axis=1)
    width = end - start
    back = pltpu.roll(row, 1, 1)[:, LANES : LANES + width]
    ahead = pltpu.roll(row, row.shape[1] - 1, 1)[:, LANES : LANES + width]
    return back, here, ahead


def neighbour_kernel(tile, reach, shear_ref, step_ref, raw_ref, msg_ref, _, out_ref, near, words):
    bands = shear_ref.shape[1]
    make = neighbour_chunks(reach, bands, shear_ref, step_ref, raw_ref, msg_ref, near, words)
    cols = near.shape[1]
    slots = near.shape[0] // 2
    made = 0
    for start in range(0, cols, tile):
        while made < min((start + tile) // LANES + 1, cols // LANES):
            make(made)
            made += 1
        three = shifted(near, start, start + tile)
        for part in range(2):
            rows = [x[part * slots : (part + 1) * slots] for x in three]
            out_ref[part * 3 * slots : (part + 1) * 3 * slots, start : start + tile] = (
                jnp.concatenate(rows, axis=0)
            )


def denoise_kernel(
    tile,
    reach,
    ow_ref,
    mid_ref,
    shear_ref,
    step_ref,
    near0,
    raw_ref,
    msg_ref,
    main_ref,
    halo_ref,
    first_ref,
    second_ref,
    out_ref,
    act,
    near1,
    words,
):
    bands, cols = out_ref.shape
    slots = 16
    ch = main_ref.shape[0] // slots
    tiles = cols // tile
    inner = cols // LANES
    groups = -(-bands // SUB)
    ones = jnp.where(rows_of((slots, tile)) < 3, 1.0, 0.0).astype(BF16)
    neighbours = neighbour_chunks(
        reach, bands, shear_ref, step_ref, raw_ref, msg_ref, near1, words
    )

    def silu_twice(half):
        return half + half * jnp.tanh(half)

    inputs, halves, blocks, sums = {}, {}, {}, {}
    made = 0

    def update_up_to(t):
        nonlocal made
        while made < min((t + 1) * tile // LANES + 1, inner):
            neighbours(made)
            made += 1

    def patches(t):
        start = t * tile
        end = start + tile
        three = shifted(near1, start, end)
        for part in range(2):
            rows = slice(part * 3 * slots, (part + 1) * 3 * slots)
            x = [near0[rows, start:end], mid_ref[rows, start:end]]
            x += [p[part * slots : (part + 1) * slots] for p in three]
            inputs[t, part] = jnp.concatenate(x + [ones], axis=0)

    def spatial(t, part):
        w_ref = halo_ref if part else main_ref
        halves[t, part] = jnp.dot(
            w_ref[...], inputs.pop((t, part)), preferred_element_type=F32
        )

    def activate(t, part):
        buf = act.at[t % act.shape[0]]
        value = silu_twice(halves.pop((t, part))).astype(BF16)
        if part == 0:
            buf[3 * ch : 19 * ch, :] = value
        else:
            buf[0 : 3 * ch, :] = value[0 : 3 * ch]
            buf[19 * ch : 28 * ch, :] = value[3 * ch :]

    def spectral(t, i):
        buf = act.at[t % act.shape[0]]
        w_ref = second_ref if i == groups - 1 else first_ref
        first = i * SUB * ch
        x = jnp.concatenate([buf[first : first + w_ref.shape[1] - slots, :], ones], axis=0)
        blocks[t, i] = jnp.dot(w_ref[...], x, preferred_element_type=F32)

    def project(t, i):
        half = blocks.pop((t, i))
        total = None
        for k in range(ch):
            weight = ow_ref[k * SUB : (k + 1) * SUB, :]
            weight = jnp.concatenate([weight] * (tile // LANES), axis=1)
            term = weight * silu_twice(half[k * SUB : (k + 1) * SUB])
            total = term if total is None else total + term
        sums[t, i] = total
        if i == groups - 1:
            start = t * tile
            update = jnp.concatenate([sums.pop((t, n)) for n in range(groups)], axis=0)[0:bands]
            center = [
                mid_ref[at : at + slots, start : start + tile].astype(F32)
                for at in (slots, 4 * slots)
            ]
            center = jnp.concatenate(center, axis=0)[0:bands]
            out_ref[:, start : start + tile] = (center + update).astype(BF16)

    update_up_to(0)
    patches(0)
    spatial(0, 0)
    spatial(0, 1)
    update_up_to(1)
    activate(0, 0)
    patches(1)
    activate(0, 1)
    for t in range(tiles):
        if t + 1 < tiles:
            spatial(t + 1, 0)
        if t:
            project(t - 1, groups - 1)
        if t + 2 < tiles:
            update_up_to(t + 2)
        if t + 1 < tiles:
            spatial(t + 1, 1)
            activate(t + 1, 0)
        spectral(t, 0)
        if t + 1 < tiles:
            activate(t + 1, 1)
        for i in range(1, groups):
            spectral(t, i)
            project(t, i - 1)
        if t + 2 < tiles:
            patches(t + 2)
    project(tiles - 1, groups - 1)


def vmem(n):
    return [pl.BlockSpec(memory_space=pltpu.VMEM)] * n


def hbm(n):
    return [pl.BlockSpec(memory_space=pltpu.HBM)] * n


def in_hbm(arrays):
    return [pltpu.with_memory_space_constraint(x, pltpu.HBM) for x in arrays]


ANY = pl.BlockSpec(memory_space=pl.ANY)


def on_device(
    spectral_cube,
    aperture,
    measurement,
    shears,
    step_sizes,
    spatial_weight,
    spatial_bias,
    spectral_weight,
    spectral_bias,
    out_weight,
):
    bands, row_count, cols = spectral_cube.shape
    width = measurement.shape[1]
    reach = (width - cols) // LANES + 2
    outer = -(-width // LANES)
    groups = -(-bands // SUB)
    slots = (groups + 1) * SUB
    taps, ch = spectral_weight.shape[:2]
    taps2 = spatial_weight.shape[1]
    count = lax.axis_size("band")
    cube = spectral_cube.reshape(bands, cols)
    shear_row = shears.reshape(1, bands)
    step_row = step_sizes.reshape(1, bands)
    params = pltpu.CompilerParams(vmem_limit_bytes=48 * 2**20)

    tall = -(-outer // SUB) * SUB
    side = (cols // LANES // 2 + 2) * SUB
    inputs = (cube, aperture, measurement, shear_row, step_row)
    part, up, dn, *kept = pl.pallas_call(
        functools.partial(project_kernel, reach),
        out_shape=(
            jax.ShapeDtypeStruct((2 * tall, LANES), BF16),
            jax.ShapeDtypeStruct((2 * tall + side, LANES), BF16),
            jax.ShapeDtypeStruct((2 * tall + side, LANES), BF16),
        )
        + (jax.ShapeDtypeStruct((groups * SUB, cols), BF16),)
        + tuple(jax.ShapeDtypeStruct(x.shape, x.dtype) for x in inputs[1:]),
        in_specs=hbm(5),
        out_specs=tuple(vmem(8)),
        scratch_shapes=[
            pltpu.VMEM((bands, cols), BF16),
            pltpu.VMEM((groups * SUB, cols), F32),
            pltpu.SemaphoreType.DMA((5,)),
        ],
        compiler_params=params,
        name="project",
    )(*in_hbm(inputs))

    def around(x, shift):
        return lax.ppermute(x, "band", [(i, (i + shift) % count) for i in range(count)])

    below = around(up, 1)
    above = around(dn, -1)
    far = [around(part, s) for s in range(2, count - 1)]

    line = pl.pallas_call(
        gate_kernel,
        out_shape=jax.ShapeDtypeStruct(kept[0].shape, BF16),
        in_specs=[ANY, ANY],
        out_specs=ANY,
        input_output_aliases={1: 0},
        compiler_params=pltpu.CompilerParams(vmem_limit_bytes=2**20),
        name="gate",
    )(part, kept[0])

    lines = lax.axis_size(("row", "col"))
    pairs = [(i, i ^ 1) for i in range(lines)]
    others = [(i, (i - 1 + i % 2 * 2) % lines) for i in range(lines)]
    raw1 = lax.ppermute(kept[0], ("row", "col"), others)
    raw0 = lax.ppermute(line, ("row", "col"), pairs)

    small = (
        spatial_weight,
        spatial_bias.reshape(1, ch),
        spectral_weight,
        spectral_bias.reshape(1, ch),
        out_weight.reshape(1, ch),
    )
    reached = (SUB + taps - 1) * ch
    last = (bands - (groups - 1) * SUB + taps - 1) * ch
    main_w, halo_w, first_w, second_w, out_w = pl.pallas_call(
        weights_kernel,
        out_shape=(
            jax.ShapeDtypeStruct((16 * ch, taps2 * 16 + 16), BF16),
            jax.ShapeDtypeStruct((12 * ch, taps2 * 16 + 16), BF16),
            jax.ShapeDtypeStruct((SUB * ch, reached + 16), BF16),
            jax.ShapeDtypeStruct((SUB * ch, last + 16), BF16),
            jax.ShapeDtypeStruct((SUB * ch, LANES), F32),
        ),
        in_specs=[ANY] + hbm(5),
        out_specs=tuple(vmem(5)),
        scratch_shapes=[pltpu.VMEM(x.shape, x.dtype) for x in small]
        + [pltpu.SemaphoreType.DMA((5,))],
        compiler_params=params,
        name="weights",
    )(line, *in_hbm(small))

    words = (outer + 1) * SUB
    message, longer = pl.pallas_call(
        functools.partial(update_kernel, reach, len(far)),
        out_shape=(
            jax.ShapeDtypeStruct((words, LANES), BF16),
            jax.ShapeDtypeStruct((words + EXTRA, LANES), BF16),
        ),
        in_specs=vmem(5) + [ANY] + vmem(len(far)),
        out_specs=tuple(vmem(2)),
        scratch_shapes=[
            pltpu.VMEM((1, outer * LANES), F32),
            pltpu.VMEM((tall, LANES), F32),
        ],
        compiler_params=params,
        cost_estimate=pl.CostEstimate(
            flops=10**10, bytes_accessed=4 * 10**7, transcendentals=0
        ),
        name="update",
    )(*kept[1:3], part, below, above, out_w, *far)

    message0 = lax.ppermute(message, ("row", "col"), pairs)
    message1 = lax.ppermute(longer, ("row", "col"), others)

    tile = 1024

    def renewed(raw, words_of, after, name):
        return pl.pallas_call(
            functools.partial(neighbour_kernel, tile, reach),
            out_shape=jax.ShapeDtypeStruct((3 * slots, cols), BF16),
            in_specs=vmem(4) + [ANY],
            out_specs=vmem(1)[0],
            scratch_shapes=[pltpu.VMEM((slots, cols), BF16), pltpu.VMEM((words, LANES), F32)],
            compiler_params=params,
            cost_estimate=pl.CostEstimate(flops=1, bytes_accessed=1, transcendentals=0),
            name=name,
        )(kept[3], kept[4], raw, words_of, after)

    updated = renewed(kept[0], message, message, "own")
    near0 = renewed(raw0, message0, updated, "partner")

    result = pl.pallas_call(
        functools.partial(denoise_kernel, tile, reach),
        out_shape=jax.ShapeDtypeStruct((bands, cols), BF16),
        in_specs=vmem(11),
        out_specs=vmem(1)[0],
        scratch_shapes=[
            pltpu.VMEM((4, 28 * ch, tile), BF16),
            pltpu.VMEM((slots, cols), BF16),
            pltpu.VMEM((words, LANES), F32),
        ],
        compiler_params=params,
        name="denoise",
    )(
        out_w,
        updated,
        kept[3],
        kept[4],
        near0,
        raw1,
        message1,
        main_w,
        halo_w,
        first_w,
        second_w,
    )
    return result.reshape(bands, 1, cols)


def solution(mesh):
    in_specs = (
        P("band", ("row", "col"), None),
        P(("row", "col"), None),
        P(("row", "col"), None),
        P("band"),
        P("band"),
        P(),
        P(),
        P(),
        P(),
        P(),
    )
    out_specs = P("band", ("row", "col"), None)
    return jax.shard_map(
        on_device, mesh=mesh, in_specs=in_specs, out_specs=out_specs, check_vma=False
    )
```
